32 devices in a mesh: dp: 8 (over y, x, core), tensor: 4 (over z).
Axes of the slice: x: 2, y: 2, z: 4, core: 2. Of those that a mesh axis runs over, the one named last changes fastest.
Arguments:
- tokens: bfloat16 [8192, 2048], P(('dp', 'tensor')), may hold values from -6 to 6
- first_gain: float32 [2048], replicated, may hold values from 0.1 to 1.9
- first_bias: float32 [2048], replicated, may hold values from -3 to 3
- query_weight: bfloat16 [2048, 2048], P(None, 'tensor'), may hold values from -0.125 to 0.125
- key_weight: bfloat16 [2048, 2048], P(None, 'tensor'), may hold values from -0.125 to 0.125
- value_weight: bfloat16 [2048, 3456], P(None, 'tensor'), may hold values from -0.125 to 0.125
- gate_weight: bfloat16 [2048, 3456], P(None, 'tensor'), may hold values from -0.125 to 0.125
- out_weight: bfloat16 [3456, 2048], P('tensor'), may hold values from -0.21875 to 0.21875
- second_gain: float32 [2048], replicated, may hold values from 0.1 to 1.9
- second_bias: float32 [2048], replicated, may hold values from -3 to 3
- hidden_gate: bfloat16 [2048, 3456], P(None, 'tensor'), may hold values from -0.125 to 0.125
- hidden_up: bfloat16 [2048, 3456], P(None, 'tensor'), may hold values from -0.125 to 0.125
- hidden_down: bfloat16 [3456, 2048], P('tensor'), may hold values from -0.21875 to 0.21875
- segments: int32 [8, 1024], P('dp'), may hold values from 0 to 5, as said below
- cotangent: bfloat16 [8192, 2048], P(('dp', 'tensor')), may hold values from -6 to 6
Outputs:
- output: bfloat16 [8192, 2048], P(('dp', 'tensor'))
- grad_tokens: float32 [8192, 2048], P(('dp', 'tensor'))
- grad_first_gain: float32 [2048], replicated
- grad_first_bias: float32 [2048], replicated
- grad_query: float32 [2048, 2048], P(None, 'tensor')
- grad_key: float32 [2048, 2048], P(None, 'tensor')
- grad_value: float32 [2048, 3456], P(None, 'tensor')
- grad_gate: float32 [2048, 3456], P(None, 'tensor')
- grad_out: float32 [3456, 2048], P('tensor')
- grad_second_gain: float32 [2048], replicated
- grad_second_bias: float32 [2048], replicated
- grad_hidden_gate: float32 [2048, 3456], P(None, 'tensor')
- grad_hidden_up: float32 [2048, 3456], P(None, 'tensor')
- grad_hidden_down: float32 [3456, 2048], P('tensor')
The draws below stay inside these ranges and needn't reach their ends.
Inputs may be any that keep to these rules, and one draw needn't show every extreme that they name: `segments`: along each packed sequence the document numbers start at 0 and never fall; every document but the last of a sequence covers 1024 // 5 to 2048 positions.
All inputs are finite; a program needn't handle non-finite values.
Results may differ from the reference program's by a relative error of at most 0.019.
The reference program's roundings to bfloat16 on the way count: a program that leaves them out, or rounds other values in their place, can miss the bound.
Values may be sent and summed in bfloat16 or wider, within the bound.
A program may use at most 256 MiB of HBM per device.

```python
import jax
import jax.numpy as jnp
from jax import lax

D = 2048
H = 8
KD = 256
VD = 432
FF = 3456
SEQ = 1024
NSEQ = 8
TOKENS = 8192


def draw_segments(key, part):
    key = jax.random.fold_in(key, 11)
    doc_lengths = jax.random.randint(key, (NSEQ, 6), SEQ // 5, 2 * SEQ + 1)
    chosen = jax.random.randint(jax.random.fold_in(key, 12), (), 0, NSEQ)
    rows_index = jnp.arange(NSEQ, dtype=jnp.int32)
    doc_lengths = jnp.where(rows_index[:, None] == chosen, SEQ // 5, doc_lengths)
    doc_ends = jnp.cumsum(doc_lengths, axis=1)
    place = jnp.arange(SEQ, dtype=jnp.int32)
    return jnp.sum((place[None, :, None] >= doc_ends[:, None, :]).astype(jnp.int32), axis=2)


def level_of(key, shape, shards, least, largest):
    loudness = 1.0
    for axis_at, shards_of in shards:
        heights = jax.random.uniform(jax.random.fold_in(jax.random.fold_in(key, 6), axis_at), (shards_of,), jnp.float32, least / len(shards), largest / len(shards))
        loudness = loudness * jnp.repeat(jnp.exp(heights), shape[axis_at] // shards_of).reshape((-1,) + (1,) * (len(shape) - 1 - axis_at))
    return loudness


def bell_draw(key, shape, width, limit, pieces=(), held_as=jnp.bfloat16):
    level = level_of(key, shape, pieces, -0.22, 0.18) if pieces else 1.0
    values = jax.random.normal(key, shape, jnp.float32) * width * level
    return jnp.minimum(jnp.maximum(values, -limit), limit).astype(held_as)


def setup_inputs(seed: int = 0) -> dict:
    splits = jax.random.split(jax.random.key(seed), 16)
    return {
        "tokens": bell_draw(splits[0], (TOKENS, D), 1.0, 6.0, ((0, 32),)),
        "first_gain": jnp.clip(1.0 + 0.18 * jax.random.normal(splits[1], (D,), jnp.float32), 0.1, 1.9),
        "first_bias": bell_draw(splits[2], (D,), 0.5, 3.0, (), jnp.float32),
        "query_weight": bell_draw(splits[3], (D, H * KD), D ** -0.5, 0.125, ((1, 4),)),
        "key_weight": bell_draw(splits[4], (D, H * KD), D ** -0.5, 0.125, ((1, 4),)),
        "value_weight": bell_draw(splits[5], (D, H * VD), D ** -0.5, 0.125, ((1, 4),)),
        "gate_weight": bell_draw(splits[6], (D, H * VD), D ** -0.5, 0.125, ((1, 4),)),
        "out_weight": bell_draw(splits[7], (H * VD, D), (H * VD // 4) ** -0.5, 0.21875, ((0, 4),)),
        "second_gain": jnp.clip(1.0 + 0.18 * jax.random.normal(splits[8], (D,), jnp.float32), 0.1, 1.9),
        "second_bias": bell_draw(splits[9], (D,), 0.5, 3.0, (), jnp.float32),
        "hidden_gate": bell_draw(splits[10], (D, FF), D ** -0.5, 0.125, ((1, 4),)),
        "hidden_up": bell_draw(splits[11], (D, FF), D ** -0.5, 0.125, ((1, 4),)),
        "hidden_down": bell_draw(splits[12], (FF, D), (FF // 4) ** -0.5, 0.21875, ((0, 4),)),
        "segments": draw_segments(jax.random.fold_in(splits[15], 71), 0),
        "cotangent": bell_draw(splits[14], (TOKENS, D), 1.0, 6.0, ((0, 32),)),
    }


EPS = 1e-05
GROUP_EPS = 0.1
HIGH = lax.Precision.HIGHEST

@jax.custom_vjp
def low(v):
    return lax.optimization_barrier(v.astype(jnp.bfloat16)).astype(jnp.float32)

@jax.custom_vjp
def low_back(v):
    return v

def low_keep(v):
    return (low(v), None)

def low_pass(kept, grad):
    return (grad,)

def back_keep(v):
    return (v, None)

def back_low(kept, grad):
    return (low(grad),)
low.defvjp(low_keep, low_pass)
low_back.defvjp(back_keep, back_low)

def norm_rows(rows, gain, bias):
    centered = rows - lax.optimization_barrier(jnp.mean(rows, axis=-1, keepdims=True))
    scale = lax.rsqrt(lax.optimization_barrier(jnp.mean(centered * centered, axis=-1, keepdims=True)) + EPS)
    return centered * scale * gain + bias

def decay_table(segments, rates):
    place = jnp.arange(segments.shape[-1], dtype=jnp.int32)
    offset = place[:, None] - place[None, :]
    same_doc = (segments[..., :, None] == segments[..., None, :]) & (offset >= 0)
    distance = jnp.maximum(offset, 0).astype(jnp.float32)
    decay = jnp.where(same_doc[..., None, :, :], jnp.exp(-rates[:, None, None] * distance), 0.0)
    return decay * lax.rsqrt(lax.optimization_barrier(jnp.sum(decay, axis=-1, keepdims=True)))

def normalize_scores(scores, table):
    weighted = scores * table
    total = lax.optimization_barrier(jnp.sum(weighted, axis=-1, keepdims=True))
    return weighted * lax.rsqrt(total * total + 1.0)

def gated_norm(gates, retained):
    centered = retained - lax.optimization_barrier(jnp.mean(retained, axis=-1, keepdims=True))
    normed = centered * lax.rsqrt(lax.optimization_barrier(jnp.mean(centered * centered, axis=-1, keepdims=True)) + GROUP_EPS)
    return jax.nn.silu(gates) * normed

def gelu_product(gate_in, lin_in):
    return jax.nn.gelu(gate_in) * lin_in

def matmul(left, right):
    return jnp.dot(left, right, precision=HIGH, preferred_element_type=jnp.float32)

def forward(rows, table, params):
    first_gain, first_bias, query_weight, key_weight, value_weight, gate_weight, out_weight, second_gain, second_bias, hidden_gate, hidden_up, hidden_down = params
    first = low(norm_rows(rows, first_gain, first_bias))
    queries = low(low_back(matmul(first, query_weight))).reshape(SEQ, H, KD)
    keys_all = low(low_back(matmul(first, key_weight))).reshape(SEQ, H, KD)
    values = low(low_back(matmul(first, value_weight))).reshape(SEQ, H, VD)
    gates = low_back(matmul(first, gate_weight)).reshape(SEQ, H, VD)
    scores = low_back(jnp.einsum('nhk,mhk->hnm', queries, keys_all, precision=HIGH) * KD ** (-0.5))
    retain = low(normalize_scores(scores, table))
    retained = low_back(jnp.einsum('hnm,mhv->nhv', retain, values, precision=HIGH))
    mixed = low(gated_norm(gates, retained).reshape(SEQ, H * VD))
    middle = rows + low_back(matmul(mixed, out_weight))
    second = low(norm_rows(middle, second_gain, second_bias))
    gate_in = low_back(matmul(second, hidden_gate))
    lin_in = low_back(matmul(second, hidden_up))
    inner = low(gelu_product(gate_in, lin_in))
    return middle + matmul(inner, hidden_down)

def reference(tokens, first_gain, first_bias, query_weight, key_weight, value_weight, gate_weight, out_weight, second_gain, second_bias, hidden_gate, hidden_up, hidden_down, segments, cotangent):
    params = tuple((item.astype(jnp.float32) for item in (first_gain, first_bias, query_weight, key_weight, value_weight, gate_weight, out_weight, second_gain, second_bias, hidden_gate, hidden_up, hidden_down)))
    rows_in = tokens.astype(jnp.float32).reshape(NSEQ, SEQ, D)
    seeds = cotangent.astype(jnp.float32).reshape(NSEQ, SEQ, D)
    head_index = jnp.arange(H).astype(jnp.float32)
    rates = -jnp.log1p(-jnp.exp2(-5.0 - head_index))

    def one_sequence(totals, inputs):
        seq_rows, seq_segments, seq_seed = inputs
        table = decay_table(seq_segments, rates)

        def apply_layer(rows, weights):
            return forward(rows, table, weights)
        result, pullback = jax.vjp(apply_layer, seq_rows, params)
        grad_rows, grad_params = pullback(seq_seed)
        totals = jax.tree.map(jnp.add, totals, grad_params)
        return (totals, (result, grad_rows))
    zeros = jax.tree.map(jnp.zeros_like, params)
    totals, (results, grad_rows) = lax.scan(one_sequence, zeros, (rows_in, segments, seeds))
    g_fgain, g_fbias, g_query, g_key, g_value, g_gate, g_out, g_sgain, g_sbias, g_hgate, g_hup, g_hdown = totals
    return (results.reshape(TOKENS, D).astype(jnp.bfloat16), grad_rows.reshape(TOKENS, D), g_fgain, g_fbias, g_query, g_key, g_value, g_gate, g_out, g_sgain, g_sbias, g_hgate, g_hup, g_hdown)
```

```python
import jax
import jax.numpy as jnp
from jax import lax
from jax.sharding import PartitionSpec as P

KD = 256
VD = 432


EPS = 1e-05
GROUP_EPS = 0.1


def norm_parts(rows, gain, bias):
    centered = rows - jnp.mean(rows, axis=-1, keepdims=True)
    scale = lax.rsqrt(jnp.mean(centered * centered, axis=-1, keepdims=True) + EPS)
    normed = centered * scale
    return (normed * gain + bias, normed, scale)


def norm_back(grad_out, gain, normed, scale):
    shaped = grad_out * gain
    return scale * (
        shaped
        - jnp.mean(shaped, axis=-1, keepdims=True)
        - normed * jnp.mean(shaped * normed, axis=-1, keepdims=True)
    )


def decay_table(segments, rates):
    place = jnp.arange(segments.shape[-1], dtype=jnp.int32)
    offset = place[:, None] - place[None, :]
    same_doc = (segments[..., :, None] == segments[..., None, :]) & (offset >= 0)
    distance = jnp.maximum(offset, 0).astype(jnp.float32)
    decay = jnp.where(same_doc[..., None, :, :], jnp.exp(-rates[:, None, None] * distance), 0.0)
    return decay * lax.rsqrt(jnp.sum(decay, axis=-1, keepdims=True))


def normalize_scores(scores, table):
    weighted = scores * table
    total = jnp.sum(weighted, axis=-1, keepdims=True)
    return weighted * lax.rsqrt(total * total + 1.0)


def gated_norm(gates, retained):
    centered = retained - jnp.mean(retained, axis=-1, keepdims=True)
    normed = centered * lax.rsqrt(jnp.mean(centered * centered, axis=-1, keepdims=True) + GROUP_EPS)
    return jax.nn.silu(gates) * normed


def gelu_product(gate_in, lin_in):
    return jax.nn.gelu(gate_in) * lin_in


def product(left, right):
    return jnp.dot(left, right, preferred_element_type=jnp.float32)


def product_nt(left, right):
    return lax.dot_general(
        left, right, (((1,), (1,)), ((), ())), preferred_element_type=jnp.float32
    )


def product_tn(left, right):
    return lax.dot_general(
        left, right, (((0,), (0,)), ((), ())), preferred_element_type=jnp.float32
    )


def scatter_rows(partial):
    summed = lax.psum_scatter(
        partial.astype(jnp.bfloat16), "tensor", scatter_dimension=0, tiled=True
    )
    return summed.astype(jnp.float32)


def sum_dp(after, *grads):
    lows = tuple(grad.astype(jnp.bfloat16) for grad in grads)
    if after:
        lows = lax.optimization_barrier(tuple(after) + lows)[len(after) :]
    return lax.psum(lows, "dp")


def per_device(
    tokens,
    first_gain,
    first_bias,
    query_weight,
    key_weight,
    value_weight,
    gate_weight,
    out_weight,
    second_gain,
    second_bias,
    hidden_gate,
    hidden_up,
    hidden_down,
    segments,
    cotangent,
):
    seq_count, seq_len = segments.shape
    group_rows = seq_count * seq_len
    head_local = query_weight.shape[1] // KD
    scale_factor = KD ** (-0.5)
    inputs = tokens.astype(jnp.float32)
    seed_all = lax.all_gather(cotangent, "tensor", axis=0, tiled=True)
    first_out, first_normed, first_scale = norm_parts(inputs, first_gain, first_bias)
    first_all = lax.all_gather(first_out.astype(jnp.bfloat16), "tensor", axis=0, tiled=True)
    queries = product(first_all, query_weight).astype(jnp.bfloat16)
    keys_low = product(first_all, key_weight).astype(jnp.bfloat16)
    values = product(first_all, value_weight).astype(jnp.bfloat16)
    gates = product(first_all, gate_weight)
    head_index = (lax.axis_index("tensor") * head_local + jnp.arange(head_local)).astype(
        jnp.float32
    )
    rates = -jnp.log1p(-jnp.exp2(-5.0 - head_index))
    table = decay_table(segments, rates)
    query_heads = queries.reshape(seq_count, seq_len, head_local, KD)
    key_heads = keys_low.reshape(seq_count, seq_len, head_local, KD)
    value_heads = values.reshape(seq_count, seq_len, head_local, VD)
    scores = (
        jnp.einsum("bnhk,bmhk->bhnm", query_heads, key_heads, preferred_element_type=jnp.float32)
        * scale_factor
    )

    def score_step(raw):
        return normalize_scores(raw, table)

    retain_full, score_pull = jax.vjp(score_step, scores)
    retain = retain_full.astype(jnp.bfloat16)
    retained = jnp.einsum(
        "bhnm,bmhv->bnhv", retain, value_heads, preferred_element_type=jnp.float32
    )
    gate_heads = gates.reshape(seq_count, seq_len, head_local, VD)
    mixed_full, mix_pull = jax.vjp(gated_norm, gate_heads, retained)
    mixed = mixed_full.reshape(group_rows, head_local * VD).astype(jnp.bfloat16)
    middle = inputs + scatter_rows(product(mixed, out_weight))
    second_out, second_normed, second_scale = norm_parts(middle, second_gain, second_bias)
    second_all = lax.all_gather(second_out.astype(jnp.bfloat16), "tensor", axis=0, tiled=True)
    gate_in = product(second_all, hidden_gate)
    lin_in = product(second_all, hidden_up)
    inner_full, inner_pull = jax.vjp(gelu_product, gate_in, lin_in)
    inner = inner_full.astype(jnp.bfloat16)
    output = (
        middle
        + scatter_rows(product(inner, hidden_down))
    ).astype(jnp.bfloat16)
    grad_inner = product_nt(seed_all, hidden_down)
    grad_hdown = product_tn(inner, seed_all)
    grad_gate_in, grad_lin_in = inner_pull(grad_inner)
    gate_in_low = grad_gate_in.astype(jnp.bfloat16)
    lin_in_low = grad_lin_in.astype(jnp.bfloat16)
    grad_hgate = product_tn(second_all, gate_in_low)
    grad_hup = product_tn(second_all, lin_in_low)
    grad_second = scatter_rows(product_nt(gate_in_low, hidden_gate) + product_nt(lin_in_low, hidden_up))
    grad_hdown, grad_hgate, grad_hup = sum_dp((), grad_hdown, grad_hgate, grad_hup)
    grad_sgain = jnp.sum(grad_second * second_normed, axis=0)
    grad_sbias = jnp.sum(grad_second, axis=0)
    grad_middle = cotangent.astype(jnp.float32) + norm_back(
        grad_second, second_gain, second_normed, second_scale
    )
    branch_all = lax.all_gather(grad_middle.astype(jnp.bfloat16), "tensor", axis=0, tiled=True)
    grad_mixed = product_nt(branch_all, out_weight)
    grad_outw = product_tn(mixed, branch_all)
    (grad_outw,) = sum_dp((grad_hdown, grad_hgate, grad_hup), grad_outw)
    grad_gates, grad_retained = mix_pull(grad_mixed.reshape(seq_count, seq_len, head_local, VD))
    gates_low = grad_gates.reshape(group_rows, head_local * VD).astype(jnp.bfloat16)
    retained_low = grad_retained.astype(jnp.bfloat16)
    grad_retain = jnp.einsum(
        "bnhv,bmhv->bhnm", retained_low, value_heads, preferred_element_type=jnp.float32
    )
    grad_values = jnp.einsum(
        "bhnm,bnhv->bmhv", retain, retained_low, preferred_element_type=jnp.float32
    )
    values_low = grad_values.reshape(group_rows, head_local * VD).astype(jnp.bfloat16)
    (grad_scores,) = score_pull(grad_retain)
    scores_low = grad_scores.astype(jnp.bfloat16)
    grad_queries = (
        jnp.einsum("bhnm,bmhk->bnhk", scores_low, key_heads, preferred_element_type=jnp.float32)
        * scale_factor
    )
    grad_keys = (
        jnp.einsum("bhnm,bnhk->bmhk", scores_low, query_heads, preferred_element_type=jnp.float32)
        * scale_factor
    )
    queries_low = grad_queries.reshape(group_rows, head_local * KD).astype(jnp.bfloat16)
    keys_back = grad_keys.reshape(group_rows, head_local * KD).astype(jnp.bfloat16)
    grad_queryw = product_tn(first_all, queries_low)
    grad_keyw = product_tn(first_all, keys_back)
    grad_valuew = product_tn(first_all, values_low)
    grad_gatew = product_tn(first_all, gates_low)
    total = product_nt(queries_low, query_weight)
    total = total + product_nt(keys_back, key_weight)
    total = total + product_nt(values_low, value_weight)
    grad_first = scatter_rows(total + product_nt(gates_low, gate_weight))
    grad_fgain = jnp.sum(grad_first * first_normed, axis=0)
    grad_fbias = jnp.sum(grad_first, axis=0)
    grad_tokens = grad_middle + norm_back(grad_first, first_gain, first_normed, first_scale)
    grad_valuew, grad_gatew, grad_queryw, grad_keyw = sum_dp(
        (grad_outw,), grad_valuew, grad_gatew, grad_queryw, grad_keyw
    )
    grad_queryw, grad_keyw, grad_valuew, grad_gatew, grad_outw, grad_hgate, grad_hup, grad_hdown = (
        item.astype(jnp.float32)
        for item in (
            grad_queryw,
            grad_keyw,
            grad_valuew,
            grad_gatew,
            grad_outw,
            grad_hgate,
            grad_hup,
            grad_hdown,
        )
    )
    grad_fgain, grad_fbias, grad_sgain, grad_sbias = lax.psum(
        (grad_fgain, grad_fbias, grad_sgain, grad_sbias), ("dp", "tensor")
    )
    return (
        output,
        grad_tokens,
        grad_fgain,
        grad_fbias,
        grad_queryw,
        grad_keyw,
        grad_valuew,
        grad_gatew,
        grad_outw,
        grad_sgain,
        grad_sbias,
        grad_hgate,
        grad_hup,
        grad_hdown,
    )


def solution(mesh):
    return jax.shard_map(
        per_device,
        mesh=mesh,
        in_specs=(
            P(("dp", "tensor"), None),
            P(),
            P(),
            P(None, "tensor"),
            P(None, "tensor"),
            P(None, "tensor"),
            P(None, "tensor"),
            P("tensor", None),
            P(),
            P(),
            P(None, "tensor"),
            P(None, "tensor"),
            P("tensor", None),
            P("dp", None),
            P(("dp", "tensor"), None),
        ),
        out_specs=(
            P(("dp", "tensor"), None),
            P(("dp", "tensor"), None),
            P(),
            P(),
            P(None, "tensor"),
            P(None, "tensor"),
            P(None, "tensor"),
            P(None, "tensor"),
            P("tensor", None),
            P(),
            P(),
            P(None, "tensor"),
            P(None, "tensor"),
            P("tensor", None),
        ),
        check_vma=False,
    )
```

```python
import functools
import itertools

import jax
import jax.numpy as jnp
from jax import lax
from jax.experimental import pallas as pl
from jax.experimental.pallas import tpu as pltpu
from jax.sharding import PartitionSpec as P

KD = 256
VD = 432


EPS = 1e-05
GROUP_EPS = 0.1
GELU_SCALE = 0.7978845608028654
CHUNKS = 4

MESH = pl.DeviceIdType.MESH
VMEM_BYTES = 60 * 2**20
TILE = 256
LINE = 16


def norm_parts(rows, gain, bias):
    centered = rows - jnp.mean(rows, axis=-1, keepdims=True)
    scale = lax.rsqrt(jnp.mean(centered * centered, axis=-1, keepdims=True) + EPS)
    normed = centered * scale
    return (normed * gain + bias, normed, scale)


def norm_back(grad_out, gain, normed, scale):
    shaped = grad_out * gain
    return scale * (
        shaped
        - jnp.mean(shaped, axis=-1, keepdims=True)
        - normed * jnp.mean(shaped * normed, axis=-1, keepdims=True)
    )


def decay_table(segments, rates):
    place = jnp.arange(segments.shape[-1], dtype=jnp.int32)
    offset = place[:, None] - place[None, :]
    same_doc = (segments[..., :, None] == segments[..., None, :]) & (offset >= 0)
    distance = jnp.maximum(offset, 0).astype(jnp.float32)
    decay = jnp.where(same_doc[..., None, :, :], jnp.exp(-rates[:, None, None] * distance), 0.0)
    return decay * lax.rsqrt(jnp.sum(decay, axis=-1, keepdims=True))


def normalize_scores(scores, table):
    weighted = scores * table
    total = jnp.sum(weighted, axis=-1, keepdims=True)
    return weighted * lax.rsqrt(total * total + 1.0)


def gated_norm(gates, retained):
    centered = retained - jnp.mean(retained, axis=-1, keepdims=True)
    normed = centered * lax.rsqrt(jnp.mean(centered * centered, axis=-1, keepdims=True) + GROUP_EPS)
    return jax.nn.silu(gates) * normed


def product(left, right):
    return jnp.dot(left, right, preferred_element_type=jnp.float32)


def product_nt(left, right):
    return lax.dot_general(
        left, right, (((1,), (1,)), ((), ())), preferred_element_type=jnp.float32
    )


def product_tn(left, right):
    return lax.dot_general(
        left, right, (((0,), (0,)), ((), ())), preferred_element_type=jnp.float32
    )


def for_columns(width, body):
    full = width // TILE

    def step(index, carry):
        body(pl.multiple_of(index * TILE, TILE), TILE)
        return carry

    if full:
        lax.fori_loop(0, full, step, 0)
    if width % TILE:
        body(full * TILE, width % TILE)


def for_rows(count, body):
    def step(index, carry):
        body(pl.ds(pl.multiple_of(index * LINE, LINE), LINE))
        return carry

    lax.fori_loop(0, count // LINE, step, 0)


def dot_nn(left, right):
    return lax.dot_general(left, right, (((1,), (0,)), ((), ())), preferred_element_type=jnp.float32)


def dot_nt(left, right):
    return lax.dot_general(left, right, (((1,), (1,)), ((), ())), preferred_element_type=jnp.float32)


def enter(peers, line):
    barrier = pltpu.get_barrier_semaphore()
    for peer in peers:
        pl.semaphore_signal(barrier, inc=1, device_id=peer, device_id_type=MESH)
    if line is not None:
        size, me = line

        @pl.when(me > 0)
        def _():
            pl.semaphore_signal(barrier, inc=1, device_id={"tensor": me - 1}, device_id_type=MESH)

        @pl.when(me < size - 1)
        def _():
            pl.semaphore_signal(barrier, inc=1, device_id={"tensor": me + 1}, device_id_type=MESH)

    count = len(peers)
    if line is not None:
        count = count + (me > 0).astype(jnp.int32) + (me < size - 1).astype(jnp.int32)
    pl.semaphore_wait(barrier, count)


class LineScatter:
    def __init__(self, size, me, rows, part, inbox, send, recv):
        self.size, self.me, self.rows = size, me, rows
        self.part, self.inbox, self.send, self.recv = part, inbox, send, recv

    def at(self, chunk):
        return pl.ds(chunk * self.rows, self.rows)

    def copy(self, target, slot, chunk, device):
        return pltpu.make_async_remote_copy(
            src_ref=self.part.at[target, self.at(chunk)],
            dst_ref=self.inbox.at[slot, self.at(chunk)],
            send_sem=self.send.at[target, chunk],
            recv_sem=self.recv.at[slot, chunk],
            device_id={"tensor": device},
            device_id_type=MESH,
        )

    def add(self, target, chunk):
        def body(rows):
            at = pl.ds(chunk * self.rows + rows.start, LINE)
            total = self.part[target, at, :].astype(jnp.float32)
            total = total + self.inbox[target, at, :].astype(jnp.float32)
            self.part[target, at, :] = total.astype(jnp.bfloat16)

        for_rows(self.rows, body)

    def go_right(self, chunk, target):
        self.copy(target, target, chunk, self.me + 1).start()

    def go_left(self, chunk, target):
        last = self.me - 1 == target
        self.copy(target, jnp.where(last, self.size, target), chunk, self.me - 1).start()

    def begin(self, chunk):
        @pl.when(self.me == 0)
        def _():
            for target in range(self.size - 1, 0, -1):
                self.go_right(chunk, target)

        @pl.when(self.me == self.size - 1)
        def _():
            for target in range(self.size - 1):
                self.go_left(chunk, target)

    def put(self, chunk, step):
        size, me = self.size, self.me
        right, left = size - 1 - step, step

        @pl.when((me < right) & (me > 0))
        def _():
            self.copy(right, right, chunk, me).wait_recv()
            self.add(right, chunk)
            self.go_right(chunk, right)

        @pl.when((me > left) & (me < size - 1))
        def _():
            self.copy(left, left, chunk, me).wait_recv()
            self.add(left, chunk)
            self.go_left(chunk, left)

    def arrive(self, chunk):
        size, me = self.size, self.me

        @pl.when(me > 0)
        def _():
            self.copy(me, me, chunk, me - 1).wait_recv()

        @pl.when(me < size - 1)
        def _():
            self.copy(me, size, chunk, me + 1).wait_recv()

    def total(self, rows):
        size, me = self.size, self.me
        own = self.part[me, rows, :].astype(jnp.float32)
        low = self.inbox[me, rows, :].astype(jnp.float32)
        high = self.inbox[size, rows, :].astype(jnp.float32)
        return own + jnp.where(me > 0, low, 0.0) + jnp.where(me < size - 1, high, 0.0)

    def drain(self, chunk):
        for target in range(self.size):

            @pl.when(self.me != target)
            def _():
                self.copy(target, target, chunk, self.me).wait_send()


class LineGather:
    def __init__(self, size, me, rows, held, send, recv):
        self.size, self.me, self.rows = size, me, rows
        self.held, self.send, self.recv = held, send, recv

    def copy(self, block, chunk, way, device):
        at = pl.ds(chunk * self.rows, self.rows)
        return pltpu.make_async_remote_copy(
            src_ref=self.held.at[block, at],
            dst_ref=self.held.at[block, at],
            send_sem=self.send.at[way, block, chunk],
            recv_sem=self.recv.at[block, chunk],
            device_id={"tensor": device},
            device_id_type=MESH,
        )

    def put(self, chunk, step):
        size, me = self.size, self.me

        @pl.when(me >= step)
        def _():
            if step:
                self.copy(me - step, chunk, 0, me).wait_recv()

            @pl.when(me < size - 1)
            def _():
                self.copy(me - step, chunk, 0, me + 1).start()

        @pl.when(me + step < size)
        def _():
            if step:
                self.copy(me + step, chunk, 1, me).wait_recv()

            @pl.when(me > 0)
            def _():
                self.copy(me + step, chunk, 1, me - 1).start()

    def drain(self, chunk):
        size, me = self.size, self.me
        for step in range(size):

            @pl.when((me >= step) & (me < size - 1))
            def _():
                self.copy(me - step, chunk, 0, me + 1).wait_send()

            @pl.when((me + step < size) & (me > 0))
            def _():
                self.copy(me + step, chunk, 1, me - 1).wait_send()


class CubeSum:
    def __init__(self, bits, me, sources, results, parts, firsts, nexts, load, store, send, recv, free):
        self.bits, self.me = bits, me
        self.sources, self.results, self.parts = sources, results, parts
        self.firsts, self.nexts = firsts, nexts
        self.load_sem, self.store_sem, self.send, self.recv = load, store, send, recv
        self.free = free
        self.orders = (tuple(range(bits)), (0,) + tuple(range(bits - 1, 0, -1)))
        self.mine = [(me // 2**bit) % 2 for bit in range(bits)]
        self.steps = 2 * bits + 1

    def partner(self, bit):
        return self.me + (1 - 2 * self.mine[bit]) * 2**bit

    def band(self, which, color):
        count = self.parts[which].shape[-2]
        cut = cut_rows(count)
        return ((0, cut), (cut, count - cut), (0, count))[color]

    def lead(self, fixed):
        return tuple(fixed.get(bit, slice(None)) for bit in range(self.bits - 1, -1, -1))

    def moved(self, src, dst, which, color, step, bit):
        return pltpu.make_async_remote_copy(
            src_ref=src,
            dst_ref=dst,
            send_sem=self.send.at[which, color % 2, step],
            recv_sem=self.recv.at[which, color % 2, step],
            device_id={"dp": self.partner(bit)},
            device_id_type=MESH,
        )

    def halve(self, which, color, step):
        order = self.orders[color % 2]
        start, count = self.band(which, color)
        fixed = {bit: self.mine[bit] for bit in order[:step]}
        fixed[order[step]] = 1 - self.mine[order[step]]
        src = self.parts[which].at[self.lead(fixed) + (pl.ds(start, count), slice(None))]
        dst = self.firsts[which] if step == 0 else self.nexts[which][color][step - 1]
        return self.moved(src, dst, which, color, step, order[step])

    def double(self, which, color, step):
        order = self.orders[color % 2]
        start, count = self.band(which, color)
        fixed = {bit: self.mine[bit] for bit in order[: step + 1]}
        held = self.parts[which].at[self.lead(fixed) + (pl.ds(start, count), slice(None))]
        return self.moved(held, held, which, color, 2 * self.bits - 1 - step, order[step])

    def freed(self, which, color, step):
        return self.free.at[which, color % 2, step]

    def land(self, which, color, step):
        copy = self.halve(which, color, step)
        copy.wait_send()
        partner = {"dp": self.partner(self.orders[color % 2][step])}
        pl.semaphore_signal(
            self.freed(which, color, step), inc=1, device_id=partner, device_id_type=MESH
        )
        copy.wait_recv()
        self.add(which, color, step)

    def grow(self, which, color, step):
        pl.semaphore_wait(self.freed(which, color, step), 1)
        self.double(which, color, step).start()

    def add(self, which, color, step):
        order = self.orders[color % 2]
        part, (start, count) = self.parts[which], self.band(which, color)
        box = self.firsts[which] if step == 0 else self.nexts[which][color][step - 1]
        fixed = {bit: self.mine[bit] for bit in order[: step + 1]}
        free = [bit for bit in range(self.bits - 1, -1, -1) if bit not in fixed]
        for choice in itertools.product((0, 1), repeat=len(free)):
            lead = self.lead({**fixed, **dict(zip(free, choice))})

            def body(begin, size):
                there = lead + (pl.ds(start + begin, size), slice(None))
                total = part[there].astype(jnp.float32)
                total = total + box[choice + (pl.ds(begin, size), slice(None))].astype(jnp.float32)
                part[there] = total.astype(jnp.bfloat16)

            for_blocks(count, part.shape[-1], body)

    def slices(self, which, ref):
        rows, columns = self.parts[which].shape[-2:]
        for index in range(2**self.bits):
            lead = tuple((index >> bit) & 1 for bit in range(self.bits - 1, -1, -1))
            if ref.shape[0] == rows:
                whole = ref.at[:, pl.ds(index * columns, columns)]
            else:
                whole = ref.at[pl.ds(index * rows, rows), :]
            yield index, self.parts[which].at[lead], whole

    def load(self, which):
        for index, part, whole in self.slices(which, self.sources[which]):
            pltpu.make_async_copy(whole, part, self.load_sem.at[which, index]).start()

    def step(self, which, stage):
        bits = self.bits
        if stage == 0:
            for index, part, whole in self.slices(which, self.sources[which]):
                pltpu.make_async_copy(whole, part, self.load_sem.at[which, index]).wait()
            self.halve(which, 2, 0).start()
        elif stage < bits:
            if stage == 1:
                self.land(which, 2, 0)
            for color in range(2):
                if stage > 1:
                    self.land(which, color, stage - 1)
                self.halve(which, color, stage).start()
        elif stage < 2 * bits - 1:
            back = 2 * bits - 1 - stage
            for color in range(2):
                if back == bits - 1:
                    self.land(which, color, back)
                else:
                    self.double(which, color, back + 1).wait_recv()
                self.grow(which, color, back)
        elif stage == 2 * bits - 1:
            for color in range(2):
                self.double(which, color, 1).wait_recv()
            self.grow(which, 2, 0)
        else:
            self.double(which, 2, 0).wait_recv()
            for index, part, whole in self.slices(which, self.results[which]):
                pltpu.make_async_copy(part, whole, self.store_sem.at[which, index]).start()

    def calls(self):
        for tick in range(len(self.parts) + self.steps - 1):
            for stage in range(self.steps - 1, -1, -1):
                if 0 <= tick - stage < len(self.parts):
                    yield functools.partial(self.step, tick - stage, stage)

    def drain(self):
        for which in range(len(self.parts)):
            self.double(which, 2, 0).wait_send()
            for color in range(2):
                for step in range(1, self.bits):
                    self.double(which, color, step).wait_send()
            for index, part, whole in self.slices(which, self.results[which]):
                pltpu.make_async_copy(part, whole, self.store_sem.at[which, index]).wait()


def cut_rows(count):
    return count // (2 * LINE) * LINE


def for_blocks(count, columns, body):
    size = LINE
    while count % (2 * size) == 0 and 2 * size * columns <= 2**14:
        size *= 2
    for factor in (3, 5):
        if count % (factor * size) == 0 and factor * size * columns <= 2**14:
            size *= factor

    def step(index, carry):
        body(pl.multiple_of(index * size, LINE), size)
        return carry

    lax.fori_loop(0, count // size, step, 0)


def cube_scratch(bits, shapes):
    low = jnp.bfloat16
    parts, firsts, nexts = [], [], []
    for rows, columns in shapes:
        if columns >= rows:
            columns = columns // 2**bits
        else:
            rows = rows // 2**bits
        cut = cut_rows(rows)
        parts.append(pltpu.VMEM((2,) * bits + (rows, columns), low))
        firsts.append(pltpu.VMEM((2,) * (bits - 1) + (rows, columns), low))
        nexts.append(
            [
                [
                    pltpu.VMEM((2,) * (bits - 1 - step) + (count, columns), low)
                    for step in range(1, bits)
                ]
                for count in (cut, rows - cut)
            ]
        )
    dma = pltpu.SemaphoreType.DMA
    return [
        parts,
        firsts,
        nexts,
        dma((len(shapes), 2**bits)),
        dma((len(shapes), 2**bits)),
        dma((len(shapes), 2, 2 * bits)),
        dma((len(shapes), 2, 2 * bits)),
        pltpu.SemaphoreType.REGULAR((len(shapes), 2, bits)),
    ]


def interleave(first, second):
    places = [((index + 0.5) / len(first), call) for index, call in enumerate(first)]
    places += [((index + 0.5) / len(second), call) for index, call in enumerate(second)]
    for _, call in sorted(places, key=lambda item: item[0]):
        call()


def feed_kernel(
    size,
    chunks,
    mixed_hbm,
    out_hbm,
    tokens_hbm,
    seed_hbm,
    gate_hbm,
    up_hbm,
    down_hbm,
    gain_ref,
    bias_ref,
    second_hbm,
    seeds_hbm,
    inner_hbm,
    dgate_hbm,
    dlin_hbm,
    dsecond_hbm,
    outp_hbm,
    middle_ref,
    mixed,
    out_weight,
    tokens,
    hidden_gate,
    hidden_up,
    hidden_down,
    second,
    seeds,
    part,
    inbox,
    gate_in,
    lin_in,
    dinner,
    inner,
    dgate,
    dlin,
    wide,
    load_sem,
    store_sem,
    rs_send,
    rs_recv,
    ag_send,
    ag_recv,
    seed_send,
    seed_recv,
):
    me = lax.axis_index("tensor")
    own, depth = tokens.shape
    rows = own // chunks
    hidden = inner.shape[-1]
    loads = [
        pltpu.make_async_copy(src, dst, load_sem.at[index])
        for index, (src, dst) in enumerate(
            (
                (mixed_hbm, mixed),
                (out_hbm, out_weight),
                (seed_hbm, seeds.at[me]),
                (tokens_hbm, tokens),
                (gate_hbm, hidden_gate),
                (up_hbm, hidden_up),
                (down_hbm, hidden_down),
            )
        )
    ]
    for load in loads:
        load.start()
    enter((), (size, me))
    scatter = LineScatter(size, me, rows, part, inbox, rs_send, rs_recv)
    gather = LineGather(size, me, rows, second, ag_send, ag_recv)
    gather_seed = LineGather(size, me, rows, seeds, seed_send, seed_recv)

    def at(chunk):
        return pl.ds(chunk * rows, rows)

    def flat(ref, chunk):
        value = ref[:, at(chunk), :]
        return value.reshape(size * rows, value.shape[-1])

    def store(kind, chunk):
        slot = chunk % 2
        src, dst = (
            (second.at[:, at(chunk)], second_hbm),
            (seeds.at[:, at(chunk)], seeds_hbm),
            (inner.at[slot], inner_hbm),
            (dgate.at[slot], dgate_hbm),
            (dlin.at[slot], dlin_hbm),
            (wide.at[slot, 0], dsecond_hbm),
            (wide.at[slot, 1], outp_hbm),
        )[kind]
        return pltpu.make_async_copy(src, dst.at[:, at(chunk)], store_sem.at[kind, chunk])

    def project(chunk):
        def body(start, width):
            value = dot_nn(flat(mixed, chunk), out_weight[:, pl.ds(start, width)])
            part[:, at(chunk), pl.ds(start, width)] = value.astype(jnp.bfloat16).reshape(
                size, rows, width
            )

        for_columns(depth, body)

    def normalize(chunk):
        scatter.arrive(chunk)

        def body(block):
            here = pl.ds(chunk * rows + block.start, LINE)
            middle = tokens[here, :].astype(jnp.float32) + scatter.total(here)
            middle_ref[here, :] = middle
            centered = middle - jnp.mean(middle, axis=-1, keepdims=True)
            scale = lax.rsqrt(jnp.mean(centered * centered, axis=-1, keepdims=True) + EPS)
            value = centered * scale * gain_ref[...] + bias_ref[...]
            second[me, here, :] = value.astype(jnp.bfloat16)

        for_rows(rows, body)
        gather.put(chunk, 0)

    def feed(chunk):
        slot = chunk % 2
        if chunk >= 2:
            for kind in range(2, 7):
                store(kind, chunk - 2).wait()
        def body_in(start, width):
            columns = pl.ds(start, width)
            left = flat(second, chunk)
            gate_in[:, columns] = dot_nt(left, hidden_gate[columns, :])
            lin_in[:, columns] = dot_nt(left, hidden_up[columns, :])
            dinner[:, columns] = dot_nt(flat(seeds, chunk), hidden_down[columns, :])

        for_columns(hidden, body_in)

        def body_act(block):
            gate, lin, grad = gate_in[block, :], lin_in[block, :], dinner[block, :]
            cube = GELU_SCALE * (gate + 0.044715 * (gate * gate * gate))
            tanh = jnp.tanh(cube)
            half = 0.5 * (1.0 + tanh)
            active = gate * half
            slope = half + 0.5 * gate * (1.0 - tanh * tanh) * (
                GELU_SCALE * (1.0 + 3.0 * 0.044715 * (gate * gate))
            )
            owner = block.start // rows
            inside = pl.ds(block.start - owner * rows, LINE)
            inner[slot, owner, inside, :] = (active * lin).astype(jnp.bfloat16)
            dlin[slot, owner, inside, :] = (grad * active).astype(jnp.bfloat16)
            dgate[slot, owner, inside, :] = (grad * lin * slope).astype(jnp.bfloat16)

        for_rows(size * rows, body_act)
        def body_out(start, width):
            columns = pl.ds(start, width)
            inner_all = inner[slot].reshape(size * rows, hidden)
            dgate_all = dgate[slot].reshape(size * rows, hidden)
            dlin_all = dlin[slot].reshape(size * rows, hidden)
            grad = dot_nn(dgate_all, hidden_gate[:, columns])
            grad = grad + dot_nn(dlin_all, hidden_up[:, columns])
            wide[slot, 0, :, :, columns] = grad.astype(jnp.bfloat16).reshape(size, rows, width)
            value = dot_nn(inner_all, hidden_down[:, columns])
            wide[slot, 1, :, :, columns] = value.astype(jnp.bfloat16).reshape(size, rows, width)

        for_columns(depth, body_out)
        for kind in range(7):
            store(kind, chunk).start()

    loads[2].wait()
    gather_seed.put(0, 0)
    loads[0].wait()
    loads[1].wait()
    project(0)
    scatter.begin(0)
    for tick in range(chunks + 1):
        for step in range(size - 1):
            if tick < chunks:
                scatter.put(tick, step)
            if tick:
                gather.put(tick - 1, step + 1)
            if tick < chunks and step:
                gather_seed.put(tick, step)
        if tick == 0:
            loads[3].wait()
        if tick < chunks:
            normalize(tick)
            gather_seed.put(tick, size - 1)
        if tick < chunks - 1:
            project(tick + 1)
            scatter.begin(tick + 1)
            gather_seed.put(tick + 1, 0)
        if tick == 0:
            for load in loads[4:]:
                load.wait()
        if tick:
            feed(tick - 1)
    for chunk in range(chunks):
        scatter.drain(chunk)
        gather.drain(chunk)
        gather_seed.drain(chunk)
        for kind in range(7 if chunk >= chunks - 2 else 2):
            store(kind, chunk).wait()


def feed_forward(size, chunks, mixed, out_weight, tokens, cotangent, hidden_gate, hidden_up, hidden_down, gain, bias):
    own, depth = tokens.shape
    hidden = hidden_gate.shape[0]
    rows = own // chunks
    low, full = jnp.bfloat16, jnp.float32

    def blocks(width):
        return jax.ShapeDtypeStruct((size, own, width), low)

    dma = pltpu.SemaphoreType.DMA
    wide, thin = (size, own, depth), (2, size, rows, hidden)
    return pl.pallas_call(
        functools.partial(feed_kernel, size, chunks),
        out_shape=(
            blocks(depth),
            blocks(depth),
            blocks(hidden),
            blocks(hidden),
            blocks(hidden),
            blocks(depth),
            blocks(depth),
            jax.ShapeDtypeStruct((own, depth), full),
        ),
        in_specs=[pl.BlockSpec(memory_space=pl.ANY)] * 7
        + [pl.BlockSpec(memory_space=pltpu.VMEM)] * 2,
        out_specs=(pl.BlockSpec(memory_space=pl.ANY),) * 7
        + (pl.BlockSpec(memory_space=pltpu.VMEM),),
        scratch_shapes=[
            pltpu.VMEM((size, own, mixed.shape[-1]), low),
            pltpu.VMEM(out_weight.shape, low),
            pltpu.VMEM((own, depth), low),
            pltpu.VMEM((hidden, depth), low),
            pltpu.VMEM((hidden, depth), low),
            pltpu.VMEM((hidden, depth), low),
            pltpu.VMEM(wide, low),
            pltpu.VMEM(wide, low),
            pltpu.VMEM(wide, low),
            pltpu.VMEM((size + 1, own, depth), low),
            pltpu.VMEM((size * rows, hidden), full),
            pltpu.VMEM((size * rows, hidden), full),
            pltpu.VMEM((size * rows, hidden), full),
            pltpu.VMEM(thin, low),
            pltpu.VMEM(thin, low),
            pltpu.VMEM(thin, low),
            pltpu.VMEM((2, 2, size, rows, depth), low),
            dma((7,)),
            dma((7, chunks)),
            dma((size, chunks)),
            dma((size + 1, chunks)),
            dma((2, size, chunks)),
            dma((size, chunks)),
            dma((2, size, chunks)),
            dma((size, chunks)),
        ],
        compiler_params=pltpu.CompilerParams(
            collective_id=0, has_side_effects=True, vmem_limit_bytes=VMEM_BYTES
        ),
        cost_estimate=pl.CostEstimate(
            flops=14 * size * own * depth * hidden, bytes_accessed=2**26, transcendentals=0
        ),
    )(mixed, out_weight, tokens, cotangent, hidden_gate, hidden_up, hidden_down, gain, bias)


def back_kernel(
    size,
    bits,
    chunks,
    dsecond_hbm,
    out_hbm,
    middle_ref,
    seed_ref,
    gain_ref,
    grads_hbm,
    branch_hbm,
    dmixed_hbm,
    dmiddle_ref,
    sums_ref,
    totals_hbm,
    part,
    out_weight,
    branch,
    inbox,
    dmixed,
    load_sem,
    store_sem,
    rs_send,
    rs_recv,
    ag_send,
    ag_recv,
    cube_parts,
    cube_firsts,
    cube_nexts,
    cube_load,
    cube_store,
    cube_send,
    cube_recv,
    cube_free,
):
    me = lax.axis_index("tensor")
    own, depth = seed_ref.shape
    rows = own // chunks
    load_part = pltpu.make_async_copy(dsecond_hbm, part, load_sem.at[0])
    load_out = pltpu.make_async_copy(out_hbm, out_weight, load_sem.at[1])
    load_part.start()
    cube = CubeSum(
        bits,
        lax.axis_index("dp"),
        grads_hbm,
        totals_hbm,
        cube_parts,
        cube_firsts,
        cube_nexts,
        cube_load,
        cube_store,
        cube_send,
        cube_recv,
        cube_free,
    )
    for which in range(len(cube_parts)):
        cube.load(which)
    load_out.start()
    enter([{"dp": cube.partner(bit)} for bit in range(bits)], (size, me))
    scatter = LineScatter(size, me, rows, part, inbox, rs_send, rs_recv)
    gather = LineGather(size, me, rows, branch, ag_send, ag_recv)

    def at(chunk):
        return pl.ds(chunk * rows, rows)

    def store(kind, chunk):
        if kind == 0:
            src, dst = branch.at[:, at(chunk)], branch_hbm
        else:
            src, dst = dmixed.at[chunk % 2], dmixed_hbm
        return pltpu.make_async_copy(src, dst.at[:, at(chunk)], store_sem.at[kind, chunk])

    def normalize(chunk):
        scatter.arrive(chunk)

        def body(block):
            here = pl.ds(chunk * rows + block.start, LINE)
            middle = middle_ref[here, :]
            centered = middle - jnp.mean(middle, axis=-1, keepdims=True)
            scale = lax.rsqrt(jnp.mean(centered * centered, axis=-1, keepdims=True) + EPS)
            normed = centered * scale
            grad = scatter.total(here)
            shaped = grad * gain_ref[...]
            sums_ref[0:1, :] += jnp.sum(grad * normed, axis=0, keepdims=True)
            sums_ref[1:2, :] += jnp.sum(grad, axis=0, keepdims=True)
            dmiddle = seed_ref[here, :].astype(jnp.float32) + scale * (
                shaped
                - jnp.mean(shaped, axis=-1, keepdims=True)
                - normed * jnp.mean(shaped * normed, axis=-1, keepdims=True)
            )
            dmiddle_ref[here, :] = dmiddle
            branch[me, here, :] = dmiddle.astype(jnp.bfloat16)

        for_rows(rows, body)
        gather.put(chunk, 0)

    def unproject(chunk):
        if chunk >= 2:
            store(1, chunk - 2).wait()

        def body(start, width):
            columns = pl.ds(start, width)
            left = branch[:, at(chunk), :].reshape(size * rows, depth)
            value = dot_nt(left, out_weight[columns, :])
            dmixed[chunk % 2, :, :, columns] = value.reshape(size, rows, width)

        for_columns(out_weight.shape[0], body)
        for kind in range(2):
            store(kind, chunk).start()

    def line_calls():
        for tick in range(chunks + 1):
            for step in range(size - 1):
                if tick < chunks:
                    yield functools.partial(scatter.put, tick, step)
                if tick:
                    yield functools.partial(gather.put, tick - 1, step + 1)
            if tick < chunks - 1:
                yield functools.partial(scatter.begin, tick + 1)
            if tick < chunks:
                yield functools.partial(normalize, tick)
            if tick == 0:
                yield load_out.wait
            if tick:
                yield functools.partial(unproject, tick - 1)

    sums_ref[...] = jnp.zeros_like(sums_ref)
    load_part.wait()
    scatter.begin(0)
    interleave(list(cube.calls()), list(line_calls()))
    for chunk in range(chunks):
        scatter.drain(chunk)
        gather.drain(chunk)
        for kind in range(2 if chunk >= chunks - 2 else 1):
            store(kind, chunk).wait()
    cube.drain()


def feed_back(size, bits, chunks, dsecond, out_weight, middle, cotangent, gain, grads):
    own, depth = cotangent.shape
    rows = own // chunks
    width = out_weight.shape[0]
    low, full = jnp.bfloat16, jnp.float32
    dma = pltpu.SemaphoreType.DMA
    vmem, anywhere = pl.BlockSpec(memory_space=pltpu.VMEM), pl.BlockSpec(memory_space=pl.ANY)
    many = [anywhere] * len(grads)
    return pl.pallas_call(
        functools.partial(back_kernel, size, bits, chunks),
        out_shape=(
            jax.ShapeDtypeStruct((size, own, depth), low),
            jax.ShapeDtypeStruct((size, own, width), full),
            jax.ShapeDtypeStruct((own, depth), full),
            jax.ShapeDtypeStruct((8, depth), full),
            [jax.ShapeDtypeStruct(grad.shape, low) for grad in grads],
        ),
        in_specs=[anywhere, anywhere, vmem, vmem, vmem, many],
        out_specs=(anywhere, anywhere, vmem, vmem, many),
        scratch_shapes=[
            pltpu.VMEM((size, own, depth), low),
            pltpu.VMEM(out_weight.shape, low),
            pltpu.VMEM((size, own, depth), low),
            pltpu.VMEM((size + 1, own, depth), low),
            pltpu.VMEM((2, size, rows, width), full),
            dma((2,)),
            dma((2, chunks)),
            dma((size, chunks)),
            dma((size + 1, chunks)),
            dma((2, size, chunks)),
            dma((size, chunks)),
        ]
        + cube_scratch(bits, [grad.shape for grad in grads]),
        compiler_params=pltpu.CompilerParams(
            collective_id=1, has_side_effects=True, vmem_limit_bytes=VMEM_BYTES
        ),
        cost_estimate=pl.CostEstimate(
            flops=2 * size * own * depth * width, bytes_accessed=2**26, transcendentals=0
        ),
    )(dsecond, out_weight, middle, cotangent, gain, grads)


def last_kernel(
    size,
    bits,
    chunks,
    dfirst_hbm,
    outp_hbm,
    tokens_ref,
    middle_ref,
    dmiddle_ref,
    gain_ref,
    sums_ref,
    grads_hbm,
    output_ref,
    dtokens_ref,
    totals_ref,
    totals_hbm,
    first_part,
    first_inbox,
    out_part,
    out_inbox,
    line_box,
    dp_box,
    load_sem,
    line_send,
    line_recv,
    dp_send,
    dp_recv,
    rs_send,
    rs_recv,
    out_send,
    out_recv,
    cube_parts,
    cube_firsts,
    cube_nexts,
    cube_load,
    cube_store,
    cube_send,
    cube_recv,
    cube_free,
):
    me = lax.axis_index("tensor")
    mine = lax.axis_index("dp")
    own = tokens_ref.shape[0]
    rows = own // chunks
    load_first = pltpu.make_async_copy(dfirst_hbm, first_part, load_sem.at[0])
    load_out = pltpu.make_async_copy(outp_hbm, out_part, load_sem.at[1])
    load_first.start()
    cube = CubeSum(
        bits,
        mine,
        grads_hbm,
        totals_hbm,
        cube_parts,
        cube_firsts,
        cube_nexts,
        cube_load,
        cube_store,
        cube_send,
        cube_recv,
        cube_free,
    )
    for which in range(len(cube_parts)):
        cube.load(which)
    load_out.start()
    groups = 2**bits
    peers = [{"dp": (mine + step) % groups} for step in range(1, groups)]
    others = [{"tensor": (me + step) % size} for step in range(1, size)]
    enter(peers + others, None)
    first = LineScatter(size, me, rows, first_part, first_inbox, rs_send, rs_recv)
    last = LineScatter(size, me, rows, out_part, out_inbox, out_send, out_recv)

    def back(chunk):
        first.arrive(chunk)

        def body(block):
            here = pl.ds(chunk * rows + block.start, LINE)
            values = tokens_ref[here, :].astype(jnp.float32)
            centered = values - jnp.mean(values, axis=-1, keepdims=True)
            scale = lax.rsqrt(jnp.mean(centered * centered, axis=-1, keepdims=True) + EPS)
            normed = centered * scale
            grad = first.total(here)
            shaped = grad * gain_ref[...]
            line_box[me, 2:3, :] += jnp.sum(grad * normed, axis=0, keepdims=True)
            line_box[me, 3:4, :] += jnp.sum(grad, axis=0, keepdims=True)
            dtokens_ref[here, :] = dmiddle_ref[here, :] + scale * (
                shaped
                - jnp.mean(shaped, axis=-1, keepdims=True)
                - normed * jnp.mean(shaped * normed, axis=-1, keepdims=True)
            )

        for_rows(rows, body)

    def finish(chunk):
        last.arrive(chunk)

        def body(block):
            here = pl.ds(chunk * rows + block.start, LINE)
            output_ref[here, :] = (middle_ref[here, :] + last.total(here)).astype(jnp.bfloat16)

        for_rows(rows, body)

    def line_copy(step, slot):
        return pltpu.make_async_remote_copy(
            src_ref=line_box.at[me],
            dst_ref=line_box.at[slot],
            send_sem=line_send.at[step],
            recv_sem=line_recv.at[slot],
            device_id={"tensor": (me + step) % size},
            device_id_type=MESH,
        )

    def dp_copy(step, slot):
        return pltpu.make_async_remote_copy(
            src_ref=dp_box.at[mine],
            dst_ref=dp_box.at[slot],
            send_sem=dp_send.at[step],
            recv_sem=dp_recv.at[slot],
            device_id={"dp": (mine + step) % groups},
            device_id_type=MESH,
        )

    def sums_on_line():
        for step in range(1, size):
            line_copy(step, me).start()

    def sums_on_dp():
        for step in range(1, size):
            line_copy(step, (me + step) % size).wait_recv()
        dp_box[mine] = jnp.sum(line_box[...], axis=0)
        for step in range(1, groups):
            dp_copy(step, mine).start()

    def sums_done():
        for step in range(1, groups):
            dp_copy(step, (mine + step) % groups).wait_recv()
        totals_ref[...] = jnp.sum(dp_box[...], axis=0)

    def line_calls():
        yield functools.partial(first.begin, 0)
        for chunk in range(chunks):
            for step in range(size - 1):
                yield functools.partial(first.put, chunk, step)
            yield functools.partial((first if chunk < chunks - 1 else last).begin, (chunk + 1) % chunks)
            yield functools.partial(back, chunk)
        yield sums_on_line
        for chunk in range(chunks):
            for step in range(size - 1):
                yield functools.partial(last.put, chunk, step)
            if chunk < chunks - 1:
                yield functools.partial(last.begin, chunk + 1)
            yield functools.partial(finish, chunk)
            if chunk == 0:
                yield sums_on_dp
        yield sums_done

    line_box[me] = sums_ref[...]
    load_first.wait()
    load_out.wait()
    interleave(list(cube.calls()), list(line_calls()))
    for chunk in range(chunks):
        first.drain(chunk)
        last.drain(chunk)
    for step in range(1, size):
        line_copy(step, me).wait_send()
    for step in range(1, groups):
        dp_copy(step, mine).wait_send()
    cube.drain()


def last_sums(size, bits, chunks, dfirst, partial, tokens, middle, dmiddle, gain, sums, grads):
    own, depth = tokens.shape
    low, full = jnp.bfloat16, jnp.float32
    dma = pltpu.SemaphoreType.DMA
    vmem, anywhere = pl.BlockSpec(memory_space=pltpu.VMEM), pl.BlockSpec(memory_space=pl.ANY)
    many = [anywhere] * len(grads)
    return pl.pallas_call(
        functools.partial(last_kernel, size, bits, chunks),
        out_shape=(
            jax.ShapeDtypeStruct((own, depth), low),
            jax.ShapeDtypeStruct((own, depth), full),
            jax.ShapeDtypeStruct((8, depth), full),
            [jax.ShapeDtypeStruct(grad.shape, low) for grad in grads],
        ),
        in_specs=[anywhere, anywhere, vmem, vmem, vmem, vmem, vmem, many],
        out_specs=(vmem, vmem, vmem, many),
        scratch_shapes=[
            pltpu.VMEM((size, own, depth), low),
            pltpu.VMEM((size + 1, own, depth), low),
            pltpu.VMEM((size, own, depth), low),
            pltpu.VMEM((size + 1, own, depth), low),
            pltpu.VMEM((size, 8, depth), full),
            pltpu.VMEM((2**bits, 8, depth), full),
            dma((2,)),
            dma((size,)),
            dma((size,)),
            dma((2**bits,)),
            dma((2**bits,)),
            dma((size, chunks)),
            dma((size + 1, chunks)),
            dma((size, chunks)),
            dma((size + 1, chunks)),
        ]
        + cube_scratch(bits, [grad.shape for grad in grads]),
        compiler_params=pltpu.CompilerParams(
            collective_id=2, has_side_effects=True, vmem_limit_bytes=VMEM_BYTES
        ),
        cost_estimate=pl.CostEstimate(flops=2**30, bytes_accessed=2**26, transcendentals=0),
    )(dfirst, partial, tokens, middle, dmiddle, gain, sums, grads)


def per_device(
    tokens,
    first_gain,
    first_bias,
    query_weight,
    key_weight,
    value_weight,
    gate_weight,
    out_weight,
    second_gain,
    second_bias,
    hidden_gate,
    hidden_up,
    hidden_down,
    segments,
    cotangent,
):
    seq_count, seq_len = segments.shape
    group_rows = seq_count * seq_len
    head_local = query_weight.shape[1] // KD
    scale_factor = KD ** (-0.5)
    inputs = tokens.astype(jnp.float32)
    seed_all = lax.all_gather(cotangent, "tensor", axis=0, tiled=True)
    first_out, first_normed, first_scale = norm_parts(inputs, first_gain, first_bias)
    first_all = lax.all_gather(first_out.astype(jnp.bfloat16), "tensor", axis=0, tiled=True)
    queries = product(first_all, query_weight).astype(jnp.bfloat16)
    keys_low = product(first_all, key_weight).astype(jnp.bfloat16)
    values = product(first_all, value_weight).astype(jnp.bfloat16)
    gates = product(first_all, gate_weight)
    head_index = (lax.axis_index("tensor") * head_local + jnp.arange(head_local)).astype(
        jnp.float32
    )
    rates = -jnp.log1p(-jnp.exp2(-5.0 - head_index))
    table = decay_table(segments, rates)
    query_heads = queries.reshape(seq_count, seq_len, head_local, KD)
    key_heads = keys_low.reshape(seq_count, seq_len, head_local, KD)
    value_heads = values.reshape(seq_count, seq_len, head_local, VD)
    scores = (
        jnp.einsum("bnhk,bmhk->bhnm", query_heads, key_heads, preferred_element_type=jnp.float32)
        * scale_factor
    )

    def score_step(raw):
        return normalize_scores(raw, table)

    retain_full, score_pull = jax.vjp(score_step, scores)
    retain = retain_full.astype(jnp.bfloat16)
    retained = jnp.einsum(
        "bhnm,bmhv->bnhv", retain, value_heads, preferred_element_type=jnp.float32
    )
    gate_heads = gates.reshape(seq_count, seq_len, head_local, VD)
    mixed_full, mix_pull = jax.vjp(gated_norm, gate_heads, retained)
    mixed = mixed_full.reshape(group_rows, head_local * VD).astype(jnp.bfloat16)
    size = lax.axis_size("tensor")
    bits = lax.axis_size("dp").bit_length() - 1
    own = tokens.shape[0]
    second_all, seed_all, inner, gate_in_low, lin_in_low, grad_second, partial, middle = feed_forward(
        size,
        CHUNKS,
        mixed.reshape(size, own, head_local * VD),
        out_weight,
        tokens,
        cotangent,
        hidden_gate.T,
        hidden_up.T,
        hidden_down,
        second_gain[None],
        second_bias[None],
    )

    def flat(item):
        return item.reshape(group_rows, item.shape[-1])

    second_all, seed_all = flat(second_all), flat(seed_all)
    feed_grads = [
        product_tn(flat(inner), seed_all).astype(jnp.bfloat16),
        product_tn(flat(gate_in_low), second_all).astype(jnp.bfloat16),
        product_tn(flat(lin_in_low), second_all).astype(jnp.bfloat16),
    ]
    branch_all, grad_mixed, grad_middle, second_sums, feed_grads = feed_back(
        size, bits, CHUNKS, grad_second, out_weight, middle, cotangent, second_gain[None], feed_grads
    )
    branch_all = flat(branch_all)
    grad_gates, grad_retained = mix_pull(grad_mixed.reshape(seq_count, seq_len, head_local, VD))
    gates_low = grad_gates.reshape(group_rows, head_local * VD).astype(jnp.bfloat16)
    retained_low = grad_retained.astype(jnp.bfloat16)
    grad_retain = jnp.einsum(
        "bnhv,bmhv->bhnm", retained_low, value_heads, preferred_element_type=jnp.float32
    )
    grad_values = jnp.einsum(
        "bhnm,bnhv->bmhv", retain, retained_low, preferred_element_type=jnp.float32
    )
    values_low = grad_values.reshape(group_rows, head_local * VD).astype(jnp.bfloat16)
    (grad_scores,) = score_pull(grad_retain)
    scores_low = grad_scores.astype(jnp.bfloat16)
    grad_queries = (
        jnp.einsum("bhnm,bmhk->bnhk", scores_low, key_heads, preferred_element_type=jnp.float32)
        * scale_factor
    )
    grad_keys = (
        jnp.einsum("bhnm,bnhk->bmhk", scores_low, query_heads, preferred_element_type=jnp.float32)
        * scale_factor
    )
    queries_low = grad_queries.reshape(group_rows, head_local * KD).astype(jnp.bfloat16)
    keys_back = grad_keys.reshape(group_rows, head_local * KD).astype(jnp.bfloat16)
    grads = [
        product_tn(mixed, branch_all).astype(jnp.bfloat16),
        product_tn(values_low, first_all).astype(jnp.bfloat16),
        product_tn(gates_low, first_all).astype(jnp.bfloat16),
        product_tn(first_all, queries_low).astype(jnp.bfloat16),
        product_tn(first_all, keys_back).astype(jnp.bfloat16),
    ]
    total = product_nt(queries_low, query_weight)
    total = total + product_nt(keys_back, key_weight)
    total = total + product_nt(values_low, value_weight)
    total = (total + product_nt(gates_low, gate_weight)).astype(jnp.bfloat16)
    output, grad_tokens, sums, grads = last_sums(
        size,
        bits,
        CHUNKS,
        total.reshape(size, own, total.shape[-1]),
        partial,
        tokens,
        middle,
        grad_middle,
        first_gain[None],
        second_sums,
        grads,
    )
    grad_sgain, grad_sbias, grad_fgain, grad_fbias = sums[0], sums[1], sums[2], sums[3]
    grad_outw, grad_valuew, grad_gatew, grad_queryw, grad_keyw = (
        item.astype(jnp.float32) for item in grads
    )
    grad_hdown, grad_hgate, grad_hup = (item.astype(jnp.float32) for item in feed_grads)
    grad_valuew, grad_gatew, grad_hgate, grad_hup = (
        item.T for item in (grad_valuew, grad_gatew, grad_hgate, grad_hup)
    )
    return (
        output,
        grad_tokens,
        grad_fgain,
        grad_fbias,
        grad_queryw,
        grad_keyw,
        grad_valuew,
        grad_gatew,
        grad_outw,
        grad_sgain,
        grad_sbias,
        grad_hgate,
        grad_hup,
        grad_hdown,
    )


def solution(mesh):
    return jax.shard_map(
        per_device,
        mesh=mesh,
        in_specs=(
            P(("dp", "tensor"), None),
            P(),
            P(),
            P(None, "tensor"),
            P(None, "tensor"),
            P(None, "tensor"),
            P(None, "tensor"),
            P("tensor", None),
            P(),
            P(),
            P(None, "tensor"),
            P(None, "tensor"),
            P("tensor", None),
            P("dp", None),
            P(("dp", "tensor"), None),
        ),
        out_specs=(
            P(("dp", "tensor"), None),
            P(("dp", "tensor"), None),
            P(),
            P(),
            P(None, "tensor"),
            P(None, "tensor"),
            P(None, "tensor"),
            P(None, "tensor"),
            P("tensor", None),
            P(),
            P(),
            P(None, "tensor"),
            P(None, "tensor"),
            P("tensor", None),
        ),
        check_vma=False,
    )
```

```python
import functools
import itertools

import jax
import jax.numpy as jnp
from jax import lax
from jax.experimental import pallas as pl
from jax.experimental.pallas import tpu as pltpu
from jax.sharding import PartitionSpec as P

KD = 256
VD = 432


EPS = 1e-05
GROUP_EPS = 0.1
GELU_SCALE = 0.7978845608028654
CHUNKS = 4

MESH = pl.DeviceIdType.MESH
VMEM_BYTES = 60 * 2**20
TILE = 256
LINE = 16


def norm_parts(rows, gain, bias):
    centered = rows - jnp.mean(rows, axis=-1, keepdims=True)
    scale = lax.rsqrt(jnp.mean(centered * centered, axis=-1, keepdims=True) + EPS)
    normed = centered * scale
    return (normed * gain + bias, normed, scale)


def norm_back(grad_out, gain, normed, scale):
    shaped = grad_out * gain
    return scale * (
        shaped
        - jnp.mean(shaped, axis=-1, keepdims=True)
        - normed * jnp.mean(shaped * normed, axis=-1, keepdims=True)
    )


def decay_table(segments, rates):
    place = jnp.arange(segments.shape[-1], dtype=jnp.int32)
    offset = place[:, None] - place[None, :]
    same_doc = (segments[..., :, None] == segments[..., None, :]) & (offset >= 0)
    distance = jnp.maximum(offset, 0).astype(jnp.float32)
    decay = jnp.where(same_doc[..., None, :, :], jnp.exp(-rates[:, None, None] * distance), 0.0)
    return decay * lax.rsqrt(jnp.sum(decay, axis=-1, keepdims=True))


def normalize_scores(scores, table):
    weighted = scores * table
    total = jnp.sum(weighted, axis=-1, keepdims=True)
    return weighted * lax.rsqrt(total * total + 1.0)


def gated_norm(gates, retained):
    centered = retained - jnp.mean(retained, axis=-1, keepdims=True)
    normed = centered * lax.rsqrt(jnp.mean(centered * centered, axis=-1, keepdims=True) + GROUP_EPS)
    return jax.nn.silu(gates) * normed


def product(left, right):
    return jnp.dot(left, right, preferred_element_type=jnp.float32)


def product_nt(left, right):
    return lax.dot_general(
        left, right, (((1,), (1,)), ((), ())), preferred_element_type=jnp.float32
    )


def product_tn(left, right):
    return lax.dot_general(
        left, right, (((0,), (0,)), ((), ())), preferred_element_type=jnp.float32
    )


def for_columns(width, body):
    full = width // TILE

    def step(index, carry):
        body(pl.multiple_of(index * TILE, TILE), TILE)
        return carry

    if full:
        lax.fori_loop(0, full, step, 0)
    if width % TILE:
        body(full * TILE, width % TILE)


def for_rows(count, body):
    def step(index, carry):
        body(pl.ds(pl.multiple_of(index * LINE, LINE), LINE))
        return carry

    lax.fori_loop(0, count // LINE, step, 0)


def dot_nn(left, right):
    return lax.dot_general(left, right, (((1,), (0,)), ((), ())), preferred_element_type=jnp.float32)


def dot_nt(left, right):
    return lax.dot_general(left, right, (((1,), (1,)), ((), ())), preferred_element_type=jnp.float32)


def enter(peers, line):
    barrier = pltpu.get_barrier_semaphore()
    for peer in peers:
        pl.semaphore_signal(barrier, inc=1, device_id=peer, device_id_type=MESH)
    if line is not None:
        size, me = line

        @pl.when(me > 0)
        def _():
            pl.semaphore_signal(barrier, inc=1, device_id={"tensor": me - 1}, device_id_type=MESH)

        @pl.when(me < size - 1)
        def _():
            pl.semaphore_signal(barrier, inc=1, device_id={"tensor": me + 1}, device_id_type=MESH)

    count = len(peers)
    if line is not None:
        count = count + (me > 0).astype(jnp.int32) + (me < size - 1).astype(jnp.int32)
    pl.semaphore_wait(barrier, count)


class LineScatter:
    def __init__(self, size, me, rows, part, inbox, send, recv):
        self.size, self.me, self.rows = size, me, rows
        self.part, self.inbox, self.send, self.recv = part, inbox, send, recv

    def at(self, chunk):
        return pl.ds(chunk * self.rows, self.rows)

    def copy(self, target, slot, chunk, device):
        return pltpu.make_async_remote_copy(
            src_ref=self.part.at[target, self.at(chunk)],
            dst_ref=self.inbox.at[slot, self.at(chunk)],
            send_sem=self.send.at[target, chunk],
            recv_sem=self.recv.at[slot, chunk],
            device_id={"tensor": device},
            device_id_type=MESH,
        )

    def add(self, target, chunk):
        def body(rows):
            at = pl.ds(chunk * self.rows + rows.start, LINE)
            total = self.part[target, at, :].astype(jnp.float32)
            total = total + self.inbox[target, at, :].astype(jnp.float32)
            self.part[target, at, :] = total.astype(jnp.bfloat16)

        for_rows(self.rows, body)

    def go_right(self, chunk, target):
        self.copy(target, target, chunk, self.me + 1).start()

    def go_left(self, chunk, target):
        last = self.me - 1 == target
        self.copy(target, jnp.where(last, self.size, target), chunk, self.me - 1).start()

    def begin(self, chunk):
        @pl.when(self.me == 0)
        def _():
            for target in range(self.size - 1, 0, -1):
                self.go_right(chunk, target)

        @pl.when(self.me == self.size - 1)
        def _():
            for target in range(self.size - 1):
                self.go_left(chunk, target)

    def right(self, chunk, target):
        @pl.when((self.me < target) & (self.me > 0))
        def _():
            self.copy(target, target, chunk, self.me).wait_recv()
            self.add(target, chunk)
            self.go_right(chunk, target)

    def left(self, chunk, target):
        @pl.when((self.me > target) & (self.me < self.size - 1))
        def _():
            self.copy(target, target, chunk, self.me).wait_recv()
            self.add(target, chunk)
            self.go_left(chunk, target)

    def calls(self, chunk):
        for step in range(self.size - 1):
            if step < self.size - 2:
                yield functools.partial(self.right, chunk, self.size - 1 - step)
                yield functools.partial(self.left, chunk, step)

    def arrive(self, chunk):
        size, me = self.size, self.me

        @pl.when(me > 0)
        def _():
            self.copy(me, me, chunk, me - 1).wait_recv()

        @pl.when(me < size - 1)
        def _():
            self.copy(me, size, chunk, me + 1).wait_recv()

    def total(self, rows):
        size, me = self.size, self.me
        own = self.part[me, rows, :].astype(jnp.float32)
        low = self.inbox[me, rows, :].astype(jnp.float32)
        high = self.inbox[size, rows, :].astype(jnp.float32)
        return own + jnp.where(me > 0, low, 0.0) + jnp.where(me < size - 1, high, 0.0)

    def drain(self, chunk):
        for target in range(self.size):

            @pl.when(self.me != target)
            def _():
                self.copy(target, target, chunk, self.me).wait_send()


class LineGather:
    def __init__(self, size, me, rows, held, send, recv):
        self.size, self.me, self.rows = size, me, rows
        self.held, self.send, self.recv = held, send, recv

    def copy(self, block, chunk, way, device):
        at = pl.ds(chunk * self.rows, self.rows)
        return pltpu.make_async_remote_copy(
            src_ref=self.held.at[block, at],
            dst_ref=self.held.at[block, at],
            send_sem=self.send.at[way, block, chunk],
            recv_sem=self.recv.at[block, chunk],
            device_id={"tensor": device},
            device_id_type=MESH,
        )

    def begin(self, chunk):
        self.right(chunk, 0)
        self.left(chunk, 0)

    def right(self, chunk, step):
        size, me = self.size, self.me

        @pl.when(me >= step)
        def _():
            if step:
                self.copy(me - step, chunk, 0, me).wait_recv()

            @pl.when(me < size - 1)
            def _():
                self.copy(me - step, chunk, 0, me + 1).start()

    def left(self, chunk, step):
        size, me = self.size, self.me

        @pl.when(me + step < size)
        def _():
            if step:
                self.copy(me + step, chunk, 1, me).wait_recv()

            @pl.when(me > 0)
            def _():
                self.copy(me + step, chunk, 1, me - 1).start()

    def calls(self, chunk):
        for step in range(1, self.size):
            yield functools.partial(self.right, chunk, step)
            yield functools.partial(self.left, chunk, step)

    def drain(self, chunk):
        size, me = self.size, self.me
        for step in range(size):

            @pl.when((me >= step) & (me < size - 1))
            def _():
                self.copy(me - step, chunk, 0, me + 1).wait_send()

            @pl.when((me + step < size) & (me > 0))
            def _():
                self.copy(me + step, chunk, 1, me - 1).wait_send()


class CubeSum:
    def __init__(self, bits, me, sources, results, parts, firsts, nexts, load, store, send, recv, free):
        self.bits, self.me = bits, me
        self.sources, self.results, self.parts = sources, results, parts
        self.firsts, self.nexts = firsts, nexts
        self.load_sem, self.store_sem, self.send, self.recv = load, store, send, recv
        self.free = free
        self.orders = (tuple(range(bits)), (0,) + tuple(range(bits - 1, 0, -1)))
        self.mine = [(me // 2**bit) % 2 for bit in range(bits)]

    def partner(self, bit):
        return self.me + (1 - 2 * self.mine[bit]) * 2**bit

    def band(self, which, color):
        count = self.parts[which].shape[-2]
        cut = cut_rows(count)
        return ((0, cut), (cut, count - cut), (0, count))[color]

    def lead(self, fixed):
        return tuple(fixed.get(bit, slice(None)) for bit in range(self.bits - 1, -1, -1))

    def moved(self, src, dst, which, color, step, bit):
        return pltpu.make_async_remote_copy(
            src_ref=src,
            dst_ref=dst,
            send_sem=self.send.at[which, color % 2, step],
            recv_sem=self.recv.at[which, color % 2, step],
            device_id={"dp": self.partner(bit)},
            device_id_type=MESH,
        )

    def halve(self, which, color, step):
        order = self.orders[color % 2]
        start, count = self.band(which, color)
        fixed = {bit: self.mine[bit] for bit in order[:step]}
        fixed[order[step]] = 1 - self.mine[order[step]]
        src = self.parts[which].at[self.lead(fixed) + (pl.ds(start, count), slice(None))]
        dst = self.firsts[which] if step == 0 else self.nexts[which][color][step - 1]
        return self.moved(src, dst, which, color, step, order[step])

    def double(self, which, color, step):
        order = self.orders[color % 2]
        start, count = self.band(which, color)
        fixed = {bit: self.mine[bit] for bit in order[: step + 1]}
        held = self.parts[which].at[self.lead(fixed) + (pl.ds(start, count), slice(None))]
        return self.moved(held, held, which, color, 2 * self.bits - 1 - step, order[step])

    def freed(self, which, color, step):
        return self.free.at[which, color % 2, step]

    def land(self, which, color, step):
        copy = self.halve(which, color, step)
        copy.wait_send()
        partner = {"dp": self.partner(self.orders[color % 2][step])}
        pl.semaphore_signal(
            self.freed(which, color, step), inc=1, device_id=partner, device_id_type=MESH
        )
        copy.wait_recv()
        self.add(which, color, step)

    def grow(self, which, color, step):
        pl.semaphore_wait(self.freed(which, color, step), 1)
        self.double(which, color, step).start()

    def add(self, which, color, step):
        order = self.orders[color % 2]
        part, (start, count) = self.parts[which], self.band(which, color)
        box = self.firsts[which] if step == 0 else self.nexts[which][color][step - 1]
        fixed = {bit: self.mine[bit] for bit in order[: step + 1]}
        free = [bit for bit in range(self.bits - 1, -1, -1) if bit not in fixed]
        for choice in itertools.product((0, 1), repeat=len(free)):
            lead = self.lead({**fixed, **dict(zip(free, choice))})

            def body(begin, size):
                there = lead + (pl.ds(start + begin, size), slice(None))
                total = part[there].astype(jnp.float32)
                total = total + box[choice + (pl.ds(begin, size), slice(None))].astype(jnp.float32)
                part[there] = total.astype(jnp.bfloat16)

            for_blocks(count, part.shape[-1], body)

    def slices(self, which, ref):
        rows, columns = self.parts[which].shape[-2:]
        for index in range(2**self.bits):
            lead = tuple((index >> bit) & 1 for bit in range(self.bits - 1, -1, -1))
            if ref.shape[0] == rows:
                whole = ref.at[:, pl.ds(index * columns, columns)]
            else:
                whole = ref.at[pl.ds(index * rows, rows), :]
            yield index, self.parts[which].at[lead], whole

    def load(self, which):
        for index, part, whole in self.slices(which, self.sources[which]):
            pltpu.make_async_copy(whole, part, self.load_sem.at[which, index]).start()

    def open(self, which):
        for index, part, whole in self.slices(which, self.sources[which]):
            pltpu.make_async_copy(whole, part, self.load_sem.at[which, index]).wait()
        self.halve(which, 2, 0).start()

    def split(self, which):
        self.land(which, 2, 0)
        for color in range(2):
            self.halve(which, color, 1).start()

    def down(self, which, color, step):
        self.land(which, color, step - 1)
        self.halve(which, color, step).start()

    def turn(self, which, color):
        self.land(which, color, self.bits - 1)
        self.grow(which, color, self.bits - 1)

    def up(self, which, color, step):
        self.double(which, color, step + 1).wait_recv()
        self.grow(which, color, step)

    def join(self, which):
        for color in range(2):
            self.double(which, color, 1).wait_recv()
        self.grow(which, 2, 0)

    def close(self, which):
        self.double(which, 2, 0).wait_recv()
        for index, part, whole in self.slices(which, self.results[which]):
            pltpu.make_async_copy(part, whole, self.store_sem.at[which, index]).start()

    def calls(self, which):
        yield functools.partial(self.open, which)
        yield functools.partial(self.split, which)
        for step in range(2, self.bits):
            for color in range(2):
                yield functools.partial(self.down, which, color, step)
        for color in range(2):
            yield functools.partial(self.turn, which, color)
        for step in range(self.bits - 2, 0, -1):
            for color in range(2):
                yield functools.partial(self.up, which, color, step)
        yield functools.partial(self.join, which)
        yield functools.partial(self.close, which)

    def drain(self):
        for which in range(len(self.parts)):
            self.double(which, 2, 0).wait_send()
            for color in range(2):
                for step in range(1, self.bits):
                    self.double(which, color, step).wait_send()
            for index, part, whole in self.slices(which, self.results[which]):
                pltpu.make_async_copy(part, whole, self.store_sem.at[which, index]).wait()


def cut_rows(count):
    return count // (2 * LINE) * LINE


def for_blocks(count, columns, body):
    size = LINE
    while count % (2 * size) == 0 and 2 * size * columns <= 2**14:
        size *= 2
    for factor in (3, 5):
        if count % (factor * size) == 0 and factor * size * columns <= 2**14:
            size *= factor

    def step(index, carry):
        body(pl.multiple_of(index * size, LINE), size)
        return carry

    lax.fori_loop(0, count // size, step, 0)


def cube_scratch(bits, shapes):
    low = jnp.bfloat16
    parts, firsts, nexts = [], [], []
    for rows, columns in shapes:
        if columns >= rows:
            columns = columns // 2**bits
        else:
            rows = rows // 2**bits
        cut = cut_rows(rows)
        parts.append(pltpu.VMEM((2,) * bits + (rows, columns), low))
        firsts.append(pltpu.VMEM((2,) * (bits - 1) + (rows, columns), low))
        nexts.append(
            [
                [
                    pltpu.VMEM((2,) * (bits - 1 - step) + (count, columns), low)
                    for step in range(1, bits)
                ]
                for count in (cut, rows - cut)
            ]
        )
    dma = pltpu.SemaphoreType.DMA
    return [
        parts,
        firsts,
        nexts,
        dma((len(shapes), 2**bits)),
        dma((len(shapes), 2**bits)),
        dma((len(shapes), 2, 2 * bits)),
        dma((len(shapes), 2, 2 * bits)),
        pltpu.SemaphoreType.REGULAR((len(shapes), 2, bits)),
    ]


ORDERS = {
    ("feed", 4, 4): (
        4, 6, 4, 0, 5, 4, 4, 0, 4, 6, 5, 0, 5, 0, 0, 2, 5, 6, 1, 2, 0, 3, 4, 4,
        6, 1, 6, 7, 5, 0, 6, 1, 1, 5, 2, 0, 0, 1, 3, 2, 0, 1, 7, 3, 3, 0, 5, 1,
        0, 2, 0, 1, 0, 3, 2, 0, 0, 1, 1, 1, 3, 0, 1, 1, 1, 2, 2, 1, 1, 2, 1, 6,
        0, 2, 3, 3, 2, 7, 7, 2, 2, 2, 3, 2, 2, 1, 3, 3, 7, 0, 0, 2, 3, 3, 1, 2,
        7, 1, 7, 0, 3, 1, 3, 3, 3, 3, 2, 2, 0, 3, 2, 3, 3, 2, 1, 3,
    ),
    ("back", 4, 4, 3): (
        0, 8, 9, 4, 10, 1, 5, 2, 8, 9, 4, 3, 10, 8, 8, 6, 0, 1, 9, 9, 4, 0, 1, 0,
        10, 10, 5, 8, 4, 8, 9, 0, 2, 9, 3, 5, 10, 8, 8, 2, 0, 10, 0, 9, 0, 9, 7, 3,
        1, 6, 1, 5, 6, 5, 1, 8, 4, 1, 3, 2, 10, 10, 7, 6, 3, 2, 7, 3, 9, 6, 7, 1,
        2, 3, 8, 10, 5, 4, 2, 6, 7, 2, 9, 3, 10, 7,
    ),
    ("last", 4, 4, 3): (
        7, 0, 4, 7, 4, 6, 0, 6, 4, 5, 2, 4, 3, 0, 6, 6, 8, 1, 0, 0, 7, 4, 5, 7,
        2, 0, 6, 4, 8, 5, 7, 4, 6, 3, 8, 5, 1, 4, 6, 1, 8, 7, 7, 6, 5, 3, 1, 2,
        2, 5, 8, 2, 1, 3, 8, 5, 7, 4, 3, 1, 2, 8, 5, 6, 3, 7, 9, 4, 8, 9, 5, 7,
        9, 8, 6, 5, 8,
    ),
    ("feed", 4, 8): (
        11, 10, 13, 8, 9, 13, 1, 8, 13, 8, 10, 0, 14, 10, 12, 8, 13, 10, 13, 0, 1, 10, 8, 11,
        9, 12, 2, 14, 0, 0, 1, 1, 11, 8, 1, 3, 0, 9, 11, 9, 5, 12, 2, 1, 3, 10, 12, 11,
        9, 14, 0, 8, 7, 6, 5, 1, 12, 0, 3, 3, 2, 2, 4, 5, 0, 0, 2, 9, 3, 9, 11, 15,
        6, 14, 0, 1, 1, 0, 0, 2, 3, 4, 12, 0, 7, 5, 13, 1, 15, 2, 7, 0, 7, 0, 4, 0,
        4, 6, 6, 10, 4, 2, 0, 2, 1, 12, 5, 1, 1, 1, 4, 1, 3, 1, 1, 2, 11, 3, 6, 2,
        5, 2, 4, 13, 2, 3, 2, 2, 4, 7, 2, 3, 15, 0, 2, 6, 3, 4, 3, 15, 3, 3, 3, 5,
        3, 4, 4, 3, 4, 5, 1, 4, 7, 4, 5, 4, 4, 2, 5, 5, 14, 6, 1, 1, 4, 7, 5, 5,
        2, 5, 14, 5, 14, 0, 6, 1, 6, 4, 5, 6, 7, 5, 3, 6, 6, 6, 6, 7, 6, 5, 7, 2,
        0, 7, 15, 3, 3, 6, 4, 15, 4, 6, 7, 7, 5, 5, 0, 15, 3, 2, 5, 7, 1, 4, 7, 6,
        7, 7, 7, 6, 6, 3, 5, 7, 7, 6, 7, 6, 2, 0, 4, 7,
    ),
    ("back", 4, 8, 3): (
        0, 16, 8, 1, 18, 0, 9, 2, 3, 16, 0, 17, 0, 4, 18, 5, 17, 8, 16, 6, 16, 9, 0, 18,
        0, 3, 2, 18, 4, 1, 10, 9, 8, 6, 5, 17, 3, 6, 17, 11, 9, 6, 16, 12, 4, 3, 16, 18,
        7, 18, 2, 5, 10, 17, 17, 11, 1, 16, 12, 16, 0, 3, 18, 2, 5, 18, 2, 5, 7, 8, 1, 10,
        4, 13, 14, 3, 6, 10, 11, 11, 6, 15, 17, 1, 4, 1, 3, 5, 12, 8, 7, 10, 17, 14, 11, 2,
        16, 1, 8, 12, 0, 2, 7, 9, 1, 2, 12, 7, 5, 6, 13, 3, 18, 15, 13, 4, 13, 10, 12, 14,
        14, 4, 4, 11, 17, 15, 15, 7, 16, 13, 7, 18, 14, 5, 6, 13, 7, 15, 9, 14, 17, 15,
    ),
    ("last", 4, 8, 3): (
        11, 0, 9, 11, 10, 8, 12, 6, 9, 11, 10, 3, 2, 0, 6, 11, 9, 5, 1, 11, 8, 3, 6, 12,
        7, 0, 9, 4, 5, 12, 10, 11, 9, 6, 9, 10, 11, 2, 11, 12, 8, 7, 12, 1, 6, 4, 10, 9,
        4, 2, 12, 8, 5, 2, 10, 2, 8, 9, 3, 4, 7, 1, 0, 8, 10, 3, 4, 11, 1, 8, 1, 10,
        5, 0, 3, 5, 7, 0, 7, 8, 9, 1, 11, 2, 3, 4, 5, 6, 9, 12, 12, 10, 7, 13, 13, 8,
        13, 12, 8, 10, 12,
    ),
}


def run_streams(streams, order, after):
    streams = [list(stream) for stream in streams]
    done = [0] * len(streams)

    def ready(stream):
        place = done[stream]
        return place < len(streams[stream]) and all(
            done[other] >= count for other, count in after.get((stream, place), ())
        )

    def take(stream):
        streams[stream][done[stream]]()
        done[stream] += 1

    if order is not None:
        for stream in order:
            assert ready(stream)
            take(stream)
    while any(done[index] < len(stream) for index, stream in enumerate(streams)):
        for stream in range(len(streams)):
            if ready(stream):
                take(stream)


def feed_kernel(
    size,
    chunks,
    mixed_hbm,
    out_hbm,
    tokens_hbm,
    seed_hbm,
    gate_hbm,
    up_hbm,
    down_hbm,
    gain_ref,
    bias_ref,
    second_hbm,
    seeds_hbm,
    inner_hbm,
    dgate_hbm,
    dlin_hbm,
    outp_hbm,
    middle_ref,
    dmiddle_ref,
    branch_ref,
    sums_ref,
    mixed,
    out_weight,
    tokens,
    hidden_gate,
    hidden_up,
    hidden_down,
    second,
    seeds,
    part,
    inbox,
    gate_in,
    lin_in,
    dinner,
    inner,
    dgate,
    dlin,
    wide,
    load_sem,
    store_sem,
    rs_send,
    rs_recv,
    back_send,
    back_recv,
    ag_send,
    ag_recv,
    seed_send,
    seed_recv,
):
    me = lax.axis_index("tensor")
    own, depth = tokens.shape
    rows = own // chunks
    hidden = inner.shape[-1]
    loads = [
        pltpu.make_async_copy(src, dst, load_sem.at[index])
        for index, (src, dst) in enumerate(
            (
                (mixed_hbm, mixed),
                (out_hbm, out_weight),
                (seed_hbm, seeds.at[me]),
                (tokens_hbm, tokens),
                (gate_hbm, hidden_gate),
                (up_hbm, hidden_up),
                (down_hbm, hidden_down),
            )
        )
    ]
    for load in loads:
        load.start()
    enter((), (size, me))
    scatter = LineScatter(size, me, rows, part, inbox, rs_send, rs_recv)
    scatter_back = LineScatter(size, me, rows, part, inbox, back_send, back_recv)
    gather = LineGather(size, me, rows, second, ag_send, ag_recv)
    gather_seed = LineGather(size, me, rows, seeds, seed_send, seed_recv)

    def at(chunk):
        return pl.ds(chunk * rows, rows)

    def flat(ref, chunk):
        value = ref[:, at(chunk), :]
        return value.reshape(size * rows, value.shape[-1])

    def store(kind, chunk):
        slot = chunk % 2
        src, dst = (
            (second.at[:, at(chunk)], second_hbm),
            (seeds.at[:, at(chunk)], seeds_hbm),
            (inner.at[slot], inner_hbm),
            (dgate.at[slot], dgate_hbm),
            (dlin.at[slot], dlin_hbm),
            (wide.at[slot], outp_hbm),
        )[kind]
        return pltpu.make_async_copy(src, dst.at[:, at(chunk)], store_sem.at[kind, chunk])

    waited = set()

    def need(*indices):
        for index in indices:
            if index not in waited:
                waited.add(index)
                loads[index].wait()

    def project(chunk):
        need(0, 1)

        def body(start, width):
            value = dot_nn(flat(mixed, chunk), out_weight[:, pl.ds(start, width)])
            part[:, at(chunk), pl.ds(start, width)] = value.astype(jnp.bfloat16).reshape(
                size, rows, width
            )

        for_columns(depth, body)
        scatter.begin(chunk)

    def normalize(chunk):
        need(3)
        scatter.arrive(chunk)

        def body(block):
            here = pl.ds(chunk * rows + block.start, LINE)
            middle = tokens[here, :].astype(jnp.float32) + scatter.total(here)
            middle_ref[here, :] = middle
            centered = middle - jnp.mean(middle, axis=-1, keepdims=True)
            scale = lax.rsqrt(jnp.mean(centered * centered, axis=-1, keepdims=True) + EPS)
            value = centered * scale * gain_ref[...] + bias_ref[...]
            second[me, here, :] = value.astype(jnp.bfloat16)

        for_rows(rows, body)
        gather.begin(chunk)

    def feed_in(chunk):
        need(4, 5)

        def body(start, width):
            columns = pl.ds(start, width)
            gate_in[:, columns] = dot_nt(flat(second, chunk), hidden_gate[columns, :])
            lin_in[:, columns] = dot_nt(flat(second, chunk), hidden_up[columns, :])

        for_columns(hidden, body)
        store(0, chunk).start()

    def feed_seed(chunk):
        need(6)

        def body(start, width):
            columns = pl.ds(start, width)
            dinner[:, columns] = dot_nt(flat(seeds, chunk), hidden_down[columns, :])

        for_columns(hidden, body)
        store(1, chunk).start()

    def feed_act(chunk):
        slot = chunk % 2
        if chunk >= 2:
            for kind in range(2, 5):
                store(kind, chunk - 2).wait()

        def body(block):
            gate, lin, grad = gate_in[block, :], lin_in[block, :], dinner[block, :]
            cube = GELU_SCALE * (gate + 0.044715 * (gate * gate * gate))
            tanh = jnp.tanh(cube)
            half = 0.5 * (1.0 + tanh)
            active = gate * half
            slope = half + 0.5 * gate * (1.0 - tanh * tanh) * (
                GELU_SCALE * (1.0 + 3.0 * 0.044715 * (gate * gate))
            )
            owner = block.start // rows
            inside = pl.ds(block.start - owner * rows, LINE)
            inner[slot, owner, inside, :] = (active * lin).astype(jnp.bfloat16)
            dlin[slot, owner, inside, :] = (grad * active).astype(jnp.bfloat16)
            dgate[slot, owner, inside, :] = (grad * lin * slope).astype(jnp.bfloat16)

        for_rows(size * rows, body)
        for kind in range(2, 5):
            store(kind, chunk).start()

    def feed_back(chunk):
        slot = chunk % 2
        scatter.drain(chunk)

        def body(start, width):
            columns = pl.ds(start, width)
            dgate_all = dgate[slot].reshape(size * rows, hidden)
            dlin_all = dlin[slot].reshape(size * rows, hidden)
            grad = dot_nn(dgate_all, hidden_gate[:, columns])
            grad = grad + dot_nn(dlin_all, hidden_up[:, columns])
            part[:, at(chunk), columns] = grad.astype(jnp.bfloat16).reshape(size, rows, width)

        for_columns(depth, body)
        scatter_back.begin(chunk)

    def feed_out(chunk):
        slot = chunk % 2
        if chunk >= 2:
            store(5, chunk - 2).wait()

        def body(start, width):
            columns = pl.ds(start, width)
            inner_all = inner[slot].reshape(size * rows, hidden)
            value = dot_nn(inner_all, hidden_down[:, columns])
            wide[slot, :, :, columns] = value.astype(jnp.bfloat16).reshape(size, rows, width)

        for_columns(depth, body)
        store(5, chunk).start()

    def normalize_back(chunk):
        scatter_back.arrive(chunk)

        def body(block):
            here = pl.ds(chunk * rows + block.start, LINE)
            middle = middle_ref[here, :]
            centered = middle - jnp.mean(middle, axis=-1, keepdims=True)
            scale = lax.rsqrt(jnp.mean(centered * centered, axis=-1, keepdims=True) + EPS)
            normed = centered * scale
            grad = scatter_back.total(here)
            shaped = grad * gain_ref[...]
            sums_ref[0:1, :] += jnp.sum(grad * normed, axis=0, keepdims=True)
            sums_ref[1:2, :] += jnp.sum(grad, axis=0, keepdims=True)
            dmiddle = seeds[me, here, :].astype(jnp.float32) + scale * (
                shaped
                - jnp.mean(shaped, axis=-1, keepdims=True)
                - normed * jnp.mean(shaped * normed, axis=-1, keepdims=True)
            )
            dmiddle_ref[here, :] = dmiddle
            branch_ref[here, :] = dmiddle.astype(jnp.bfloat16)

        for_rows(rows, body)

    def begin_seed(chunk):
        need(2)
        gather_seed.begin(chunk)

    streams, after = [], {}
    for chunk in range(chunks):
        steps = [project, *scatter.calls(chunk), normalize, *gather.calls(chunk)]
        first_feed = len(steps)
        steps += [feed_in, feed_seed, feed_act, feed_back, feed_out]
        steps += [*scatter_back.calls(chunk), normalize_back]
        streams.append(
            [step if isinstance(step, functools.partial) else functools.partial(step, chunk) for step in steps]
        )
        if chunk:
            after[chunk, first_feed] = ((chunk - 1, first_feed + 5),)
        after[chunk, first_feed + 1] = ((chunks + chunk, 2 * size - 1),)
    for chunk in range(chunks):
        streams.append([functools.partial(begin_seed, chunk), *gather_seed.calls(chunk)])
    sums_ref[...] = jnp.zeros_like(sums_ref)
    run_streams(streams, ORDERS.get(("feed", size, chunks)), after)
    for chunk in range(chunks):
        scatter_back.drain(chunk)
        gather.drain(chunk)
        gather_seed.drain(chunk)
        for kind in range(6 if chunk >= chunks - 2 else 2):
            store(kind, chunk).wait()


def feed_forward(size, chunks, mixed, out_weight, tokens, cotangent, hidden_gate, hidden_up, hidden_down, gain, bias):
    own, depth = tokens.shape
    hidden = hidden_gate.shape[0]
    rows = own // chunks
    low, full = jnp.bfloat16, jnp.float32

    def blocks(width):
        return jax.ShapeDtypeStruct((size, own, width), low)

    dma = pltpu.SemaphoreType.DMA
    wide, thin = (size, own, depth), (2, size, rows, hidden)
    return pl.pallas_call(
        functools.partial(feed_kernel, size, chunks),
        out_shape=(
            blocks(depth),
            blocks(depth),
            blocks(hidden),
            blocks(hidden),
            blocks(hidden),
            blocks(depth),
            jax.ShapeDtypeStruct((own, depth), full),
            jax.ShapeDtypeStruct((own, depth), full),
            jax.ShapeDtypeStruct((own, depth), low),
            jax.ShapeDtypeStruct((8, depth), full),
        ),
        in_specs=[pl.BlockSpec(memory_space=pl.ANY)] * 7
        + [pl.BlockSpec(memory_space=pltpu.VMEM)] * 2,
        out_specs=(pl.BlockSpec(memory_space=pl.ANY),) * 6
        + (pl.BlockSpec(memory_space=pltpu.VMEM),) * 4,
        scratch_shapes=[
            pltpu.VMEM((size, own, mixed.shape[-1]), low),
            pltpu.VMEM(out_weight.shape, low),
            pltpu.VMEM((own, depth), low),
            pltpu.VMEM((hidden, depth), low),
            pltpu.VMEM((hidden, depth), low),
            pltpu.VMEM((hidden, depth), low),
            pltpu.VMEM(wide, low),
            pltpu.VMEM(wide, low),
            pltpu.VMEM(wide, low),
            pltpu.VMEM((size + 1, own, depth), low),
            pltpu.VMEM((size * rows, hidden), full),
            pltpu.VMEM((size * rows, hidden), full),
            pltpu.VMEM((size * rows, hidden), full),
            pltpu.VMEM(thin, low),
            pltpu.VMEM(thin, low),
            pltpu.VMEM(thin, low),
            pltpu.VMEM((2, size, rows, depth), low),
            dma((7,)),
            dma((6, chunks)),
            dma((size, chunks)),
            dma((size + 1, chunks)),
            dma((size, chunks)),
            dma((size + 1, chunks)),
            dma((2, size, chunks)),
            dma((size, chunks)),
            dma((2, size, chunks)),
            dma((size, chunks)),
        ],
        compiler_params=pltpu.CompilerParams(
            collective_id=0, has_side_effects=True, vmem_limit_bytes=VMEM_BYTES
        ),
        cost_estimate=pl.CostEstimate(
            flops=14 * size * own * depth * hidden, bytes_accessed=2**26, transcendentals=0
        ),
    )(mixed, out_weight, tokens, cotangent, hidden_gate, hidden_up, hidden_down, gain, bias)


def back_kernel(
    size,
    bits,
    chunks,
    outp_hbm,
    out_hbm,
    own_hbm,
    middle_ref,
    grads_hbm,
    branch_hbm,
    dmixed_hbm,
    output_ref,
    totals_hbm,
    part,
    out_weight,
    branch,
    inbox,
    dmixed,
    load_sem,
    store_sem,
    rs_send,
    rs_recv,
    ag_send,
    ag_recv,
    cube_parts,
    cube_firsts,
    cube_nexts,
    cube_load,
    cube_store,
    cube_send,
    cube_recv,
    cube_free,
):
    me = lax.axis_index("tensor")
    own, depth = middle_ref.shape
    rows = own // chunks
    load_own = pltpu.make_async_copy(own_hbm, branch.at[me], load_sem.at[0])
    load_part = pltpu.make_async_copy(outp_hbm, part, load_sem.at[1])
    load_out = pltpu.make_async_copy(out_hbm, out_weight, load_sem.at[2])
    load_own.start()
    load_part.start()
    cube = CubeSum(
        bits,
        lax.axis_index("dp"),
        grads_hbm,
        totals_hbm,
        cube_parts,
        cube_firsts,
        cube_nexts,
        cube_load,
        cube_store,
        cube_send,
        cube_recv,
        cube_free,
    )
    for which in range(len(cube_parts)):
        cube.load(which)
    load_out.start()
    enter([{"dp": cube.partner(bit)} for bit in range(bits)], (size, me))
    scatter = LineScatter(size, me, rows, part, inbox, rs_send, rs_recv)
    gather = LineGather(size, me, rows, branch, ag_send, ag_recv)

    def at(chunk):
        return pl.ds(chunk * rows, rows)

    def store(kind, chunk):
        if kind == 0:
            src, dst = branch.at[:, at(chunk)], branch_hbm
        else:
            src, dst = dmixed.at[chunk % 2], dmixed_hbm
        return pltpu.make_async_copy(src, dst.at[:, at(chunk)], store_sem.at[kind, chunk])

    def finish(chunk):
        scatter.arrive(chunk)

        def body(block):
            here = pl.ds(chunk * rows + block.start, LINE)
            output_ref[here, :] = (middle_ref[here, :] + scatter.total(here)).astype(jnp.bfloat16)

        for_rows(rows, body)

    def unproject(chunk):
        if chunk == 0:
            load_out.wait()
        if chunk >= 2:
            store(1, chunk - 2).wait()

        def body(start, width):
            columns = pl.ds(start, width)
            left = branch[:, at(chunk), :].reshape(size * rows, depth)
            value = dot_nt(left, out_weight[columns, :])
            dmixed[chunk % 2, :, :, columns] = value.reshape(size, rows, width)

        for_columns(out_weight.shape[0], body)
        for kind in range(2):
            store(kind, chunk).start()

    def begin_branch(chunk):
        if chunk == 0:
            load_own.wait()
        gather.begin(chunk)

    def begin_out(chunk):
        if chunk == 0:
            load_part.wait()
        scatter.begin(chunk)

    streams, after = [], {}
    for chunk in range(chunks):
        steps = [functools.partial(begin_branch, chunk), *gather.calls(chunk)]
        if chunk:
            after[chunk, 0] = ((chunk - 1, 1),)
            after[chunk, len(steps)] = ((chunk - 1, len(steps) + 1),)
        streams.append(steps + [functools.partial(unproject, chunk)])
    for chunk in range(chunks):
        steps = [functools.partial(begin_out, chunk), *scatter.calls(chunk)]
        if chunk:
            after[chunks + chunk, 0] = ((chunks + chunk - 1, 1),)
        streams.append(steps + [functools.partial(finish, chunk)])
    for which in range(len(cube_parts)):
        streams.append(cube.calls(which))
    run_streams(streams, ORDERS.get(("back", size, chunks, bits)), after)
    for chunk in range(chunks):
        scatter.drain(chunk)
        gather.drain(chunk)
        for kind in range(2 if chunk >= chunks - 2 else 1):
            store(kind, chunk).wait()
    cube.drain()


def feed_back(size, bits, chunks, partial, out_weight, branch, middle, grads):
    own, depth = middle.shape
    rows = own // chunks
    width = out_weight.shape[0]
    low, full = jnp.bfloat16, jnp.float32
    dma = pltpu.SemaphoreType.DMA
    vmem, anywhere = pl.BlockSpec(memory_space=pltpu.VMEM), pl.BlockSpec(memory_space=pl.ANY)
    many = [anywhere] * len(grads)
    return pl.pallas_call(
        functools.partial(back_kernel, size, bits, chunks),
        out_shape=(
            jax.ShapeDtypeStruct((size, own, depth), low),
            jax.ShapeDtypeStruct((size, own, width), full),
            jax.ShapeDtypeStruct((own, depth), low),
            [jax.ShapeDtypeStruct(grad.shape, low) for grad in grads],
        ),
        in_specs=[anywhere, anywhere, anywhere, vmem, many],
        out_specs=(anywhere, anywhere, vmem, many),
        scratch_shapes=[
            pltpu.VMEM((size, own, depth), low),
            pltpu.VMEM(out_weight.shape, low),
            pltpu.VMEM((size, own, depth), low),
            pltpu.VMEM((size + 1, own, depth), low),
            pltpu.VMEM((2, size, rows, width), full),
            dma((3,)),
            dma((2, chunks)),
            dma((size, chunks)),
            dma((size + 1, chunks)),
            dma((2, size, chunks)),
            dma((size, chunks)),
        ]
        + cube_scratch(bits, [grad.shape for grad in grads]),
        compiler_params=pltpu.CompilerParams(
            collective_id=1, has_side_effects=True, vmem_limit_bytes=VMEM_BYTES
        ),
        cost_estimate=pl.CostEstimate(
            flops=2 * size * own * depth * width, bytes_accessed=2**26, transcendentals=0
        ),
    )(partial, out_weight, branch, middle, grads)


def last_kernel(
    size,
    bits,
    chunks,
    dfirst_hbm,
    tokens_ref,
    dmiddle_ref,
    gain_ref,
    sums_ref,
    grads_hbm,
    dtokens_ref,
    totals_ref,
    totals_hbm,
    first_part,
    first_inbox,
    line_box,
    dp_box,
    load_sem,
    line_send,
    line_recv,
    dp_send,
    dp_recv,
    rs_send,
    rs_recv,
    cube_parts,
    cube_firsts,
    cube_nexts,
    cube_load,
    cube_store,
    cube_send,
    cube_recv,
    cube_free,
):
    me = lax.axis_index("tensor")
    mine = lax.axis_index("dp")
    own = tokens_ref.shape[0]
    rows = own // chunks
    load_first = pltpu.make_async_copy(dfirst_hbm, first_part, load_sem.at[0])
    load_first.start()
    cube = CubeSum(
        bits,
        mine,
        grads_hbm,
        totals_hbm,
        cube_parts,
        cube_firsts,
        cube_nexts,
        cube_load,
        cube_store,
        cube_send,
        cube_recv,
        cube_free,
    )
    for which in range(len(cube_parts)):
        cube.load(which)
    groups = 2**bits
    peers = [{"dp": (mine + step) % groups} for step in range(1, groups)]
    others = [{"tensor": (me + step) % size} for step in range(1, size)]
    enter(peers + others, None)
    first = LineScatter(size, me, rows, first_part, first_inbox, rs_send, rs_recv)

    def back(chunk):
        first.arrive(chunk)

        def body(block):
            here = pl.ds(chunk * rows + block.start, LINE)
            values = tokens_ref[here, :].astype(jnp.float32)
            centered = values - jnp.mean(values, axis=-1, keepdims=True)
            scale = lax.rsqrt(jnp.mean(centered * centered, axis=-1, keepdims=True) + EPS)
            normed = centered * scale
            grad = first.total(here)
            shaped = grad * gain_ref[...]
            line_box[me, 2:3, :] += jnp.sum(grad * normed, axis=0, keepdims=True)
            line_box[me, 3:4, :] += jnp.sum(grad, axis=0, keepdims=True)
            dtokens_ref[here, :] = dmiddle_ref[here, :] + scale * (
                shaped
                - jnp.mean(shaped, axis=-1, keepdims=True)
                - normed * jnp.mean(shaped * normed, axis=-1, keepdims=True)
            )

        for_rows(rows, body)

    def line_copy(step, slot):
        return pltpu.make_async_remote_copy(
            src_ref=line_box.at[me],
            dst_ref=line_box.at[slot],
            send_sem=line_send.at[step],
            recv_sem=line_recv.at[slot],
            device_id={"tensor": (me + step) % size},
            device_id_type=MESH,
        )

    def dp_copy(step, slot):
        return pltpu.make_async_remote_copy(
            src_ref=dp_box.at[mine],
            dst_ref=dp_box.at[slot],
            send_sem=dp_send.at[step],
            recv_sem=dp_recv.at[slot],
            device_id={"dp": (mine + step) % groups},
            device_id_type=MESH,
        )

    def sums_on_line():
        for step in range(1, size):
            line_copy(step, me).start()

    def sums_on_dp():
        for step in range(1, size):
            line_copy(step, (me + step) % size).wait_recv()
        dp_box[mine] = jnp.sum(line_box[...], axis=0)
        for step in range(1, groups):
            dp_copy(step, mine).start()

    def sums_done():
        for step in range(1, groups):
            dp_copy(step, (mine + step) % groups).wait_recv()
        totals_ref[...] = jnp.sum(dp_box[...], axis=0)

    line_box[me] = sums_ref[...]
    load_first.wait()
    streams = []
    for chunk in range(chunks):
        streams.append(
            [
                functools.partial(first.begin, chunk),
                *first.calls(chunk),
                functools.partial(back, chunk),
            ]
        )
    after = {(chunks + len(cube_parts), 0): [(chunk, 2 * size - 2) for chunk in range(chunks)]}
    for which in range(len(cube_parts)):
        streams.append(cube.calls(which))
    streams.append([sums_on_line, sums_on_dp, sums_done])
    run_streams(streams, ORDERS.get(("last", size, chunks, bits)), after)
    for chunk in range(chunks):
        first.drain(chunk)
    for step in range(1, size):
        line_copy(step, me).wait_send()
    for step in range(1, groups):
        dp_copy(step, mine).wait_send()
    cube.drain()


def last_sums(size, bits, chunks, dfirst, tokens, dmiddle, gain, sums, grads):
    own, depth = tokens.shape
    low, full = jnp.bfloat16, jnp.float32
    dma = pltpu.SemaphoreType.DMA
    vmem, anywhere = pl.BlockSpec(memory_space=pltpu.VMEM), pl.BlockSpec(memory_space=pl.ANY)
    many = [anywhere] * len(grads)
    return pl.pallas_call(
        functools.partial(last_kernel, size, bits, chunks),
        out_shape=(
            jax.ShapeDtypeStruct((own, depth), full),
            jax.ShapeDtypeStruct((8, depth), full),
            [jax.ShapeDtypeStruct(grad.shape, low) for grad in grads],
        ),
        in_specs=[anywhere, vmem, vmem, vmem, vmem, many],
        out_specs=(vmem, vmem, many),
        scratch_shapes=[
            pltpu.VMEM((size, own, depth), low),
            pltpu.VMEM((size + 1, own, depth), low),
            pltpu.VMEM((size, 8, depth), full),
            pltpu.VMEM((2**bits, 8, depth), full),
            dma((1,)),
            dma((size,)),
            dma((size,)),
            dma((2**bits,)),
            dma((2**bits,)),
            dma((size, chunks)),
            dma((size + 1, chunks)),
        ]
        + cube_scratch(bits, [grad.shape for grad in grads]),
        compiler_params=pltpu.CompilerParams(
            collective_id=2, has_side_effects=True, vmem_limit_bytes=VMEM_BYTES
        ),
        cost_estimate=pl.CostEstimate(flops=2**30, bytes_accessed=2**26, transcendentals=0),
    )(dfirst, tokens, dmiddle, gain, sums, grads)


def per_device(
    tokens,
    first_gain,
    first_bias,
    query_weight,
    key_weight,
    value_weight,
    gate_weight,
    out_weight,
    second_gain,
    second_bias,
    hidden_gate,
    hidden_up,
    hidden_down,
    segments,
    cotangent,
):
    seq_count, seq_len = segments.shape
    group_rows = seq_count * seq_len
    head_local = query_weight.shape[1] // KD
    scale_factor = KD ** (-0.5)
    inputs = tokens.astype(jnp.float32)
    seed_all = lax.all_gather(cotangent, "tensor", axis=0, tiled=True)
    first_out, first_normed, first_scale = norm_parts(inputs, first_gain, first_bias)
    first_all = lax.all_gather(first_out.astype(jnp.bfloat16), "tensor", axis=0, tiled=True)
    queries = product(first_all, query_weight).astype(jnp.bfloat16)
    keys_low = product(first_all, key_weight).astype(jnp.bfloat16)
    values = product(first_all, value_weight).astype(jnp.bfloat16)
    gates = product(first_all, gate_weight)
    head_index = (lax.axis_index("tensor") * head_local + jnp.arange(head_local)).astype(
        jnp.float32
    )
    rates = -jnp.log1p(-jnp.exp2(-5.0 - head_index))
    table = decay_table(segments, rates)
    query_heads = queries.reshape(seq_count, seq_len, head_local, KD)
    key_heads = keys_low.reshape(seq_count, seq_len, head_local, KD)
    value_heads = values.reshape(seq_count, seq_len, head_local, VD)
    scores = (
        jnp.einsum("bnhk,bmhk->bhnm", query_heads, key_heads, preferred_element_type=jnp.float32)
        * scale_factor
    )

    def score_step(raw):
        return normalize_scores(raw, table)

    retain_full, score_pull = jax.vjp(score_step, scores)
    retain = retain_full.astype(jnp.bfloat16)
    retained = jnp.einsum(
        "bhnm,bmhv->bnhv", retain, value_heads, preferred_element_type=jnp.float32
    )
    gate_heads = gates.reshape(seq_count, seq_len, head_local, VD)
    mixed_full, mix_pull = jax.vjp(gated_norm, gate_heads, retained)
    mixed = mixed_full.reshape(group_rows, head_local * VD).astype(jnp.bfloat16)
    size = lax.axis_size("tensor")
    bits = lax.axis_size("dp").bit_length() - 1
    own = tokens.shape[0]
    (
        second_all,
        seed_all,
        inner,
        gate_in_low,
        lin_in_low,
        partial,
        middle,
        grad_middle,
        branch,
        second_sums,
    ) = feed_forward(
        size,
        CHUNKS,
        mixed.reshape(size, own, head_local * VD),
        out_weight,
        tokens,
        cotangent,
        hidden_gate.T,
        hidden_up.T,
        hidden_down,
        second_gain[None],
        second_bias[None],
    )

    def flat(item):
        return item.reshape(group_rows, item.shape[-1])

    second_all, seed_all = flat(second_all), flat(seed_all)
    feed_grads = [
        product_tn(flat(inner), seed_all).astype(jnp.bfloat16),
        product_tn(flat(gate_in_low), second_all).astype(jnp.bfloat16),
        product_tn(flat(lin_in_low), second_all).astype(jnp.bfloat16),
    ]
    branch_all, grad_mixed, output, feed_grads = feed_back(
        size, bits, CHUNKS, partial, out_weight, branch, middle, feed_grads
    )
    branch_all = flat(branch_all)
    grad_gates, grad_retained = mix_pull(grad_mixed.reshape(seq_count, seq_len, head_local, VD))
    gates_low = grad_gates.reshape(group_rows, head_local * VD).astype(jnp.bfloat16)
    retained_low = grad_retained.astype(jnp.bfloat16)
    grad_retain = jnp.einsum(
        "bnhv,bmhv->bhnm", retained_low, value_heads, preferred_element_type=jnp.float32
    )
    grad_values = jnp.einsum(
        "bhnm,bnhv->bmhv", retain, retained_low, preferred_element_type=jnp.float32
    )
    values_low = grad_values.reshape(group_rows, head_local * VD).astype(jnp.bfloat16)
    (grad_scores,) = score_pull(grad_retain)
    scores_low = grad_scores.astype(jnp.bfloat16)
    grad_queries = (
        jnp.einsum("bhnm,bmhk->bnhk", scores_low, key_heads, preferred_element_type=jnp.float32)
        * scale_factor
    )
    grad_keys = (
        jnp.einsum("bhnm,bnhk->bmhk", scores_low, query_heads, preferred_element_type=jnp.float32)
        * scale_factor
    )
    queries_low = grad_queries.reshape(group_rows, head_local * KD).astype(jnp.bfloat16)
    keys_back = grad_keys.reshape(group_rows, head_local * KD).astype(jnp.bfloat16)
    grads = [
        product_tn(mixed, branch_all).astype(jnp.bfloat16),
        product_tn(values_low, first_all).astype(jnp.bfloat16),
        product_tn(gates_low, first_all).astype(jnp.bfloat16),
        product_tn(first_all, queries_low).astype(jnp.bfloat16),
        product_tn(first_all, keys_back).astype(jnp.bfloat16),
    ]
    total = product_nt(queries_low, query_weight)
    total = total + product_nt(keys_back, key_weight)
    total = total + product_nt(values_low, value_weight)
    total = (total + product_nt(gates_low, gate_weight)).astype(jnp.bfloat16)
    grad_tokens, sums, grads = last_sums(
        size,
        bits,
        CHUNKS,
        total.reshape(size, own, total.shape[-1]),
        tokens,
        grad_middle,
        first_gain[None],
        second_sums,
        grads,
    )
    grad_sgain, grad_sbias, grad_fgain, grad_fbias = sums[0], sums[1], sums[2], sums[3]
    grad_outw, grad_valuew, grad_gatew, grad_queryw, grad_keyw = (
        item.astype(jnp.float32) for item in grads
    )
    grad_hdown, grad_hgate, grad_hup = (item.astype(jnp.float32) for item in feed_grads)
    grad_valuew, grad_gatew, grad_hgate, grad_hup = (
        item.T for item in (grad_valuew, grad_gatew, grad_hgate, grad_hup)
    )
    return (
        output,
        grad_tokens,
        grad_fgain,
        grad_fbias,
        grad_queryw,
        grad_keyw,
        grad_valuew,
        grad_gatew,
        grad_outw,
        grad_sgain,
        grad_sbias,
        grad_hgate,
        grad_hup,
        grad_hdown,
    )


def solution(mesh):
    return jax.shard_map(
        per_device,
        mesh=mesh,
        in_specs=(
            P(("dp", "tensor"), None),
            P(),
            P(),
            P(None, "tensor"),
            P(None, "tensor"),
            P(None, "tensor"),
            P(None, "tensor"),
            P("tensor", None),
            P(),
            P(),
            P(None, "tensor"),
            P(None, "tensor"),
            P("tensor", None),
            P("dp", None),
            P(("dp", "tensor"), None),
        ),
        out_specs=(
            P(("dp", "tensor"), None),
            P(("dp", "tensor"), None),
            P(),
            P(),
            P(None, "tensor"),
            P(None, "tensor"),
            P(None, "tensor"),
            P(None, "tensor"),
            P("tensor", None),
            P(),
            P(),
            P(None, "tensor"),
            P(None, "tensor"),
            P("tensor", None),
        ),
        check_vma=False,
    )
```

```python
import functools
import itertools

import jax
import jax.numpy as jnp
from jax import lax
from jax.experimental import pallas as pl
from jax.experimental.pallas import tpu as pltpu
from jax.sharding import PartitionSpec as P

KD = 256
VD = 432


EPS = 1e-05
GROUP_EPS = 0.1
GELU_SCALE = 0.7978845608028654
CHUNKS = 4

MESH = pl.DeviceIdType.MESH
VMEM_BYTES = 60 * 2**20
TILE = 256
LINE = 16
BAND = 64


def product_tn(left, right):
    return lax.dot_general(
        left, right, (((0,), (0,)), ((), ())), preferred_element_type=jnp.float32
    )


def for_columns(width, body):
    full = width // TILE

    def step(index, carry):
        body(pl.multiple_of(index * TILE, TILE), TILE)
        return carry

    if full:
        lax.fori_loop(0, full, step, 0)
    if width % TILE:
        body(full * TILE, width % TILE)


def for_rows(count, body, size=LINE):
    def step(index, carry):
        body(pl.ds(pl.multiple_of(index * size, LINE), size))
        return carry

    lax.fori_loop(0, count // size, step, 0)


def dot_nn(left, right):
    return lax.dot_general(left, right, (((1,), (0,)), ((), ())), preferred_element_type=jnp.float32)


def dot_nt(left, right):
    return lax.dot_general(left, right, (((1,), (1,)), ((), ())), preferred_element_type=jnp.float32)


def dot_tn(left, right):
    return lax.dot_general(left, right, (((0,), (0,)), ((), ())), preferred_element_type=jnp.float32)


def enter(peers, line):
    barrier = pltpu.get_barrier_semaphore()
    for peer in peers:
        pl.semaphore_signal(barrier, inc=1, device_id=peer, device_id_type=MESH)
    if line is not None:
        size, me = line

        @pl.when(me > 0)
        def _():
            pl.semaphore_signal(barrier, inc=1, device_id={"tensor": me - 1}, device_id_type=MESH)

        @pl.when(me < size - 1)
        def _():
            pl.semaphore_signal(barrier, inc=1, device_id={"tensor": me + 1}, device_id_type=MESH)

    count = len(peers)
    if line is not None:
        count = count + (me > 0).astype(jnp.int32) + (me < size - 1).astype(jnp.int32)
    pl.semaphore_wait(barrier, count)


class LineScatter:
    def __init__(self, size, me, rows, part, inbox, send, recv):
        self.size, self.me, self.rows = size, me, rows
        self.part, self.inbox, self.send, self.recv = part, inbox, send, recv

    def at(self, chunk):
        return pl.ds(chunk * self.rows, self.rows)

    def copy(self, target, slot, chunk, device):
        return pltpu.make_async_remote_copy(
            src_ref=self.part.at[target, self.at(chunk)],
            dst_ref=self.inbox.at[slot, self.at(chunk)],
            send_sem=self.send.at[target, chunk],
            recv_sem=self.recv.at[slot, chunk],
            device_id={"tensor": device},
            device_id_type=MESH,
        )

    def add(self, target, chunk):
        def body(rows):
            at = pl.ds(chunk * self.rows + rows.start, LINE)
            total = self.part[target, at, :].astype(jnp.float32)
            total = total + self.inbox[target, at, :].astype(jnp.float32)
            self.part[target, at, :] = total.astype(jnp.bfloat16)

        for_rows(self.rows, body)

    def go_right(self, chunk, target):
        self.copy(target, target, chunk, self.me + 1).start()

    def go_left(self, chunk, target):
        last = self.me - 1 == target
        self.copy(target, jnp.where(last, self.size, target), chunk, self.me - 1).start()

    def begin(self, chunk):
        @pl.when(self.me == 0)
        def _():
            for target in range(self.size - 1, 0, -1):
                self.go_right(chunk, target)

        @pl.when(self.me == self.size - 1)
        def _():
            for target in range(self.size - 1):
                self.go_left(chunk, target)

    def right(self, chunk, target):
        @pl.when((self.me < target) & (self.me > 0))
        def _():
            self.copy(target, target, chunk, self.me).wait_recv()
            self.add(target, chunk)
            self.go_right(chunk, target)

    def left(self, chunk, target):
        @pl.when((self.me > target) & (self.me < self.size - 1))
        def _():
            self.copy(target, target, chunk, self.me).wait_recv()
            self.add(target, chunk)
            self.go_left(chunk, target)

    def calls(self, chunk):
        for step in range(self.size - 1):
            if step < self.size - 2:
                yield functools.partial(self.right, chunk, self.size - 1 - step)
                yield functools.partial(self.left, chunk, step)

    def arrive(self, chunk):
        size, me = self.size, self.me

        @pl.when(me > 0)
        def _():
            self.copy(me, me, chunk, me - 1).wait_recv()

        @pl.when(me < size - 1)
        def _():
            self.copy(me, size, chunk, me + 1).wait_recv()

    def total(self, rows):
        size, me = self.size, self.me
        own = self.part[me, rows, :].astype(jnp.float32)
        low = self.inbox[me, rows, :].astype(jnp.float32)
        high = self.inbox[size, rows, :].astype(jnp.float32)
        return own + jnp.where(me > 0, low, 0.0) + jnp.where(me < size - 1, high, 0.0)

    def drain(self, chunk):
        for target in range(self.size):

            @pl.when(self.me != target)
            def _():
                self.copy(target, target, chunk, self.me).wait_send()


class LineGather:
    def __init__(self, size, me, rows, held, send, recv):
        self.size, self.me, self.rows = size, me, rows
        self.held, self.send, self.recv = held, send, recv

    def copy(self, block, chunk, way, device):
        at = pl.ds(chunk * self.rows, self.rows)
        return pltpu.make_async_remote_copy(
            src_ref=self.held.at[block, at],
            dst_ref=self.held.at[block, at],
            send_sem=self.send.at[way, block, chunk],
            recv_sem=self.recv.at[block, chunk],
            device_id={"tensor": device},
            device_id_type=MESH,
        )

    def begin(self, chunk):
        self.right(chunk, 0)
        self.left(chunk, 0)

    def right(self, chunk, step):
        size, me = self.size, self.me

        @pl.when(me >= step)
        def _():
            if step:
                self.copy(me - step, chunk, 0, me).wait_recv()

            @pl.when(me < size - 1)
            def _():
                self.copy(me - step, chunk, 0, me + 1).start()

    def left(self, chunk, step):
        size, me = self.size, self.me

        @pl.when(me + step < size)
        def _():
            if step:
                self.copy(me + step, chunk, 1, me).wait_recv()

            @pl.when(me > 0)
            def _():
                self.copy(me + step, chunk, 1, me - 1).start()

    def calls(self, chunk):
        for step in range(1, self.size):
            yield functools.partial(self.right, chunk, step)
            yield functools.partial(self.left, chunk, step)

    def drain(self, chunk):
        size, me = self.size, self.me
        for step in range(size):

            @pl.when((me >= step) & (me < size - 1))
            def _():
                self.copy(me - step, chunk, 0, me + 1).wait_send()

            @pl.when((me + step < size) & (me > 0))
            def _():
                self.copy(me + step, chunk, 1, me - 1).wait_send()


class CubeSum:
    def __init__(self, bits, me, sources, results, parts, firsts, nexts, load, store, send, recv, free):
        self.bits, self.me = bits, me
        self.sources, self.results, self.parts = sources, results, parts
        self.firsts, self.nexts = firsts, nexts
        self.load_sem, self.store_sem, self.send, self.recv = load, store, send, recv
        self.free = free
        self.orders = (tuple(range(bits)), (0,) + tuple(range(bits - 1, 0, -1)))
        self.mine = [(me // 2**bit) % 2 for bit in range(bits)]

    def partner(self, bit):
        return self.me + (1 - 2 * self.mine[bit]) * 2**bit

    def band(self, which, color):
        count = self.parts[which].shape[-2]
        cut = cut_rows(count)
        return ((0, cut), (cut, count - cut), (0, count))[color]

    def lead(self, fixed):
        return tuple(fixed.get(bit, slice(None)) for bit in range(self.bits - 1, -1, -1))

    def moved(self, src, dst, which, color, step, bit):
        return pltpu.make_async_remote_copy(
            src_ref=src,
            dst_ref=dst,
            send_sem=self.send.at[which, color % 2, step],
            recv_sem=self.recv.at[which, color % 2, step],
            device_id={"dp": self.partner(bit)},
            device_id_type=MESH,
        )

    def halve(self, which, color, step):
        order = self.orders[color % 2]
        start, count = self.band(which, color)
        fixed = {bit: self.mine[bit] for bit in order[:step]}
        fixed[order[step]] = 1 - self.mine[order[step]]
        src = self.parts[which].at[self.lead(fixed) + (pl.ds(start, count), slice(None))]
        dst = self.firsts[which] if step == 0 else self.nexts[which][color][step - 1]
        return self.moved(src, dst, which, color, step, order[step])

    def double(self, which, color, step):
        order = self.orders[color % 2]
        start, count = self.band(which, color)
        fixed = {bit: self.mine[bit] for bit in order[: step + 1]}
        held = self.parts[which].at[self.lead(fixed) + (pl.ds(start, count), slice(None))]
        return self.moved(held, held, which, color, 2 * self.bits - 1 - step, order[step])

    def freed(self, which, color, step):
        return self.free.at[which, color % 2, step]

    def land(self, which, color, step):
        copy = self.halve(which, color, step)
        copy.wait_send()
        partner = {"dp": self.partner(self.orders[color % 2][step])}
        pl.semaphore_signal(
            self.freed(which, color, step), inc=1, device_id=partner, device_id_type=MESH
        )
        copy.wait_recv()
        self.add(which, color, step)

    def grow(self, which, color, step):
        pl.semaphore_wait(self.freed(which, color, step), 1)
        self.double(which, color, step).start()

    def add(self, which, color, step):
        order = self.orders[color % 2]
        part, (start, count) = self.parts[which], self.band(which, color)
        box = self.firsts[which] if step == 0 else self.nexts[which][color][step - 1]
        fixed = {bit: self.mine[bit] for bit in order[: step + 1]}
        free = [bit for bit in range(self.bits - 1, -1, -1) if bit not in fixed]
        for choice in itertools.product((0, 1), repeat=len(free)):
            lead = self.lead({**fixed, **dict(zip(free, choice))})

            def body(begin, size):
                there = lead + (pl.ds(start + begin, size), slice(None))
                total = part[there].astype(jnp.float32)
                total = total + box[choice + (pl.ds(begin, size), slice(None))].astype(jnp.float32)
                part[there] = total.astype(jnp.bfloat16)

            for_blocks(count, part.shape[-1], body)

    def slices(self, which, ref):
        rows, columns = self.parts[which].shape[-2:]
        for index in range(2**self.bits):
            lead = tuple((index >> bit) & 1 for bit in range(self.bits - 1, -1, -1))
            if ref.shape[0] == rows:
                whole = ref.at[:, pl.ds(index * columns, columns)]
            else:
                whole = ref.at[pl.ds(index * rows, rows), :]
            yield index, self.parts[which].at[lead], whole

    def load(self, which):
        for index, part, whole in self.slices(which, self.sources[which]):
            pltpu.make_async_copy(whole, part, self.load_sem.at[which, index]).start()

    def open(self, which):
        for index, part, whole in self.slices(which, self.sources[which]):
            pltpu.make_async_copy(whole, part, self.load_sem.at[which, index]).wait()
        self.halve(which, 2, 0).start()

    def split(self, which):
        self.land(which, 2, 0)
        for color in range(2):
            self.halve(which, color, 1).start()

    def down(self, which, color, step):
        self.land(which, color, step - 1)
        self.halve(which, color, step).start()

    def turn(self, which, color):
        self.land(which, color, self.bits - 1)
        self.grow(which, color, self.bits - 1)

    def up(self, which, color, step):
        self.double(which, color, step + 1).wait_recv()
        self.grow(which, color, step)

    def join(self, which):
        for color in range(2):
            self.double(which, color, 1).wait_recv()
        self.grow(which, 2, 0)

    def close(self, which):
        self.double(which, 2, 0).wait_recv()
        for index, part, whole in self.slices(which, self.results[which]):
            pltpu.make_async_copy(part, whole, self.store_sem.at[which, index]).start()

    def calls(self, which):
        yield functools.partial(self.open, which)
        yield functools.partial(self.split, which)
        for step in range(2, self.bits):
            for color in range(2):
                yield functools.partial(self.down, which, color, step)
        for color in range(2):
            yield functools.partial(self.turn, which, color)
        for step in range(self.bits - 2, 0, -1):
            for color in range(2):
                yield functools.partial(self.up, which, color, step)
        yield functools.partial(self.join, which)
        yield functools.partial(self.close, which)

    def drain(self):
        for which in range(len(self.parts)):
            self.double(which, 2, 0).wait_send()
            for color in range(2):
                for step in range(1, self.bits):
                    self.double(which, color, step).wait_send()
            for index, part, whole in self.slices(which, self.results[which]):
                pltpu.make_async_copy(part, whole, self.store_sem.at[which, index]).wait()


def cut_rows(count):
    return count // (2 * LINE) * LINE


def for_blocks(count, columns, body):
    size = LINE
    while count % (2 * size) == 0 and 2 * size * columns <= 2**14:
        size *= 2
    for factor in (3, 5):
        if count % (factor * size) == 0 and factor * size * columns <= 2**14:
            size *= factor

    def step(index, carry):
        body(pl.multiple_of(index * size, LINE), size)
        return carry

    lax.fori_loop(0, count // size, step, 0)


def cube_scratch(bits, shapes):
    low = jnp.bfloat16
    parts, firsts, nexts = [], [], []
    for rows, columns in shapes:
        if columns >= rows:
            columns = columns // 2**bits
        else:
            rows = rows // 2**bits
        cut = cut_rows(rows)
        parts.append(pltpu.VMEM((2,) * bits + (rows, columns), low))
        firsts.append(pltpu.VMEM((2,) * (bits - 1) + (rows, columns), low))
        nexts.append(
            [
                [
                    pltpu.VMEM((2,) * (bits - 1 - step) + (count, columns), low)
                    for step in range(1, bits)
                ]
                for count in (cut, rows - cut)
            ]
        )
    dma = pltpu.SemaphoreType.DMA
    return [
        parts,
        firsts,
        nexts,
        dma((len(shapes), 2**bits)),
        dma((len(shapes), 2**bits)),
        dma((len(shapes), 2, 2 * bits)),
        dma((len(shapes), 2, 2 * bits)),
        pltpu.SemaphoreType.REGULAR((len(shapes), 2, bits)),
    ]


ORDERS = {
    ("feed", 4, 4): (
        4, 6, 4, 0, 5, 4, 4, 0, 4, 6, 5, 0, 5, 0, 0, 2, 5, 6, 1, 2, 0, 3, 4, 4,
        6, 1, 6, 7, 5, 0, 6, 1, 1, 5, 2, 0, 0, 1, 3, 2, 0, 1, 7, 3, 3, 0, 5, 1,
        0, 2, 0, 1, 0, 3, 2, 0, 0, 1, 1, 1, 3, 0, 1, 1, 1, 2, 2, 1, 1, 2, 1, 6,
        0, 2, 3, 3, 2, 7, 7, 2, 2, 2, 3, 2, 2, 1, 3, 3, 7, 0, 0, 2, 3, 3, 1, 2,
        7, 1, 7, 0, 3, 1, 3, 3, 3, 3, 2, 2, 0, 3, 2, 3, 3, 2, 1, 3,
    ),
    ("back", 4, 4, 3): (
        0, 8, 9, 4, 10, 1, 5, 2, 8, 9, 4, 3, 10, 8, 8, 6, 0, 1, 9, 9, 4, 0, 1, 0,
        10, 10, 5, 8, 4, 8, 9, 0, 2, 9, 3, 5, 10, 8, 8, 2, 0, 10, 0, 9, 0, 9, 7, 3,
        1, 6, 1, 5, 6, 5, 1, 8, 4, 1, 3, 2, 10, 10, 7, 6, 3, 2, 7, 3, 9, 6, 7, 1,
        2, 3, 8, 10, 5, 4, 2, 6, 7, 2, 9, 3, 10, 7,
    ),
    ("last", 4, 4, 3): (
        7, 0, 4, 7, 4, 6, 0, 6, 4, 5, 2, 4, 3, 0, 6, 6, 8, 1, 0, 0, 7, 4, 5, 7,
        2, 0, 6, 4, 8, 5, 7, 4, 6, 3, 8, 5, 1, 4, 6, 1, 8, 7, 7, 6, 5, 3, 1, 2,
        2, 5, 8, 2, 1, 3, 8, 5, 7, 4, 3, 1, 2, 8, 5, 6, 3, 7, 9, 4, 8, 9, 5, 7,
        9, 8, 6, 5, 8,
    ),
    ("feed", 4, 8): (
        11, 10, 13, 8, 9, 13, 1, 8, 13, 8, 10, 0, 14, 10, 12, 8, 13, 10, 13, 0, 1, 10, 8, 11,
        9, 12, 2, 14, 0, 0, 1, 1, 11, 8, 1, 3, 0, 9, 11, 9, 5, 12, 2, 1, 3, 10, 12, 11,
        9, 14, 0, 8, 7, 6, 5, 1, 12, 0, 3, 3, 2, 2, 4, 5, 0, 0, 2, 9, 3, 9, 11, 15,
        6, 14, 0, 1, 1, 0, 0, 2, 3, 4, 12, 0, 7, 5, 13, 1, 15, 2, 7, 0, 7, 0, 4, 0,
        4, 6, 6, 10, 4, 2, 0, 2, 1, 12, 5, 1, 1, 1, 4, 1, 3, 1, 1, 2, 11, 3, 6, 2,
        5, 2, 4, 13, 2, 3, 2, 2, 4, 7, 2, 3, 15, 0, 2, 6, 3, 4, 3, 15, 3, 3, 3, 5,
        3, 4, 4, 3, 4, 5, 1, 4, 7, 4, 5, 4, 4, 2, 5, 5, 14, 6, 1, 1, 4, 7, 5, 5,
        2, 5, 14, 5, 14, 0, 6, 1, 6, 4, 5, 6, 7, 5, 3, 6, 6, 6, 6, 7, 6, 5, 7, 2,
        0, 7, 15, 3, 3, 6, 4, 15, 4, 6, 7, 7, 5, 5, 0, 15, 3, 2, 5, 7, 1, 4, 7, 6,
        7, 7, 7, 6, 6, 3, 5, 7, 7, 6, 7, 6, 2, 0, 4, 7,
    ),
    ("back", 4, 8, 3): (
        0, 16, 8, 1, 18, 0, 9, 2, 3, 16, 0, 17, 0, 4, 18, 5, 17, 8, 16, 6, 16, 9, 0, 18,
        0, 3, 2, 18, 4, 1, 10, 9, 8, 6, 5, 17, 3, 6, 17, 11, 9, 6, 16, 12, 4, 3, 16, 18,
        7, 18, 2, 5, 10, 17, 17, 11, 1, 16, 12, 16, 0, 3, 18, 2, 5, 18, 2, 5, 7, 8, 1, 10,
        4, 13, 14, 3, 6, 10, 11, 11, 6, 15, 17, 1, 4, 1, 3, 5, 12, 8, 7, 10, 17, 14, 11, 2,
        16, 1, 8, 12, 0, 2, 7, 9, 1, 2, 12, 7, 5, 6, 13, 3, 18, 15, 13, 4, 13, 10, 12, 14,
        14, 4, 4, 11, 17, 15, 15, 7, 16, 13, 7, 18, 14, 5, 6, 13, 7, 15, 9, 14, 17, 15,
    ),
    ("last", 4, 8, 3): (
        11, 0, 9, 11, 10, 8, 12, 6, 9, 11, 10, 3, 2, 0, 6, 11, 9, 5, 1, 11, 8, 3, 6, 12,
        7, 0, 9, 4, 5, 12, 10, 11, 9, 6, 9, 10, 11, 2, 11, 12, 8, 7, 12, 1, 6, 4, 10, 9,
        4, 2, 12, 8, 5, 2, 10, 2, 8, 9, 3, 4, 7, 1, 0, 8, 10, 3, 4, 11, 1, 8, 1, 10,
        5, 0, 3, 5, 7, 0, 7, 8, 9, 1, 11, 2, 3, 4, 5, 6, 9, 12, 12, 10, 7, 13, 13, 8,
        13, 12, 8, 10, 12,
    ),
}


def run_streams(streams, order, after):
    streams = [list(stream) for stream in streams]
    done = [0] * len(streams)

    def ready(stream):
        place = done[stream]
        return place < len(streams[stream]) and all(
            done[other] >= count for other, count in after.get((stream, place), ())
        )

    def take(stream):
        streams[stream][done[stream]]()
        done[stream] += 1

    if order is not None:
        for stream in order:
            assert ready(stream)
            take(stream)
    while any(done[index] < len(stream) for index, stream in enumerate(streams)):
        for stream in range(len(streams)):
            if ready(stream):
                take(stream)


def feed_kernel(
    size,
    chunks,
    mixed_hbm,
    out_hbm,
    tokens_hbm,
    seed_hbm,
    gate_hbm,
    up_hbm,
    down_hbm,
    gain_ref,
    bias_ref,
    second_hbm,
    seeds_hbm,
    inner_hbm,
    dgate_hbm,
    dlin_hbm,
    outp_hbm,
    middle_ref,
    dmiddle_ref,
    branch_ref,
    sums_ref,
    mixed,
    out_weight,
    tokens,
    hidden_gate,
    hidden_up,
    hidden_down,
    second,
    seeds,
    part,
    inbox,
    gate_in,
    lin_in,
    dinner,
    inner,
    dgate,
    dlin,
    wide,
    load_sem,
    store_sem,
    rs_send,
    rs_recv,
    back_send,
    back_recv,
    ag_send,
    ag_recv,
    seed_send,
    seed_recv,
):
    me = lax.axis_index("tensor")
    own, depth = tokens.shape
    rows = own // chunks
    hidden = inner.shape[-1]
    loads = [
        pltpu.make_async_copy(src, dst, load_sem.at[index])
        for index, (src, dst) in enumerate(
            (
                (mixed_hbm, mixed),
                (out_hbm, out_weight),
                (seed_hbm, seeds.at[me]),
                (tokens_hbm, tokens),
                (gate_hbm, hidden_gate),
                (up_hbm, hidden_up),
                (down_hbm, hidden_down),
            )
        )
    ]
    for load in loads:
        load.start()
    enter((), (size, me))
    scatter = LineScatter(size, me, rows, part, inbox, rs_send, rs_recv)
    scatter_back = LineScatter(size, me, rows, part, inbox, back_send, back_recv)
    gather = LineGather(size, me, rows, second, ag_send, ag_recv)
    gather_seed = LineGather(size, me, rows, seeds, seed_send, seed_recv)

    def at(chunk):
        return pl.ds(chunk * rows, rows)

    def flat(ref, chunk):
        value = ref[:, at(chunk), :]
        return value.reshape(size * rows, value.shape[-1])

    def store(kind, chunk):
        slot = chunk % 2
        src, dst = (
            (second.at[:, at(chunk)], second_hbm),
            (seeds.at[:, at(chunk)], seeds_hbm),
            (inner.at[slot], inner_hbm),
            (dgate.at[slot], dgate_hbm),
            (dlin.at[slot], dlin_hbm),
            (wide.at[slot], outp_hbm),
        )[kind]
        return pltpu.make_async_copy(src, dst.at[:, at(chunk)], store_sem.at[kind, chunk])

    waited = set()

    def need(*indices):
        for index in indices:
            if index not in waited:
                waited.add(index)
                loads[index].wait()

    def project(chunk):
        need(0, 1)

        def body(start, width):
            value = dot_nn(flat(mixed, chunk), out_weight[:, pl.ds(start, width)])
            part[:, at(chunk), pl.ds(start, width)] = value.astype(jnp.bfloat16).reshape(
                size, rows, width
            )

        for_columns(depth, body)
        scatter.begin(chunk)

    def normalize(chunk):
        need(3)
        scatter.arrive(chunk)

        def body(block):
            here = pl.ds(chunk * rows + block.start, LINE)
            middle = tokens[here, :].astype(jnp.float32) + scatter.total(here)
            middle_ref[here, :] = middle
            centered = middle - jnp.mean(middle, axis=-1, keepdims=True)
            scale = lax.rsqrt(jnp.mean(centered * centered, axis=-1, keepdims=True) + EPS)
            value = centered * scale * gain_ref[...] + bias_ref[...]
            second[me, here, :] = value.astype(jnp.bfloat16)

        for_rows(rows, body)
        gather.begin(chunk)

    def feed_in(chunk):
        need(4, 5)

        def body(start, width):
            columns = pl.ds(start, width)
            gate_in[:, columns] = dot_nt(flat(second, chunk), hidden_gate[columns, :])
            lin_in[:, columns] = dot_nt(flat(second, chunk), hidden_up[columns, :])

        for_columns(hidden, body)
        store(0, chunk).start()

    def feed_seed(chunk):
        need(6)

        def body(start, width):
            columns = pl.ds(start, width)
            dinner[:, columns] = dot_nt(flat(seeds, chunk), hidden_down[columns, :])

        for_columns(hidden, body)
        store(1, chunk).start()

    def feed_act(chunk):
        slot = chunk % 2
        if chunk >= 2:
            for kind in range(2, 5):
                store(kind, chunk - 2).wait()

        def body(block):
            gate, lin, grad = gate_in[block, :], lin_in[block, :], dinner[block, :]
            cube = GELU_SCALE * (gate + 0.044715 * (gate * gate * gate))
            tanh = jnp.tanh(cube)
            half = 0.5 * (1.0 + tanh)
            active = gate * half
            slope = half + 0.5 * gate * (1.0 - tanh * tanh) * (
                GELU_SCALE * (1.0 + 3.0 * 0.044715 * (gate * gate))
            )
            owner = block.start // rows
            inside = pl.ds(block.start - owner * rows, LINE)
            inner[slot, owner, inside, :] = (active * lin).astype(jnp.bfloat16)
            dlin[slot, owner, inside, :] = (grad * active).astype(jnp.bfloat16)
            dgate[slot, owner, inside, :] = (grad * lin * slope).astype(jnp.bfloat16)

        for_rows(size * rows, body)
        for kind in range(2, 5):
            store(kind, chunk).start()

    def feed_back(chunk):
        slot = chunk % 2
        scatter.drain(chunk)

        def body(start, width):
            columns = pl.ds(start, width)
            dgate_all = dgate[slot].reshape(size * rows, hidden)
            dlin_all = dlin[slot].reshape(size * rows, hidden)
            grad = dot_nn(dgate_all, hidden_gate[:, columns])
            grad = grad + dot_nn(dlin_all, hidden_up[:, columns])
            part[:, at(chunk), columns] = grad.astype(jnp.bfloat16).reshape(size, rows, width)

        for_columns(depth, body)
        scatter_back.begin(chunk)

    def feed_out(chunk):
        slot = chunk % 2
        if chunk >= 2:
            store(5, chunk - 2).wait()

        def body(start, width):
            columns = pl.ds(start, width)
            inner_all = inner[slot].reshape(size * rows, hidden)
            value = dot_nn(inner_all, hidden_down[:, columns])
            wide[slot, :, :, columns] = value.astype(jnp.bfloat16).reshape(size, rows, width)

        for_columns(depth, body)
        store(5, chunk).start()

    def normalize_back(chunk):
        scatter_back.arrive(chunk)

        def body(block):
            here = pl.ds(chunk * rows + block.start, LINE)
            middle = middle_ref[here, :]
            centered = middle - jnp.mean(middle, axis=-1, keepdims=True)
            scale = lax.rsqrt(jnp.mean(centered * centered, axis=-1, keepdims=True) + EPS)
            normed = centered * scale
            grad = scatter_back.total(here)
            shaped = grad * gain_ref[...]
            sums_ref[0:1, :] += jnp.sum(grad * normed, axis=0, keepdims=True)
            sums_ref[1:2, :] += jnp.sum(grad, axis=0, keepdims=True)
            dmiddle = seeds[me, here, :].astype(jnp.float32) + scale * (
                shaped
                - jnp.mean(shaped, axis=-1, keepdims=True)
                - normed * jnp.mean(shaped * normed, axis=-1, keepdims=True)
            )
            dmiddle_ref[here, :] = dmiddle
            branch_ref[here, :] = dmiddle.astype(jnp.bfloat16)

        for_rows(rows, body)

    def begin_seed(chunk):
        need(2)
        gather_seed.begin(chunk)

    streams, after = [], {}
    for chunk in range(chunks):
        steps = [project, *scatter.calls(chunk), normalize, *gather.calls(chunk)]
        first_feed = len(steps)
        steps += [feed_in, feed_seed, feed_act, feed_back, feed_out]
        steps += [*scatter_back.calls(chunk), normalize_back]
        streams.append(
            [step if isinstance(step, functools.partial) else functools.partial(step, chunk) for step in steps]
        )
        if chunk:
            after[chunk, first_feed] = ((chunk - 1, first_feed + 5),)
        after[chunk, first_feed + 1] = ((chunks + chunk, 2 * size - 1),)
    for chunk in range(chunks):
        streams.append([functools.partial(begin_seed, chunk), *gather_seed.calls(chunk)])
    sums_ref[...] = jnp.zeros_like(sums_ref)
    run_streams(streams, ORDERS.get(("feed", size, chunks)), after)
    for chunk in range(chunks):
        scatter_back.drain(chunk)
        gather.drain(chunk)
        gather_seed.drain(chunk)
        for kind in range(6 if chunk >= chunks - 2 else 2):
            store(kind, chunk).wait()


def feed_forward(size, chunks, mixed, out_weight, tokens, cotangent, hidden_gate, hidden_up, hidden_down, gain, bias):
    own, depth = tokens.shape
    hidden = hidden_gate.shape[0]
    rows = own // chunks
    low, full = jnp.bfloat16, jnp.float32

    def blocks(width):
        return jax.ShapeDtypeStruct((size, own, width), low)

    dma = pltpu.SemaphoreType.DMA
    wide, thin = (size, own, depth), (2, size, rows, hidden)
    return pl.pallas_call(
        functools.partial(feed_kernel, size, chunks),
        out_shape=(
            blocks(depth),
            blocks(depth),
            blocks(hidden),
            blocks(hidden),
            blocks(hidden),
            blocks(depth),
            jax.ShapeDtypeStruct((own, depth), full),
            jax.ShapeDtypeStruct((own, depth), full),
            jax.ShapeDtypeStruct((own, depth), low),
            jax.ShapeDtypeStruct((8, depth), full),
        ),
        in_specs=[pl.BlockSpec(memory_space=pl.ANY)] * 7
        + [pl.BlockSpec(memory_space=pltpu.VMEM)] * 2,
        out_specs=(pl.BlockSpec(memory_space=pl.ANY),) * 6
        + (pl.BlockSpec(memory_space=pltpu.VMEM),) * 4,
        scratch_shapes=[
            pltpu.VMEM((size, own, mixed.shape[-1]), low),
            pltpu.VMEM(out_weight.shape, low),
            pltpu.VMEM((own, depth), low),
            pltpu.VMEM((hidden, depth), low),
            pltpu.VMEM((hidden, depth), low),
            pltpu.VMEM((hidden, depth), low),
            pltpu.VMEM(wide, low),
            pltpu.VMEM(wide, low),
            pltpu.VMEM(wide, low),
            pltpu.VMEM((size + 1, own, depth), low),
            pltpu.VMEM((size * rows, hidden), full),
            pltpu.VMEM((size * rows, hidden), full),
            pltpu.VMEM((size * rows, hidden), full),
            pltpu.VMEM(thin, low),
            pltpu.VMEM(thin, low),
            pltpu.VMEM(thin, low),
            pltpu.VMEM((2, size, rows, depth), low),
            dma((7,)),
            dma((6, chunks)),
            dma((size, chunks)),
            dma((size + 1, chunks)),
            dma((size, chunks)),
            dma((size + 1, chunks)),
            dma((2, size, chunks)),
            dma((size, chunks)),
            dma((2, size, chunks)),
            dma((size, chunks)),
        ],
        compiler_params=pltpu.CompilerParams(
            collective_id=0, has_side_effects=True, vmem_limit_bytes=VMEM_BYTES
        ),
        cost_estimate=pl.CostEstimate(
            flops=14 * size * own * depth * hidden, bytes_accessed=2**26, transcendentals=0
        ),
    )(mixed, out_weight, tokens, cotangent, hidden_gate, hidden_up, hidden_down, gain, bias)


def back_kernel(
    size,
    bits,
    chunks,
    outp_hbm,
    out_hbm,
    own_hbm,
    middle_ref,
    grads_hbm,
    branch_hbm,
    dmixed_hbm,
    output_ref,
    totals_hbm,
    part,
    out_weight,
    branch,
    inbox,
    dmixed,
    load_sem,
    store_sem,
    rs_send,
    rs_recv,
    ag_send,
    ag_recv,
    cube_parts,
    cube_firsts,
    cube_nexts,
    cube_load,
    cube_store,
    cube_send,
    cube_recv,
    cube_free,
):
    me = lax.axis_index("tensor")
    own, depth = middle_ref.shape
    rows = own // chunks
    load_own = pltpu.make_async_copy(own_hbm, branch.at[me], load_sem.at[0])
    load_part = pltpu.make_async_copy(outp_hbm, part, load_sem.at[1])
    load_out = pltpu.make_async_copy(out_hbm, out_weight, load_sem.at[2])
    load_own.start()
    load_part.start()
    cube = CubeSum(
        bits,
        lax.axis_index("dp"),
        grads_hbm,
        totals_hbm,
        cube_parts,
        cube_firsts,
        cube_nexts,
        cube_load,
        cube_store,
        cube_send,
        cube_recv,
        cube_free,
    )
    for which in range(len(cube_parts)):
        cube.load(which)
    load_out.start()
    enter([{"dp": cube.partner(bit)} for bit in range(bits)], (size, me))
    scatter = LineScatter(size, me, rows, part, inbox, rs_send, rs_recv)
    gather = LineGather(size, me, rows, branch, ag_send, ag_recv)

    def at(chunk):
        return pl.ds(chunk * rows, rows)

    def store(kind, chunk):
        if kind == 0:
            src, dst = branch.at[:, at(chunk)], branch_hbm
        else:
            return pltpu.make_async_copy(
                dmixed.at[chunk % 2], dmixed_hbm.at[:, :, at(chunk)], store_sem.at[kind, chunk]
            )
        return pltpu.make_async_copy(src, dst.at[:, at(chunk)], store_sem.at[kind, chunk])

    def finish(chunk):
        scatter.arrive(chunk)

        def body(block):
            here = pl.ds(chunk * rows + block.start, LINE)
            output_ref[here, :] = (middle_ref[here, :] + scatter.total(here)).astype(jnp.bfloat16)

        for_rows(rows, body)

    def unproject(chunk):
        if chunk == 0:
            load_out.wait()
        if chunk >= 2:
            store(1, chunk - 2).wait()

        def body(start, width):
            columns = pl.ds(start, width)
            left = branch[:, at(chunk), :].reshape(size * rows, depth)
            for head in range(dmixed.shape[1]):
                value = dot_nt(left, out_weight[pl.ds(head * VD + start, width), :])
                dmixed[chunk % 2, head, :, :, columns] = value.reshape(size, rows, width)

        for_columns(VD, body)
        for kind in range(2):
            store(kind, chunk).start()

    def begin_branch(chunk):
        if chunk == 0:
            load_own.wait()
        gather.begin(chunk)

    def begin_out(chunk):
        if chunk == 0:
            load_part.wait()
        scatter.begin(chunk)

    streams, after = [], {}
    for chunk in range(chunks):
        steps = [functools.partial(begin_branch, chunk), *gather.calls(chunk)]
        if chunk:
            after[chunk, 0] = ((chunk - 1, 1),)
            after[chunk, len(steps)] = ((chunk - 1, len(steps) + 1),)
        streams.append(steps + [functools.partial(unproject, chunk)])
    for chunk in range(chunks):
        steps = [functools.partial(begin_out, chunk), *scatter.calls(chunk)]
        if chunk:
            after[chunks + chunk, 0] = ((chunks + chunk - 1, 1),)
        streams.append(steps + [functools.partial(finish, chunk)])
    for which in range(len(cube_parts)):
        streams.append(cube.calls(which))
    run_streams(streams, ORDERS.get(("back", size, chunks, bits)), after)
    for chunk in range(chunks):
        scatter.drain(chunk)
        gather.drain(chunk)
        for kind in range(2 if chunk >= chunks - 2 else 1):
            store(kind, chunk).wait()
    cube.drain()


def feed_back(size, bits, chunks, partial, out_weight, branch, middle, grads):
    own, depth = middle.shape
    rows = own // chunks
    width = out_weight.shape[0]
    low, full = jnp.bfloat16, jnp.float32
    dma = pltpu.SemaphoreType.DMA
    vmem, anywhere = pl.BlockSpec(memory_space=pltpu.VMEM), pl.BlockSpec(memory_space=pl.ANY)
    many = [anywhere] * len(grads)
    return pl.pallas_call(
        functools.partial(back_kernel, size, bits, chunks),
        out_shape=(
            jax.ShapeDtypeStruct((size, own, depth), low),
            jax.ShapeDtypeStruct((width // VD, size, own, VD), full),
            jax.ShapeDtypeStruct((own, depth), low),
            [jax.ShapeDtypeStruct(grad.shape, low) for grad in grads],
        ),
        in_specs=[anywhere, anywhere, anywhere, vmem, many],
        out_specs=(anywhere, anywhere, vmem, many),
        scratch_shapes=[
            pltpu.VMEM((size, own, depth), low),
            pltpu.VMEM(out_weight.shape, low),
            pltpu.VMEM((size, own, depth), low),
            pltpu.VMEM((size + 1, own, depth), low),
            pltpu.VMEM((2, width // VD, size, rows, VD), full),
            dma((3,)),
            dma((2, chunks)),
            dma((size, chunks)),
            dma((size + 1, chunks)),
            dma((2, size, chunks)),
            dma((size, chunks)),
        ]
        + cube_scratch(bits, [grad.shape for grad in grads]),
        compiler_params=pltpu.CompilerParams(
            collective_id=1, has_side_effects=True, vmem_limit_bytes=VMEM_BYTES
        ),
        cost_estimate=pl.CostEstimate(
            flops=2 * size * own * depth * width, bytes_accessed=2**26, transcendentals=0
        ),
    )(partial, out_weight, branch, middle, grads)


def last_kernel(
    size,
    bits,
    chunks,
    dfirst_hbm,
    tokens_ref,
    dmiddle_ref,
    gain_ref,
    sums_ref,
    grads_hbm,
    dtokens_ref,
    totals_ref,
    totals_hbm,
    first_part,
    first_inbox,
    line_box,
    dp_box,
    load_sem,
    line_send,
    line_recv,
    dp_send,
    dp_recv,
    rs_send,
    rs_recv,
    cube_parts,
    cube_firsts,
    cube_nexts,
    cube_load,
    cube_store,
    cube_send,
    cube_recv,
    cube_free,
):
    me = lax.axis_index("tensor")
    mine = lax.axis_index("dp")
    own = tokens_ref.shape[0]
    rows = own // chunks
    load_first = pltpu.make_async_copy(dfirst_hbm, first_part, load_sem.at[0])
    load_first.start()
    cube = CubeSum(
        bits,
        mine,
        grads_hbm,
        totals_hbm,
        cube_parts,
        cube_firsts,
        cube_nexts,
        cube_load,
        cube_store,
        cube_send,
        cube_recv,
        cube_free,
    )
    for which in range(len(cube_parts)):
        cube.load(which)
    groups = 2**bits
    peers = [{"dp": (mine + step) % groups} for step in range(1, groups)]
    others = [{"tensor": (me + step) % size} for step in range(1, size)]
    enter(peers + others, None)
    first = LineScatter(size, me, rows, first_part, first_inbox, rs_send, rs_recv)

    def back(chunk):
        first.arrive(chunk)

        def body(block):
            here = pl.ds(chunk * rows + block.start, LINE)
            values = tokens_ref[here, :].astype(jnp.float32)
            centered = values - jnp.mean(values, axis=-1, keepdims=True)
            scale = lax.rsqrt(jnp.mean(centered * centered, axis=-1, keepdims=True) + EPS)
            normed = centered * scale
            grad = first.total(here)
            shaped = grad * gain_ref[...]
            line_box[me, 2:3, :] += jnp.sum(grad * normed, axis=0, keepdims=True)
            line_box[me, 3:4, :] += jnp.sum(grad, axis=0, keepdims=True)
            dtokens_ref[here, :] = dmiddle_ref[here, :] + scale * (
                shaped
                - jnp.mean(shaped, axis=-1, keepdims=True)
                - normed * jnp.mean(shaped * normed, axis=-1, keepdims=True)
            )

        for_rows(rows, body)

    def line_copy(step, slot):
        return pltpu.make_async_remote_copy(
            src_ref=line_box.at[me],
            dst_ref=line_box.at[slot],
            send_sem=line_send.at[step],
            recv_sem=line_recv.at[slot],
            device_id={"tensor": (me + step) % size},
            device_id_type=MESH,
        )

    def dp_copy(step, slot):
        return pltpu.make_async_remote_copy(
            src_ref=dp_box.at[mine],
            dst_ref=dp_box.at[slot],
            send_sem=dp_send.at[step],
            recv_sem=dp_recv.at[slot],
            device_id={"dp": (mine + step) % groups},
            device_id_type=MESH,
        )

    def sums_on_line():
        for step in range(1, size):
            line_copy(step, me).start()

    def sums_on_dp():
        for step in range(1, size):
            line_copy(step, (me + step) % size).wait_recv()
        dp_box[mine] = jnp.sum(line_box[...], axis=0)
        for step in range(1, groups):
            dp_copy(step, mine).start()

    def sums_done():
        for step in range(1, groups):
            dp_copy(step, (mine + step) % groups).wait_recv()
        totals_ref[...] = jnp.sum(dp_box[...], axis=0)

    line_box[me] = sums_ref[...]
    load_first.wait()
    streams = []
    for chunk in range(chunks):
        streams.append(
            [
                functools.partial(first.begin, chunk),
                *first.calls(chunk),
                functools.partial(back, chunk),
            ]
        )
    after = {(chunks + len(cube_parts), 0): [(chunk, 2 * size - 2) for chunk in range(chunks)]}
    for which in range(len(cube_parts)):
        streams.append(cube.calls(which))
    streams.append([sums_on_line, sums_on_dp, sums_done])
    run_streams(streams, ORDERS.get(("last", size, chunks, bits)), after)
    for chunk in range(chunks):
        first.drain(chunk)
    for step in range(1, size):
        line_copy(step, me).wait_send()
    for step in range(1, groups):
        dp_copy(step, mine).wait_send()
    cube.drain()


def last_sums(size, bits, chunks, dfirst, tokens, dmiddle, gain, sums, grads):
    own, depth = tokens.shape
    low, full = jnp.bfloat16, jnp.float32
    dma = pltpu.SemaphoreType.DMA
    vmem, anywhere = pl.BlockSpec(memory_space=pltpu.VMEM), pl.BlockSpec(memory_space=pl.ANY)
    many = [anywhere] * len(grads)
    return pl.pallas_call(
        functools.partial(last_kernel, size, bits, chunks),
        out_shape=(
            jax.ShapeDtypeStruct((own, depth), full),
            jax.ShapeDtypeStruct((8, depth), full),
            [jax.ShapeDtypeStruct(grad.shape, low) for grad in grads],
        ),
        in_specs=[anywhere, vmem, vmem, vmem, vmem, many],
        out_specs=(vmem, vmem, many),
        scratch_shapes=[
            pltpu.VMEM((size, own, depth), low),
            pltpu.VMEM((size + 1, own, depth), low),
            pltpu.VMEM((size, 8, depth), full),
            pltpu.VMEM((2**bits, 8, depth), full),
            dma((1,)),
            dma((size,)),
            dma((size,)),
            dma((2**bits,)),
            dma((2**bits,)),
            dma((size, chunks)),
            dma((size + 1, chunks)),
        ]
        + cube_scratch(bits, [grad.shape for grad in grads]),
        compiler_params=pltpu.CompilerParams(
            collective_id=2, has_side_effects=True, vmem_limit_bytes=VMEM_BYTES
        ),
        cost_estimate=pl.CostEstimate(flops=2**30, bytes_accessed=2**26, transcendentals=0),
    )(dfirst, tokens, dmiddle, gain, sums, grads)


def decay_rows(rate, column, row, first):
    shape = (column.shape[0], row.shape[1])
    here = first + lax.broadcasted_iota(jnp.int32, shape, 0)
    offset = here - lax.broadcasted_iota(jnp.int32, shape, 1)
    inside = (column == row) & (offset >= 0)
    distance = jnp.maximum(offset, 0).astype(jnp.float32)
    decay = jnp.where(inside, jnp.exp(-rate * distance), 0.0)
    return decay * lax.rsqrt(jnp.sum(decay, axis=-1, keepdims=True))


def group_parts(values):
    centered = values - jnp.mean(values, axis=-1, keepdims=True)
    scale = lax.rsqrt(jnp.mean(centered * centered, axis=-1, keepdims=True) + GROUP_EPS)
    return centered * scale, scale


def sigmoid(values):
    return 1.0 / (1.0 + jnp.exp(-values))


def first_kernel(
    size,
    chunks,
    heads,
    tokens_ref,
    gain_ref,
    bias_ref,
    column_ref,
    row_ref,
    rates_ref,
    query_hbm,
    key_hbm,
    value_hbm,
    gate_hbm,
    first_hbm,
    queries_hbm,
    keys_hbm,
    values_hbm,
    gates_hbm,
    retained_hbm,
    mixed_hbm,
    table_hbm,
    query_weight,
    key_weight,
    value_weight,
    gate_weight,
    first,
    queries,
    keys,
    values,
    gates,
    retained,
    mixed,
    table,
    raw,
    retain,
    load_sem,
    store_sem,
    done_sem,
    ag_send,
    ag_recv,
):
    me = lax.axis_index("tensor")
    own, depth = tokens_ref.shape
    rows = own // chunks
    pairs = (
        (query_hbm, query_weight),
        (key_hbm, key_weight),
        (value_hbm, value_weight),
        (gate_hbm, gate_weight),
    )
    loads = [
        pltpu.make_async_copy(src, dst, load_sem.at[index])
        for index, (src, dst) in enumerate(pairs)
    ]
    for load in loads:
        load.start()
    enter((), (size, me))
    gather = LineGather(size, me, rows, first, ag_send, ag_recv)
    waited = set()

    def need(index):
        if index not in waited:
            waited.add(index)
            loads[index].wait()

    def at(chunk):
        return pl.ds(chunk * rows, rows)

    def flat(chunk):
        return first[:, at(chunk), :].reshape(size * rows, depth)

    def store(kind, block):
        src, dst = (
            (queries, queries_hbm),
            (keys, keys_hbm),
            (first, first_hbm),
            (mixed, mixed_hbm),
        )[kind]
        return pltpu.make_async_copy(src.at[block], dst.at[block], store_sem.at[kind, block])

    def store_head(kind, head, block):
        src, dst = (
            (values, values_hbm),
            (gates, gates_hbm),
            (retained, retained_hbm),
            (table, table_hbm),
        )[kind]
        return pltpu.make_async_copy(
            src.at[head, block], dst.at[head, block], done_sem.at[kind, head, block]
        )

    def normalize(chunk):
        def body(block):
            here = pl.ds(chunk * rows + block.start, LINE)
            tokens = tokens_ref[here, :].astype(jnp.float32)
            centered = tokens - jnp.mean(tokens, axis=-1, keepdims=True)
            scale = lax.rsqrt(jnp.mean(centered * centered, axis=-1, keepdims=True) + EPS)
            value = centered * scale * gain_ref[...] + bias_ref[...]
            first[me, here, :] = value.astype(jnp.bfloat16)

        for_rows(rows, body)
        gather.begin(chunk)

    def project_pair(chunk):
        need(0)
        need(1)

        def body(start, width):
            columns = pl.ds(start, width)
            value = dot_nn(flat(chunk), query_weight[:, columns])
            queries[:, at(chunk), columns] = value.astype(jnp.bfloat16).reshape(size, rows, width)
            value = dot_nn(flat(chunk), key_weight[:, columns])
            keys[:, at(chunk), columns] = value.astype(jnp.bfloat16).reshape(size, rows, width)

        for_columns(heads * KD, body)

    def project_value(chunk, head):
        need(2)

        def body(start, width):
            weight = value_weight[pl.ds(head * VD + start, width), :]
            value = dot_nt(flat(chunk), weight).astype(jnp.bfloat16)
            values[head, :, at(chunk), pl.ds(start, width)] = value.reshape(size, rows, width)

        for_columns(VD, body)

    def project_gate(chunk, head):
        need(3)

        def body(start, width):
            weight = gate_weight[pl.ds(head * VD + start, width), :]
            value = dot_nt(flat(chunk), weight)
            gates[head, :, at(chunk), pl.ds(start, width)] = value.reshape(size, rows, width)

        for_columns(VD, body)

    def tabulate(head, block):
        seen = (block + 1) * own

        def body(part):
            there = pl.ds(block * own + part.start, part.size)
            table[head, block, part, :seen] = decay_rows(
                rates_ref[head], column_ref[there, :], row_ref[:, :seen], block * own + part.start
            )

        for_rows(own, body, BAND)
        store_head(3, head, block).start()

    def attend(head, block):
        seen = (block + 1) * own
        lanes = pl.ds(head * KD, KD)
        query = queries[block, :, lanes]
        raw[:, :seen] = dot_nt(query, keys[: block + 1, :, lanes].reshape(seen, KD))

        def body(part):
            weighted = raw[part, :seen] * (KD**-0.5) * table[head, block, part, :seen]
            total = jnp.sum(weighted, axis=-1, keepdims=True)
            retain[part, :seen] = (weighted * lax.rsqrt(total * total + 1.0)).astype(jnp.bfloat16)

        for_rows(own, body, BAND)
        value = values[head, : block + 1].reshape(seen, VD)
        retained[head, block] = dot_nn(retain[:, :seen], value)

        def body_mix(part):
            normed, _ = group_parts(retained[head, block, part, :])
            gate = gates[head, block, part, :]
            value = (gate * sigmoid(gate) * normed).astype(jnp.bfloat16)
            mixed[block, part, pl.ds(head * VD, VD)] = value

        for_rows(own, body_mix, BAND)
        store_head(2, head, block).start()
        if head == heads - 1:
            store(3, block).start()

    streams, after = [], {}
    for chunk in range(chunks):
        steps = [functools.partial(normalize, chunk), *gather.calls(chunk)]
        if chunk:
            after[chunk, 0] = ((chunk - 1, 1),)
        steps.append(functools.partial(project_pair, chunk))
        for head in range(heads):
            steps.append(functools.partial(project_value, chunk, head))
            steps.append(functools.partial(project_gate, chunk, head))
        streams.append(steps)
    streams.append(
        [functools.partial(tabulate, head, block) for head in range(heads) for block in range(size)]
    )
    run_streams(streams, ORDERS.get(("first", size, chunks, heads)), after)
    for block in range(size):
        for kind in range(3):
            store(kind, block).start()
        for head in range(heads):
            for kind in range(2):
                store_head(kind, head, block).start()
    for head in range(heads):
        for block in range(size):
            attend(head, block)
    for chunk in range(chunks):
        gather.drain(chunk)
    for block in range(size):
        for kind in range(4):
            store(kind, block).wait()
        for head in range(heads):
            for kind in range(4):
                store_head(kind, head, block).wait()


def first_part(size, chunks, tokens, gain, bias, segments, rates, query, key, value, gate):
    own, depth = tokens.shape
    heads = query.shape[1] // KD
    rows = size * own
    low, full = jnp.bfloat16, jnp.float32
    dma = pltpu.SemaphoreType.DMA
    vmem, anywhere = pl.BlockSpec(memory_space=pltpu.VMEM), pl.BlockSpec(memory_space=pl.ANY)
    shapes = (
        ((size, own, depth), low),
        ((size, own, heads * KD), low),
        ((size, own, heads * KD), low),
        ((heads, size, own, VD), low),
        ((heads, size, own, VD), full),
        ((heads, size, own, VD), full),
        ((size, own, heads * VD), low),
        ((heads, size, own, rows), full),
    )
    return pl.pallas_call(
        functools.partial(first_kernel, size, chunks, heads),
        out_shape=tuple(jax.ShapeDtypeStruct(*item) for item in shapes),
        in_specs=[vmem] * 5 + [pl.BlockSpec(memory_space=pltpu.SMEM)] + [anywhere] * 4,
        out_specs=(anywhere,) * 8,
        scratch_shapes=[pltpu.VMEM(item.shape, low) for item in (query, key, value, gate)]
        + [pltpu.VMEM(*item) for item in shapes]
        + [
            pltpu.VMEM((own, rows), full),
            pltpu.VMEM((own, rows), low),
            dma((4,)),
            dma((4, size)),
            dma((4, heads, size)),
            dma((2, size, chunks)),
            dma((size, chunks)),
        ],
        compiler_params=pltpu.CompilerParams(
            collective_id=3, has_side_effects=True, vmem_limit_bytes=VMEM_BYTES
        ),
        cost_estimate=pl.CostEstimate(flops=2**33, bytes_accessed=2**26, transcendentals=0),
    )(
        tokens,
        gain,
        bias,
        segments.reshape(rows, 1),
        segments.reshape(1, rows),
        rates,
        query,
        key,
        value,
        gate,
    )


def retain_kernel(
    size,
    heads,
    queries_hbm,
    keys_hbm,
    values_hbm,
    gates_hbm,
    retained_hbm,
    dmixed_hbm,
    table_hbm,
    query_hbm,
    key_hbm,
    value_hbm,
    gate_hbm,
    dqueries_hbm,
    dkeys_hbm,
    dvalues_hbm,
    dgates_hbm,
    dfirst_hbm,
    queries,
    keys,
    values,
    gates,
    retained,
    dmixed,
    table,
    query_weight,
    key_weight,
    value_weight,
    gate_weight,
    dqueries,
    dkeys,
    dvalues,
    dgates,
    dfirst,
    raw,
    grad,
    retain,
    dscores,
    dretained,
    dkey_sum,
    dvalue_sum,
    load_sem,
    block_sem,
    store_sem,
):
    own = queries.shape[1]
    depth = query_weight.shape[0]

    def load_whole(kind):
        src, dst = (
            (queries_hbm, queries),
            (keys_hbm, keys),
            (query_hbm, query_weight),
            (key_hbm, key_weight),
            (value_hbm, value_weight),
            (gate_hbm, gate_weight),
        )[kind]
        return pltpu.make_async_copy(src, dst, load_sem.at[kind])

    def load_block(kind, head, block):
        src, dst = (
            (values_hbm, values),
            (gates_hbm, gates),
            (retained_hbm, retained),
            (dmixed_hbm, dmixed),
            (table_hbm, table),
        )[kind]
        return pltpu.make_async_copy(
            src.at[head, block], dst.at[head, block], block_sem.at[kind, head, block]
        )

    def store(kind, block):
        src, dst = (
            (dqueries, dqueries_hbm),
            (dkeys, dkeys_hbm),
            (dvalues, dvalues_hbm),
            (dgates, dgates_hbm),
            (dfirst, dfirst_hbm),
        )[kind]
        return pltpu.make_async_copy(src.at[block], dst.at[block], store_sem.at[kind, block])

    for kind in range(2):
        load_whole(kind).start()
    for head in range(heads):
        for block in range(size):
            for kind in range(5):
                load_block(kind, head, block).start()
    for kind in range(2, 6):
        load_whole(kind).start()
    for kind in range(2):
        load_whole(kind).wait()

    def attend(head, block):
        seen = (block + 1) * own
        lanes = pl.ds(head * KD, KD)

        for kind in range(5):
            load_block(kind, head, block).wait()

        def body_mix(part):
            normed, scale = group_parts(retained[head, block, part, :])
            gate = gates[head, block, part, :]
            dmix = dmixed[head, block, part, :]
            half = sigmoid(gate)
            dgate = dmix * normed * (half * (1.0 + gate * (1.0 - half)))
            dgates[block, part, pl.ds(head * VD, VD)] = dgate.astype(jnp.bfloat16)
            dnormed = dmix * (gate * half)
            value = scale * (
                dnormed
                - jnp.mean(dnormed, axis=-1, keepdims=True)
                - normed * jnp.mean(dnormed * normed, axis=-1, keepdims=True)
            )
            dretained[part, :] = value.astype(jnp.bfloat16)

        for_rows(own, body_mix, BAND)
        query = queries[block, :, lanes]
        key = keys[: block + 1, :, lanes].reshape(seen, KD)
        raw[:, :seen] = dot_nt(query, key)
        value = values[head, : block + 1].reshape(seen, VD)
        grad[:, :seen] = dot_nt(dretained[...], value)

        def body(part):
            decay = table[head, block, part, :seen]
            weighted = raw[part, :seen] * (KD**-0.5) * decay
            dretain = grad[part, :seen]
            total = jnp.sum(weighted, axis=-1, keepdims=True)
            along = jnp.sum(dretain * weighted, axis=-1, keepdims=True)
            inverse = lax.rsqrt(total * total + 1.0)
            retain[part, :seen] = (weighted * inverse).astype(jnp.bfloat16)
            along = along * total * inverse * inverse
            dscores[part, :seen] = (decay * inverse * (dretain - along)).astype(jnp.bfloat16)

        for_rows(own, body, BAND)
        dquery = dot_nn(dscores[:, :seen], key) * (KD**-0.5)
        dqueries[block, :, lanes] = dquery.astype(jnp.bfloat16)
        for other in range(block + 1):
            there = pl.ds(other * own, own)
            dkey = dot_tn(dscores[:, there], query)
            dvalue = dot_tn(retain[:, there], dretained[...])
            if other == block:
                dkey_sum[other] = dkey
                dvalue_sum[other] = dvalue
            else:
                dkey_sum[other] += dkey
                dvalue_sum[other] += dvalue

    for head in range(heads):
        for block in range(size):
            attend(head, block)

        lanes = pl.ds(head * KD, KD)
        for block in range(size):
            dkeys[block, :, lanes] = (dkey_sum[block] * (KD**-0.5)).astype(jnp.bfloat16)
            dvalues[block, :, pl.ds(head * VD, VD)] = dvalue_sum[block].astype(jnp.bfloat16)

    for kind in range(2, 6):
        load_whole(kind).wait()
    for block in range(size):
        for kind in range(4):
            store(kind, block).start()

        def body(start, width):
            columns = pl.ds(start, width)
            total = dot_nt(dqueries[block], query_weight[columns, :])
            total = total + dot_nt(dkeys[block], key_weight[columns, :])
            total = total + dot_nn(dvalues[block], value_weight[:, columns])
            total = total + dot_nn(dgates[block], gate_weight[:, columns])
            dfirst[block, :, columns] = total.astype(jnp.bfloat16)

        for_columns(depth, body)
        store(4, block).start()
    for block in range(size):
        for kind in range(5):
            store(kind, block).wait()


def retain_back(size, queries, keys, values, gates, retained, dmixed, table, query, key, value, gate):
    own = queries.shape[1]
    heads = values.shape[0]
    rows, depth = size * own, query.shape[0]
    low, full = jnp.bfloat16, jnp.float32
    dma = pltpu.SemaphoreType.DMA
    anywhere = pl.BlockSpec(memory_space=pl.ANY)
    inputs = (queries, keys, values, gates, retained, dmixed, table, query, key, value, gate)
    shapes = (
        queries.shape,
        keys.shape,
        (size, own, heads * VD),
        (size, own, heads * VD),
        (size, own, depth),
    )
    return pl.pallas_call(
        functools.partial(retain_kernel, size, heads),
        out_shape=tuple(jax.ShapeDtypeStruct(shape, low) for shape in shapes),
        in_specs=[anywhere] * len(inputs),
        out_specs=(anywhere,) * 5,
        scratch_shapes=[pltpu.VMEM(item.shape, item.dtype) for item in inputs]
        + [pltpu.VMEM(shape, low) for shape in shapes]
        + [
            pltpu.VMEM((own, rows), full),
            pltpu.VMEM((own, rows), full),
            pltpu.VMEM((own, rows), low),
            pltpu.VMEM((own, rows), low),
            pltpu.VMEM((own, VD), low),
            pltpu.VMEM((size, own, KD), full),
            pltpu.VMEM((size, own, VD), full),
            dma((6,)),
            dma((5, heads, size)),
            dma((5, size)),
        ],
        compiler_params=pltpu.CompilerParams(vmem_limit_bytes=VMEM_BYTES),
        cost_estimate=pl.CostEstimate(flops=2**34, bytes_accessed=2**26, transcendentals=0),
    )(*inputs)


def per_device(
    tokens,
    first_gain,
    first_bias,
    query_weight,
    key_weight,
    value_weight,
    gate_weight,
    out_weight,
    second_gain,
    second_bias,
    hidden_gate,
    hidden_up,
    hidden_down,
    segments,
    cotangent,
):
    size = lax.axis_size("tensor")
    group_rows = segments.size
    head_local = query_weight.shape[1] // KD
    head_index = (lax.axis_index("tensor") * head_local + jnp.arange(head_local)).astype(
        jnp.float32
    )
    rates = -jnp.log1p(-jnp.exp2(-5.0 - head_index))
    first_all, queries, keys, values, gates, retained, mixed, table = first_part(
        size,
        CHUNKS,
        tokens,
        first_gain[None],
        first_bias[None],
        segments,
        rates,
        query_weight,
        key_weight,
        value_weight.T,
        gate_weight.T,
    )
    bits = lax.axis_size("dp").bit_length() - 1
    own = tokens.shape[0]
    (
        second_all,
        seed_all,
        inner,
        gate_in_low,
        lin_in_low,
        partial,
        middle,
        grad_middle,
        branch,
        second_sums,
    ) = feed_forward(
        size,
        CHUNKS,
        mixed,
        out_weight,
        tokens,
        cotangent,
        hidden_gate.T,
        hidden_up.T,
        hidden_down,
        second_gain[None],
        second_bias[None],
    )

    def flat(item):
        return item.reshape(group_rows, item.shape[-1])

    second_all, seed_all = flat(second_all), flat(seed_all)
    feed_grads = [
        product_tn(flat(inner), seed_all).astype(jnp.bfloat16),
        product_tn(flat(gate_in_low), second_all).astype(jnp.bfloat16),
        product_tn(flat(lin_in_low), second_all).astype(jnp.bfloat16),
    ]
    branch_all, grad_mixed, output, feed_grads = feed_back(
        size, bits, CHUNKS, partial, out_weight, branch, middle, feed_grads
    )
    branch_all = flat(branch_all)
    grad_queries, grad_keys, grad_values, grad_gates, grad_first = retain_back(
        size,
        queries,
        keys,
        values,
        gates,
        retained,
        grad_mixed,
        table,
        query_weight,
        key_weight,
        value_weight.T,
        gate_weight.T,
    )
    first_all = flat(first_all)

    grads = [
        product_tn(flat(mixed), branch_all).astype(jnp.bfloat16),
        product_tn(flat(grad_values), first_all).astype(jnp.bfloat16),
        product_tn(flat(grad_gates), first_all).astype(jnp.bfloat16),
        product_tn(first_all, flat(grad_queries)).astype(jnp.bfloat16),
        product_tn(first_all, flat(grad_keys)).astype(jnp.bfloat16),
    ]
    grad_tokens, sums, grads = last_sums(
        size,
        bits,
        CHUNKS,
        grad_first,
        tokens,
        grad_middle,
        first_gain[None],
        second_sums,
        grads,
    )
    grad_sgain, grad_sbias, grad_fgain, grad_fbias = sums[0], sums[1], sums[2], sums[3]
    grad_outw, grad_valuew, grad_gatew, grad_queryw, grad_keyw = (
        item.astype(jnp.float32) for item in grads
    )
    grad_hdown, grad_hgate, grad_hup = (item.astype(jnp.float32) for item in feed_grads)
    grad_valuew, grad_gatew, grad_hgate, grad_hup = (
        item.T for item in (grad_valuew, grad_gatew, grad_hgate, grad_hup)
    )
    return (
        output,
        grad_tokens,
        grad_fgain,
        grad_fbias,
        grad_queryw,
        grad_keyw,
        grad_valuew,
        grad_gatew,
        grad_outw,
        grad_sgain,
        grad_sbias,
        grad_hgate,
        grad_hup,
        grad_hdown,
    )


def solution(mesh):
    return jax.shard_map(
        per_device,
        mesh=mesh,
        in_specs=(
            P(("dp", "tensor"), None),
            P(),
            P(),
            P(None, "tensor"),
            P(None, "tensor"),
            P(None, "tensor"),
            P(None, "tensor"),
            P("tensor", None),
            P(),
            P(),
            P(None, "tensor"),
            P(None, "tensor"),
            P("tensor", None),
            P("dp", None),
            P(("dp", "tensor"), None),
        ),
        out_specs=(
            P(("dp", "tensor"), None),
            P(("dp", "tensor"), None),
            P(),
            P(),
            P(None, "tensor"),
            P(None, "tensor"),
            P(None, "tensor"),
            P(None, "tensor"),
            P("tensor", None),
            P(),
            P(),
            P(None, "tensor"),
            P(None, "tensor"),
            P("tensor", None),
        ),
        check_vma=False,
    )
```

```python
import functools
import itertools

import jax
import jax.numpy as jnp
from jax import lax
from jax.experimental import pallas as pl
from jax.experimental.pallas import tpu as pltpu
from jax.sharding import PartitionSpec as P

KD = 256
VD = 432


EPS = 1e-05
GROUP_EPS = 0.1
GELU_SCALE = 0.7978845608028654
CHUNKS = 4

MESH = pl.DeviceIdType.MESH
VMEM_BYTES = 60 * 2**20
TILE = 256
LINE = 16
BAND = 64


def for_columns(width, body):
    full = width // TILE

    def step(index, carry):
        body(pl.multiple_of(index * TILE, TILE), TILE)
        return carry

    if full:
        lax.fori_loop(0, full, step, 0)
    if width % TILE:
        body(full * TILE, width % TILE)


def for_rows(count, body, size=LINE):
    def step(index, carry):
        body(pl.ds(pl.multiple_of(index * size, LINE), size))
        return carry

    lax.fori_loop(0, count // size, step, 0)


def dot_nn(left, right):
    return lax.dot_general(left, right, (((1,), (0,)), ((), ())), preferred_element_type=jnp.float32)


def dot_nt(left, right):
    return lax.dot_general(left, right, (((1,), (1,)), ((), ())), preferred_element_type=jnp.float32)


def dot_tn(left, right):
    return lax.dot_general(left, right, (((0,), (0,)), ((), ())), preferred_element_type=jnp.float32)


def enter(peers, line):
    barrier = pltpu.get_barrier_semaphore()
    for peer in peers:
        pl.semaphore_signal(barrier, inc=1, device_id=peer, device_id_type=MESH)
    if line is not None:
        size, me = line

        @pl.when(me > 0)
        def _():
            pl.semaphore_signal(barrier, inc=1, device_id={"tensor": me - 1}, device_id_type=MESH)

        @pl.when(me < size - 1)
        def _():
            pl.semaphore_signal(barrier, inc=1, device_id={"tensor": me + 1}, device_id_type=MESH)

    count = len(peers)
    if line is not None:
        count = count + (me > 0).astype(jnp.int32) + (me < size - 1).astype(jnp.int32)
    pl.semaphore_wait(barrier, count)


class LineScatter:
    def __init__(self, size, me, rows, part, inbox, send, recv):
        self.size, self.me, self.rows = size, me, rows
        self.part, self.inbox, self.send, self.recv = part, inbox, send, recv

    def at(self, chunk):
        return pl.ds(chunk * self.rows, self.rows)

    def copy(self, target, slot, chunk, device):
        return pltpu.make_async_remote_copy(
            src_ref=self.part.at[target, self.at(chunk)],
            dst_ref=self.inbox.at[slot, self.at(chunk)],
            send_sem=self.send.at[target, chunk],
            recv_sem=self.recv.at[slot, chunk],
            device_id={"tensor": device},
            device_id_type=MESH,
        )

    def add(self, target, chunk):
        def body(rows):
            at = pl.ds(chunk * self.rows + rows.start, LINE)
            total = self.part[target, at, :].astype(jnp.float32)
            total = total + self.inbox[target, at, :].astype(jnp.float32)
            self.part[target, at, :] = total.astype(jnp.bfloat16)

        for_rows(self.rows, body)

    def go_right(self, chunk, target):
        self.copy(target, target, chunk, self.me + 1).start()

    def go_left(self, chunk, target):
        last = self.me - 1 == target
        self.copy(target, jnp.where(last, self.size, target), chunk, self.me - 1).start()

    def begin(self, chunk):
        @pl.when(self.me == 0)
        def _():
            for target in range(self.size - 1, 0, -1):
                self.go_right(chunk, target)

        @pl.when(self.me == self.size - 1)
        def _():
            for target in range(self.size - 1):
                self.go_left(chunk, target)

    def right(self, chunk, target):
        @pl.when((self.me < target) & (self.me > 0))
        def _():
            self.copy(target, target, chunk, self.me).wait_recv()
            self.add(target, chunk)
            self.go_right(chunk, target)

    def left(self, chunk, target):
        @pl.when((self.me > target) & (self.me < self.size - 1))
        def _():
            self.copy(target, target, chunk, self.me).wait_recv()
            self.add(target, chunk)
            self.go_left(chunk, target)

    def calls(self, chunk):
        for step in range(self.size - 1):
            if step < self.size - 2:
                yield functools.partial(self.right, chunk, self.size - 1 - step)
                yield functools.partial(self.left, chunk, step)

    def arrive(self, chunk):
        size, me = self.size, self.me

        @pl.when(me > 0)
        def _():
            self.copy(me, me, chunk, me - 1).wait_recv()

        @pl.when(me < size - 1)
        def _():
            self.copy(me, size, chunk, me + 1).wait_recv()

    def total(self, rows):
        size, me = self.size, self.me
        own = self.part[me, rows, :].astype(jnp.float32)
        low = self.inbox[me, rows, :].astype(jnp.float32)
        high = self.inbox[size, rows, :].astype(jnp.float32)
        return own + jnp.where(me > 0, low, 0.0) + jnp.where(me < size - 1, high, 0.0)

    def drain(self, chunk):
        for target in range(self.size):

            @pl.when(self.me != target)
            def _():
                self.copy(target, target, chunk, self.me).wait_send()


class LineGather:
    def __init__(self, size, me, rows, held, send, recv):
        self.size, self.me, self.rows = size, me, rows
        self.held, self.send, self.recv = held, send, recv

    def copy(self, block, chunk, way, device):
        at = pl.ds(chunk * self.rows, self.rows)
        return pltpu.make_async_remote_copy(
            src_ref=self.held.at[block, at],
            dst_ref=self.held.at[block, at],
            send_sem=self.send.at[way, block, chunk],
            recv_sem=self.recv.at[block, chunk],
            device_id={"tensor": device},
            device_id_type=MESH,
        )

    def begin(self, chunk):
        self.right(chunk, 0)
        self.left(chunk, 0)

    def right(self, chunk, step):
        size, me = self.size, self.me

        @pl.when(me >= step)
        def _():
            if step:
                self.copy(me - step, chunk, 0, me).wait_recv()

            @pl.when(me < size - 1)
            def _():
                self.copy(me - step, chunk, 0, me + 1).start()

    def left(self, chunk, step):
        size, me = self.size, self.me

        @pl.when(me + step < size)
        def _():
            if step:
                self.copy(me + step, chunk, 1, me).wait_recv()

            @pl.when(me > 0)
            def _():
                self.copy(me + step, chunk, 1, me - 1).start()

    def calls(self, chunk):
        for step in range(1, self.size):
            yield functools.partial(self.right, chunk, step)
            yield functools.partial(self.left, chunk, step)

    def drain(self, chunk):
        size, me = self.size, self.me
        for step in range(size):

            @pl.when((me >= step) & (me < size - 1))
            def _():
                self.copy(me - step, chunk, 0, me + 1).wait_send()

            @pl.when((me + step < size) & (me > 0))
            def _():
                self.copy(me + step, chunk, 1, me - 1).wait_send()


class CubeSum:
    def __init__(self, bits, me, results, parts, firsts, nexts, store, send, recv, free):
        self.bits, self.me = bits, me
        self.results, self.parts = results, parts
        self.firsts, self.nexts = firsts, nexts
        self.store_sem, self.send, self.recv = store, send, recv
        self.free = free
        self.orders = (tuple(range(bits)), (0,) + tuple(range(bits - 1, 0, -1)))
        self.mine = [(me // 2**bit) % 2 for bit in range(bits)]

    def partner(self, bit):
        return self.me + (1 - 2 * self.mine[bit]) * 2**bit

    def band(self, which, color):
        count = self.parts[which].shape[-2]
        cut = cut_rows(count)
        return ((0, cut), (cut, count - cut), (0, count))[color]

    def lead(self, fixed):
        return tuple(fixed.get(bit, slice(None)) for bit in range(self.bits - 1, -1, -1))

    def moved(self, src, dst, which, color, step, bit):
        return pltpu.make_async_remote_copy(
            src_ref=src,
            dst_ref=dst,
            send_sem=self.send.at[which, color % 2, step],
            recv_sem=self.recv.at[which, color % 2, step],
            device_id={"dp": self.partner(bit)},
            device_id_type=MESH,
        )

    def halve(self, which, color, step):
        order = self.orders[color % 2]
        start, count = self.band(which, color)
        fixed = {bit: self.mine[bit] for bit in order[:step]}
        fixed[order[step]] = 1 - self.mine[order[step]]
        src = self.parts[which].at[self.lead(fixed) + (pl.ds(start, count), slice(None))]
        dst = self.firsts[which] if step == 0 else self.nexts[which][color][step - 1]
        return self.moved(src, dst, which, color, step, order[step])

    def double(self, which, color, step):
        order = self.orders[color % 2]
        start, count = self.band(which, color)
        fixed = {bit: self.mine[bit] for bit in order[: step + 1]}
        held = self.parts[which].at[self.lead(fixed) + (pl.ds(start, count), slice(None))]
        return self.moved(held, held, which, color, 2 * self.bits - 1 - step, order[step])

    def freed(self, which, color, step):
        return self.free.at[which, color % 2, step]

    def land(self, which, color, step):
        copy = self.halve(which, color, step)
        copy.wait_send()
        partner = {"dp": self.partner(self.orders[color % 2][step])}
        pl.semaphore_signal(
            self.freed(which, color, step), inc=1, device_id=partner, device_id_type=MESH
        )
        copy.wait_recv()
        self.add(which, color, step)

    def grow(self, which, color, step):
        pl.semaphore_wait(self.freed(which, color, step), 1)
        self.double(which, color, step).start()

    def add(self, which, color, step):
        order = self.orders[color % 2]
        part, (start, count) = self.parts[which], self.band(which, color)
        box = self.firsts[which] if step == 0 else self.nexts[which][color][step - 1]
        fixed = {bit: self.mine[bit] for bit in order[: step + 1]}
        free = [bit for bit in range(self.bits - 1, -1, -1) if bit not in fixed]
        for choice in itertools.product((0, 1), repeat=len(free)):
            lead = self.lead({**fixed, **dict(zip(free, choice))})

            def body(begin, size):
                there = lead + (pl.ds(start + begin, size), slice(None))
                total = part[there].astype(jnp.float32)
                total = total + box[choice + (pl.ds(begin, size), slice(None))].astype(jnp.float32)
                part[there] = total.astype(jnp.bfloat16)

            for_blocks(count, part.shape[-1], body)

    def slices(self, which, ref):
        rows, columns = self.parts[which].shape[-2:]
        for index in range(2**self.bits):
            lead = tuple((index >> bit) & 1 for bit in range(self.bits - 1, -1, -1))
            if ref.shape[0] == rows:
                whole = ref.at[:, pl.ds(index * columns, columns)]
            else:
                whole = ref.at[pl.ds(index * rows, rows), :]
            yield index, self.parts[which].at[lead], whole

    def make_wide(self, which, left, right):
        columns = self.parts[which].shape[-1]
        half = 2 ** (self.bits - 1)

        def some(start):
            for index in range(start, start + half):
                lead = tuple((index >> bit) & 1 for bit in range(self.bits - 1, -1, -1))
                value = dot_nn(left[...], right(pl.ds(index * columns, columns)))
                self.parts[which][lead] = value.astype(jnp.bfloat16)

        return [functools.partial(some, 0), functools.partial(some, half)]

    def open(self, which):
        self.halve(which, 2, 0).start()

    def split(self, which):
        self.land(which, 2, 0)
        for color in range(2):
            self.halve(which, color, 1).start()

    def down(self, which, color, step):
        self.land(which, color, step - 1)
        self.halve(which, color, step).start()

    def turn(self, which, color):
        self.land(which, color, self.bits - 1)
        self.grow(which, color, self.bits - 1)

    def up(self, which, color, step):
        self.double(which, color, step + 1).wait_recv()
        self.grow(which, color, step)

    def join(self, which):
        for color in range(2):
            self.double(which, color, 1).wait_recv()
        self.grow(which, 2, 0)

    def close(self, which):
        self.double(which, 2, 0).wait_recv()
        for index, part, whole in self.slices(which, self.results[which]):
            pltpu.make_async_copy(part, whole, self.store_sem.at[which, index]).start()

    def calls(self, which):
        yield functools.partial(self.open, which)
        yield functools.partial(self.split, which)
        for step in range(2, self.bits):
            for color in range(2):
                yield functools.partial(self.down, which, color, step)
        for color in range(2):
            yield functools.partial(self.turn, which, color)
        for step in range(self.bits - 2, 0, -1):
            for color in range(2):
                yield functools.partial(self.up, which, color, step)
        yield functools.partial(self.join, which)
        yield functools.partial(self.close, which)

    def drain(self):
        for which in range(len(self.parts)):
            self.double(which, 2, 0).wait_send()
            for color in range(2):
                for step in range(1, self.bits):
                    self.double(which, color, step).wait_send()
            for index, part, whole in self.slices(which, self.results[which]):
                pltpu.make_async_copy(part, whole, self.store_sem.at[which, index]).wait()


def cut_rows(count):
    return count // (2 * LINE) * LINE


def for_blocks(count, columns, body):
    size = LINE
    while count % (2 * size) == 0 and 2 * size * columns <= 2**14:
        size *= 2
    for factor in (3, 5):
        if count % (factor * size) == 0 and factor * size * columns <= 2**14:
            size *= factor

    def step(index, carry):
        body(pl.multiple_of(index * size, LINE), size)
        return carry

    lax.fori_loop(0, count // size, step, 0)


def cube_scratch(bits, shapes):
    low = jnp.bfloat16
    parts, firsts, nexts = [], [], []
    for rows, columns in shapes:
        if columns >= rows:
            columns = columns // 2**bits
        else:
            rows = rows // 2**bits
        cut = cut_rows(rows)
        parts.append(pltpu.VMEM((2,) * bits + (rows, columns), low))
        firsts.append(pltpu.VMEM((2,) * (bits - 1) + (rows, columns), low))
        nexts.append(
            [
                [
                    pltpu.VMEM((2,) * (bits - 1 - step) + (count, columns), low)
                    for step in range(1, bits)
                ]
                for count in (cut, rows - cut)
            ]
        )
    dma = pltpu.SemaphoreType.DMA
    return [
        parts,
        firsts,
        nexts,
        dma((len(shapes), 2**bits)),
        dma((len(shapes), 2, 2 * bits)),
        dma((len(shapes), 2, 2 * bits)),
        pltpu.SemaphoreType.REGULAR((len(shapes), 2, bits)),
    ]


ORDERS = {
    ("first", 4, 4, 2): (
        0, 1, 2, 4, 4, 0, 0, 4, 4, 2, 2, 4, 0, 1, 4, 3, 4, 0, 2, 2, 0, 4, 1, 0,
        2, 2, 2, 0, 0, 2, 2, 1, 0, 0, 2, 3, 3, 2, 1, 1, 1, 1, 1, 0, 1, 1, 1, 3,
        3, 3, 3, 3, 3, 3, 3, 3,
    ),
    ("feed", 4, 4): (
        4, 6, 4, 0, 5, 4, 4, 0, 4, 6, 5, 0, 5, 0, 0, 2, 5, 6, 1, 2, 0, 3, 4, 4,
        6, 1, 6, 7, 5, 0, 6, 1, 1, 5, 2, 0, 0, 1, 3, 2, 0, 1, 7, 3, 3, 0, 5, 1,
        0, 2, 0, 1, 0, 3, 2, 0, 0, 1, 1, 1, 3, 0, 1, 1, 1, 2, 2, 1, 1, 2, 1, 6,
        0, 2, 3, 3, 2, 7, 7, 2, 2, 2, 3, 2, 2, 1, 3, 3, 7, 0, 0, 2, 3, 3, 1, 2,
        7, 1, 7, 0, 3, 1, 3, 3, 3, 3, 2, 2, 0, 3, 2, 3, 3, 2, 1, 3,
    ),
    ("back", 4, 4, 3): (
        0, 1, 8, 8, 8, 8, 4, 5, 2, 0, 9, 9, 3, 8, 9, 1, 9, 1, 10, 10, 0, 10, 9, 10,
        0, 10, 8, 4, 9, 6, 0, 0, 9, 8, 5, 10, 2, 10, 7, 4, 0, 8, 3, 8, 4, 5, 10, 2,
        10, 9, 3, 5, 1, 9, 2, 10, 1, 10, 8, 2, 8, 3, 1, 4, 1, 5, 6, 9, 9, 7, 3, 7,
        7, 10, 0, 1, 2, 2, 6, 8, 3, 6, 5, 7, 6, 3, 2, 9, 3, 4, 10, 8, 7, 9, 6,
    ),
    ("retain", 4, 3, 2): (
        0, 0, 0, 0, 1, 1, 0, 1, 1, 1, 0, 0, 1, 1, 0, 0, 1, 0, 0, 1, 1, 1, 0, 1,
        0,
    ),
    ("last", 4, 4, 3): (
        0, 4, 4, 4, 4, 5, 5, 2, 4, 5, 5, 6, 6, 6, 5, 6, 3, 6, 4, 4, 1, 0, 6, 7,
        2, 5, 5, 7, 4, 4, 3, 2, 5, 5, 6, 2, 7, 6, 3, 7, 4, 4, 3, 0, 2, 3, 6, 5,
        6, 5, 1, 0, 4, 1, 0, 1, 7, 7, 4, 6, 1, 6, 5, 2, 7, 3, 7, 0, 5, 1, 8, 6,
        8, 7, 8, 6, 7,
    ),
}


def run_streams(streams, order, after):
    streams = [list(stream) for stream in streams]
    done = [0] * len(streams)

    def ready(stream):
        place = done[stream]
        return place < len(streams[stream]) and all(
            done[other] >= count for other, count in after.get((stream, place), ())
        )

    def take(stream):
        streams[stream][done[stream]]()
        done[stream] += 1

    if order is not None:
        for stream in order:
            assert ready(stream)
            take(stream)
    while any(done[index] < len(stream) for index, stream in enumerate(streams)):
        for stream in range(len(streams)):
            if ready(stream):
                take(stream)


def feed_kernel(
    size,
    chunks,
    mixed_hbm,
    out_hbm,
    tokens_hbm,
    seed_hbm,
    gate_hbm,
    up_hbm,
    down_hbm,
    gain_ref,
    bias_ref,
    second_hbm,
    seeds_hbm,
    inner_hbm,
    dgate_hbm,
    dlin_hbm,
    outp_hbm,
    middle_ref,
    dmiddle_ref,
    branch_ref,
    sums_ref,
    mixed,
    out_weight,
    tokens,
    hidden_gate,
    hidden_up,
    hidden_down,
    second,
    seeds,
    part,
    inbox,
    gate_in,
    lin_in,
    dinner,
    inner,
    dgate,
    dlin,
    wide,
    load_sem,
    store_sem,
    rs_send,
    rs_recv,
    back_send,
    back_recv,
    ag_send,
    ag_recv,
    seed_send,
    seed_recv,
):
    me = lax.axis_index("tensor")
    own, depth = tokens.shape
    rows = own // chunks
    hidden = inner.shape[-1]
    loads = [
        pltpu.make_async_copy(src, dst, load_sem.at[index])
        for index, (src, dst) in enumerate(
            (
                (mixed_hbm, mixed),
                (out_hbm, out_weight),
                (seed_hbm, seeds.at[me]),
                (tokens_hbm, tokens),
                (gate_hbm, hidden_gate),
                (up_hbm, hidden_up),
                (down_hbm, hidden_down),
            )
        )
    ]
    for load in loads:
        load.start()
    enter((), (size, me))
    scatter = LineScatter(size, me, rows, part, inbox, rs_send, rs_recv)
    scatter_back = LineScatter(size, me, rows, part, inbox, back_send, back_recv)
    gather = LineGather(size, me, rows, second, ag_send, ag_recv)
    gather_seed = LineGather(size, me, rows, seeds, seed_send, seed_recv)

    def at(chunk):
        return pl.ds(chunk * rows, rows)

    def flat(ref, chunk):
        value = ref[:, at(chunk), :]
        return value.reshape(size * rows, value.shape[-1])

    def store(kind, chunk):
        slot = chunk % 2
        src, dst = (
            (second.at[:, at(chunk)], second_hbm),
            (seeds.at[:, at(chunk)], seeds_hbm),
            (inner.at[slot], inner_hbm),
            (dgate.at[slot], dgate_hbm),
            (dlin.at[slot], dlin_hbm),
            (wide.at[slot], outp_hbm),
        )[kind]
        return pltpu.make_async_copy(src, dst.at[:, at(chunk)], store_sem.at[kind, chunk])

    waited = set()

    def need(*indices):
        for index in indices:
            if index not in waited:
                waited.add(index)
                loads[index].wait()

    def project(chunk):
        need(0, 1)

        def body(start, width):
            value = dot_nn(flat(mixed, chunk), out_weight[:, pl.ds(start, width)])
            part[:, at(chunk), pl.ds(start, width)] = value.astype(jnp.bfloat16).reshape(
                size, rows, width
            )

        for_columns(depth, body)
        scatter.begin(chunk)

    def normalize(chunk):
        need(3)
        scatter.arrive(chunk)

        def body(block):
            here = pl.ds(chunk * rows + block.start, LINE)
            middle = tokens[here, :].astype(jnp.float32) + scatter.total(here)
            middle_ref[here, :] = middle
            centered = middle - jnp.mean(middle, axis=-1, keepdims=True)
            scale = lax.rsqrt(jnp.mean(centered * centered, axis=-1, keepdims=True) + EPS)
            value = centered * scale * gain_ref[...] + bias_ref[...]
            second[me, here, :] = value.astype(jnp.bfloat16)

        for_rows(rows, body)
        gather.begin(chunk)

    def feed_in(chunk):
        need(4, 5)

        def body(start, width):
            columns = pl.ds(start, width)
            gate_in[:, columns] = dot_nt(flat(second, chunk), hidden_gate[columns, :])
            lin_in[:, columns] = dot_nt(flat(second, chunk), hidden_up[columns, :])

        for_columns(hidden, body)
        store(0, chunk).start()

    def feed_seed(chunk):
        need(6)

        def body(start, width):
            columns = pl.ds(start, width)
            dinner[:, columns] = dot_nt(flat(seeds, chunk), hidden_down[columns, :])

        for_columns(hidden, body)
        store(1, chunk).start()

    def feed_act(chunk):
        slot = chunk % 2
        if chunk >= 2:
            for kind in range(2, 5):
                store(kind, chunk - 2).wait()

        def body(block):
            gate, lin, grad = gate_in[block, :], lin_in[block, :], dinner[block, :]
            cube = GELU_SCALE * (gate + 0.044715 * (gate * gate * gate))
            tanh = jnp.tanh(cube)
            half = 0.5 * (1.0 + tanh)
            active = gate * half
            slope = half + 0.5 * gate * (1.0 - tanh * tanh) * (
                GELU_SCALE * (1.0 + 3.0 * 0.044715 * (gate * gate))
            )
            owner = block.start // rows
            inside = pl.ds(block.start - owner * rows, LINE)
            inner[slot, owner, inside, :] = (active * lin).astype(jnp.bfloat16)
            dlin[slot, owner, inside, :] = (grad * active).astype(jnp.bfloat16)
            dgate[slot, owner, inside, :] = (grad * lin * slope).astype(jnp.bfloat16)

        for_rows(size * rows, body)
        for kind in range(2, 5):
            store(kind, chunk).start()

    def feed_back(chunk):
        slot = chunk % 2
        scatter.drain(chunk)

        def body(start, width):
            columns = pl.ds(start, width)
            dgate_all = dgate[slot].reshape(size * rows, hidden)
            dlin_all = dlin[slot].reshape(size * rows, hidden)
            grad = dot_nn(dgate_all, hidden_gate[:, columns])
            grad = grad + dot_nn(dlin_all, hidden_up[:, columns])
            part[:, at(chunk), columns] = grad.astype(jnp.bfloat16).reshape(size, rows, width)

        for_columns(depth, body)
        scatter_back.begin(chunk)

    def feed_out(chunk):
        slot = chunk % 2
        if chunk >= 2:
            store(5, chunk - 2).wait()

        def body(start, width):
            columns = pl.ds(start, width)
            inner_all = inner[slot].reshape(size * rows, hidden)
            value = dot_nn(inner_all, hidden_down[:, columns])
            wide[slot, :, :, columns] = value.astype(jnp.bfloat16).reshape(size, rows, width)

        for_columns(depth, body)
        store(5, chunk).start()

    def normalize_back(chunk):
        scatter_back.arrive(chunk)

        def body(block):
            here = pl.ds(chunk * rows + block.start, LINE)
            middle = middle_ref[here, :]
            centered = middle - jnp.mean(middle, axis=-1, keepdims=True)
            scale = lax.rsqrt(jnp.mean(centered * centered, axis=-1, keepdims=True) + EPS)
            normed = centered * scale
            grad = scatter_back.total(here)
            shaped = grad * gain_ref[...]
            sums_ref[0:1, :] += jnp.sum(grad * normed, axis=0, keepdims=True)
            sums_ref[1:2, :] += jnp.sum(grad, axis=0, keepdims=True)
            dmiddle = seeds[me, here, :].astype(jnp.float32) + scale * (
                shaped
                - jnp.mean(shaped, axis=-1, keepdims=True)
                - normed * jnp.mean(shaped * normed, axis=-1, keepdims=True)
            )
            dmiddle_ref[here, :] = dmiddle
            branch_ref[here, :] = dmiddle.astype(jnp.bfloat16)

        for_rows(rows, body)

    def begin_seed(chunk):
        need(2)
        gather_seed.begin(chunk)

    streams, after = [], {}
    for chunk in range(chunks):
        steps = [project, *scatter.calls(chunk), normalize, *gather.calls(chunk)]
        first_feed = len(steps)
        steps += [feed_in, feed_seed, feed_act, feed_back, feed_out]
        steps += [*scatter_back.calls(chunk), normalize_back]
        streams.append(
            [step if isinstance(step, functools.partial) else functools.partial(step, chunk) for step in steps]
        )
        if chunk:
            after[chunk, first_feed] = ((chunk - 1, first_feed + 5),)
        after[chunk, first_feed + 1] = ((chunks + chunk, 2 * size - 1),)
    for chunk in range(chunks):
        streams.append([functools.partial(begin_seed, chunk), *gather_seed.calls(chunk)])
    sums_ref[...] = jnp.zeros_like(sums_ref)
    run_streams(streams, ORDERS.get(("feed", size, chunks)), after)
    for chunk in range(chunks):
        scatter_back.drain(chunk)
        gather.drain(chunk)
        gather_seed.drain(chunk)
        for kind in range(6 if chunk >= chunks - 2 else 2):
            store(kind, chunk).wait()


def feed_forward(size, chunks, mixed, out_weight, tokens, cotangent, hidden_gate, hidden_up, hidden_down, gain, bias):
    own, depth = tokens.shape
    hidden = hidden_gate.shape[0]
    rows = own // chunks
    low, full = jnp.bfloat16, jnp.float32

    def blocks(width):
        return jax.ShapeDtypeStruct((size, own, width), low)

    dma = pltpu.SemaphoreType.DMA
    wide, thin = (size, own, depth), (2, size, rows, hidden)
    return pl.pallas_call(
        functools.partial(feed_kernel, size, chunks),
        out_shape=(
            blocks(depth),
            blocks(depth),
            blocks(hidden),
            blocks(hidden),
            blocks(hidden),
            blocks(depth),
            jax.ShapeDtypeStruct((own, depth), full),
            jax.ShapeDtypeStruct((own, depth), full),
            jax.ShapeDtypeStruct((own, depth), low),
            jax.ShapeDtypeStruct((8, depth), full),
        ),
        in_specs=[pl.BlockSpec(memory_space=pl.ANY)] * 7
        + [pl.BlockSpec(memory_space=pltpu.VMEM)] * 2,
        out_specs=(pl.BlockSpec(memory_space=pl.ANY),) * 6
        + (pl.BlockSpec(memory_space=pltpu.VMEM),) * 4,
        scratch_shapes=[
            pltpu.VMEM((size, own, mixed.shape[-1]), low),
            pltpu.VMEM(out_weight.shape, low),
            pltpu.VMEM((own, depth), low),
            pltpu.VMEM((hidden, depth), low),
            pltpu.VMEM((hidden, depth), low),
            pltpu.VMEM((hidden, depth), low),
            pltpu.VMEM(wide, low),
            pltpu.VMEM(wide, low),
            pltpu.VMEM(wide, low),
            pltpu.VMEM((size + 1, own, depth), low),
            pltpu.VMEM((size * rows, hidden), full),
            pltpu.VMEM((size * rows, hidden), full),
            pltpu.VMEM((size * rows, hidden), full),
            pltpu.VMEM(thin, low),
            pltpu.VMEM(thin, low),
            pltpu.VMEM(thin, low),
            pltpu.VMEM((2, size, rows, depth), low),
            dma((7,)),
            dma((6, chunks)),
            dma((size, chunks)),
            dma((size + 1, chunks)),
            dma((size, chunks)),
            dma((size + 1, chunks)),
            dma((2, size, chunks)),
            dma((size, chunks)),
            dma((2, size, chunks)),
            dma((size, chunks)),
        ],
        compiler_params=pltpu.CompilerParams(
            collective_id=0, has_side_effects=True, vmem_limit_bytes=VMEM_BYTES
        ),
        cost_estimate=pl.CostEstimate(
            flops=14 * size * own * depth * hidden, bytes_accessed=2**26, transcendentals=0
        ),
    )(mixed, out_weight, tokens, cotangent, hidden_gate, hidden_up, hidden_down, gain, bias)


def back_kernel(
    size,
    bits,
    chunks,
    outp_hbm,
    out_hbm,
    own_hbm,
    middle_ref,
    seeds_hbm,
    second_hbm,
    inner_hbm,
    dgate_hbm,
    dlin_hbm,
    branch_hbm,
    dmixed_hbm,
    output_ref,
    totals_hbm,
    part,
    out_weight,
    branch,
    inbox,
    dmixed,
    seeds,
    second,
    thin,
    turned,
    load_sem,
    grad_sem,
    store_sem,
    rs_send,
    rs_recv,
    ag_send,
    ag_recv,
    cube_parts,
    cube_firsts,
    cube_nexts,
    cube_store,
    cube_send,
    cube_recv,
    cube_free,
):
    me = lax.axis_index("tensor")
    own, depth = middle_ref.shape
    rows = own // chunks
    load_own = pltpu.make_async_copy(own_hbm, branch.at[me], load_sem.at[0])
    load_part = pltpu.make_async_copy(outp_hbm, part, load_sem.at[1])
    load_out = pltpu.make_async_copy(out_hbm, out_weight, load_sem.at[2])
    load_own.start()
    load_part.start()
    cube = CubeSum(
        bits,
        lax.axis_index("dp"),
        totals_hbm,
        cube_parts,
        cube_firsts,
        cube_nexts,
        cube_store,
        cube_send,
        cube_recv,
        cube_free,
    )
    grad_loads = [
        pltpu.make_async_copy(src, dst, grad_sem.at[index])
        for index, (src, dst) in enumerate(
            (
                (inner_hbm, thin.at[0]),
                (seeds_hbm, seeds),
                (dgate_hbm, thin.at[1]),
                (second_hbm, second),
                (dlin_hbm, thin.at[0]),
            )
        )
    ]
    for load in grad_loads[:4]:
        load.start()
    load_out.start()
    enter([{"dp": cube.partner(bit)} for bit in range(bits)], (size, me))
    scatter = LineScatter(size, me, rows, part, inbox, rs_send, rs_recv)
    gather = LineGather(size, me, rows, branch, ag_send, ag_recv)

    def at(chunk):
        return pl.ds(chunk * rows, rows)

    def store(kind, chunk):
        if kind == 0:
            src, dst = branch.at[:, at(chunk)], branch_hbm
        else:
            return pltpu.make_async_copy(
                dmixed.at[chunk % 2], dmixed_hbm.at[:, :, at(chunk)], store_sem.at[kind, chunk]
            )
        return pltpu.make_async_copy(src, dst.at[:, at(chunk)], store_sem.at[kind, chunk])

    def finish(chunk):
        scatter.arrive(chunk)

        def body(block):
            here = pl.ds(chunk * rows + block.start, LINE)
            output_ref[here, :] = (middle_ref[here, :] + scatter.total(here)).astype(jnp.bfloat16)

        for_rows(rows, body)

    def unproject(chunk):
        if chunk == 0:
            load_out.wait()
        if chunk >= 2:
            store(1, chunk - 2).wait()

        def body(start, width):
            columns = pl.ds(start, width)
            left = branch[:, at(chunk), :].reshape(size * rows, depth)
            for head in range(dmixed.shape[1]):
                value = dot_nt(left, out_weight[pl.ds(head * VD + start, width), :])
                dmixed[chunk % 2, head, :, :, columns] = value.reshape(size, rows, width)

        for_columns(VD, body)
        for kind in range(2):
            store(kind, chunk).start()

    def begin_branch(chunk):
        if chunk == 0:
            load_own.wait()
        gather.begin(chunk)

    def begin_out(chunk):
        if chunk == 0:
            load_part.wait()
        scatter.begin(chunk)

    def turn(which):
        needs = ((0, 1), (2, 3), (4,))[which]
        for index in needs:
            grad_loads[index].wait()
        for owner in range(size):
            turned[:, pl.ds(owner * own, own)] = thin[which % 2, owner].T
        if which == 0:
            grad_loads[4].start()

    def wide_columns(which):
        ref = (seeds, second, second)[which]
        return lambda columns: ref[:, :, columns].reshape(size * own, columns.size)

    streams, after = [], {}
    for chunk in range(chunks):
        steps = [functools.partial(begin_branch, chunk), *gather.calls(chunk)]
        if chunk:
            after[chunk, 0] = ((chunk - 1, 1),)
            after[chunk, len(steps)] = ((chunk - 1, len(steps) + 1),)
        streams.append(steps + [functools.partial(unproject, chunk)])
    for chunk in range(chunks):
        steps = [functools.partial(begin_out, chunk), *scatter.calls(chunk)]
        if chunk:
            after[chunks + chunk, 0] = ((chunks + chunk - 1, 1),)
        streams.append(steps + [functools.partial(finish, chunk)])
    for which in range(len(cube_parts)):
        if which:
            after[2 * chunks + which, 0] = ((2 * chunks + which - 1, 3),)
        streams.append(
            [
                functools.partial(turn, which),
                *cube.make_wide(which, turned, wide_columns(which)),
                *cube.calls(which),
            ]
        )
    run_streams(streams, ORDERS.get(("back", size, chunks, bits)), after)
    for chunk in range(chunks):
        scatter.drain(chunk)
        gather.drain(chunk)
        for kind in range(2 if chunk >= chunks - 2 else 1):
            store(kind, chunk).wait()
    cube.drain()


def feed_back(size, bits, chunks, partial, out_weight, branch, middle, seeds, second, thins):
    own, depth = middle.shape
    rows = own // chunks
    width = out_weight.shape[0]
    low, full = jnp.bfloat16, jnp.float32
    dma = pltpu.SemaphoreType.DMA
    vmem, anywhere = pl.BlockSpec(memory_space=pltpu.VMEM), pl.BlockSpec(memory_space=pl.ANY)
    grads = [jax.ShapeDtypeStruct((thin.shape[-1], depth), low) for thin in thins]
    many = [anywhere] * len(grads)
    return pl.pallas_call(
        functools.partial(back_kernel, size, bits, chunks),
        out_shape=(
            jax.ShapeDtypeStruct((size, own, depth), low),
            jax.ShapeDtypeStruct((width // VD, size, own, VD), full),
            jax.ShapeDtypeStruct((own, depth), low),
            grads,
        ),
        in_specs=[anywhere, anywhere, anywhere, vmem] + [anywhere] * 5,
        out_specs=(anywhere, anywhere, vmem, many),
        scratch_shapes=[
            pltpu.VMEM((size, own, depth), low),
            pltpu.VMEM(out_weight.shape, low),
            pltpu.VMEM((size, own, depth), low),
            pltpu.VMEM((size + 1, own, depth), low),
            pltpu.VMEM((2, width // VD, size, rows, VD), full),
            pltpu.VMEM((size, own, depth), low),
            pltpu.VMEM((size, own, depth), low),
            pltpu.VMEM((2,) + thins[0].shape, low),
            pltpu.VMEM((thins[0].shape[-1], size * own), low),
            dma((3,)),
            dma((5,)),
            dma((2, chunks)),
            dma((size, chunks)),
            dma((size + 1, chunks)),
            dma((2, size, chunks)),
            dma((size, chunks)),
        ]
        + cube_scratch(bits, [grad.shape for grad in grads]),
        compiler_params=pltpu.CompilerParams(
            collective_id=1, has_side_effects=True, vmem_limit_bytes=VMEM_BYTES
        ),
        cost_estimate=pl.CostEstimate(
            flops=2 * size * own * depth * width, bytes_accessed=2**26, transcendentals=0
        ),
    )(partial, out_weight, branch, middle, seeds, second, *thins)


def last_kernel(
    size,
    bits,
    chunks,
    dfirst_hbm,
    tokens_ref,
    dmiddle_ref,
    gain_ref,
    sums_ref,
    firsts_hbm,
    dvalues_hbm,
    dgates_hbm,
    dqueries_hbm,
    dkeys_hbm,
    dtokens_ref,
    totals_ref,
    totals_hbm,
    first_part,
    first_inbox,
    line_box,
    dp_box,
    firsts,
    dvalues,
    dgates,
    dqueries,
    dkeys,
    turned,
    slice_turned,
    load_sem,
    line_send,
    line_recv,
    dp_send,
    dp_recv,
    rs_send,
    rs_recv,
    cube_parts,
    cube_firsts,
    cube_nexts,
    cube_store,
    cube_send,
    cube_recv,
    cube_free,
):
    me = lax.axis_index("tensor")
    mine = lax.axis_index("dp")
    own = tokens_ref.shape[0]
    rows = own // chunks
    load_first = pltpu.make_async_copy(dfirst_hbm, first_part, load_sem.at[0])
    load_first.start()
    cube = CubeSum(
        bits,
        mine,
        totals_hbm,
        cube_parts,
        cube_firsts,
        cube_nexts,
        cube_store,
        cube_send,
        cube_recv,
        cube_free,
    )
    loads = [
        pltpu.make_async_copy(src, dst, load_sem.at[1 + index])
        for index, (src, dst) in enumerate(
            (
                (dvalues_hbm, dvalues),
                (firsts_hbm, firsts),
                (dgates_hbm, dgates),
                (dqueries_hbm, dqueries),
                (dkeys_hbm, dkeys),
            )
        )
    ]
    for load in loads:
        load.start()
    groups = 2**bits
    peers = [{"dp": (mine + step) % groups} for step in range(1, groups)]
    others = [{"tensor": (me + step) % size} for step in range(1, size)]
    enter(peers + others, None)
    first = LineScatter(size, me, rows, first_part, first_inbox, rs_send, rs_recv)

    def back(chunk):
        first.arrive(chunk)

        def body(block):
            here = pl.ds(chunk * rows + block.start, LINE)
            values = tokens_ref[here, :].astype(jnp.float32)
            centered = values - jnp.mean(values, axis=-1, keepdims=True)
            scale = lax.rsqrt(jnp.mean(centered * centered, axis=-1, keepdims=True) + EPS)
            normed = centered * scale
            grad = first.total(here)
            shaped = grad * gain_ref[...]
            line_box[me, 2:3, :] += jnp.sum(grad * normed, axis=0, keepdims=True)
            line_box[me, 3:4, :] += jnp.sum(grad, axis=0, keepdims=True)
            dtokens_ref[here, :] = dmiddle_ref[here, :] + scale * (
                shaped
                - jnp.mean(shaped, axis=-1, keepdims=True)
                - normed * jnp.mean(shaped * normed, axis=-1, keepdims=True)
            )

        for_rows(rows, body)

    def line_copy(step, slot):
        return pltpu.make_async_remote_copy(
            src_ref=line_box.at[me],
            dst_ref=line_box.at[slot],
            send_sem=line_send.at[step],
            recv_sem=line_recv.at[slot],
            device_id={"tensor": (me + step) % size},
            device_id_type=MESH,
        )

    def dp_copy(step, slot):
        return pltpu.make_async_remote_copy(
            src_ref=dp_box.at[mine],
            dst_ref=dp_box.at[slot],
            send_sem=dp_send.at[step],
            recv_sem=dp_recv.at[slot],
            device_id={"dp": (mine + step) % groups},
            device_id_type=MESH,
        )

    def sums_on_line():
        for step in range(1, size):
            line_copy(step, me).start()

    def sums_on_dp():
        for step in range(1, size):
            line_copy(step, (me + step) % size).wait_recv()
        dp_box[mine] = jnp.sum(line_box[...], axis=0)
        for step in range(1, groups):
            dp_copy(step, mine).start()

    def sums_done():
        for step in range(1, groups):
            dp_copy(step, (mine + step) % groups).wait_recv()
        totals_ref[...] = jnp.sum(dp_box[...], axis=0)

    line_box[me] = sums_ref[...]
    load_first.wait()
    def turn(which):
        for index in ((0, 1), (2,))[which]:
            loads[index].wait()
        ref = (dvalues, dgates)[which]
        for owner in range(size):
            turned[:, pl.ds(owner * own, own)] = ref[owner].T

    def first_columns(columns):
        return firsts[:, :, columns].reshape(size * own, columns.size)

    def make_tall(start):
        if start == 0:
            loads[3].wait()
            loads[4].wait()
        lines = cube_parts[2].shape[-2]
        for index in range(start, start + groups // 4):
            lead = tuple((index >> bit) & 1 for bit in range(bits - 1, -1, -1))
            for owner in range(size):
                piece = firsts[owner, :, pl.ds(index * lines, lines)]
                slice_turned[:, pl.ds(owner * own, own)] = piece.T
            for which, ref in ((2, dqueries), (3, dkeys)):
                value = dot_nn(slice_turned[...], ref[...].reshape(size * own, ref.shape[-1]))
                cube_parts[which][lead] = value.astype(jnp.bfloat16)

    streams = []
    for chunk in range(chunks):
        streams.append(
            [
                functools.partial(first.begin, chunk),
                *first.calls(chunk),
                functools.partial(back, chunk),
            ]
        )
    after = {(chunks + 4, 0): [(chunk, 2 * size - 2) for chunk in range(chunks)]}
    for which in range(2):
        if which:
            after[chunks + which, 0] = ((chunks + which - 1, 3),)
        streams.append(
            [
                functools.partial(turn, which),
                *cube.make_wide(which, turned, first_columns),
                *cube.calls(which),
            ]
        )
    quarters = [functools.partial(make_tall, quarter * (groups // 4)) for quarter in range(4)]
    after[chunks + 2, 0] = ((chunks, 1),)
    after[chunks + 3, 0] = ((chunks + 2, 4),)
    streams.append([*quarters, *cube.calls(2)])
    streams.append(cube.calls(3))
    streams.append([sums_on_line, sums_on_dp, sums_done])
    run_streams(streams, ORDERS.get(("last", size, chunks, bits)), after)
    for chunk in range(chunks):
        first.drain(chunk)
    for step in range(1, size):
        line_copy(step, me).wait_send()
    for step in range(1, groups):
        dp_copy(step, mine).wait_send()
    cube.drain()


def last_sums(size, bits, chunks, dfirst, tokens, dmiddle, gain, sums, firsts, parts):
    own, depth = tokens.shape
    low, full = jnp.bfloat16, jnp.float32
    dma = pltpu.SemaphoreType.DMA
    vmem, anywhere = pl.BlockSpec(memory_space=pltpu.VMEM), pl.BlockSpec(memory_space=pl.ANY)
    grads = [
        jax.ShapeDtypeStruct((part.shape[-1], depth) if place < 2 else (depth, part.shape[-1]), low)
        for place, part in enumerate(parts)
    ]
    many = [anywhere] * len(grads)
    group = size * own
    return pl.pallas_call(
        functools.partial(last_kernel, size, bits, chunks),
        out_shape=(
            jax.ShapeDtypeStruct((own, depth), full),
            jax.ShapeDtypeStruct((8, depth), full),
            grads,
        ),
        in_specs=[anywhere, vmem, vmem, vmem, vmem] + [anywhere] * 5,
        out_specs=(vmem, vmem, many),
        scratch_shapes=[
            pltpu.VMEM((size, own, depth), low),
            pltpu.VMEM((size + 1, own, depth), low),
            pltpu.VMEM((size, 8, depth), full),
            pltpu.VMEM((2**bits, 8, depth), full),
            pltpu.VMEM(firsts.shape, low),
            *[pltpu.VMEM(part.shape, low) for part in parts],
            pltpu.VMEM((parts[0].shape[-1], group), low),
            pltpu.VMEM((depth // 2**bits, group), low),
            dma((6,)),
            dma((size,)),
            dma((size,)),
            dma((2**bits,)),
            dma((2**bits,)),
            dma((size, chunks)),
            dma((size + 1, chunks)),
        ]
        + cube_scratch(bits, [grad.shape for grad in grads]),
        compiler_params=pltpu.CompilerParams(
            collective_id=2, has_side_effects=True, vmem_limit_bytes=VMEM_BYTES
        ),
        cost_estimate=pl.CostEstimate(flops=2**30, bytes_accessed=2**26, transcendentals=0),
    )(dfirst, tokens, dmiddle, gain, sums, firsts, *parts)


def decay_rows(rate, column, row, first):
    shape = (column.shape[0], row.shape[1])
    here = first + lax.broadcasted_iota(jnp.int32, shape, 0)
    offset = here - lax.broadcasted_iota(jnp.int32, shape, 1)
    inside = (column == row) & (offset >= 0)
    distance = jnp.maximum(offset, 0).astype(jnp.float32)
    decay = jnp.where(inside, jnp.exp(-rate * distance), 0.0)
    return decay * lax.rsqrt(jnp.sum(decay, axis=-1, keepdims=True))


def group_parts(values):
    centered = values - jnp.mean(values, axis=-1, keepdims=True)
    scale = lax.rsqrt(jnp.mean(centered * centered, axis=-1, keepdims=True) + GROUP_EPS)
    return centered * scale, scale


def sigmoid(values):
    return 1.0 / (1.0 + jnp.exp(-values))


def first_kernel(
    size,
    chunks,
    heads,
    tokens_ref,
    gain_ref,
    bias_ref,
    column_ref,
    row_ref,
    rates_ref,
    query_hbm,
    key_hbm,
    value_hbm,
    gate_hbm,
    first_hbm,
    queries_hbm,
    keys_hbm,
    values_hbm,
    gates_hbm,
    retained_hbm,
    mixed_hbm,
    table_hbm,
    query_weight,
    key_weight,
    value_weight,
    gate_weight,
    first,
    queries,
    keys,
    values,
    gates,
    retained,
    mixed,
    table,
    raw,
    retain,
    load_sem,
    store_sem,
    done_sem,
    ag_send,
    ag_recv,
):
    me = lax.axis_index("tensor")
    own, depth = tokens_ref.shape
    rows = own // chunks
    pairs = (
        (query_hbm, query_weight),
        (key_hbm, key_weight),
        (value_hbm, value_weight),
        (gate_hbm, gate_weight),
    )
    loads = [
        pltpu.make_async_copy(src, dst, load_sem.at[index])
        for index, (src, dst) in enumerate(pairs)
    ]
    for load in loads:
        load.start()
    enter((), (size, me))
    gather = LineGather(size, me, rows, first, ag_send, ag_recv)
    waited = set()

    def need(index):
        if index not in waited:
            waited.add(index)
            loads[index].wait()

    def at(chunk):
        return pl.ds(chunk * rows, rows)

    def flat(chunk):
        return first[:, at(chunk), :].reshape(size * rows, depth)

    def store(kind, block):
        src, dst = (
            (queries, queries_hbm),
            (keys, keys_hbm),
            (first, first_hbm),
            (mixed, mixed_hbm),
        )[kind]
        return pltpu.make_async_copy(src.at[block], dst.at[block], store_sem.at[kind, block])

    def store_head(kind, head, block):
        src, dst = (
            (values, values_hbm),
            (gates, gates_hbm),
            (retained, retained_hbm),
            (table, table_hbm),
        )[kind]
        return pltpu.make_async_copy(
            src.at[head, block], dst.at[head, block], done_sem.at[kind, head, block]
        )

    def normalize(chunk):
        def body(block):
            here = pl.ds(chunk * rows + block.start, LINE)
            tokens = tokens_ref[here, :].astype(jnp.float32)
            centered = tokens - jnp.mean(tokens, axis=-1, keepdims=True)
            scale = lax.rsqrt(jnp.mean(centered * centered, axis=-1, keepdims=True) + EPS)
            value = centered * scale * gain_ref[...] + bias_ref[...]
            first[me, here, :] = value.astype(jnp.bfloat16)

        for_rows(rows, body)
        gather.begin(chunk)

    def project_pair(chunk):
        need(0)
        need(1)

        def body(start, width):
            columns = pl.ds(start, width)
            value = dot_nn(flat(chunk), query_weight[:, columns])
            queries[:, at(chunk), columns] = value.astype(jnp.bfloat16).reshape(size, rows, width)
            value = dot_nn(flat(chunk), key_weight[:, columns])
            keys[:, at(chunk), columns] = value.astype(jnp.bfloat16).reshape(size, rows, width)

        for_columns(heads * KD, body)

    def project_value(chunk, head):
        need(2)

        def body(start, width):
            weight = value_weight[pl.ds(head * VD + start, width), :]
            value = dot_nt(flat(chunk), weight).astype(jnp.bfloat16)
            values[head, :, at(chunk), pl.ds(start, width)] = value.reshape(size, rows, width)

        for_columns(VD, body)

    def project_gate(chunk, head):
        need(3)

        def body(start, width):
            weight = gate_weight[pl.ds(head * VD + start, width), :]
            value = dot_nt(flat(chunk), weight)
            gates[head, :, at(chunk), pl.ds(start, width)] = value.reshape(size, rows, width)

        for_columns(VD, body)

    def tabulate(head, block):
        seen = (block + 1) * own

        def body(part):
            there = pl.ds(block * own + part.start, part.size)
            table[head, block, part, :seen] = decay_rows(
                rates_ref[head], column_ref[there, :], row_ref[:, :seen], block * own + part.start
            )

        for_rows(own, body, BAND)
        store_head(3, head, block).start()

    def attend(head, block):
        seen = (block + 1) * own
        lanes = pl.ds(head * KD, KD)
        query = queries[block, :, lanes]
        raw[:, :seen] = dot_nt(query, keys[: block + 1, :, lanes].reshape(seen, KD))

        def body(part):
            weighted = raw[part, :seen] * (KD**-0.5) * table[head, block, part, :seen]
            total = jnp.sum(weighted, axis=-1, keepdims=True)
            retain[part, :seen] = (weighted * lax.rsqrt(total * total + 1.0)).astype(jnp.bfloat16)

        for_rows(own, body, BAND)
        value = values[head, : block + 1].reshape(seen, VD)
        retained[head, block] = dot_nn(retain[:, :seen], value)

        def body_mix(part):
            normed, _ = group_parts(retained[head, block, part, :])
            gate = gates[head, block, part, :]
            value = (gate * sigmoid(gate) * normed).astype(jnp.bfloat16)
            mixed[block, part, pl.ds(head * VD, VD)] = value

        for_rows(own, body_mix, BAND)
        store_head(2, head, block).start()
        if head == heads - 1:
            store(3, block).start()

    streams, after = [], {}
    for chunk in range(chunks):
        steps = [functools.partial(normalize, chunk), *gather.calls(chunk)]
        if chunk:
            after[chunk, 0] = ((chunk - 1, 1),)
        steps.append(functools.partial(project_pair, chunk))
        for head in range(heads):
            steps.append(functools.partial(project_value, chunk, head))
            steps.append(functools.partial(project_gate, chunk, head))
        streams.append(steps)
    streams.append(
        [functools.partial(tabulate, head, block) for head in range(heads) for block in range(size)]
    )
    run_streams(streams, ORDERS.get(("first", size, chunks, heads)), after)
    for block in range(size):
        for kind in range(3):
            store(kind, block).start()
        for head in range(heads):
            for kind in range(2):
                store_head(kind, head, block).start()
    for head in range(heads):
        for block in range(size):
            attend(head, block)
    for chunk in range(chunks):
        gather.drain(chunk)
    for block in range(size):
        for kind in range(4):
            store(kind, block).wait()
        for head in range(heads):
            for kind in range(4):
                store_head(kind, head, block).wait()


def first_part(size, chunks, tokens, gain, bias, segments, rates, query, key, value, gate):
    own, depth = tokens.shape
    heads = query.shape[1] // KD
    rows = size * own
    low, full = jnp.bfloat16, jnp.float32
    dma = pltpu.SemaphoreType.DMA
    vmem, anywhere = pl.BlockSpec(memory_space=pltpu.VMEM), pl.BlockSpec(memory_space=pl.ANY)
    shapes = (
        ((size, own, depth), low),
        ((size, own, heads * KD), low),
        ((size, own, heads * KD), low),
        ((heads, size, own, VD), low),
        ((heads, size, own, VD), full),
        ((heads, size, own, VD), full),
        ((size, own, heads * VD), low),
        ((heads, size, own, rows), full),
    )
    return pl.pallas_call(
        functools.partial(first_kernel, size, chunks, heads),
        out_shape=tuple(jax.ShapeDtypeStruct(*item) for item in shapes),
        in_specs=[vmem] * 5 + [pl.BlockSpec(memory_space=pltpu.SMEM)] + [anywhere] * 4,
        out_specs=(anywhere,) * 8,
        scratch_shapes=[pltpu.VMEM(item.shape, low) for item in (query, key, value, gate)]
        + [pltpu.VMEM(*item) for item in shapes]
        + [
            pltpu.VMEM((own, rows), full),
            pltpu.VMEM((own, rows), low),
            dma((4,)),
            dma((4, size)),
            dma((4, heads, size)),
            dma((2, size, chunks)),
            dma((size, chunks)),
        ],
        compiler_params=pltpu.CompilerParams(
            collective_id=3, has_side_effects=True, vmem_limit_bytes=VMEM_BYTES
        ),
        cost_estimate=pl.CostEstimate(flops=2**33, bytes_accessed=2**26, transcendentals=0),
    )(
        tokens,
        gain,
        bias,
        segments.reshape(rows, 1),
        segments.reshape(1, rows),
        rates,
        query,
        key,
        value,
        gate,
    )


def retain_kernel(
    size,
    bits,
    heads,
    queries_hbm,
    keys_hbm,
    values_hbm,
    gates_hbm,
    retained_hbm,
    dmixed_hbm,
    table_hbm,
    query_hbm,
    key_hbm,
    value_hbm,
    gate_hbm,
    mixed_hbm,
    branch_hbm,
    dqueries_hbm,
    dkeys_hbm,
    dvalues_hbm,
    dgates_hbm,
    dfirst_hbm,
    totals_hbm,
    queries,
    keys,
    values,
    gates,
    retained,
    dmixed,
    table,
    query_weight,
    key_weight,
    value_weight,
    gate_weight,
    mixed,
    branch,
    dqueries,
    dkeys,
    dvalues,
    dgates,
    dfirst,
    turned,
    raw,
    grad,
    retain,
    dscores,
    dretained,
    dkey_sum,
    dvalue_sum,
    load_sem,
    block_sem,
    store_sem,
    cube_parts,
    cube_firsts,
    cube_nexts,
    cube_store,
    cube_send,
    cube_recv,
    cube_free,
):
    own = queries.shape[1]
    depth = query_weight.shape[0]

    def load_whole(kind):
        src, dst = (
            (queries_hbm, queries),
            (keys_hbm, keys),
            (mixed_hbm, mixed),
            (branch_hbm, branch),
            (query_hbm, query_weight),
            (key_hbm, key_weight),
            (value_hbm, value_weight),
            (gate_hbm, gate_weight),
        )[kind]
        return pltpu.make_async_copy(src, dst, load_sem.at[kind])

    def load_block(kind, head, block):
        slot = (head * size + block) % 2
        src, dst = (
            (values_hbm, values.at[head, block]),
            (gates_hbm, gates.at[slot]),
            (retained_hbm, retained.at[slot]),
            (dmixed_hbm, dmixed.at[slot]),
            (table_hbm, table.at[slot]),
        )[kind]
        return pltpu.make_async_copy(src.at[head, block], dst, block_sem.at[kind, head, block])

    def load_blocks(place):
        if place < heads * size:
            for kind in range(5):
                load_block(kind, place // size, place % size).start()

    def store(kind, block):
        src, dst = (
            (dqueries, dqueries_hbm),
            (dkeys, dkeys_hbm),
            (dvalues, dvalues_hbm),
            (dgates, dgates_hbm),
            (dfirst, dfirst_hbm),
        )[kind]
        return pltpu.make_async_copy(src.at[block], dst.at[block], store_sem.at[kind, block])

    for kind in range(2):
        load_whole(kind).start()
    load_blocks(0)
    for kind in range(2, 4):
        load_whole(kind).start()
    load_blocks(1)
    for kind in range(4, 8):
        load_whole(kind).start()
    cube = CubeSum(
        bits,
        lax.axis_index("dp"),
        totals_hbm,
        cube_parts,
        cube_firsts,
        cube_nexts,
        cube_store,
        cube_send,
        cube_recv,
        cube_free,
    )
    enter([{"dp": cube.partner(bit)} for bit in range(bits)], None)

    def attend(head, block):
        seen = (block + 1) * own
        slot = (head * size + block) % 2
        if head == 0 and block == 0:
            for kind in range(2):
                load_whole(kind).wait()
        lanes = pl.ds(head * KD, KD)

        for kind in range(5):
            load_block(kind, head, block).wait()

        def body_mix(part):
            normed, scale = group_parts(retained[slot, part, :])
            gate = gates[slot, part, :]
            dmix = dmixed[slot, part, :]
            half = sigmoid(gate)
            dgate = dmix * normed * (half * (1.0 + gate * (1.0 - half)))
            dgates[block, part, pl.ds(head * VD, VD)] = dgate.astype(jnp.bfloat16)
            dnormed = dmix * (gate * half)
            value = scale * (
                dnormed
                - jnp.mean(dnormed, axis=-1, keepdims=True)
                - normed * jnp.mean(dnormed * normed, axis=-1, keepdims=True)
            )
            dretained[part, :] = value.astype(jnp.bfloat16)

        for_rows(own, body_mix, BAND)
        query = queries[block, :, lanes]
        key = keys[: block + 1, :, lanes].reshape(seen, KD)
        raw[:, :seen] = dot_nt(query, key)
        value = values[head, : block + 1].reshape(seen, VD)
        grad[:, :seen] = dot_nt(dretained[...], value)

        def body(part):
            decay = table[slot, part, :seen]
            weighted = raw[part, :seen] * (KD**-0.5) * decay
            dretain = grad[part, :seen]
            total = jnp.sum(weighted, axis=-1, keepdims=True)
            along = jnp.sum(dretain * weighted, axis=-1, keepdims=True)
            inverse = lax.rsqrt(total * total + 1.0)
            retain[part, :seen] = (weighted * inverse).astype(jnp.bfloat16)
            along = along * total * inverse * inverse
            dscores[part, :seen] = (decay * inverse * (dretain - along)).astype(jnp.bfloat16)

        for_rows(own, body, BAND)
        dquery = dot_nn(dscores[:, :seen], key) * (KD**-0.5)
        dqueries[block, :, lanes] = dquery.astype(jnp.bfloat16)
        for other in range(block + 1):
            there = pl.ds(other * own, own)
            dkey = dot_tn(dscores[:, there], query)
            dvalue = dot_tn(retain[:, there], dretained[...])
            if other == block:
                dkey_sum[other] = dkey
                dvalue_sum[other] = dvalue
            else:
                dkey_sum[other] += dkey
                dvalue_sum[other] += dvalue

        load_blocks(head * size + block + 2)
        if block == size - 1:
            for other in range(size):
                dkeys[other, :, lanes] = (dkey_sum[other] * (KD**-0.5)).astype(jnp.bfloat16)
                there = pl.ds(head * VD, VD)
                dvalues[other, :, there] = dvalue_sum[other].astype(jnp.bfloat16)

    def combine(block):
        if block == 0:
            for kind in range(4, 8):
                load_whole(kind).wait()
        for kind in range(4):
            store(kind, block).start()

        def body(start, width):
            columns = pl.ds(start, width)
            total = dot_nt(dqueries[block], query_weight[columns, :])
            total = total + dot_nt(dkeys[block], key_weight[columns, :])
            total = total + dot_nn(dvalues[block], value_weight[:, columns])
            total = total + dot_nn(dgates[block], gate_weight[:, columns])
            dfirst[block, :, columns] = total.astype(jnp.bfloat16)

        for_columns(depth, body)
        store(4, block).start()

    def turn():
        for kind in range(2, 4):
            load_whole(kind).wait()
        for owner in range(size):
            turned[:, pl.ds(owner * own, own)] = mixed[owner].T

    def branch_columns(columns):
        return branch[:, :, columns].reshape(size * own, columns.size)

    steps = [
        functools.partial(attend, head, block) for head in range(heads) for block in range(size)
    ]
    steps += [functools.partial(combine, block) for block in range(size)]
    sums = [turn, *cube.make_wide(0, turned, branch_columns), *cube.calls(0)]
    run_streams([sums, steps], ORDERS.get(("retain", size, bits, heads)), {})
    for block in range(size):
        for kind in range(5):
            store(kind, block).wait()
    cube.drain()


def retain_back(
    size, bits, queries, keys, values, gates, retained, dmixed, table, query, key, value, gate, mixed, branch
):
    own = queries.shape[1]
    heads = values.shape[0]
    rows, depth = size * own, query.shape[0]
    low, full = jnp.bfloat16, jnp.float32
    dma = pltpu.SemaphoreType.DMA
    anywhere = pl.BlockSpec(memory_space=pl.ANY)
    inputs = (queries, keys, values, gates, retained, dmixed, table, query, key, value, gate)
    inputs = inputs + (mixed, branch)
    slots = [
        jax.ShapeDtypeStruct((2,) + item.shape[2:], item.dtype) if 3 <= place < 7 else item
        for place, item in enumerate(inputs)
    ]
    total = jax.ShapeDtypeStruct((heads * VD, depth), low)
    shapes = (
        queries.shape,
        keys.shape,
        (size, own, heads * VD),
        (size, own, heads * VD),
        (size, own, depth),
    )
    return pl.pallas_call(
        functools.partial(retain_kernel, size, bits, heads),
        out_shape=tuple(jax.ShapeDtypeStruct(shape, low) for shape in shapes) + ([total],),
        in_specs=[anywhere] * len(inputs),
        out_specs=(anywhere,) * 5 + ([anywhere],),
        scratch_shapes=[pltpu.VMEM(item.shape, item.dtype) for item in slots]
        + [pltpu.VMEM(shape, low) for shape in shapes]
        + [
            pltpu.VMEM((heads * VD, rows), low),
            pltpu.VMEM((own, rows), full),
            pltpu.VMEM((own, rows), full),
            pltpu.VMEM((own, rows), low),
            pltpu.VMEM((own, rows), low),
            pltpu.VMEM((own, VD), low),
            pltpu.VMEM((size, own, KD), full),
            pltpu.VMEM((size, own, VD), full),
            dma((8,)),
            dma((5, heads, size)),
            dma((5, size)),
        ]
        + cube_scratch(bits, [total.shape]),
        compiler_params=pltpu.CompilerParams(
            collective_id=4, has_side_effects=True, vmem_limit_bytes=VMEM_BYTES
        ),
        cost_estimate=pl.CostEstimate(flops=2**34, bytes_accessed=2**26, transcendentals=0),
    )(*inputs)


def per_device(
    tokens,
    first_gain,
    first_bias,
    query_weight,
    key_weight,
    value_weight,
    gate_weight,
    out_weight,
    second_gain,
    second_bias,
    hidden_gate,
    hidden_up,
    hidden_down,
    segments,
    cotangent,
):
    size = lax.axis_size("tensor")
    group_rows = segments.size
    head_local = query_weight.shape[1] // KD
    head_index = (lax.axis_index("tensor") * head_local + jnp.arange(head_local)).astype(
        jnp.float32
    )
    rates = -jnp.log1p(-jnp.exp2(-5.0 - head_index))
    first_all, queries, keys, values, gates, retained, mixed, table = first_part(
        size,
        CHUNKS,
        tokens,
        first_gain[None],
        first_bias[None],
        segments,
        rates,
        query_weight,
        key_weight,
        value_weight.T,
        gate_weight.T,
    )
    bits = lax.axis_size("dp").bit_length() - 1
    own = tokens.shape[0]
    (
        second_all,
        seed_all,
        inner,
        gate_in_low,
        lin_in_low,
        partial,
        middle,
        grad_middle,
        branch,
        second_sums,
    ) = feed_forward(
        size,
        CHUNKS,
        mixed,
        out_weight,
        tokens,
        cotangent,
        hidden_gate.T,
        hidden_up.T,
        hidden_down,
        second_gain[None],
        second_bias[None],
    )

    branch_all, grad_mixed, output, feed_grads = feed_back(
        size,
        bits,
        CHUNKS,
        partial,
        out_weight,
        branch,
        middle,
        seed_all,
        second_all,
        (inner, gate_in_low, lin_in_low),
    )
    grad_queries, grad_keys, grad_values, grad_gates, grad_first, (grad_outw,) = retain_back(
        size,
        bits,
        queries,
        keys,
        values,
        gates,
        retained,
        grad_mixed,
        table,
        query_weight,
        key_weight,
        value_weight.T,
        gate_weight.T,
        mixed,
        branch_all,
    )
    grad_tokens, sums, grads = last_sums(
        size,
        bits,
        CHUNKS,
        grad_first,
        tokens,
        grad_middle,
        first_gain[None],
        second_sums,
        first_all,
        (grad_values, grad_gates, grad_queries, grad_keys),
    )
    grad_sgain, grad_sbias, grad_fgain, grad_fbias = sums[0], sums[1], sums[2], sums[3]
    grad_outw, grad_valuew, grad_gatew, grad_queryw, grad_keyw = (
        item.astype(jnp.float32) for item in (grad_outw, *grads)
    )
    grad_hdown, grad_hgate, grad_hup = (item.astype(jnp.float32) for item in feed_grads)
    grad_valuew, grad_gatew, grad_hgate, grad_hup = (
        item.T for item in (grad_valuew, grad_gatew, grad_hgate, grad_hup)
    )
    return (
        output,
        grad_tokens,
        grad_fgain,
        grad_fbias,
        grad_queryw,
        grad_keyw,
        grad_valuew,
        grad_gatew,
        grad_outw,
        grad_sgain,
        grad_sbias,
        grad_hgate,
        grad_hup,
        grad_hdown,
    )


def solution(mesh):
    return jax.shard_map(
        per_device,
        mesh=mesh,
        in_specs=(
            P(("dp", "tensor"), None),
            P(),
            P(),
            P(None, "tensor"),
            P(None, "tensor"),
            P(None, "tensor"),
            P(None, "tensor"),
            P("tensor", None),
            P(),
            P(),
            P(None, "tensor"),
            P(None, "tensor"),
            P("tensor", None),
            P("dp", None),
            P(("dp", "tensor"), None),
        ),
        out_specs=(
            P(("dp", "tensor"), None),
            P(("dp", "tensor"), None),
            P(),
            P(),
            P(None, "tensor"),
            P(None, "tensor"),
            P(None, "tensor"),
            P(None, "tensor"),
            P("tensor", None),
            P(),
            P(),
            P(None, "tensor"),
            P(None, "tensor"),
            P("tensor", None),
        ),
        check_vma=False,
    )
```

```python
import functools
import itertools

import jax
import jax.numpy as jnp
from jax import lax
from jax.experimental import pallas as pl
from jax.experimental.pallas import tpu as pltpu
from jax.sharding import PartitionSpec as P

KD = 256
VD = 432


EPS = 1e-05
GROUP_EPS = 0.1
GELU_SCALE = 0.7978845608028654
CHUNKS = 4

MESH = pl.DeviceIdType.MESH
VMEM_BYTES = 60 * 2**20
TILE = 1024
LINE = 16
BAND = 64
ACT = 64
WHOLE = 256


def for_columns(width, body):
    full = width // TILE

    def step(index, carry):
        body(pl.multiple_of(index * TILE, TILE), TILE)
        return carry

    if full:
        lax.fori_loop(0, full, step, 0)
    if width % TILE:
        body(full * TILE, width % TILE)


def for_rows(count, body, size=None):
    size = min(count, size or BAND)

    def step(index, carry):
        body(pl.ds(pl.multiple_of(index * size, LINE), size))
        return carry

    lax.fori_loop(0, count // size, step, 0)


def dot_nn(left, right):
    return lax.dot_general(left, right, (((1,), (0,)), ((), ())), preferred_element_type=jnp.float32)


def dot_nt(left, right):
    return lax.dot_general(left, right, (((1,), (1,)), ((), ())), preferred_element_type=jnp.float32)


def dot_tn(left, right):
    return lax.dot_general(left, right, (((0,), (0,)), ((), ())), preferred_element_type=jnp.float32)


def enter(peers, line):
    barrier = pltpu.get_barrier_semaphore()
    for peer in peers:
        pl.semaphore_signal(barrier, inc=1, device_id=peer, device_id_type=MESH)
    if line is not None:
        size, me = line

        @pl.when(me > 0)
        def _():
            pl.semaphore_signal(barrier, inc=1, device_id={"tensor": me - 1}, device_id_type=MESH)

        @pl.when(me < size - 1)
        def _():
            pl.semaphore_signal(barrier, inc=1, device_id={"tensor": me + 1}, device_id_type=MESH)

    count = len(peers)
    if line is not None:
        count = count + (me > 0).astype(jnp.int32) + (me < size - 1).astype(jnp.int32)
    pl.semaphore_wait(barrier, count)


class LineScatter:
    def __init__(self, size, me, rows, part, inbox, send, recv):
        self.size, self.me, self.rows = size, me, rows
        self.part, self.inbox, self.send, self.recv = part, inbox, send, recv

    def at(self, chunk):
        return pl.ds(chunk * self.rows, self.rows)

    def copy(self, target, slot, chunk, device):
        return pltpu.make_async_remote_copy(
            src_ref=self.part.at[target, self.at(chunk)],
            dst_ref=self.inbox.at[slot, self.at(chunk)],
            send_sem=self.send.at[target, chunk],
            recv_sem=self.recv.at[slot, chunk],
            device_id={"tensor": device},
            device_id_type=MESH,
        )

    def add(self, target, chunk):
        def body(rows):
            at = pl.ds(chunk * self.rows + rows.start, rows.size)
            total = self.part[target, at, :].astype(jnp.float32)
            total = total + self.inbox[target, at, :].astype(jnp.float32)
            self.part[target, at, :] = total.astype(jnp.bfloat16)

        for_rows(self.rows, body)

    def go_right(self, chunk, target):
        self.copy(target, target, chunk, self.me + 1).start()

    def go_left(self, chunk, target):
        last = self.me - 1 == target
        self.copy(target, jnp.where(last, self.size, target), chunk, self.me - 1).start()

    def begin(self, chunk):
        @pl.when(self.me == 0)
        def _():
            for target in range(self.size - 1, 0, -1):
                self.go_right(chunk, target)

        @pl.when(self.me == self.size - 1)
        def _():
            for target in range(self.size - 1):
                self.go_left(chunk, target)

    def right(self, chunk, target):
        @pl.when((self.me < target) & (self.me > 0))
        def _():
            self.copy(target, target, chunk, self.me).wait_recv()
            self.add(target, chunk)
            self.go_right(chunk, target)

    def left(self, chunk, target):
        @pl.when((self.me > target) & (self.me < self.size - 1))
        def _():
            self.copy(target, target, chunk, self.me).wait_recv()
            self.add(target, chunk)
            self.go_left(chunk, target)

    def calls(self, chunk):
        for step in range(self.size - 1):
            if step < self.size - 2:
                yield functools.partial(self.right, chunk, self.size - 1 - step)
                yield functools.partial(self.left, chunk, step)

    def arrive(self, chunk):
        size, me = self.size, self.me

        @pl.when(me > 0)
        def _():
            self.copy(me, me, chunk, me - 1).wait_recv()

        @pl.when(me < size - 1)
        def _():
            self.copy(me, size, chunk, me + 1).wait_recv()

    def total(self, rows):
        size, me = self.size, self.me
        own = self.part[me, rows, :].astype(jnp.float32)
        low = self.inbox[me, rows, :].astype(jnp.float32)
        high = self.inbox[size, rows, :].astype(jnp.float32)
        return own + jnp.where(me > 0, low, 0.0) + jnp.where(me < size - 1, high, 0.0)

    def drain(self, chunk):
        for target in range(self.size):

            @pl.when(self.me != target)
            def _():
                self.copy(target, target, chunk, self.me).wait_send()


class LineGather:
    def __init__(self, size, me, rows, held, send, recv):
        self.size, self.me, self.rows = size, me, rows
        self.held, self.send, self.recv = held, send, recv

    def copy(self, block, chunk, way, device):
        at = pl.ds(chunk * self.rows, self.rows)
        return pltpu.make_async_remote_copy(
            src_ref=self.held.at[block, at],
            dst_ref=self.held.at[block, at],
            send_sem=self.send.at[way, block, chunk],
            recv_sem=self.recv.at[block, chunk],
            device_id={"tensor": device},
            device_id_type=MESH,
        )

    def begin(self, chunk):
        self.right(chunk, 0)
        self.left(chunk, 0)

    def right(self, chunk, step):
        size, me = self.size, self.me

        @pl.when(me >= step)
        def _():
            if step:
                self.copy(me - step, chunk, 0, me).wait_recv()

            @pl.when(me < size - 1)
            def _():
                self.copy(me - step, chunk, 0, me + 1).start()

    def left(self, chunk, step):
        size, me = self.size, self.me

        @pl.when(me + step < size)
        def _():
            if step:
                self.copy(me + step, chunk, 1, me).wait_recv()

            @pl.when(me > 0)
            def _():
                self.copy(me + step, chunk, 1, me - 1).start()

    def calls(self, chunk):
        for step in range(1, self.size):
            yield functools.partial(self.right, chunk, step)
            yield functools.partial(self.left, chunk, step)

    def drain(self, chunk):
        size, me = self.size, self.me
        for step in range(size):

            @pl.when((me >= step) & (me < size - 1))
            def _():
                self.copy(me - step, chunk, 0, me + 1).wait_send()

            @pl.when((me + step < size) & (me > 0))
            def _():
                self.copy(me + step, chunk, 1, me - 1).wait_send()


class CubeSum:
    def __init__(self, bits, me, results, parts, firsts, nexts, store, send, recv, free):
        self.bits, self.me = bits, me
        self.results, self.parts = results, parts
        self.firsts, self.nexts = firsts, nexts
        self.store_sem, self.send, self.recv = store, send, recv
        self.free = free
        self.orders = (tuple(range(bits)), (0,) + tuple(range(bits - 1, 0, -1)))
        self.mine = [(me // 2**bit) % 2 for bit in range(bits)]

    def partner(self, bit):
        return self.me + (1 - 2 * self.mine[bit]) * 2**bit

    def band(self, which, color):
        count = self.parts[which].shape[-2]
        cut = cut_rows(count)
        return ((0, cut), (cut, count - cut), (0, count))[color]

    def lead(self, fixed):
        return tuple(fixed.get(bit, slice(None)) for bit in range(self.bits - 1, -1, -1))

    def moved(self, src, dst, which, color, step, bit):
        return pltpu.make_async_remote_copy(
            src_ref=src,
            dst_ref=dst,
            send_sem=self.send.at[which, color % 2, step],
            recv_sem=self.recv.at[which, color % 2, step],
            device_id={"dp": self.partner(bit)},
            device_id_type=MESH,
        )

    def halve(self, which, color, step):
        order = self.orders[color % 2]
        start, count = self.band(which, color)
        fixed = {bit: self.mine[bit] for bit in order[:step]}
        fixed[order[step]] = 1 - self.mine[order[step]]
        src = self.parts[which].at[self.lead(fixed) + (pl.ds(start, count), slice(None))]
        dst = self.firsts[which] if step == 0 else self.nexts[which][color][step - 1]
        return self.moved(src, dst, which, color, step, order[step])

    def double(self, which, color, step):
        order = self.orders[color % 2]
        start, count = self.band(which, color)
        fixed = {bit: self.mine[bit] for bit in order[: step + 1]}
        held = self.parts[which].at[self.lead(fixed) + (pl.ds(start, count), slice(None))]
        return self.moved(held, held, which, color, 2 * self.bits - 1 - step, order[step])

    def freed(self, which, color, step):
        return self.free.at[which, color % 2, step]

    def land(self, which, color, step):
        copy = self.halve(which, color, step)
        copy.wait_send()
        partner = {"dp": self.partner(self.orders[color % 2][step])}
        pl.semaphore_signal(
            self.freed(which, color, step), inc=1, device_id=partner, device_id_type=MESH
        )
        copy.wait_recv()
        self.add(which, color, step)

    def grow(self, which, color, step):
        pl.semaphore_wait(self.freed(which, color, step), 1)
        self.double(which, color, step).start()

    def add(self, which, color, step):
        order = self.orders[color % 2]
        part, (start, count) = self.parts[which], self.band(which, color)
        box = self.firsts[which] if step == 0 else self.nexts[which][color][step - 1]
        fixed = {bit: self.mine[bit] for bit in order[: step + 1]}
        free = [bit for bit in range(self.bits - 1, -1, -1) if bit not in fixed]
        for choice in itertools.product((0, 1), repeat=len(free)):
            lead = self.lead({**fixed, **dict(zip(free, choice))})

            def body(begin, size):
                there = lead + (pl.ds(start + begin, size), slice(None))
                total = part[there].astype(jnp.float32)
                total = total + box[choice + (pl.ds(begin, size), slice(None))].astype(jnp.float32)
                part[there] = total.astype(jnp.bfloat16)

            for_blocks(count, part.shape[-1], body)

    def slices(self, which, ref):
        rows, columns = self.parts[which].shape[-2:]
        for index in range(2**self.bits):
            lead = tuple((index >> bit) & 1 for bit in range(self.bits - 1, -1, -1))
            if ref.shape[0] == rows:
                whole = ref.at[:, pl.ds(index * columns, columns)]
            else:
                whole = ref.at[pl.ds(index * rows, rows), :]
            yield index, self.parts[which].at[lead], whole

    def make_wide(self, which, left, right):
        columns = self.parts[which].shape[-1]
        half = 2 ** (self.bits - 1)

        def some(start):
            for index in range(start, start + half):
                lead = tuple((index >> bit) & 1 for bit in range(self.bits - 1, -1, -1))
                value = dot_nn(left[...], right(pl.ds(index * columns, columns)))
                self.parts[which][lead] = value.astype(jnp.bfloat16)

        return [functools.partial(some, 0), functools.partial(some, half)]

    def open(self, which):
        self.halve(which, 2, 0).start()

    def split(self, which):
        self.land(which, 2, 0)
        for color in range(2):
            self.halve(which, color, 1).start()

    def down(self, which, color, step):
        self.land(which, color, step - 1)
        self.halve(which, color, step).start()

    def turn(self, which, color):
        self.land(which, color, self.bits - 1)
        self.grow(which, color, self.bits - 1)

    def up(self, which, color, step):
        self.double(which, color, step + 1).wait_recv()
        self.grow(which, color, step)

    def join(self, which):
        for color in range(2):
            self.double(which, color, 1).wait_recv()
        self.grow(which, 2, 0)

    def close(self, which):
        self.double(which, 2, 0).wait_recv()
        for index, part, whole in self.slices(which, self.results[which]):
            pltpu.make_async_copy(part, whole, self.store_sem.at[which, index]).start()

    def calls(self, which):
        yield functools.partial(self.open, which)
        yield functools.partial(self.split, which)
        for step in range(2, self.bits):
            for color in range(2):
                yield functools.partial(self.down, which, color, step)
        for color in range(2):
            yield functools.partial(self.turn, which, color)
        for step in range(self.bits - 2, 0, -1):
            for color in range(2):
                yield functools.partial(self.up, which, color, step)
        yield functools.partial(self.join, which)
        yield functools.partial(self.close, which)

    def drain(self):
        for which in range(len(self.parts)):
            self.double(which, 2, 0).wait_send()
            for color in range(2):
                for step in range(1, self.bits):
                    self.double(which, color, step).wait_send()
            for index, part, whole in self.slices(which, self.results[which]):
                pltpu.make_async_copy(part, whole, self.store_sem.at[which, index]).wait()


def cut_rows(count):
    return count // (2 * LINE) * LINE


def for_blocks(count, columns, body):
    size = LINE
    while count % (2 * size) == 0 and 2 * size * columns <= 2**14:
        size *= 2
    for factor in (3, 5):
        if count % (factor * size) == 0 and factor * size * columns <= 2**14:
            size *= factor

    def step(index, carry):
        body(pl.multiple_of(index * size, LINE), size)
        return carry

    lax.fori_loop(0, count // size, step, 0)


def cube_scratch(bits, shapes):
    low = jnp.bfloat16
    parts, firsts, nexts = [], [], []
    for rows, columns in shapes:
        if columns >= rows:
            columns = columns // 2**bits
        else:
            rows = rows // 2**bits
        cut = cut_rows(rows)
        parts.append(pltpu.VMEM((2,) * bits + (rows, columns), low))
        firsts.append(pltpu.VMEM((2,) * (bits - 1) + (rows, columns), low))
        nexts.append(
            [
                [
                    pltpu.VMEM((2,) * (bits - 1 - step) + (count, columns), low)
                    for step in range(1, bits)
                ]
                for count in (cut, rows - cut)
            ]
        )
    dma = pltpu.SemaphoreType.DMA
    return [
        parts,
        firsts,
        nexts,
        dma((len(shapes), 2**bits)),
        dma((len(shapes), 2, 2 * bits)),
        dma((len(shapes), 2, 2 * bits)),
        pltpu.SemaphoreType.REGULAR((len(shapes), 2, bits)),
    ]


ORDERS = {
    ("first", 4, 4, 2): (
        0, 1, 0, 2, 1, 3, 4, 0, 1, 2, 0, 2, 0, 0, 4, 4, 4, 3, 0, 3, 0, 4, 0, 4,
        4, 2, 1, 2, 3, 1, 3, 6, 2, 1, 4, 1, 2, 0, 2, 2, 0, 1, 2, 1, 0, 1, 3, 3,
        3, 3, 3, 1, 3, 2, 3, 1, 2, 5, 5, 5, 6, 6, 5, 5, 5, 5, 5, 5, 6, 6, 6, 6,
    ),
    ("feed", 4, 4): (
        4, 0, 5, 1, 6, 0, 4, 5, 0, 5, 0, 0, 4, 4, 5, 1, 0, 2, 3, 5, 6, 4, 0, 1,
        6, 0, 0, 2, 0, 4, 4, 5, 0, 1, 0, 2, 1, 5, 6, 2, 2, 0, 1, 2, 3, 1, 1, 0,
        0, 0, 1, 2, 1, 1, 3, 1, 3, 3, 2, 0, 1, 1, 3, 1, 1, 1, 2, 2, 2, 2, 0, 2,
        2, 3, 2, 3, 2, 3, 2, 1, 6, 3, 3, 1, 1, 0, 2, 3, 0, 6, 0, 6, 1, 3, 3, 3,
        3, 3, 3, 2, 2, 1, 3, 3, 0, 2, 3, 2, 3,
    ),
    ("back", 4, 4, 3): (
        0, 8, 8, 8, 8, 1, 4, 9, 9, 9, 9, 0, 8, 10, 10, 5, 10, 1, 0, 2, 0, 9, 10, 10,
        1, 4, 8, 1, 8, 9, 3, 9, 5, 10, 0, 10, 2, 8, 8, 1, 3, 5, 9, 5, 9, 4, 3, 2,
        6, 1, 10, 10, 0, 8, 2, 7, 8, 9, 9, 0, 3, 6, 4, 2, 5, 0, 10, 3, 10, 1, 2, 1,
        3, 3, 4, 7, 7, 8, 7, 2, 9, 4, 6, 6, 7, 5, 8, 6, 2, 10, 7, 3, 9, 10, 6,
    ),
    ("retain", 4, 3, 2): (
        0, 0, 0, 0, 0, 1, 1, 0, 0, 1, 0, 0, 0, 0, 1, 1, 1, 1, 0, 1, 0,
    ),
    ("last", 4, 4, 3): (
        4, 4, 4, 4, 0, 6, 6, 4, 6, 6, 7, 5, 6, 2, 7, 5, 5, 5, 4, 4, 6, 0, 7, 7,
        5, 2, 0, 0, 4, 4, 3, 6, 2, 2, 6, 5, 5, 1, 4, 2, 4, 0, 3, 7, 7, 6, 6, 5,
        5, 1, 1, 7, 7, 1, 0, 3, 5, 1, 5, 3, 7, 6, 4, 3, 7, 1, 6, 2, 3, 8, 5, 8,
        4, 6, 8, 5, 6,
    ),
}


def run_streams(streams, order, after):
    streams = [list(stream) for stream in streams]
    done = [0] * len(streams)

    def ready(stream):
        place = done[stream]
        return place < len(streams[stream]) and all(
            done[other] >= count for other, count in after.get((stream, place), ())
        )

    def take(stream):
        streams[stream][done[stream]]()
        done[stream] += 1

    if order is not None:
        for stream in order:
            assert ready(stream)
            take(stream)
    while any(done[index] < len(stream) for index, stream in enumerate(streams)):
        for stream in range(len(streams)):
            if ready(stream):
                take(stream)


def feed_kernel(
    size,
    chunks,
    mixed_hbm,
    out_hbm,
    tokens_hbm,
    seed_hbm,
    seed_first_hbm,
    gate_hbm,
    up_hbm,
    down_hbm,
    gain_ref,
    bias_ref,
    second_hbm,
    seeds_hbm,
    inner_hbm,
    dgate_hbm,
    dlin_hbm,
    outp_hbm,
    middle_ref,
    dmiddle_ref,
    branch_ref,
    sums_ref,
    mixed,
    out_weight,
    tokens,
    hidden_gate,
    hidden_up,
    hidden_down,
    second,
    seeds,
    part,
    inbox,
    gate_in,
    lin_in,
    dinner,
    inner,
    dgate,
    dlin,
    wide,
    load_sem,
    store_sem,
    rs_send,
    rs_recv,
    back_send,
    back_recv,
    ag_send,
    ag_recv,
    seed_send,
    seed_recv,
):
    me = lax.axis_index("tensor")
    own, depth = tokens.shape
    rows = own // chunks
    hidden = inner.shape[-1]
    loads = [
        pltpu.make_async_copy(src, dst, load_sem.at[index])
        for index, (src, dst) in enumerate(
            (
                (mixed_hbm, mixed),
                (out_hbm, out_weight),
                (seed_hbm.at[pl.ds(rows, own - rows)], seeds.at[me, pl.ds(rows, own - rows)]),
                (tokens_hbm, tokens),
                (gate_hbm, hidden_gate),
                (up_hbm, hidden_up),
                (down_hbm, hidden_down),
                (seed_first_hbm, seeds.at[:, pl.ds(0, rows)]),
            )
        )
    ]
    for load in loads:
        load.start()
    enter((), (size, me))
    scatter = LineScatter(size, me, rows, part, inbox, rs_send, rs_recv)
    scatter_back = LineScatter(size, me, rows, part, inbox, back_send, back_recv)
    gather = LineGather(size, me, rows, second, ag_send, ag_recv)
    gather_seed = LineGather(size, me, rows, seeds, seed_send, seed_recv)

    def at(chunk):
        return pl.ds(chunk * rows, rows)

    def flat(ref, chunk):
        value = ref[:, at(chunk), :]
        return value.reshape(size * rows, value.shape[-1])

    def store(kind, chunk):
        slot = chunk % 2
        src, dst = (
            (second.at[:, at(chunk)], second_hbm),
            (seeds.at[:, at(chunk)], seeds_hbm),
            (inner.at[slot], inner_hbm),
            (dgate.at[slot], dgate_hbm),
            (dlin.at[slot], dlin_hbm),
            (wide.at[slot], outp_hbm),
        )[kind]
        return pltpu.make_async_copy(src, dst.at[:, at(chunk)], store_sem.at[kind, chunk])

    waited = set()

    def need(*indices):
        for index in indices:
            if index not in waited:
                waited.add(index)
                loads[index].wait()

    def project(chunk):
        need(0, 1)

        def body(start, width):
            value = dot_nn(flat(mixed, chunk), out_weight[:, pl.ds(start, width)])
            part[:, at(chunk), pl.ds(start, width)] = value.astype(jnp.bfloat16).reshape(
                size, rows, width
            )

        for_columns(depth, body)
        scatter.begin(chunk)

    def normalize(chunk):
        need(3)
        scatter.arrive(chunk)

        def body(block):
            here = pl.ds(chunk * rows + block.start, block.size)
            middle = tokens[here, :].astype(jnp.float32) + scatter.total(here)
            middle_ref[here, :] = middle
            centered = middle - jnp.mean(middle, axis=-1, keepdims=True)
            scale = lax.rsqrt(jnp.mean(centered * centered, axis=-1, keepdims=True) + EPS)
            value = centered * scale * gain_ref[...] + bias_ref[...]
            second[me, here, :] = value.astype(jnp.bfloat16)

        for_rows(rows, body)
        gather.begin(chunk)

    def feed_in(chunk):
        need(4, 5)

        def body(start, width):
            columns = pl.ds(start, width)
            gate_in[:, columns] = dot_nt(flat(second, chunk), hidden_gate[columns, :])
            lin_in[:, columns] = dot_nt(flat(second, chunk), hidden_up[columns, :])

        for_columns(hidden, body)
        store(0, chunk).start()

    def feed_seed(chunk):
        need(6, 7)

        def body(start, width):
            columns = pl.ds(start, width)
            dinner[:, columns] = dot_nt(flat(seeds, chunk), hidden_down[columns, :])

        for_columns(hidden, body)
        store(1, chunk).start()

    def feed_act(chunk):
        slot = chunk % 2
        if chunk >= 2:
            for kind in range(2, 5):
                store(kind, chunk - 2).wait()

        def body(block):
            gate, lin, grad = gate_in[block, :], lin_in[block, :], dinner[block, :]
            cube = GELU_SCALE * (gate + 0.044715 * (gate * gate * gate))
            tanh = jnp.tanh(cube)
            half = 0.5 * (1.0 + tanh)
            active = gate * half
            slope = half + 0.5 * gate * (1.0 - tanh * tanh) * (
                GELU_SCALE * (1.0 + 3.0 * 0.044715 * (gate * gate))
            )
            owner = block.start // rows
            inside = pl.ds(block.start - owner * rows, block.size)
            inner[slot, owner, inside, :] = (active * lin).astype(jnp.bfloat16)
            dlin[slot, owner, inside, :] = (grad * active).astype(jnp.bfloat16)
            dgate[slot, owner, inside, :] = (grad * lin * slope).astype(jnp.bfloat16)

        for_rows(size * rows, body, min(ACT, rows))
        for kind in range(2, 5):
            store(kind, chunk).start()

    def feed_back(chunk):
        slot = chunk % 2
        scatter.drain(chunk)

        def body(start, width):
            columns = pl.ds(start, width)
            dgate_all = dgate[slot].reshape(size * rows, hidden)
            dlin_all = dlin[slot].reshape(size * rows, hidden)
            grad = dot_nn(dgate_all, hidden_gate[:, columns])
            grad = grad + dot_nn(dlin_all, hidden_up[:, columns])
            part[:, at(chunk), columns] = grad.astype(jnp.bfloat16).reshape(size, rows, width)

        for_columns(depth, body)
        scatter_back.begin(chunk)

    def feed_out(chunk):
        slot = chunk % 2
        if chunk >= 2:
            store(5, chunk - 2).wait()

        def body(start, width):
            columns = pl.ds(start, width)
            inner_all = inner[slot].reshape(size * rows, hidden)
            value = dot_nn(inner_all, hidden_down[:, columns])
            wide[slot, :, :, columns] = value.astype(jnp.bfloat16).reshape(size, rows, width)

        for_columns(depth, body)
        store(5, chunk).start()

    def normalize_back(chunk):
        scatter_back.arrive(chunk)

        def body(block):
            here = pl.ds(chunk * rows + block.start, block.size)
            middle = middle_ref[here, :]
            centered = middle - jnp.mean(middle, axis=-1, keepdims=True)
            scale = lax.rsqrt(jnp.mean(centered * centered, axis=-1, keepdims=True) + EPS)
            normed = centered * scale
            grad = scatter_back.total(here)
            shaped = grad * gain_ref[...]
            sums_ref[0:1, :] += jnp.sum(grad * normed, axis=0, keepdims=True)
            sums_ref[1:2, :] += jnp.sum(grad, axis=0, keepdims=True)
            dmiddle = seeds[me, here, :].astype(jnp.float32) + scale * (
                shaped
                - jnp.mean(shaped, axis=-1, keepdims=True)
                - normed * jnp.mean(shaped * normed, axis=-1, keepdims=True)
            )
            dmiddle_ref[here, :] = dmiddle
            branch_ref[here, :] = dmiddle.astype(jnp.bfloat16)

        for_rows(rows, body)

    def begin_seed(chunk):
        need(2)
        gather_seed.begin(chunk)

    streams, after = [], {}
    for chunk in range(chunks):
        steps = [project, *scatter.calls(chunk), normalize, *gather.calls(chunk)]
        first_feed = len(steps)
        steps += [feed_in, feed_seed, feed_act, feed_back, feed_out]
        steps += [*scatter_back.calls(chunk), normalize_back]
        streams.append(
            [step if isinstance(step, functools.partial) else functools.partial(step, chunk) for step in steps]
        )
        if chunk:
            after[chunk, first_feed] = ((chunk - 1, first_feed + 5),)
            after[chunk, first_feed + 1] = ((chunks + chunk - 1, 2 * size - 1),)
    for chunk in range(1, chunks):
        streams.append([functools.partial(begin_seed, chunk), *gather_seed.calls(chunk)])
    sums_ref[...] = jnp.zeros_like(sums_ref)
    run_streams(streams, ORDERS.get(("feed", size, chunks)), after)
    for chunk in range(chunks):
        scatter_back.drain(chunk)
        gather.drain(chunk)
        if chunk:
            gather_seed.drain(chunk)
        for kind in range(6 if chunk >= chunks - 2 else 2):
            store(kind, chunk).wait()


def feed_forward(size, chunks, mixed, out_weight, tokens, cotangent, seed_first, hidden_gate, hidden_up, hidden_down, gain, bias):
    own, depth = tokens.shape
    hidden = hidden_gate.shape[0]
    rows = own // chunks
    low, full = jnp.bfloat16, jnp.float32

    def blocks(width):
        return jax.ShapeDtypeStruct((size, own, width), low)

    dma = pltpu.SemaphoreType.DMA
    wide, thin = (size, own, depth), (2, size, rows, hidden)
    return pl.pallas_call(
        functools.partial(feed_kernel, size, chunks),
        out_shape=(
            blocks(depth),
            blocks(depth),
            blocks(hidden),
            blocks(hidden),
            blocks(hidden),
            blocks(depth),
            jax.ShapeDtypeStruct((own, depth), full),
            jax.ShapeDtypeStruct((own, depth), full),
            jax.ShapeDtypeStruct((own, depth), low),
            jax.ShapeDtypeStruct((8, depth), full),
        ),
        in_specs=[pl.BlockSpec(memory_space=pl.ANY)] * 8
        + [pl.BlockSpec(memory_space=pltpu.VMEM)] * 2,
        out_specs=(pl.BlockSpec(memory_space=pl.ANY),) * 6
        + (pl.BlockSpec(memory_space=pltpu.VMEM),) * 4,
        scratch_shapes=[
            pltpu.VMEM((size, own, mixed.shape[-1]), low),
            pltpu.VMEM(out_weight.shape, low),
            pltpu.VMEM((own, depth), low),
            pltpu.VMEM((hidden, depth), low),
            pltpu.VMEM((hidden, depth), low),
            pltpu.VMEM((hidden, depth), low),
            pltpu.VMEM(wide, low),
            pltpu.VMEM(wide, low),
            pltpu.VMEM(wide, low),
            pltpu.VMEM((size + 1, own, depth), low),
            pltpu.VMEM((size * rows, hidden), full),
            pltpu.VMEM((size * rows, hidden), full),
            pltpu.VMEM((size * rows, hidden), full),
            pltpu.VMEM(thin, low),
            pltpu.VMEM(thin, low),
            pltpu.VMEM(thin, low),
            pltpu.VMEM((2, size, rows, depth), low),
            dma((8,)),
            dma((6, chunks)),
            dma((size, chunks)),
            dma((size + 1, chunks)),
            dma((size, chunks)),
            dma((size + 1, chunks)),
            dma((2, size, chunks)),
            dma((size, chunks)),
            dma((2, size, chunks)),
            dma((size, chunks)),
        ],
        compiler_params=pltpu.CompilerParams(
            collective_id=0, has_side_effects=True, vmem_limit_bytes=VMEM_BYTES
        ),
        cost_estimate=pl.CostEstimate(
            flops=14 * size * own * depth * hidden, bytes_accessed=2**26, transcendentals=0
        ),
    )(mixed, out_weight, tokens, cotangent, seed_first, hidden_gate, hidden_up, hidden_down, gain, bias)


def back_kernel(
    size,
    bits,
    chunks,
    outp_hbm,
    out_hbm,
    own_hbm,
    middle_ref,
    seeds_hbm,
    second_hbm,
    inner_hbm,
    dgate_hbm,
    dlin_hbm,
    branch_hbm,
    dmixed_hbm,
    output_ref,
    totals_hbm,
    part,
    out_weight,
    branch,
    inbox,
    dmixed,
    seeds,
    second,
    thin,
    turned,
    load_sem,
    grad_sem,
    store_sem,
    rs_send,
    rs_recv,
    ag_send,
    ag_recv,
    cube_parts,
    cube_firsts,
    cube_nexts,
    cube_store,
    cube_send,
    cube_recv,
    cube_free,
):
    me = lax.axis_index("tensor")
    own, depth = middle_ref.shape
    rows = own // chunks
    load_own = pltpu.make_async_copy(own_hbm, branch.at[me], load_sem.at[0])
    load_part = pltpu.make_async_copy(outp_hbm, part, load_sem.at[1])
    load_out = pltpu.make_async_copy(out_hbm, out_weight, load_sem.at[2])
    load_own.start()
    load_part.start()
    cube = CubeSum(
        bits,
        lax.axis_index("dp"),
        totals_hbm,
        cube_parts,
        cube_firsts,
        cube_nexts,
        cube_store,
        cube_send,
        cube_recv,
        cube_free,
    )
    grad_loads = [
        pltpu.make_async_copy(src, dst, grad_sem.at[index])
        for index, (src, dst) in enumerate(
            (
                (inner_hbm, thin.at[0]),
                (seeds_hbm, seeds),
                (dgate_hbm, thin.at[1]),
                (second_hbm, second),
                (dlin_hbm, thin.at[0]),
            )
        )
    ]
    for load in grad_loads[:4]:
        load.start()
    load_out.start()
    enter([{"dp": cube.partner(bit)} for bit in range(bits)], (size, me))
    scatter = LineScatter(size, me, rows, part, inbox, rs_send, rs_recv)
    gather = LineGather(size, me, rows, branch, ag_send, ag_recv)

    def at(chunk):
        return pl.ds(chunk * rows, rows)

    def store(kind, chunk):
        if kind == 0:
            src, dst = branch.at[:, at(chunk)], branch_hbm
        else:
            return pltpu.make_async_copy(
                dmixed.at[chunk % 2], dmixed_hbm.at[:, :, at(chunk)], store_sem.at[kind, chunk]
            )
        return pltpu.make_async_copy(src, dst.at[:, at(chunk)], store_sem.at[kind, chunk])

    def finish(chunk):
        scatter.arrive(chunk)

        def body(block):
            here = pl.ds(chunk * rows + block.start, block.size)
            output_ref[here, :] = (middle_ref[here, :] + scatter.total(here)).astype(jnp.bfloat16)

        for_rows(rows, body)

    def unproject(chunk):
        if chunk == 0:
            load_out.wait()
        if chunk >= 2:
            store(1, chunk - 2).wait()

        def body(start, width):
            columns = pl.ds(start, width)
            left = branch[:, at(chunk), :].reshape(size * rows, depth)
            for head in range(dmixed.shape[1]):
                value = dot_nt(left, out_weight[pl.ds(head * VD + start, width), :])
                dmixed[chunk % 2, head, :, :, columns] = value.reshape(size, rows, width)

        for_columns(VD, body)
        for kind in range(2):
            store(kind, chunk).start()

    def begin_branch(chunk):
        if chunk == 0:
            load_own.wait()
        gather.begin(chunk)

    def begin_out(chunk):
        if chunk == 0:
            load_part.wait()
        scatter.begin(chunk)

    def turn(which):
        needs = ((0, 1), (2, 3), (4,))[which]
        for index in needs:
            grad_loads[index].wait()
        for owner in range(size):
            turned[:, pl.ds(owner * own, own)] = thin[which % 2, owner].T
        if which == 0:
            grad_loads[4].start()

    def wide_columns(which):
        ref = (seeds, second, second)[which]
        return lambda columns: ref[:, :, columns].reshape(size * own, columns.size)

    streams, after = [], {}
    for chunk in range(chunks):
        steps = [functools.partial(begin_branch, chunk), *gather.calls(chunk)]
        if chunk:
            after[chunk, 0] = ((chunk - 1, 1),)
            after[chunk, len(steps)] = ((chunk - 1, len(steps) + 1),)
        streams.append(steps + [functools.partial(unproject, chunk)])
    for chunk in range(chunks):
        steps = [functools.partial(begin_out, chunk), *scatter.calls(chunk)]
        if chunk:
            after[chunks + chunk, 0] = ((chunks + chunk - 1, 1),)
        streams.append(steps + [functools.partial(finish, chunk)])
    for which in range(len(cube_parts)):
        if which:
            after[2 * chunks + which, 0] = ((2 * chunks + which - 1, 3),)
        streams.append(
            [
                functools.partial(turn, which),
                *cube.make_wide(which, turned, wide_columns(which)),
                *cube.calls(which),
            ]
        )
    run_streams(streams, ORDERS.get(("back", size, chunks, bits)), after)
    for chunk in range(chunks):
        scatter.drain(chunk)
        gather.drain(chunk)
        for kind in range(2 if chunk >= chunks - 2 else 1):
            store(kind, chunk).wait()
    cube.drain()


def feed_back(size, bits, chunks, partial, out_weight, branch, middle, seeds, second, thins):
    own, depth = middle.shape
    rows = own // chunks
    width = out_weight.shape[0]
    low, full = jnp.bfloat16, jnp.float32
    dma = pltpu.SemaphoreType.DMA
    vmem, anywhere = pl.BlockSpec(memory_space=pltpu.VMEM), pl.BlockSpec(memory_space=pl.ANY)
    grads = [jax.ShapeDtypeStruct((thin.shape[-1], depth), low) for thin in thins]
    many = [anywhere] * len(grads)
    return pl.pallas_call(
        functools.partial(back_kernel, size, bits, chunks),
        out_shape=(
            jax.ShapeDtypeStruct((size, own, depth), low),
            jax.ShapeDtypeStruct((width // VD, size, own, VD), full),
            jax.ShapeDtypeStruct((own, depth), low),
            grads,
        ),
        in_specs=[anywhere, anywhere, anywhere, vmem] + [anywhere] * 5,
        out_specs=(anywhere, anywhere, vmem, many),
        scratch_shapes=[
            pltpu.VMEM((size, own, depth), low),
            pltpu.VMEM(out_weight.shape, low),
            pltpu.VMEM((size, own, depth), low),
            pltpu.VMEM((size + 1, own, depth), low),
            pltpu.VMEM((2, width // VD, size, rows, VD), full),
            pltpu.VMEM((size, own, depth), low),
            pltpu.VMEM((size, own, depth), low),
            pltpu.VMEM((2,) + thins[0].shape, low),
            pltpu.VMEM((thins[0].shape[-1], size * own), low),
            dma((3,)),
            dma((5,)),
            dma((2, chunks)),
            dma((size, chunks)),
            dma((size + 1, chunks)),
            dma((2, size, chunks)),
            dma((size, chunks)),
        ]
        + cube_scratch(bits, [grad.shape for grad in grads]),
        compiler_params=pltpu.CompilerParams(
            collective_id=1, has_side_effects=True, vmem_limit_bytes=VMEM_BYTES
        ),
        cost_estimate=pl.CostEstimate(
            flops=2 * size * own * depth * width, bytes_accessed=2**26, transcendentals=0
        ),
    )(partial, out_weight, branch, middle, seeds, second, *thins)


def last_kernel(
    size,
    bits,
    chunks,
    query_hbm,
    key_hbm,
    value_hbm,
    gate_hbm,
    tokens_ref,
    dmiddle_ref,
    gain_ref,
    sums_ref,
    firsts_hbm,
    dvalues_hbm,
    dgates_hbm,
    dqueries_hbm,
    dkeys_hbm,
    dtokens_ref,
    totals_ref,
    totals_hbm,
    first_part,
    first_inbox,
    line_box,
    dp_box,
    firsts,
    dvalues,
    dgates,
    dqueries,
    dkeys,
    turned,
    slice_turned,
    query_weight,
    key_weight,
    value_weight,
    gate_weight,
    load_sem,
    line_send,
    line_recv,
    dp_send,
    dp_recv,
    rs_send,
    rs_recv,
    cube_parts,
    cube_firsts,
    cube_nexts,
    cube_store,
    cube_send,
    cube_recv,
    cube_free,
):
    me = lax.axis_index("tensor")
    mine = lax.axis_index("dp")
    own = tokens_ref.shape[0]
    rows = own // chunks
    cube = CubeSum(
        bits,
        mine,
        totals_hbm,
        cube_parts,
        cube_firsts,
        cube_nexts,
        cube_store,
        cube_send,
        cube_recv,
        cube_free,
    )
    loads = [
        pltpu.make_async_copy(src, dst, load_sem.at[index])
        for index, (src, dst) in enumerate(
            (
                (dvalues_hbm, dvalues),
                (firsts_hbm, firsts),
                (dgates_hbm, dgates),
                (dqueries_hbm, dqueries),
                (dkeys_hbm, dkeys),
                (query_hbm, query_weight),
                (key_hbm, key_weight),
                (value_hbm, value_weight),
                (gate_hbm, gate_weight),
            )
        )
    ]
    for load in loads:
        load.start()
    groups = 2**bits
    peers = [{"dp": (mine + step) % groups} for step in range(1, groups)]
    others = [{"tensor": (me + step) % size} for step in range(1, size)]
    enter(peers + others, None)
    first = LineScatter(size, me, rows, first_part, first_inbox, rs_send, rs_recv)

    def back(chunk):
        first.arrive(chunk)

        def body(block):
            here = pl.ds(chunk * rows + block.start, block.size)
            values = tokens_ref[here, :].astype(jnp.float32)
            centered = values - jnp.mean(values, axis=-1, keepdims=True)
            scale = lax.rsqrt(jnp.mean(centered * centered, axis=-1, keepdims=True) + EPS)
            normed = centered * scale
            grad = first.total(here)
            shaped = grad * gain_ref[...]
            line_box[me, 2:3, :] += jnp.sum(grad * normed, axis=0, keepdims=True)
            line_box[me, 3:4, :] += jnp.sum(grad, axis=0, keepdims=True)
            dtokens_ref[here, :] = dmiddle_ref[here, :] + scale * (
                shaped
                - jnp.mean(shaped, axis=-1, keepdims=True)
                - normed * jnp.mean(shaped * normed, axis=-1, keepdims=True)
            )

        for_rows(rows, body)

    def line_copy(step, slot):
        return pltpu.make_async_remote_copy(
            src_ref=line_box.at[me],
            dst_ref=line_box.at[slot],
            send_sem=line_send.at[step],
            recv_sem=line_recv.at[slot],
            device_id={"tensor": (me + step) % size},
            device_id_type=MESH,
        )

    def dp_copy(step, slot):
        return pltpu.make_async_remote_copy(
            src_ref=dp_box.at[mine],
            dst_ref=dp_box.at[slot],
            send_sem=dp_send.at[step],
            recv_sem=dp_recv.at[slot],
            device_id={"dp": (mine + step) % groups},
            device_id_type=MESH,
        )

    def sums_on_line():
        for step in range(1, size):
            line_copy(step, me).start()

    def sums_on_dp():
        for step in range(1, size):
            line_copy(step, (me + step) % size).wait_recv()
        dp_box[mine] = jnp.sum(line_box[...], axis=0)
        for step in range(1, groups):
            dp_copy(step, mine).start()

    def sums_done():
        for step in range(1, groups):
            dp_copy(step, (mine + step) % groups).wait_recv()
        totals_ref[...] = jnp.sum(dp_box[...], axis=0)

    line_box[me] = sums_ref[...]
    waited = set()

    def need(*indices):
        for index in indices:
            if index not in waited:
                waited.add(index)
                loads[index].wait()

    def combine(chunk):
        need(0, 2, 3, 4, 5, 6, 7, 8)
        at = pl.ds(chunk * rows, rows)

        def flat(ref):
            return ref[:, at, :].reshape(size * rows, ref.shape[-1])

        def body(start, width):
            columns = pl.ds(start, width)
            total = dot_nt(flat(dqueries), query_weight[columns, :])
            total = total + dot_nt(flat(dkeys), key_weight[columns, :])
            total = total + dot_nn(flat(dvalues), value_weight[:, columns])
            total = total + dot_nn(flat(dgates), gate_weight[:, columns])
            first_part[:, at, columns] = total.astype(jnp.bfloat16).reshape(size, rows, width)

        for_columns(first_part.shape[-1], body)
        first.begin(chunk)

    def turn(which):
        need(*((0, 1), (2,))[which])
        ref = (dvalues, dgates)[which]
        for owner in range(size):
            turned[:, pl.ds(owner * own, own)] = ref[owner].T

    def first_columns(columns):
        return firsts[:, :, columns].reshape(size * own, columns.size)

    def make_tall(start):
        need(1, 3, 4)
        lines = cube_parts[2].shape[-2]
        for index in range(start, start + groups // 4):
            lead = tuple((index >> bit) & 1 for bit in range(bits - 1, -1, -1))
            for owner in range(size):
                piece = firsts[owner, :, pl.ds(index * lines, lines)]
                slice_turned[:, pl.ds(owner * own, own)] = piece.T
            for which, ref in ((2, dqueries), (3, dkeys)):
                value = dot_nn(slice_turned[...], ref[...].reshape(size * own, ref.shape[-1]))
                cube_parts[which][lead] = value.astype(jnp.bfloat16)

    streams = []
    for chunk in range(chunks):
        streams.append(
            [
                functools.partial(combine, chunk),
                *first.calls(chunk),
                functools.partial(back, chunk),
            ]
        )
    after = {(chunks + 4, 0): [(chunk, 2 * size - 2) for chunk in range(chunks)]}
    for which in range(2):
        if which:
            after[chunks + which, 0] = ((chunks + which - 1, 3),)
        streams.append(
            [
                functools.partial(turn, which),
                *cube.make_wide(which, turned, first_columns),
                *cube.calls(which),
            ]
        )
    quarters = [functools.partial(make_tall, quarter * (groups // 4)) for quarter in range(4)]
    after[chunks + 2, 0] = ((chunks, 1),)
    after[chunks + 3, 0] = ((chunks + 2, 4),)
    streams.append([*quarters, *cube.calls(2)])
    streams.append(cube.calls(3))
    streams.append([sums_on_line, sums_on_dp, sums_done])
    run_streams(streams, ORDERS.get(("last", size, chunks, bits)), after)
    for chunk in range(chunks):
        first.drain(chunk)
    for step in range(1, size):
        line_copy(step, me).wait_send()
    for step in range(1, groups):
        dp_copy(step, mine).wait_send()
    cube.drain()


def last_sums(size, bits, chunks, weights, tokens, dmiddle, gain, sums, firsts, parts):
    own, depth = tokens.shape
    low, full = jnp.bfloat16, jnp.float32
    dma = pltpu.SemaphoreType.DMA
    vmem, anywhere = pl.BlockSpec(memory_space=pltpu.VMEM), pl.BlockSpec(memory_space=pl.ANY)
    grads = [
        jax.ShapeDtypeStruct((part.shape[-1], depth) if place < 2 else (depth, part.shape[-1]), low)
        for place, part in enumerate(parts)
    ]
    many = [anywhere] * len(grads)
    group = size * own
    return pl.pallas_call(
        functools.partial(last_kernel, size, bits, chunks),
        out_shape=(
            jax.ShapeDtypeStruct((own, depth), full),
            jax.ShapeDtypeStruct((8, depth), full),
            grads,
        ),
        in_specs=[anywhere] * 4 + [vmem] * 4 + [anywhere] * 5,
        out_specs=(vmem, vmem, many),
        scratch_shapes=[
            pltpu.VMEM((size, own, depth), low),
            pltpu.VMEM((size + 1, own, depth), low),
            pltpu.VMEM((size, 8, depth), full),
            pltpu.VMEM((2**bits, 8, depth), full),
            pltpu.VMEM(firsts.shape, low),
            *[pltpu.VMEM(part.shape, low) for part in parts],
            pltpu.VMEM((parts[0].shape[-1], group), low),
            pltpu.VMEM((depth // 2**bits, group), low),
            *[pltpu.VMEM(weight.shape, low) for weight in weights],
            dma((9,)),
            dma((size,)),
            dma((size,)),
            dma((2**bits,)),
            dma((2**bits,)),
            dma((size, chunks)),
            dma((size + 1, chunks)),
        ]
        + cube_scratch(bits, [grad.shape for grad in grads]),
        compiler_params=pltpu.CompilerParams(
            collective_id=2, has_side_effects=True, vmem_limit_bytes=VMEM_BYTES
        ),
        cost_estimate=pl.CostEstimate(flops=2**30, bytes_accessed=2**26, transcendentals=0),
    )(*weights, tokens, dmiddle, gain, sums, firsts, *parts)


def decay_rows(rate, column, row, first):
    shape = (column.shape[0], row.shape[1])
    here = first + lax.broadcasted_iota(jnp.int32, shape, 0)
    offset = here - lax.broadcasted_iota(jnp.int32, shape, 1)
    inside = (column == row) & (offset >= 0)
    distance = jnp.maximum(offset, 0).astype(jnp.float32)
    decay = jnp.where(inside, jnp.exp(-rate * distance), 0.0)
    return decay * lax.rsqrt(jnp.sum(decay, axis=-1, keepdims=True))


def group_parts(values):
    centered = values - jnp.mean(values, axis=-1, keepdims=True)
    scale = lax.rsqrt(jnp.mean(centered * centered, axis=-1, keepdims=True) + GROUP_EPS)
    return centered * scale, scale


def sigmoid(values):
    return 1.0 / (1.0 + jnp.exp(-values))


def first_kernel(
    size,
    chunks,
    heads,
    tokens_ref,
    seed_hbm,
    gain_ref,
    bias_ref,
    column_ref,
    row_ref,
    rates_ref,
    query_hbm,
    key_hbm,
    value_hbm,
    gate_hbm,
    first_hbm,
    queries_hbm,
    keys_hbm,
    values_hbm,
    gates_hbm,
    retained_hbm,
    mixed_hbm,
    table_hbm,
    seeds_hbm,
    query_weight,
    key_weight,
    value_weight,
    gate_weight,
    first,
    queries,
    keys,
    values,
    gates,
    retained,
    mixed,
    table,
    seeds,
    raw,
    retain,
    load_sem,
    store_sem,
    done_sem,
    ag_send,
    ag_recv,
    seed_send,
    seed_recv,
):
    me = lax.axis_index("tensor")
    own, depth = tokens_ref.shape
    rows = own // chunks
    pairs = (
        (query_hbm, query_weight),
        (key_hbm, key_weight),
        (value_hbm, value_weight),
        (gate_hbm, gate_weight),
        (seed_hbm.at[pl.ds(0, rows)], seeds.at[me]),
    )
    loads = [
        pltpu.make_async_copy(src, dst, load_sem.at[index])
        for index, (src, dst) in enumerate(pairs)
    ]
    for load in loads:
        load.start()
    enter((), (size, me))
    gather = LineGather(size, me, rows, first, ag_send, ag_recv)
    gather_seed = LineGather(size, me, rows, seeds, seed_send, seed_recv)
    waited = set()

    def need(index):
        if index not in waited:
            waited.add(index)
            loads[index].wait()

    def at(chunk):
        return pl.ds(chunk * rows, rows)

    def flat(chunk):
        return first[:, at(chunk), :].reshape(size * rows, depth)

    def store(kind, block):
        src, dst = (
            (queries, queries_hbm),
            (keys, keys_hbm),
            (first, first_hbm),
            (mixed, mixed_hbm),
        )[kind]
        return pltpu.make_async_copy(src.at[block], dst.at[block], store_sem.at[kind, block])

    def store_head(kind, head, block):
        src, dst = (
            (values, values_hbm),
            (gates, gates_hbm),
            (retained, retained_hbm),
            (table, table_hbm),
        )[kind]
        return pltpu.make_async_copy(
            src.at[head, block], dst.at[head, block], done_sem.at[kind, head, block]
        )

    def normalize(chunk):
        def body(block):
            here = pl.ds(chunk * rows + block.start, block.size)
            tokens = tokens_ref[here, :].astype(jnp.float32)
            centered = tokens - jnp.mean(tokens, axis=-1, keepdims=True)
            scale = lax.rsqrt(jnp.mean(centered * centered, axis=-1, keepdims=True) + EPS)
            value = centered * scale * gain_ref[...] + bias_ref[...]
            first[me, here, :] = value.astype(jnp.bfloat16)

        for_rows(rows, body)
        gather.begin(chunk)

    def project_pair(chunk):
        need(0)
        need(1)

        def body(start, width):
            columns = pl.ds(start, width)
            value = dot_nn(flat(chunk), query_weight[:, columns])
            queries[:, at(chunk), columns] = value.astype(jnp.bfloat16).reshape(size, rows, width)
            value = dot_nn(flat(chunk), key_weight[:, columns])
            keys[:, at(chunk), columns] = value.astype(jnp.bfloat16).reshape(size, rows, width)

        for_columns(heads * KD, body)

    def project_value(chunk, head):
        need(2)

        def body(start, width):
            weight = value_weight[pl.ds(head * VD + start, width), :]
            value = dot_nt(flat(chunk), weight).astype(jnp.bfloat16)
            values[head, :, at(chunk), pl.ds(start, width)] = value.reshape(size, rows, width)

        for_columns(VD, body)

    def project_gate(chunk, head):
        need(3)

        def body(start, width):
            weight = gate_weight[pl.ds(head * VD + start, width), :]
            value = dot_nt(flat(chunk), weight)
            gates[head, :, at(chunk), pl.ds(start, width)] = value.reshape(size, rows, width)

        for_columns(VD, body)

    def tabulate(head, block):
        seen = (block + 1) * own

        def body(part):
            there = pl.ds(block * own + part.start, part.size)
            table[head, block, part, :seen] = decay_rows(
                rates_ref[head], column_ref[there, :], row_ref[:, :seen], block * own + part.start
            )

        for_rows(own, body, WHOLE)
        store_head(3, head, block).start()

    def attend(head, block):
        seen = (block + 1) * own
        lanes = pl.ds(head * KD, KD)
        query = queries[block, :, lanes]
        raw[:, :seen] = dot_nt(query, keys[: block + 1, :, lanes].reshape(seen, KD))

        def body(part):
            weighted = raw[part, :seen] * (KD**-0.5) * table[head, block, part, :seen]
            total = jnp.sum(weighted, axis=-1, keepdims=True)
            retain[part, :seen] = (weighted * lax.rsqrt(total * total + 1.0)).astype(jnp.bfloat16)

        for_rows(own, body, WHOLE)
        value = values[head, : block + 1].reshape(seen, VD)
        retained[head, block] = dot_nn(retain[:, :seen], value)

        def body_mix(part):
            normed, _ = group_parts(retained[head, block, part, :])
            gate = gates[head, block, part, :]
            value = (gate * sigmoid(gate) * normed).astype(jnp.bfloat16)
            mixed[block, part, pl.ds(head * VD, VD)] = value

        for_rows(own, body_mix, WHOLE)
        store_head(2, head, block).start()
        if head == heads - 1:
            store(3, block).start()

    def flush():
        for block in range(size):
            for kind in range(3):
                store(kind, block).start()
            for head in range(heads):
                for kind in range(2):
                    store_head(kind, head, block).start()

    def begin_seed():
        need(4)
        gather_seed.begin(0)

    places = [(head, block) for head in range(heads) for block in range(size)]
    streams, after = [], {}
    for chunk in range(chunks):
        steps = [functools.partial(normalize, chunk), *gather.calls(chunk)]
        if chunk:
            after[chunk, 0] = ((chunk - 1, 1),)
        steps.append(functools.partial(project_pair, chunk))
        for head in range(heads):
            steps.append(functools.partial(project_value, chunk, head))
            steps.append(functools.partial(project_gate, chunk, head))
        streams.append(steps)
    streams.append([functools.partial(tabulate, *place) for place in places])
    streams.append([flush] + [functools.partial(attend, *place) for place in places])
    after[chunks + 1, 0] = [(chunk, len(streams[chunk])) for chunk in range(chunks)]
    for index in range(len(places)):
        after[chunks + 1, index + 1] = ((chunks, index + 1),)
    streams.append([begin_seed, *gather_seed.calls(0)])
    run_streams(streams, ORDERS.get(("first", size, chunks, heads)), after)
    store_seeds = pltpu.make_async_copy(seeds, seeds_hbm, load_sem.at[5])
    store_seeds.start()
    gather_seed.drain(0)
    store_seeds.wait()
    for chunk in range(chunks):
        gather.drain(chunk)
    for block in range(size):
        for kind in range(4):
            store(kind, block).wait()
        for head in range(heads):
            for kind in range(4):
                store_head(kind, head, block).wait()


def first_part(size, chunks, tokens, seed, gain, bias, segments, rates, query, key, value, gate):
    own, depth = tokens.shape
    heads = query.shape[1] // KD
    rows = size * own
    low, full = jnp.bfloat16, jnp.float32
    dma = pltpu.SemaphoreType.DMA
    vmem, anywhere = pl.BlockSpec(memory_space=pltpu.VMEM), pl.BlockSpec(memory_space=pl.ANY)
    shapes = (
        ((size, own, depth), low),
        ((size, own, heads * KD), low),
        ((size, own, heads * KD), low),
        ((heads, size, own, VD), low),
        ((heads, size, own, VD), full),
        ((heads, size, own, VD), full),
        ((size, own, heads * VD), low),
        ((heads, size, own, rows), full),
        ((size, own // chunks, depth), low),
    )
    return pl.pallas_call(
        functools.partial(first_kernel, size, chunks, heads),
        out_shape=tuple(jax.ShapeDtypeStruct(*item) for item in shapes),
        in_specs=[vmem, anywhere] + [vmem] * 4 + [pl.BlockSpec(memory_space=pltpu.SMEM)] + [anywhere] * 4,
        out_specs=(anywhere,) * 9,
        scratch_shapes=[pltpu.VMEM(item.shape, low) for item in (query, key, value, gate)]
        + [pltpu.VMEM(*item) for item in shapes]
        + [
            pltpu.VMEM((own, rows), full),
            pltpu.VMEM((own, rows), low),
            dma((6,)),
            dma((4, size)),
            dma((4, heads, size)),
            dma((2, size, chunks)),
            dma((size, chunks)),
            dma((2, size, 1)),
            dma((size, 1)),
        ],
        compiler_params=pltpu.CompilerParams(
            collective_id=3, has_side_effects=True, vmem_limit_bytes=VMEM_BYTES
        ),
        cost_estimate=pl.CostEstimate(flops=2**33, bytes_accessed=2**26, transcendentals=0),
    )(
        tokens,
        seed,
        gain,
        bias,
        segments.reshape(rows, 1),
        segments.reshape(1, rows),
        rates,
        query,
        key,
        value,
        gate,
    )


def retain_kernel(
    size,
    bits,
    heads,
    queries_hbm,
    keys_hbm,
    values_hbm,
    gates_hbm,
    retained_hbm,
    dmixed_hbm,
    table_hbm,
    mixed_hbm,
    branch_hbm,
    dqueries_hbm,
    dkeys_hbm,
    dvalues_hbm,
    dgates_hbm,
    totals_hbm,
    queries,
    keys,
    values,
    gates,
    retained,
    dmixed,
    table,
    mixed,
    branch,
    dqueries,
    dkeys,
    dvalues,
    dgates,
    turned,
    raw,
    grad,
    retain,
    dscores,
    dretained,
    dkey_sum,
    dvalue_sum,
    load_sem,
    block_sem,
    store_sem,
    cube_parts,
    cube_firsts,
    cube_nexts,
    cube_store,
    cube_send,
    cube_recv,
    cube_free,
):
    own = queries.shape[1]

    def load_whole(kind):
        src, dst = (
            (queries_hbm, queries),
            (keys_hbm, keys),
            (mixed_hbm, mixed),
            (branch_hbm, branch),
        )[kind]
        return pltpu.make_async_copy(src, dst, load_sem.at[kind])

    def load_block(kind, head, block):
        slot = (head * size + block) % 2
        src, dst = (
            (values_hbm, values.at[head, block]),
            (gates_hbm, gates.at[slot]),
            (retained_hbm, retained.at[slot]),
            (dmixed_hbm, dmixed.at[slot]),
            (table_hbm, table.at[slot]),
        )[kind]
        return pltpu.make_async_copy(src.at[head, block], dst, block_sem.at[kind, head, block])

    def load_blocks(place):
        if place < heads * size:
            for kind in range(5):
                load_block(kind, place // size, place % size).start()

    def store(kind, block):
        src, dst = (
            (dqueries, dqueries_hbm),
            (dkeys, dkeys_hbm),
            (dvalues, dvalues_hbm),
            (dgates, dgates_hbm),
        )[kind]
        return pltpu.make_async_copy(src.at[block], dst.at[block], store_sem.at[kind, block])

    for kind in range(2):
        load_whole(kind).start()
    load_blocks(0)
    for kind in range(2, 4):
        load_whole(kind).start()
    load_blocks(1)
    cube = CubeSum(
        bits,
        lax.axis_index("dp"),
        totals_hbm,
        cube_parts,
        cube_firsts,
        cube_nexts,
        cube_store,
        cube_send,
        cube_recv,
        cube_free,
    )
    enter([{"dp": cube.partner(bit)} for bit in range(bits)], None)

    def attend(head, block):
        seen = (block + 1) * own
        slot = (head * size + block) % 2
        if head == 0 and block == 0:
            for kind in range(2):
                load_whole(kind).wait()
        lanes = pl.ds(head * KD, KD)

        for kind in range(5):
            load_block(kind, head, block).wait()

        def body_mix(part):
            normed, scale = group_parts(retained[slot, part, :])
            gate = gates[slot, part, :]
            dmix = dmixed[slot, part, :]
            half = sigmoid(gate)
            dgate = dmix * normed * (half * (1.0 + gate * (1.0 - half)))
            dgates[block, part, pl.ds(head * VD, VD)] = dgate.astype(jnp.bfloat16)
            dnormed = dmix * (gate * half)
            value = scale * (
                dnormed
                - jnp.mean(dnormed, axis=-1, keepdims=True)
                - normed * jnp.mean(dnormed * normed, axis=-1, keepdims=True)
            )
            dretained[part, :] = value.astype(jnp.bfloat16)

        for_rows(own, body_mix, WHOLE)
        query = queries[block, :, lanes]
        key = keys[: block + 1, :, lanes].reshape(seen, KD)
        raw[:, :seen] = dot_nt(query, key)
        value = values[head, : block + 1].reshape(seen, VD)
        grad[:, :seen] = dot_nt(dretained[...], value)

        def body(part):
            decay = table[slot, part, :seen]
            weighted = raw[part, :seen] * (KD**-0.5) * decay
            dretain = grad[part, :seen]
            total = jnp.sum(weighted, axis=-1, keepdims=True)
            along = jnp.sum(dretain * weighted, axis=-1, keepdims=True)
            inverse = lax.rsqrt(total * total + 1.0)
            retain[part, :seen] = (weighted * inverse).astype(jnp.bfloat16)
            along = along * total * inverse * inverse
            dscores[part, :seen] = (decay * inverse * (dretain - along)).astype(jnp.bfloat16)

        for_rows(own, body, WHOLE)
        dquery = dot_nn(dscores[:, :seen], key) * (KD**-0.5)
        dqueries[block, :, lanes] = dquery.astype(jnp.bfloat16)
        for other in range(block + 1):
            there = pl.ds(other * own, own)
            dkey = dot_tn(dscores[:, there], query)
            dvalue = dot_tn(retain[:, there], dretained[...])
            if other == block:
                dkey_sum[other] = dkey
                dvalue_sum[other] = dvalue
            else:
                dkey_sum[other] += dkey
                dvalue_sum[other] += dvalue

        load_blocks(head * size + block + 2)
        if block == size - 1:
            for other in range(size):
                dkeys[other, :, lanes] = (dkey_sum[other] * (KD**-0.5)).astype(jnp.bfloat16)
                there = pl.ds(head * VD, VD)
                dvalues[other, :, there] = dvalue_sum[other].astype(jnp.bfloat16)
                if head == heads - 1:
                    for kind in range(4):
                        store(kind, other).start()

    def turn():
        for kind in range(2, 4):
            load_whole(kind).wait()
        for owner in range(size):
            turned[:, pl.ds(owner * own, own)] = mixed[owner].T

    def branch_columns(columns):
        return branch[:, :, columns].reshape(size * own, columns.size)

    steps = [
        functools.partial(attend, head, block) for head in range(heads) for block in range(size)
    ]
    sums = [turn, *cube.make_wide(0, turned, branch_columns), *cube.calls(0)]
    run_streams([sums, steps], ORDERS.get(("retain", size, bits, heads)), {})
    for block in range(size):
        for kind in range(4):
            store(kind, block).wait()
    cube.drain()


def retain_back(
    size, bits, queries, keys, values, gates, retained, dmixed, table, mixed, branch
):
    own = queries.shape[1]
    heads = values.shape[0]
    rows, depth = size * own, branch.shape[-1]
    low, full = jnp.bfloat16, jnp.float32
    dma = pltpu.SemaphoreType.DMA
    anywhere = pl.BlockSpec(memory_space=pl.ANY)
    inputs = (queries, keys, values, gates, retained, dmixed, table, mixed, branch)
    slots = [
        jax.ShapeDtypeStruct((2,) + item.shape[2:], item.dtype) if 3 <= place < 7 else item
        for place, item in enumerate(inputs)
    ]
    total = jax.ShapeDtypeStruct((heads * VD, depth), low)
    shapes = (
        queries.shape,
        keys.shape,
        (size, own, heads * VD),
        (size, own, heads * VD),
    )
    return pl.pallas_call(
        functools.partial(retain_kernel, size, bits, heads),
        out_shape=tuple(jax.ShapeDtypeStruct(shape, low) for shape in shapes) + ([total],),
        in_specs=[anywhere] * len(inputs),
        out_specs=(anywhere,) * 4 + ([anywhere],),
        scratch_shapes=[pltpu.VMEM(item.shape, item.dtype) for item in slots]
        + [pltpu.VMEM(shape, low) for shape in shapes]
        + [
            pltpu.VMEM((heads * VD, rows), low),
            pltpu.VMEM((own, rows), full),
            pltpu.VMEM((own, rows), full),
            pltpu.VMEM((own, rows), low),
            pltpu.VMEM((own, rows), low),
            pltpu.VMEM((own, VD), low),
            pltpu.VMEM((size, own, KD), full),
            pltpu.VMEM((size, own, VD), full),
            dma((4,)),
            dma((5, heads, size)),
            dma((4, size)),
        ]
        + cube_scratch(bits, [total.shape]),
        compiler_params=pltpu.CompilerParams(
            collective_id=4, has_side_effects=True, vmem_limit_bytes=VMEM_BYTES
        ),
        cost_estimate=pl.CostEstimate(flops=2**34, bytes_accessed=2**26, transcendentals=0),
    )(*inputs)


def cast_kernel(count, *refs):
    for src, dst in zip(refs[:count], refs[count:]):
        dst[...] = src[...].astype(jnp.float32)


def cast_all(items):
    specs = []
    for item in items:
        blocks = 9 if item.shape[0] % (9 * LINE) == 0 else 8
        specs.append(
            pl.BlockSpec(
                (item.shape[0] // blocks, item.shape[1]),
                lambda step, last=blocks - 1: (jnp.minimum(step, last), 0),
            )
        )
    return pl.pallas_call(
        functools.partial(cast_kernel, len(items)),
        out_shape=[jax.ShapeDtypeStruct(item.shape, jnp.float32) for item in items],
        grid=(9,),
        in_specs=specs,
        out_specs=specs,
        compiler_params=pltpu.CompilerParams(vmem_limit_bytes=VMEM_BYTES),
    )(*items)


def per_device(
    tokens,
    first_gain,
    first_bias,
    query_weight,
    key_weight,
    value_weight,
    gate_weight,
    out_weight,
    second_gain,
    second_bias,
    hidden_gate,
    hidden_up,
    hidden_down,
    segments,
    cotangent,
):
    size = lax.axis_size("tensor")
    group_rows = segments.size
    head_local = query_weight.shape[1] // KD
    head_index = (lax.axis_index("tensor") * head_local + jnp.arange(head_local)).astype(
        jnp.float32
    )
    rates = -jnp.log1p(-jnp.exp2(-5.0 - head_index))
    first_all, queries, keys, values, gates, retained, mixed, table, seed_first = first_part(
        size,
        CHUNKS,
        tokens,
        cotangent,
        first_gain[None],
        first_bias[None],
        segments,
        rates,
        query_weight,
        key_weight,
        value_weight.T,
        gate_weight.T,
    )
    bits = lax.axis_size("dp").bit_length() - 1
    own = tokens.shape[0]
    (
        second_all,
        seed_all,
        inner,
        gate_in_low,
        lin_in_low,
        partial,
        middle,
        grad_middle,
        branch,
        second_sums,
    ) = feed_forward(
        size,
        CHUNKS,
        mixed,
        out_weight,
        tokens,
        cotangent,
        seed_first,
        hidden_gate.T,
        hidden_up.T,
        hidden_down,
        second_gain[None],
        second_bias[None],
    )

    branch_all, grad_mixed, output, feed_grads = feed_back(
        size,
        bits,
        CHUNKS,
        partial,
        out_weight,
        branch,
        middle,
        seed_all,
        second_all,
        (inner, gate_in_low, lin_in_low),
    )
    grad_queries, grad_keys, grad_values, grad_gates, (grad_outw,) = retain_back(
        size,
        bits,
        queries,
        keys,
        values,
        gates,
        retained,
        grad_mixed,
        table,
        mixed,
        branch_all,
    )
    grad_tokens, sums, grads = last_sums(
        size,
        bits,
        CHUNKS,
        (query_weight, key_weight, value_weight.T, gate_weight.T),
        tokens,
        grad_middle,
        first_gain[None],
        second_sums,
        first_all,
        (grad_values, grad_gates, grad_queries, grad_keys),
    )
    grad_sgain, grad_sbias, grad_fgain, grad_fbias = sums[0], sums[1], sums[2], sums[3]
    (
        grad_outw,
        grad_valuew,
        grad_gatew,
        grad_queryw,
        grad_keyw,
        grad_hdown,
        grad_hgate,
        grad_hup,
    ) = cast_all([grad_outw, *grads, *feed_grads])
    grad_valuew, grad_gatew, grad_hgate, grad_hup = (
        item.T for item in (grad_valuew, grad_gatew, grad_hgate, grad_hup)
    )
    return (
        output,
        grad_tokens,
        grad_fgain,
        grad_fbias,
        grad_queryw,
        grad_keyw,
        grad_valuew,
        grad_gatew,
        grad_outw,
        grad_sgain,
        grad_sbias,
        grad_hgate,
        grad_hup,
        grad_hdown,
    )


def solution(mesh):
    return jax.shard_map(
        per_device,
        mesh=mesh,
        in_specs=(
            P(("dp", "tensor"), None),
            P(),
            P(),
            P(None, "tensor"),
            P(None, "tensor"),
            P(None, "tensor"),
            P(None, "tensor"),
            P("tensor", None),
            P(),
            P(),
            P(None, "tensor"),
            P(None, "tensor"),
            P("tensor", None),
            P("dp", None),
            P(("dp", "tensor"), None),
        ),
        out_specs=(
            P(("dp", "tensor"), None),
            P(("dp", "tensor"), None),
            P(),
            P(),
            P(None, "tensor"),
            P(None, "tensor"),
            P(None, "tensor"),
            P(None, "tensor"),
            P("tensor", None),
            P(),
            P(),
            P(None, "tensor"),
            P(None, "tensor"),
            P("tensor", None),
        ),
        check_vma=False,
    )
```

```python
import functools
import itertools

import jax
import jax.numpy as jnp
from jax import lax
from jax.experimental import pallas as pl
from jax.experimental.pallas import tpu as pltpu
from jax.sharding import PartitionSpec as P

KD = 256
VD = 432


EPS = 1e-05
GROUP_EPS = 0.1
GELU_SCALE = 0.7978845608028654
CHUNKS = 4

MESH = pl.DeviceIdType.MESH
VMEM_BYTES = 60 * 2**20
TILE = 1024
LINE = 16
BAND = 64
ACT = 64
WHOLE = 256
BLOCKS = (1, 8, 9, 16, 18)


def for_columns(width, body):
    full = width // TILE

    def step(index, carry):
        body(pl.multiple_of(index * TILE, TILE), TILE)
        return carry

    if full:
        lax.fori_loop(0, full, step, 0)
    if width % TILE:
        body(full * TILE, width % TILE)


def for_rows(count, body, size=None):
    size = min(count, size or BAND)

    def step(index, carry):
        body(pl.ds(pl.multiple_of(index * size, LINE), size))
        return carry

    lax.fori_loop(0, count // size, step, 0)


def dot_nn(left, right):
    return lax.dot_general(left, right, (((1,), (0,)), ((), ())), preferred_element_type=jnp.float32)


def dot_nt(left, right):
    return lax.dot_general(left, right, (((1,), (1,)), ((), ())), preferred_element_type=jnp.float32)


def dot_tn(left, right):
    return lax.dot_general(left, right, (((0,), (0,)), ((), ())), preferred_element_type=jnp.float32)


def enter(peers, line):
    barrier = pltpu.get_barrier_semaphore()
    for peer in peers:
        pl.semaphore_signal(barrier, inc=1, device_id=peer, device_id_type=MESH)
    if line is not None:
        size, me = line

        @pl.when(me > 0)
        def _():
            pl.semaphore_signal(barrier, inc=1, device_id={"tensor": me - 1}, device_id_type=MESH)

        @pl.when(me < size - 1)
        def _():
            pl.semaphore_signal(barrier, inc=1, device_id={"tensor": me + 1}, device_id_type=MESH)

    count = len(peers)
    if line is not None:
        count = count + (me > 0).astype(jnp.int32) + (me < size - 1).astype(jnp.int32)
    pl.semaphore_wait(barrier, count)


class LineScatter:
    def __init__(self, size, me, rows, part, inbox, send, recv):
        self.size, self.me, self.rows = size, me, rows
        self.part, self.inbox, self.send, self.recv = part, inbox, send, recv

    def at(self, chunk):
        return pl.ds(chunk * self.rows, self.rows)

    def copy(self, target, slot, chunk, device):
        return pltpu.make_async_remote_copy(
            src_ref=self.part.at[target, self.at(chunk)],
            dst_ref=self.inbox.at[slot, self.at(chunk)],
            send_sem=self.send.at[target, chunk],
            recv_sem=self.recv.at[slot, chunk],
            device_id={"tensor": device},
            device_id_type=MESH,
        )

    def add(self, target, chunk):
        def body(rows):
            at = pl.ds(chunk * self.rows + rows.start, rows.size)
            total = self.part[target, at, :].astype(jnp.float32)
            total = total + self.inbox[target, at, :].astype(jnp.float32)
            self.part[target, at, :] = total.astype(jnp.bfloat16)

        for_rows(self.rows, body)

    def go_right(self, chunk, target):
        self.copy(target, target, chunk, self.me + 1).start()

    def go_left(self, chunk, target):
        last = self.me - 1 == target
        self.copy(target, jnp.where(last, self.size, target), chunk, self.me - 1).start()

    def begin(self, chunk):
        @pl.when(self.me == 0)
        def _():
            for target in range(self.size - 1, 0, -1):
                self.go_right(chunk, target)

        @pl.when(self.me == self.size - 1)
        def _():
            for target in range(self.size - 1):
                self.go_left(chunk, target)

    def right(self, chunk, target):
        @pl.when((self.me < target) & (self.me > 0))
        def _():
            self.copy(target, target, chunk, self.me).wait_recv()
            self.add(target, chunk)
            self.go_right(chunk, target)

    def left(self, chunk, target):
        @pl.when((self.me > target) & (self.me < self.size - 1))
        def _():
            self.copy(target, target, chunk, self.me).wait_recv()
            self.add(target, chunk)
            self.go_left(chunk, target)

    def calls(self, chunk):
        for step in range(self.size - 1):
            if step < self.size - 2:
                yield functools.partial(self.right, chunk, self.size - 1 - step)
                yield functools.partial(self.left, chunk, step)

    def arrive(self, chunk):
        size, me = self.size, self.me

        @pl.when(me > 0)
        def _():
            self.copy(me, me, chunk, me - 1).wait_recv()

        @pl.when(me < size - 1)
        def _():
            self.copy(me, size, chunk, me + 1).wait_recv()

    def total(self, rows):
        size, me = self.size, self.me
        own = self.part[me, rows, :].astype(jnp.float32)
        low = self.inbox[me, rows, :].astype(jnp.float32)
        high = self.inbox[size, rows, :].astype(jnp.float32)
        return own + jnp.where(me > 0, low, 0.0) + jnp.where(me < size - 1, high, 0.0)

    def drain(self, chunk):
        for target in range(self.size):

            @pl.when(self.me != target)
            def _():
                self.copy(target, target, chunk, self.me).wait_send()


class LineGather:
    def __init__(self, size, me, rows, held, send, recv):
        self.size, self.me, self.rows = size, me, rows
        self.held, self.send, self.recv = held, send, recv

    def copy(self, block, chunk, way, device):
        at = pl.ds(chunk * self.rows, self.rows)
        return pltpu.make_async_remote_copy(
            src_ref=self.held.at[block, at],
            dst_ref=self.held.at[block, at],
            send_sem=self.send.at[way, block, chunk],
            recv_sem=self.recv.at[block, chunk],
            device_id={"tensor": device},
            device_id_type=MESH,
        )

    def begin(self, chunk):
        self.right(chunk, 0)
        self.left(chunk, 0)

    def right(self, chunk, step):
        size, me = self.size, self.me

        @pl.when(me >= step)
        def _():
            if step:
                self.copy(me - step, chunk, 0, me).wait_recv()

            @pl.when(me < size - 1)
            def _():
                self.copy(me - step, chunk, 0, me + 1).start()

    def left(self, chunk, step):
        size, me = self.size, self.me

        @pl.when(me + step < size)
        def _():
            if step:
                self.copy(me + step, chunk, 1, me).wait_recv()

            @pl.when(me > 0)
            def _():
                self.copy(me + step, chunk, 1, me - 1).start()

    def calls(self, chunk):
        for step in range(1, self.size):
            yield functools.partial(self.right, chunk, step)
            yield functools.partial(self.left, chunk, step)

    def drain(self, chunk):
        size, me = self.size, self.me
        for step in range(size):

            @pl.when((me >= step) & (me < size - 1))
            def _():
                self.copy(me - step, chunk, 0, me + 1).wait_send()

            @pl.when((me + step < size) & (me > 0))
            def _():
                self.copy(me + step, chunk, 1, me - 1).wait_send()


class CubeSum:
    def __init__(self, bits, me, results, parts, firsts, nexts, store, send, recv, free):
        self.bits, self.me = bits, me
        self.results, self.parts = results, parts
        self.firsts, self.nexts = firsts, nexts
        self.store_sem, self.send, self.recv = store, send, recv
        self.free = free
        self.orders = (tuple(range(bits)), (0,) + tuple(range(bits - 1, 0, -1)))
        self.mine = [(me // 2**bit) % 2 for bit in range(bits)]

    def partner(self, bit):
        return self.me + (1 - 2 * self.mine[bit]) * 2**bit

    def band(self, which, color):
        count = self.parts[which].shape[-2]
        cut = cut_rows(count)
        return ((0, cut), (cut, count - cut), (0, count))[color]

    def lead(self, fixed):
        return tuple(fixed.get(bit, slice(None)) for bit in range(self.bits - 1, -1, -1))

    def moved(self, src, dst, which, color, step, bit):
        return pltpu.make_async_remote_copy(
            src_ref=src,
            dst_ref=dst,
            send_sem=self.send.at[which, color % 2, step],
            recv_sem=self.recv.at[which, color % 2, step],
            device_id={"dp": self.partner(bit)},
            device_id_type=MESH,
        )

    def halve(self, which, color, step):
        order = self.orders[color % 2]
        start, count = self.band(which, color)
        fixed = {bit: self.mine[bit] for bit in order[:step]}
        fixed[order[step]] = 1 - self.mine[order[step]]
        src = self.parts[which].at[self.lead(fixed) + (pl.ds(start, count), slice(None))]
        dst = self.firsts[which] if step == 0 else self.nexts[which][color][step - 1]
        return self.moved(src, dst, which, color, step, order[step])

    def double(self, which, color, step):
        order = self.orders[color % 2]
        start, count = self.band(which, color)
        fixed = {bit: self.mine[bit] for bit in order[: step + 1]}
        held = self.parts[which].at[self.lead(fixed) + (pl.ds(start, count), slice(None))]
        return self.moved(held, held, which, color, 2 * self.bits - 1 - step, order[step])

    def freed(self, which, color, step):
        return self.free.at[which, color % 2, step]

    def land(self, which, color, step):
        copy = self.halve(which, color, step)
        copy.wait_send()
        partner = {"dp": self.partner(self.orders[color % 2][step])}
        pl.semaphore_signal(
            self.freed(which, color, step), inc=1, device_id=partner, device_id_type=MESH
        )
        copy.wait_recv()
        self.add(which, color, step)

    def grow(self, which, color, step):
        pl.semaphore_wait(self.freed(which, color, step), 1)
        self.double(which, color, step).start()

    def add(self, which, color, step):
        order = self.orders[color % 2]
        part, (start, count) = self.parts[which], self.band(which, color)
        box = self.firsts[which] if step == 0 else self.nexts[which][color][step - 1]
        fixed = {bit: self.mine[bit] for bit in order[: step + 1]}
        free = [bit for bit in range(self.bits - 1, -1, -1) if bit not in fixed]
        for choice in itertools.product((0, 1), repeat=len(free)):
            lead = self.lead({**fixed, **dict(zip(free, choice))})

            def body(begin, size):
                there = lead + (pl.ds(start + begin, size), slice(None))
                total = part[there].astype(jnp.float32)
                total = total + box[choice + (pl.ds(begin, size), slice(None))].astype(jnp.float32)
                part[there] = total.astype(jnp.bfloat16)

            for_blocks(count, part.shape[-1], body)

    def slices(self, which, ref):
        rows, columns = self.parts[which].shape[-2:]
        for index in range(2**self.bits):
            lead = tuple((index >> bit) & 1 for bit in range(self.bits - 1, -1, -1))
            if ref.shape[0] == rows:
                whole = ref.at[:, pl.ds(index * columns, columns)]
            else:
                whole = ref.at[pl.ds(index * rows, rows), :]
            yield index, self.parts[which].at[lead], whole

    def make_wide(self, which, left, right):
        columns = self.parts[which].shape[-1]
        half = 2 ** (self.bits - 1)

        def some(start):
            for index in range(start, start + half):
                lead = tuple((index >> bit) & 1 for bit in range(self.bits - 1, -1, -1))
                value = dot_nn(left[...], right(pl.ds(index * columns, columns)))
                self.parts[which][lead] = value.astype(jnp.bfloat16)

        return [functools.partial(some, 0), functools.partial(some, half)]

    def open(self, which):
        self.halve(which, 2, 0).start()

    def split(self, which):
        self.land(which, 2, 0)
        for color in range(2):
            self.halve(which, color, 1).start()

    def down(self, which, color, step):
        self.land(which, color, step - 1)
        self.halve(which, color, step).start()

    def turn(self, which, color):
        self.land(which, color, self.bits - 1)
        self.grow(which, color, self.bits - 1)

    def up(self, which, color, step):
        self.double(which, color, step + 1).wait_recv()
        self.grow(which, color, step)

    def join(self, which):
        for color in range(2):
            self.double(which, color, 1).wait_recv()
        self.grow(which, 2, 0)

    def close(self, which):
        self.double(which, 2, 0).wait_recv()
        for index, part, whole in self.slices(which, self.results[which]):
            pltpu.make_async_copy(part, whole, self.store_sem.at[which, index]).start()

    def calls(self, which):
        yield functools.partial(self.open, which)
        yield functools.partial(self.split, which)
        for step in range(2, self.bits):
            for color in range(2):
                yield functools.partial(self.down, which, color, step)
        for color in range(2):
            yield functools.partial(self.turn, which, color)
        for step in range(self.bits - 2, 0, -1):
            for color in range(2):
                yield functools.partial(self.up, which, color, step)
        yield functools.partial(self.join, which)
        yield functools.partial(self.close, which)

    def drain(self):
        for which in range(len(self.parts)):
            self.double(which, 2, 0).wait_send()
            for color in range(2):
                for step in range(1, self.bits):
                    self.double(which, color, step).wait_send()
            for index, part, whole in self.slices(which, self.results[which]):
                pltpu.make_async_copy(part, whole, self.store_sem.at[which, index]).wait()


def cut_rows(count):
    return count // (2 * LINE) * LINE


def halves(rows):
    first = rows // 2 // LINE * LINE
    return ((0, first), (first, rows - first))


def for_blocks(count, columns, body):
    lines = count // LINE
    fits = [part for part in range(1, lines + 1) if lines % part == 0 and part * LINE * columns <= 2**16]
    size = fits[-1] * LINE

    def step(index, carry):
        body(pl.multiple_of(index * size, LINE), size)
        return carry

    lax.fori_loop(0, count // size, step, 0)


def cube_scratch(bits, shapes):
    low = jnp.bfloat16
    parts, firsts, nexts = [], [], []
    for rows, columns in shapes:
        if columns >= rows:
            columns = columns // 2**bits
        else:
            rows = rows // 2**bits
        cut = cut_rows(rows)
        parts.append(pltpu.VMEM((2,) * bits + (rows, columns), low))
        firsts.append(pltpu.VMEM((2,) * (bits - 1) + (rows, columns), low))
        nexts.append(
            [
                [
                    pltpu.VMEM((2,) * (bits - 1 - step) + (count, columns), low)
                    for step in range(1, bits)
                ]
                for count in (cut, rows - cut)
            ]
        )
    dma = pltpu.SemaphoreType.DMA
    return [
        parts,
        firsts,
        nexts,
        dma((len(shapes), 2**bits)),
        dma((len(shapes), 2, 2 * bits)),
        dma((len(shapes), 2, 2 * bits)),
        pltpu.SemaphoreType.REGULAR((len(shapes), 2, bits)),
    ]


ORDERS = {
    ("first", 4, 4, 2): (
        0, 1, 0, 2, 1, 3, 4, 0, 1, 2, 0, 2, 0, 0, 4, 4, 4, 3, 0, 3, 0, 4, 0, 4,
        4, 2, 1, 2, 3, 1, 3, 6, 2, 1, 4, 1, 2, 0, 2, 2, 0, 1, 2, 1, 0, 1, 3, 3,
        3, 3, 3, 1, 3, 2, 3, 1, 2, 5, 5, 5, 6, 6, 5, 5, 5, 5, 5, 5, 6, 6, 6, 6,
    ),
    ("feed", 4, 4): (
        4, 0, 5, 1, 6, 0, 4, 5, 0, 5, 0, 0, 4, 4, 5, 1, 0, 2, 3, 5, 6, 4, 0, 1,
        6, 0, 0, 2, 0, 4, 4, 5, 0, 1, 0, 2, 1, 5, 6, 2, 2, 0, 1, 2, 3, 1, 1, 0,
        0, 0, 1, 2, 1, 1, 3, 1, 3, 3, 2, 0, 1, 1, 3, 1, 1, 1, 2, 2, 2, 2, 0, 2,
        2, 3, 2, 3, 2, 3, 2, 1, 6, 3, 3, 1, 1, 0, 2, 3, 0, 6, 0, 6, 1, 3, 3, 3,
        3, 3, 3, 2, 2, 1, 3, 3, 0, 2, 3, 2, 3,
    ),
    ("back", 4, 4, 3): (
        0, 8, 8, 8, 8, 1, 4, 9, 9, 9, 9, 0, 8, 10, 10, 5, 10, 1, 0, 2, 0, 9, 10, 10,
        1, 4, 8, 1, 8, 9, 3, 9, 5, 10, 0, 10, 2, 8, 8, 1, 3, 5, 9, 5, 9, 4, 3, 2,
        6, 1, 10, 10, 0, 8, 2, 7, 8, 9, 9, 0, 3, 6, 4, 2, 5, 0, 10, 3, 10, 1, 2, 1,
        3, 3, 4, 7, 7, 8, 7, 2, 9, 4, 6, 6, 7, 5, 8, 6, 2, 10, 7, 3, 9, 10, 6,
    ),
    ("retain", 4, 3, 2): (
        0, 0, 0, 0, 1, 1, 1, 0, 2, 1, 2, 2, 0, 0, 2, 1, 1, 0, 0, 1, 1, 0, 0, 2,
        1, 1, 2, 2, 0, 2, 1, 0, 1,
    ),
    ("last", 4, 4, 3): (
        4, 4, 4, 4, 0, 6, 6, 4, 6, 6, 7, 5, 6, 2, 7, 5, 5, 5, 4, 4, 6, 0, 7, 7,
        5, 2, 0, 0, 4, 4, 3, 6, 2, 2, 6, 5, 5, 1, 4, 2, 4, 0, 3, 7, 7, 6, 6, 5,
        5, 1, 1, 7, 7, 1, 0, 3, 5, 1, 5, 3, 7, 6, 4, 3, 7, 1, 6, 2, 3, 8, 5, 8,
        4, 6, 8, 5, 6,
    ),
}


def run_streams(streams, order, after):
    streams = [list(stream) for stream in streams]
    done = [0] * len(streams)

    def ready(stream):
        place = done[stream]
        return place < len(streams[stream]) and all(
            done[other] >= count for other, count in after.get((stream, place), ())
        )

    def take(stream):
        streams[stream][done[stream]]()
        done[stream] += 1

    if order is not None:
        for stream in order:
            assert ready(stream)
            take(stream)
    while any(done[index] < len(stream) for index, stream in enumerate(streams)):
        for stream in range(len(streams)):
            if ready(stream):
                take(stream)


def feed_kernel(
    size,
    chunks,
    mixed_hbm,
    out_hbm,
    tokens_hbm,
    seed_hbm,
    seed_first_hbm,
    gate_hbm,
    up_hbm,
    down_hbm,
    gain_ref,
    bias_ref,
    second_hbm,
    seeds_hbm,
    inner_hbm,
    dgate_hbm,
    dlin_hbm,
    outp_hbm,
    middle_ref,
    dmiddle_ref,
    branch_ref,
    sums_ref,
    mixed,
    out_weight,
    tokens,
    hidden_gate,
    hidden_up,
    hidden_down,
    second,
    seeds,
    part,
    inbox,
    gate_in,
    lin_in,
    dinner,
    inner,
    dgate,
    dlin,
    wide,
    load_sem,
    store_sem,
    rs_send,
    rs_recv,
    back_send,
    back_recv,
    ag_send,
    ag_recv,
    seed_send,
    seed_recv,
):
    me = lax.axis_index("tensor")
    own, depth = tokens.shape
    rows = own // chunks
    hidden = inner.shape[-1]
    loads = [
        pltpu.make_async_copy(src, dst, load_sem.at[index])
        for index, (src, dst) in enumerate(
            (
                (mixed_hbm, mixed),
                (out_hbm, out_weight),
                (seed_hbm.at[pl.ds(rows, own - rows)], seeds.at[me, pl.ds(rows, own - rows)]),
                (tokens_hbm, tokens),
                (gate_hbm, hidden_gate),
                (up_hbm, hidden_up),
                (down_hbm, hidden_down),
                (seed_first_hbm, seeds.at[:, pl.ds(0, rows)]),
            )
        )
    ]
    for load in loads:
        load.start()
    enter((), (size, me))
    scatter = LineScatter(size, me, rows, part, inbox, rs_send, rs_recv)
    scatter_back = LineScatter(size, me, rows, part, inbox, back_send, back_recv)
    gather = LineGather(size, me, rows, second, ag_send, ag_recv)
    gather_seed = LineGather(size, me, rows, seeds, seed_send, seed_recv)

    def at(chunk):
        return pl.ds(chunk * rows, rows)

    def flat(ref, chunk):
        value = ref[:, at(chunk), :]
        return value.reshape(size * rows, value.shape[-1])

    def store(kind, chunk):
        slot = chunk % 2
        src, dst = (
            (second.at[:, at(chunk)], second_hbm),
            (seeds.at[:, at(chunk)], seeds_hbm),
            (inner.at[slot], inner_hbm),
            (dgate.at[slot], dgate_hbm),
            (dlin.at[slot], dlin_hbm),
            (wide.at[slot], outp_hbm),
        )[kind]
        return pltpu.make_async_copy(src, dst.at[:, at(chunk)], store_sem.at[kind, chunk])

    waited = set()

    def need(*indices):
        for index in indices:
            if index not in waited:
                waited.add(index)
                loads[index].wait()

    def project(chunk):
        need(0, 1)

        def body(start, width):
            value = dot_nn(flat(mixed, chunk), out_weight[:, pl.ds(start, width)])
            part[:, at(chunk), pl.ds(start, width)] = value.astype(jnp.bfloat16).reshape(
                size, rows, width
            )

        for_columns(depth, body)
        scatter.begin(chunk)

    def normalize(chunk):
        need(3)
        scatter.arrive(chunk)

        def body(block):
            here = pl.ds(chunk * rows + block.start, block.size)
            middle = tokens[here, :].astype(jnp.float32) + scatter.total(here)
            middle_ref[here, :] = middle
            centered = middle - jnp.mean(middle, axis=-1, keepdims=True)
            scale = lax.rsqrt(jnp.mean(centered * centered, axis=-1, keepdims=True) + EPS)
            value = centered * scale * gain_ref[...] + bias_ref[...]
            second[me, here, :] = value.astype(jnp.bfloat16)

        for_rows(rows, body)
        gather.begin(chunk)

    def feed_in(chunk):
        need(4, 5)

        def body(start, width):
            columns = pl.ds(start, width)
            gate_in[:, columns] = dot_nt(flat(second, chunk), hidden_gate[columns, :])
            lin_in[:, columns] = dot_nt(flat(second, chunk), hidden_up[columns, :])

        for_columns(hidden, body)
        store(0, chunk).start()

    def feed_seed(chunk):
        need(6, 7)

        def body(start, width):
            columns = pl.ds(start, width)
            dinner[:, columns] = dot_nt(flat(seeds, chunk), hidden_down[columns, :])

        for_columns(hidden, body)
        store(1, chunk).start()

    def feed_act(chunk):
        slot = chunk % 2
        if chunk >= 2:
            for kind in range(2, 5):
                store(kind, chunk - 2).wait()

        def body(block):
            gate, lin, grad = gate_in[block, :], lin_in[block, :], dinner[block, :]
            cube = GELU_SCALE * (gate + 0.044715 * (gate * gate * gate))
            tanh = jnp.tanh(cube)
            half = 0.5 * (1.0 + tanh)
            active = gate * half
            slope = half + 0.5 * gate * (1.0 - tanh * tanh) * (
                GELU_SCALE * (1.0 + 3.0 * 0.044715 * (gate * gate))
            )
            owner = block.start // rows
            inside = pl.ds(block.start - owner * rows, block.size)
            inner[slot, owner, inside, :] = (active * lin).astype(jnp.bfloat16)
            dlin[slot, owner, inside, :] = (grad * active).astype(jnp.bfloat16)
            dgate[slot, owner, inside, :] = (grad * lin * slope).astype(jnp.bfloat16)

        for_rows(size * rows, body, min(ACT, rows))
        for kind in range(2, 5):
            store(kind, chunk).start()

    def feed_back(chunk):
        slot = chunk % 2
        scatter.drain(chunk)

        def body(start, width):
            columns = pl.ds(start, width)
            dgate_all = dgate[slot].reshape(size * rows, hidden)
            dlin_all = dlin[slot].reshape(size * rows, hidden)
            grad = dot_nn(dgate_all, hidden_gate[:, columns])
            grad = grad + dot_nn(dlin_all, hidden_up[:, columns])
            part[:, at(chunk), columns] = grad.astype(jnp.bfloat16).reshape(size, rows, width)

        for_columns(depth, body)
        scatter_back.begin(chunk)

    def feed_out(chunk):
        slot = chunk % 2
        if chunk >= 2:
            store(5, chunk - 2).wait()

        def body(start, width):
            columns = pl.ds(start, width)
            inner_all = inner[slot].reshape(size * rows, hidden)
            value = dot_nn(inner_all, hidden_down[:, columns])
            wide[slot, :, :, columns] = value.astype(jnp.bfloat16).reshape(size, rows, width)

        for_columns(depth, body)
        store(5, chunk).start()

    def normalize_back(chunk):
        scatter_back.arrive(chunk)

        def body(block):
            here = pl.ds(chunk * rows + block.start, block.size)
            middle = middle_ref[here, :]
            centered = middle - jnp.mean(middle, axis=-1, keepdims=True)
            scale = lax.rsqrt(jnp.mean(centered * centered, axis=-1, keepdims=True) + EPS)
            normed = centered * scale
            grad = scatter_back.total(here)
            shaped = grad * gain_ref[...]
            sums_ref[0:1, :] += jnp.sum(grad * normed, axis=0, keepdims=True)
            sums_ref[1:2, :] += jnp.sum(grad, axis=0, keepdims=True)
            dmiddle = seeds[me, here, :].astype(jnp.float32) + scale * (
                shaped
                - jnp.mean(shaped, axis=-1, keepdims=True)
                - normed * jnp.mean(shaped * normed, axis=-1, keepdims=True)
            )
            dmiddle_ref[here, :] = dmiddle
            branch_ref[here, :] = dmiddle.astype(jnp.bfloat16)

        for_rows(rows, body)

    def begin_seed(chunk):
        need(2)
        gather_seed.begin(chunk)

    streams, after = [], {}
    for chunk in range(chunks):
        steps = [project, *scatter.calls(chunk), normalize, *gather.calls(chunk)]
        first_feed = len(steps)
        steps += [feed_in, feed_seed, feed_act, feed_back, feed_out]
        steps += [*scatter_back.calls(chunk), normalize_back]
        streams.append(
            [step if isinstance(step, functools.partial) else functools.partial(step, chunk) for step in steps]
        )
        if chunk:
            after[chunk, first_feed] = ((chunk - 1, first_feed + 5),)
            after[chunk, first_feed + 1] = ((chunks + chunk - 1, 2 * size - 1),)
    for chunk in range(1, chunks):
        streams.append([functools.partial(begin_seed, chunk), *gather_seed.calls(chunk)])
    sums_ref[...] = jnp.zeros_like(sums_ref)
    run_streams(streams, ORDERS.get(("feed", size, chunks)), after)
    for chunk in range(chunks):
        scatter_back.drain(chunk)
        gather.drain(chunk)
        if chunk:
            gather_seed.drain(chunk)
        for kind in range(6 if chunk >= chunks - 2 else 2):
            store(kind, chunk).wait()


def feed_forward(size, chunks, mixed, out_weight, tokens, cotangent, seed_first, hidden_gate, hidden_up, hidden_down, gain, bias):
    own, depth = tokens.shape
    hidden = hidden_gate.shape[0]
    rows = own // chunks
    low, full = jnp.bfloat16, jnp.float32

    def blocks(width):
        return jax.ShapeDtypeStruct((size, own, width), low)

    dma = pltpu.SemaphoreType.DMA
    wide, thin = (size, own, depth), (2, size, rows, hidden)
    return pl.pallas_call(
        functools.partial(feed_kernel, size, chunks),
        out_shape=(
            blocks(depth),
            blocks(depth),
            blocks(hidden),
            blocks(hidden),
            blocks(hidden),
            blocks(depth),
            jax.ShapeDtypeStruct((own, depth), full),
            jax.ShapeDtypeStruct((own, depth), full),
            jax.ShapeDtypeStruct((own, depth), low),
            jax.ShapeDtypeStruct((8, depth), full),
        ),
        in_specs=[pl.BlockSpec(memory_space=pl.ANY)] * 8
        + [pl.BlockSpec(memory_space=pltpu.VMEM)] * 2,
        out_specs=(pl.BlockSpec(memory_space=pl.ANY),) * 6
        + (pl.BlockSpec(memory_space=pltpu.VMEM),) * 4,
        scratch_shapes=[
            pltpu.VMEM((size, own, mixed.shape[-1]), low),
            pltpu.VMEM(out_weight.shape, low),
            pltpu.VMEM((own, depth), low),
            pltpu.VMEM((hidden, depth), low),
            pltpu.VMEM((hidden, depth), low),
            pltpu.VMEM((hidden, depth), low),
            pltpu.VMEM(wide, low),
            pltpu.VMEM(wide, low),
            pltpu.VMEM(wide, low),
            pltpu.VMEM((size + 1, own, depth), low),
            pltpu.VMEM((size * rows, hidden), full),
            pltpu.VMEM((size * rows, hidden), full),
            pltpu.VMEM((size * rows, hidden), full),
            pltpu.VMEM(thin, low),
            pltpu.VMEM(thin, low),
            pltpu.VMEM(thin, low),
            pltpu.VMEM((2, size, rows, depth), low),
            dma((8,)),
            dma((6, chunks)),
            dma((size, chunks)),
            dma((size + 1, chunks)),
            dma((size, chunks)),
            dma((size + 1, chunks)),
            dma((2, size, chunks)),
            dma((size, chunks)),
            dma((2, size, chunks)),
            dma((size, chunks)),
        ],
        compiler_params=pltpu.CompilerParams(
            collective_id=0, has_side_effects=True, vmem_limit_bytes=VMEM_BYTES
        ),
        cost_estimate=pl.CostEstimate(
            flops=14 * size * own * depth * hidden, bytes_accessed=2**26, transcendentals=0
        ),
    )(mixed, out_weight, tokens, cotangent, seed_first, hidden_gate, hidden_up, hidden_down, gain, bias)


def back_kernel(
    size,
    bits,
    chunks,
    outp_hbm,
    out_hbm,
    own_hbm,
    middle_ref,
    seeds_hbm,
    second_hbm,
    inner_hbm,
    dgate_hbm,
    dlin_hbm,
    branch_hbm,
    dmixed_hbm,
    output_ref,
    totals_hbm,
    part,
    out_weight,
    branch,
    inbox,
    dmixed,
    seeds,
    second,
    thin,
    turned,
    load_sem,
    grad_sem,
    store_sem,
    rs_send,
    rs_recv,
    ag_send,
    ag_recv,
    cube_parts,
    cube_firsts,
    cube_nexts,
    cube_store,
    cube_send,
    cube_recv,
    cube_free,
):
    me = lax.axis_index("tensor")
    own, depth = middle_ref.shape
    rows = own // chunks
    load_own = pltpu.make_async_copy(own_hbm, branch.at[me], load_sem.at[0])
    load_part = pltpu.make_async_copy(outp_hbm, part, load_sem.at[1])
    load_out = pltpu.make_async_copy(out_hbm, out_weight, load_sem.at[2])
    load_own.start()
    load_part.start()
    cube = CubeSum(
        bits,
        lax.axis_index("dp"),
        totals_hbm,
        cube_parts,
        cube_firsts,
        cube_nexts,
        cube_store,
        cube_send,
        cube_recv,
        cube_free,
    )
    grad_loads = [
        pltpu.make_async_copy(src, dst, grad_sem.at[index])
        for index, (src, dst) in enumerate(
            (
                (inner_hbm, thin.at[0]),
                (seeds_hbm, seeds),
                (dgate_hbm, thin.at[1]),
                (second_hbm, second),
                (dlin_hbm, thin.at[0]),
            )
        )
    ]
    for load in grad_loads[:4]:
        load.start()
    load_out.start()
    enter([{"dp": cube.partner(bit)} for bit in range(bits)], (size, me))
    scatter = LineScatter(size, me, rows, part, inbox, rs_send, rs_recv)
    gather = LineGather(size, me, rows, branch, ag_send, ag_recv)

    def at(chunk):
        return pl.ds(chunk * rows, rows)

    def store(kind, chunk):
        if kind == 0:
            src, dst = branch.at[:, at(chunk)], branch_hbm
        else:
            return pltpu.make_async_copy(
                dmixed.at[chunk % 2], dmixed_hbm.at[:, :, at(chunk)], store_sem.at[kind, chunk]
            )
        return pltpu.make_async_copy(src, dst.at[:, at(chunk)], store_sem.at[kind, chunk])

    def finish(chunk):
        scatter.arrive(chunk)

        def body(block):
            here = pl.ds(chunk * rows + block.start, block.size)
            output_ref[here, :] = (middle_ref[here, :] + scatter.total(here)).astype(jnp.bfloat16)

        for_rows(rows, body)

    def unproject(chunk):
        if chunk == 0:
            load_out.wait()
        if chunk >= 2:
            store(1, chunk - 2).wait()

        def body(start, width):
            columns = pl.ds(start, width)
            left = branch[:, at(chunk), :].reshape(size * rows, depth)
            for head in range(dmixed.shape[1]):
                value = dot_nt(left, out_weight[pl.ds(head * VD + start, width), :])
                dmixed[chunk % 2, head, :, :, columns] = value.reshape(size, rows, width)

        for_columns(VD, body)
        for kind in range(2):
            store(kind, chunk).start()

    def begin_branch(chunk):
        if chunk == 0:
            load_own.wait()
        gather.begin(chunk)

    def begin_out(chunk):
        if chunk == 0:
            load_part.wait()
        scatter.begin(chunk)

    def turn(which):
        needs = ((0, 1), (2, 3), (4,))[which]
        for index in needs:
            grad_loads[index].wait()
        for owner in range(size):
            turned[:, pl.ds(owner * own, own)] = thin[which % 2, owner].T
        if which == 0:
            grad_loads[4].start()

    def wide_columns(which):
        ref = (seeds, second, second)[which]
        return lambda columns: ref[:, :, columns].reshape(size * own, columns.size)

    streams, after = [], {}
    for chunk in range(chunks):
        steps = [functools.partial(begin_branch, chunk), *gather.calls(chunk)]
        if chunk:
            after[chunk, 0] = ((chunk - 1, 1),)
            after[chunk, len(steps)] = ((chunk - 1, len(steps) + 1),)
        streams.append(steps + [functools.partial(unproject, chunk)])
    for chunk in range(chunks):
        steps = [functools.partial(begin_out, chunk), *scatter.calls(chunk)]
        if chunk:
            after[chunks + chunk, 0] = ((chunks + chunk - 1, 1),)
        streams.append(steps + [functools.partial(finish, chunk)])
    for which in range(len(cube_parts)):
        if which:
            after[2 * chunks + which, 0] = ((2 * chunks + which - 1, 3),)
        streams.append(
            [
                functools.partial(turn, which),
                *cube.make_wide(which, turned, wide_columns(which)),
                *cube.calls(which),
            ]
        )
    run_streams(streams, ORDERS.get(("back", size, chunks, bits)), after)
    for chunk in range(chunks):
        scatter.drain(chunk)
        gather.drain(chunk)
        for kind in range(2 if chunk >= chunks - 2 else 1):
            store(kind, chunk).wait()
    cube.drain()


def feed_back(size, bits, chunks, partial, out_weight, branch, middle, seeds, second, thins):
    own, depth = middle.shape
    rows = own // chunks
    width = out_weight.shape[0]
    low, full = jnp.bfloat16, jnp.float32
    dma = pltpu.SemaphoreType.DMA
    vmem, anywhere = pl.BlockSpec(memory_space=pltpu.VMEM), pl.BlockSpec(memory_space=pl.ANY)
    grads = [jax.ShapeDtypeStruct((thin.shape[-1], depth), low) for thin in thins]
    many = [anywhere] * len(grads)
    return pl.pallas_call(
        functools.partial(back_kernel, size, bits, chunks),
        out_shape=(
            jax.ShapeDtypeStruct((size, own, depth), low),
            jax.ShapeDtypeStruct((width // VD, size, own, VD), full),
            jax.ShapeDtypeStruct((own, depth), low),
            grads,
        ),
        in_specs=[anywhere, anywhere, anywhere, vmem] + [anywhere] * 5,
        out_specs=(anywhere, anywhere, vmem, many),
        scratch_shapes=[
            pltpu.VMEM((size, own, depth), low),
            pltpu.VMEM(out_weight.shape, low),
            pltpu.VMEM((size, own, depth), low),
            pltpu.VMEM((size + 1, own, depth), low),
            pltpu.VMEM((2, width // VD, size, rows, VD), full),
            pltpu.VMEM((size, own, depth), low),
            pltpu.VMEM((size, own, depth), low),
            pltpu.VMEM((2,) + thins[0].shape, low),
            pltpu.VMEM((thins[0].shape[-1], size * own), low),
            dma((3,)),
            dma((5,)),
            dma((2, chunks)),
            dma((size, chunks)),
            dma((size + 1, chunks)),
            dma((2, size, chunks)),
            dma((size, chunks)),
        ]
        + cube_scratch(bits, [grad.shape for grad in grads]),
        compiler_params=pltpu.CompilerParams(
            collective_id=1, has_side_effects=True, vmem_limit_bytes=VMEM_BYTES
        ),
        cost_estimate=pl.CostEstimate(
            flops=2 * size * own * depth * width, bytes_accessed=2**26, transcendentals=0
        ),
    )(partial, out_weight, branch, middle, seeds, second, *thins)


def last_kernel(
    size,
    bits,
    chunks,
    query_hbm,
    key_hbm,
    value_hbm,
    gate_hbm,
    tokens_ref,
    dmiddle_ref,
    gain_ref,
    sums_ref,
    firsts_hbm,
    dvalues_hbm,
    dgates_hbm,
    dqueries_hbm,
    dkeys_hbm,
    dtokens_ref,
    totals_ref,
    totals_hbm,
    first_part,
    first_inbox,
    line_box,
    dp_box,
    firsts,
    dvalues,
    dgates,
    dqueries,
    dkeys,
    turned,
    slice_turned,
    query_weight,
    key_weight,
    value_weight,
    gate_weight,
    load_sem,
    line_send,
    line_recv,
    dp_send,
    dp_recv,
    rs_send,
    rs_recv,
    cube_parts,
    cube_firsts,
    cube_nexts,
    cube_store,
    cube_send,
    cube_recv,
    cube_free,
):
    me = lax.axis_index("tensor")
    mine = lax.axis_index("dp")
    own = tokens_ref.shape[0]
    rows = own // chunks
    cube = CubeSum(
        bits,
        mine,
        totals_hbm,
        cube_parts,
        cube_firsts,
        cube_nexts,
        cube_store,
        cube_send,
        cube_recv,
        cube_free,
    )
    loads = [
        pltpu.make_async_copy(src, dst, load_sem.at[index])
        for index, (src, dst) in enumerate(
            (
                (dvalues_hbm, dvalues),
                (firsts_hbm, firsts),
                (dgates_hbm, dgates),
                (dqueries_hbm, dqueries),
                (dkeys_hbm, dkeys),
                (query_hbm, query_weight),
                (key_hbm, key_weight),
                (value_hbm, value_weight),
                (gate_hbm, gate_weight),
            )
        )
    ]
    for load in loads:
        load.start()
    groups = 2**bits
    peers = [{"dp": (mine + step) % groups} for step in range(1, groups)]
    others = [{"tensor": (me + step) % size} for step in range(1, size)]
    enter(peers + others, None)
    first = LineScatter(size, me, rows, first_part, first_inbox, rs_send, rs_recv)

    def back(chunk):
        first.arrive(chunk)

        def body(block):
            here = pl.ds(chunk * rows + block.start, block.size)
            values = tokens_ref[here, :].astype(jnp.float32)
            centered = values - jnp.mean(values, axis=-1, keepdims=True)
            scale = lax.rsqrt(jnp.mean(centered * centered, axis=-1, keepdims=True) + EPS)
            normed = centered * scale
            grad = first.total(here)
            shaped = grad * gain_ref[...]
            line_box[me, 2:3, :] += jnp.sum(grad * normed, axis=0, keepdims=True)
            line_box[me, 3:4, :] += jnp.sum(grad, axis=0, keepdims=True)
            dtokens_ref[here, :] = dmiddle_ref[here, :] + scale * (
                shaped
                - jnp.mean(shaped, axis=-1, keepdims=True)
                - normed * jnp.mean(shaped * normed, axis=-1, keepdims=True)
            )

        for_rows(rows, body)

    def line_copy(step, slot):
        return pltpu.make_async_remote_copy(
            src_ref=line_box.at[me],
            dst_ref=line_box.at[slot],
            send_sem=line_send.at[step],
            recv_sem=line_recv.at[slot],
            device_id={"tensor": (me + step) % size},
            device_id_type=MESH,
        )

    def dp_copy(step, slot):
        return pltpu.make_async_remote_copy(
            src_ref=dp_box.at[mine],
            dst_ref=dp_box.at[slot],
            send_sem=dp_send.at[step],
            recv_sem=dp_recv.at[slot],
            device_id={"dp": (mine + step) % groups},
            device_id_type=MESH,
        )

    def sums_on_line():
        for step in range(1, size):
            line_copy(step, me).start()

    def sums_on_dp():
        for step in range(1, size):
            line_copy(step, (me + step) % size).wait_recv()
        dp_box[mine] = jnp.sum(line_box[...], axis=0)
        for step in range(1, groups):
            dp_copy(step, mine).start()

    def sums_done():
        for step in range(1, groups):
            dp_copy(step, (mine + step) % groups).wait_recv()
        totals_ref[...] = jnp.sum(dp_box[...], axis=0)

    line_box[me] = sums_ref[...]
    waited = set()

    def need(*indices):
        for index in indices:
            if index not in waited:
                waited.add(index)
                loads[index].wait()

    def combine(chunk):
        need(0, 2, 3, 4, 5, 6, 7, 8)
        at = pl.ds(chunk * rows, rows)

        def flat(ref):
            return ref[:, at, :].reshape(size * rows, ref.shape[-1])

        def body(start, width):
            columns = pl.ds(start, width)
            total = dot_nt(flat(dqueries), query_weight[columns, :])
            total = total + dot_nt(flat(dkeys), key_weight[columns, :])
            total = total + dot_nn(flat(dvalues), value_weight[:, columns])
            total = total + dot_nn(flat(dgates), gate_weight[:, columns])
            first_part[:, at, columns] = total.astype(jnp.bfloat16).reshape(size, rows, width)

        for_columns(first_part.shape[-1], body)
        first.begin(chunk)

    def turn(which):
        need(*((0, 1), (2,))[which])
        ref = (dvalues, dgates)[which]
        for owner in range(size):
            turned[:, pl.ds(owner * own, own)] = ref[owner].T

    def first_columns(columns):
        return firsts[:, :, columns].reshape(size * own, columns.size)

    def make_tall(start):
        need(1, 3, 4)
        lines = cube_parts[2].shape[-2]
        for index in range(start, start + groups // 4):
            lead = tuple((index >> bit) & 1 for bit in range(bits - 1, -1, -1))
            for owner in range(size):
                piece = firsts[owner, :, pl.ds(index * lines, lines)]
                slice_turned[:, pl.ds(owner * own, own)] = piece.T
            for which, ref in ((2, dqueries), (3, dkeys)):
                value = dot_nn(slice_turned[...], ref[...].reshape(size * own, ref.shape[-1]))
                cube_parts[which][lead] = value.astype(jnp.bfloat16)

    streams = []
    for chunk in range(chunks):
        streams.append(
            [
                functools.partial(combine, chunk),
                *first.calls(chunk),
                functools.partial(back, chunk),
            ]
        )
    after = {(chunks + 4, 0): [(chunk, 2 * size - 2) for chunk in range(chunks)]}
    for which in range(2):
        if which:
            after[chunks + which, 0] = ((chunks + which - 1, 3),)
        streams.append(
            [
                functools.partial(turn, which),
                *cube.make_wide(which, turned, first_columns),
                *cube.calls(which),
            ]
        )
    quarters = [functools.partial(make_tall, quarter * (groups // 4)) for quarter in range(4)]
    after[chunks + 2, 0] = ((chunks, 1),)
    after[chunks + 3, 0] = ((chunks + 2, 4),)
    streams.append([*quarters, *cube.calls(2)])
    streams.append(cube.calls(3))
    streams.append([sums_on_line, sums_on_dp, sums_done])
    run_streams(streams, ORDERS.get(("last", size, chunks, bits)), after)
    for chunk in range(chunks):
        first.drain(chunk)
    for step in range(1, size):
        line_copy(step, me).wait_send()
    for step in range(1, groups):
        dp_copy(step, mine).wait_send()
    cube.drain()


def last_sums(size, bits, chunks, weights, tokens, dmiddle, gain, sums, firsts, parts):
    own, depth = tokens.shape
    low, full = jnp.bfloat16, jnp.float32
    dma = pltpu.SemaphoreType.DMA
    vmem, anywhere = pl.BlockSpec(memory_space=pltpu.VMEM), pl.BlockSpec(memory_space=pl.ANY)
    grads = [
        jax.ShapeDtypeStruct((part.shape[-1], depth) if place < 2 else (depth, part.shape[-1]), low)
        for place, part in enumerate(parts)
    ]
    many = [anywhere] * len(grads)
    group = size * own
    return pl.pallas_call(
        functools.partial(last_kernel, size, bits, chunks),
        out_shape=(
            jax.ShapeDtypeStruct((own, depth), full),
            jax.ShapeDtypeStruct((8, depth), full),
            grads,
        ),
        in_specs=[anywhere] * 4 + [vmem] * 4 + [anywhere] * 5,
        out_specs=(vmem, vmem, many),
        scratch_shapes=[
            pltpu.VMEM((size, own, depth), low),
            pltpu.VMEM((size + 1, own, depth), low),
            pltpu.VMEM((size, 8, depth), full),
            pltpu.VMEM((2**bits, 8, depth), full),
            pltpu.VMEM(firsts.shape, low),
            *[pltpu.VMEM(part.shape, low) for part in parts],
            pltpu.VMEM((parts[0].shape[-1], group), low),
            pltpu.VMEM((depth // 2**bits, group), low),
            *[pltpu.VMEM(weight.shape, low) for weight in weights],
            dma((9,)),
            dma((size,)),
            dma((size,)),
            dma((2**bits,)),
            dma((2**bits,)),
            dma((size, chunks)),
            dma((size + 1, chunks)),
        ]
        + cube_scratch(bits, [grad.shape for grad in grads]),
        compiler_params=pltpu.CompilerParams(
            collective_id=2, has_side_effects=True, vmem_limit_bytes=VMEM_BYTES
        ),
        cost_estimate=pl.CostEstimate(flops=2**30, bytes_accessed=2**26, transcendentals=0),
    )(*weights, tokens, dmiddle, gain, sums, firsts, *parts)


def decay_rows(rate, column, row, first):
    shape = (column.shape[0], row.shape[1])
    here = first + lax.broadcasted_iota(jnp.int32, shape, 0)
    offset = here - lax.broadcasted_iota(jnp.int32, shape, 1)
    inside = (column == row) & (offset >= 0)
    distance = jnp.maximum(offset, 0).astype(jnp.float32)
    decay = jnp.where(inside, jnp.exp(-rate * distance), 0.0)
    return decay * lax.rsqrt(jnp.sum(decay, axis=-1, keepdims=True))


def group_parts(values):
    centered = values - jnp.mean(values, axis=-1, keepdims=True)
    scale = lax.rsqrt(jnp.mean(centered * centered, axis=-1, keepdims=True) + GROUP_EPS)
    return centered * scale, scale


def sigmoid(values):
    return 1.0 / (1.0 + jnp.exp(-values))


def first_kernel(
    size,
    chunks,
    heads,
    tokens_ref,
    seed_hbm,
    gain_ref,
    bias_ref,
    column_ref,
    row_ref,
    rates_ref,
    query_hbm,
    key_hbm,
    value_hbm,
    gate_hbm,
    first_hbm,
    queries_hbm,
    keys_hbm,
    values_hbm,
    gates_hbm,
    retained_hbm,
    mixed_hbm,
    table_hbm,
    seeds_hbm,
    query_weight,
    key_weight,
    value_weight,
    gate_weight,
    first,
    queries,
    keys,
    values,
    gates,
    retained,
    mixed,
    table,
    seeds,
    raw,
    retain,
    load_sem,
    store_sem,
    done_sem,
    ag_send,
    ag_recv,
    seed_send,
    seed_recv,
):
    me = lax.axis_index("tensor")
    own, depth = tokens_ref.shape
    rows = own // chunks
    pairs = (
        (query_hbm, query_weight),
        (key_hbm, key_weight),
        (value_hbm, value_weight),
        (gate_hbm, gate_weight),
        (seed_hbm.at[pl.ds(0, rows)], seeds.at[me]),
    )
    loads = [
        pltpu.make_async_copy(src, dst, load_sem.at[index])
        for index, (src, dst) in enumerate(pairs)
    ]
    for load in loads:
        load.start()
    enter((), (size, me))
    gather = LineGather(size, me, rows, first, ag_send, ag_recv)
    gather_seed = LineGather(size, me, rows, seeds, seed_send, seed_recv)
    waited = set()

    def need(index):
        if index not in waited:
            waited.add(index)
            loads[index].wait()

    def at(chunk):
        return pl.ds(chunk * rows, rows)

    def flat(chunk):
        return first[:, at(chunk), :].reshape(size * rows, depth)

    def store(kind, block):
        src, dst = (
            (queries, queries_hbm),
            (keys, keys_hbm),
            (first, first_hbm),
            (mixed, mixed_hbm),
        )[kind]
        return pltpu.make_async_copy(src.at[block], dst.at[block], store_sem.at[kind, block])

    def store_head(kind, head, block):
        src, dst = (
            (values, values_hbm),
            (gates, gates_hbm),
            (retained, retained_hbm),
            (table, table_hbm),
        )[kind]
        return pltpu.make_async_copy(
            src.at[head, block], dst.at[head, block], done_sem.at[kind, head, block]
        )

    def normalize(chunk):
        def body(block):
            here = pl.ds(chunk * rows + block.start, block.size)
            tokens = tokens_ref[here, :].astype(jnp.float32)
            centered = tokens - jnp.mean(tokens, axis=-1, keepdims=True)
            scale = lax.rsqrt(jnp.mean(centered * centered, axis=-1, keepdims=True) + EPS)
            value = centered * scale * gain_ref[...] + bias_ref[...]
            first[me, here, :] = value.astype(jnp.bfloat16)

        for_rows(rows, body)
        gather.begin(chunk)

    def project_pair(chunk):
        need(0)
        need(1)

        def body(start, width):
            columns = pl.ds(start, width)
            value = dot_nn(flat(chunk), query_weight[:, columns])
            queries[:, at(chunk), columns] = value.astype(jnp.bfloat16).reshape(size, rows, width)
            value = dot_nn(flat(chunk), key_weight[:, columns])
            keys[:, at(chunk), columns] = value.astype(jnp.bfloat16).reshape(size, rows, width)

        for_columns(heads * KD, body)

    def project_value(chunk, head):
        need(2)

        def body(start, width):
            weight = value_weight[pl.ds(head * VD + start, width), :]
            value = dot_nt(flat(chunk), weight).astype(jnp.bfloat16)
            values[head, :, at(chunk), pl.ds(start, width)] = value.reshape(size, rows, width)

        for_columns(VD, body)

    def project_gate(chunk, head):
        need(3)

        def body(start, width):
            weight = gate_weight[pl.ds(head * VD + start, width), :]
            value = dot_nt(flat(chunk), weight)
            gates[head, :, at(chunk), pl.ds(start, width)] = value.reshape(size, rows, width)

        for_columns(VD, body)

    def tabulate(head, block):
        seen = (block + 1) * own

        def body(part):
            there = pl.ds(block * own + part.start, part.size)
            table[head, block, part, :seen] = decay_rows(
                rates_ref[head], column_ref[there, :], row_ref[:, :seen], block * own + part.start
            )

        for_rows(own, body, WHOLE)
        store_head(3, head, block).start()

    def attend(head, block):
        seen = (block + 1) * own
        lanes = pl.ds(head * KD, KD)
        query = queries[block, :, lanes]
        raw[:, :seen] = dot_nt(query, keys[: block + 1, :, lanes].reshape(seen, KD))

        def body(part):
            weighted = raw[part, :seen] * (KD**-0.5) * table[head, block, part, :seen]
            total = jnp.sum(weighted, axis=-1, keepdims=True)
            retain[part, :seen] = (weighted * lax.rsqrt(total * total + 1.0)).astype(jnp.bfloat16)

        for_rows(own, body, WHOLE)
        value = values[head, : block + 1].reshape(seen, VD)
        retained[head, block] = dot_nn(retain[:, :seen], value)

        def body_mix(part):
            normed, _ = group_parts(retained[head, block, part, :])
            gate = gates[head, block, part, :]
            value = (gate * sigmoid(gate) * normed).astype(jnp.bfloat16)
            mixed[block, part, pl.ds(head * VD, VD)] = value

        for_rows(own, body_mix, WHOLE)
        store_head(2, head, block).start()
        if head == heads - 1:
            store(3, block).start()

    def flush():
        for block in range(size):
            for kind in range(3):
                store(kind, block).start()
            for head in range(heads):
                for kind in range(2):
                    store_head(kind, head, block).start()

    def begin_seed():
        need(4)
        gather_seed.begin(0)

    places = [(head, block) for head in range(heads) for block in range(size)]
    streams, after = [], {}
    for chunk in range(chunks):
        steps = [functools.partial(normalize, chunk), *gather.calls(chunk)]
        if chunk:
            after[chunk, 0] = ((chunk - 1, 1),)
        steps.append(functools.partial(project_pair, chunk))
        for head in range(heads):
            steps.append(functools.partial(project_value, chunk, head))
            steps.append(functools.partial(project_gate, chunk, head))
        streams.append(steps)
    streams.append([functools.partial(tabulate, *place) for place in places])
    streams.append([flush] + [functools.partial(attend, *place) for place in places])
    after[chunks + 1, 0] = [(chunk, len(streams[chunk])) for chunk in range(chunks)]
    for index in range(len(places)):
        after[chunks + 1, index + 1] = ((chunks, index + 1),)
    streams.append([begin_seed, *gather_seed.calls(0)])
    run_streams(streams, ORDERS.get(("first", size, chunks, heads)), after)
    store_seeds = pltpu.make_async_copy(seeds, seeds_hbm, load_sem.at[5])
    store_seeds.start()
    gather_seed.drain(0)
    store_seeds.wait()
    for chunk in range(chunks):
        gather.drain(chunk)
    for block in range(size):
        for kind in range(4):
            store(kind, block).wait()
        for head in range(heads):
            for kind in range(4):
                store_head(kind, head, block).wait()


def first_part(size, chunks, tokens, seed, gain, bias, segments, rates, query, key, value, gate):
    own, depth = tokens.shape
    heads = query.shape[1] // KD
    rows = size * own
    low, full = jnp.bfloat16, jnp.float32
    dma = pltpu.SemaphoreType.DMA
    vmem, anywhere = pl.BlockSpec(memory_space=pltpu.VMEM), pl.BlockSpec(memory_space=pl.ANY)
    shapes = (
        ((size, own, depth), low),
        ((size, own, heads * KD), low),
        ((size, own, heads * KD), low),
        ((heads, size, own, VD), low),
        ((heads, size, own, VD), full),
        ((heads, size, own, VD), full),
        ((size, own, heads * VD), low),
        ((heads, size, own, rows), full),
        ((size, own // chunks, depth), low),
    )
    return pl.pallas_call(
        functools.partial(first_kernel, size, chunks, heads),
        out_shape=tuple(jax.ShapeDtypeStruct(*item) for item in shapes),
        in_specs=[vmem, anywhere] + [vmem] * 4 + [pl.BlockSpec(memory_space=pltpu.SMEM)] + [anywhere] * 4,
        out_specs=(anywhere,) * 9,
        scratch_shapes=[pltpu.VMEM(item.shape, low) for item in (query, key, value, gate)]
        + [pltpu.VMEM(*item) for item in shapes]
        + [
            pltpu.VMEM((own, rows), full),
            pltpu.VMEM((own, rows), low),
            dma((6,)),
            dma((4, size)),
            dma((4, heads, size)),
            dma((2, size, chunks)),
            dma((size, chunks)),
            dma((2, size, 1)),
            dma((size, 1)),
        ],
        compiler_params=pltpu.CompilerParams(
            collective_id=3, has_side_effects=True, vmem_limit_bytes=VMEM_BYTES
        ),
        cost_estimate=pl.CostEstimate(flops=2**33, bytes_accessed=2**26, transcendentals=0),
    )(
        tokens,
        seed,
        gain,
        bias,
        segments.reshape(rows, 1),
        segments.reshape(1, rows),
        rates,
        query,
        key,
        value,
        gate,
    )


def retain_kernel(
    size,
    bits,
    heads,
    queries_hbm,
    keys_hbm,
    values_hbm,
    gates_hbm,
    retained_hbm,
    dmixed_hbm,
    table_hbm,
    mixed_hbm,
    branch_hbm,
    dqueries_hbm,
    dkeys_hbm,
    dvalues_hbm,
    dgates_hbm,
    totals_hbm,
    queries,
    keys,
    values,
    gates,
    retained,
    dmixed,
    table,
    mixed,
    branch,
    dqueries,
    dkeys,
    dvalues,
    dgates,
    turned,
    raw,
    grad,
    retain,
    dscores,
    dretained,
    dkey_sum,
    dvalue_sum,
    load_sem,
    block_sem,
    store_sem,
    cube_parts,
    cube_firsts,
    cube_nexts,
    cube_store,
    cube_send,
    cube_recv,
    cube_free,
):
    own = queries.shape[1]

    def load_whole(kind):
        src, dst = (
            (queries_hbm, queries),
            (keys_hbm, keys),
            (mixed_hbm, mixed),
            (branch_hbm, branch),
        )[kind]
        return pltpu.make_async_copy(src, dst, load_sem.at[kind])

    def load_block(kind, head, block):
        slot = (head * size + block) % 2
        src, dst = (
            (values_hbm, values.at[head, block]),
            (gates_hbm, gates.at[slot]),
            (retained_hbm, retained.at[slot]),
            (dmixed_hbm, dmixed.at[slot]),
            (table_hbm, table.at[slot]),
        )[kind]
        return pltpu.make_async_copy(src.at[head, block], dst, block_sem.at[kind, head, block])

    def load_blocks(place):
        if place < heads * size:
            for kind in range(5):
                load_block(kind, place // size, place % size).start()

    def store(kind, block):
        src, dst = (
            (dqueries, dqueries_hbm),
            (dkeys, dkeys_hbm),
            (dvalues, dvalues_hbm),
            (dgates, dgates_hbm),
        )[kind]
        return pltpu.make_async_copy(src.at[block], dst.at[block], store_sem.at[kind, block])

    for kind in range(2):
        load_whole(kind).start()
    load_blocks(0)
    for kind in range(2, 4):
        load_whole(kind).start()
    load_blocks(1)
    cube = CubeSum(
        bits,
        lax.axis_index("dp"),
        [ref.at[pl.ds(*half)] for ref in totals_hbm for half in halves(ref.shape[0])],
        cube_parts,
        cube_firsts,
        cube_nexts,
        cube_store,
        cube_send,
        cube_recv,
        cube_free,
    )
    enter([{"dp": cube.partner(bit)} for bit in range(bits)], None)

    def attend(head, block):
        seen = (block + 1) * own
        slot = (head * size + block) % 2
        if head == 0 and block == 0:
            for kind in range(2):
                load_whole(kind).wait()
        lanes = pl.ds(head * KD, KD)

        for kind in range(5):
            load_block(kind, head, block).wait()

        def body_mix(part):
            normed, scale = group_parts(retained[slot, part, :])
            gate = gates[slot, part, :]
            dmix = dmixed[slot, part, :]
            half = sigmoid(gate)
            dgate = dmix * normed * (half * (1.0 + gate * (1.0 - half)))
            dgates[block, part, pl.ds(head * VD, VD)] = dgate.astype(jnp.bfloat16)
            dnormed = dmix * (gate * half)
            value = scale * (
                dnormed
                - jnp.mean(dnormed, axis=-1, keepdims=True)
                - normed * jnp.mean(dnormed * normed, axis=-1, keepdims=True)
            )
            dretained[part, :] = value.astype(jnp.bfloat16)

        for_rows(own, body_mix, WHOLE)
        query = queries[block, :, lanes]
        key = keys[: block + 1, :, lanes].reshape(seen, KD)
        raw[:, :seen] = dot_nt(query, key)
        value = values[head, : block + 1].reshape(seen, VD)
        grad[:, :seen] = dot_nt(dretained[...], value)

        def body(part):
            decay = table[slot, part, :seen]
            weighted = raw[part, :seen] * (KD**-0.5) * decay
            dretain = grad[part, :seen]
            total = jnp.sum(weighted, axis=-1, keepdims=True)
            along = jnp.sum(dretain * weighted, axis=-1, keepdims=True)
            inverse = lax.rsqrt(total * total + 1.0)
            retain[part, :seen] = (weighted * inverse).astype(jnp.bfloat16)
            along = along * total * inverse * inverse
            dscores[part, :seen] = (decay * inverse * (dretain - along)).astype(jnp.bfloat16)

        for_rows(own, body, WHOLE)
        dquery = dot_nn(dscores[:, :seen], key) * (KD**-0.5)
        dqueries[block, :, lanes] = dquery.astype(jnp.bfloat16)
        for other in range(block + 1):
            there = pl.ds(other * own, own)
            dkey = dot_tn(dscores[:, there], query)
            dvalue = dot_tn(retain[:, there], dretained[...])
            if other == block:
                dkey_sum[other] = dkey
                dvalue_sum[other] = dvalue
            else:
                dkey_sum[other] += dkey
                dvalue_sum[other] += dvalue

        load_blocks(head * size + block + 2)
        if block == size - 1:
            for other in range(size):
                dkeys[other, :, lanes] = (dkey_sum[other] * (KD**-0.5)).astype(jnp.bfloat16)
                there = pl.ds(head * VD, VD)
                dvalues[other, :, there] = dvalue_sum[other].astype(jnp.bfloat16)
                if head == heads - 1:
                    for kind in range(4):
                        store(kind, other).start()

    def turn():
        for kind in range(2, 4):
            load_whole(kind).wait()
        for owner in range(size):
            turned[:, pl.ds(owner * own, own)] = mixed[owner].T

    def branch_columns(columns):
        return branch[:, :, columns].reshape(size * own, columns.size)

    steps = [
        functools.partial(attend, head, block) for head in range(heads) for block in range(size)
    ]
    streams = []
    for index, (start, count) in enumerate(halves(turned.shape[0])):
        part = turned.at[pl.ds(start, count)]
        streams.append([*cube.make_wide(index, part, branch_columns), *cube.calls(index)])
    streams[0].insert(0, turn)
    streams.append(steps)
    run_streams(streams, ORDERS.get(("retain", size, bits, heads)), {(1, 0): ((0, 1),)})
    for block in range(size):
        for kind in range(4):
            store(kind, block).wait()
    cube.drain()


def retain_back(
    size, bits, queries, keys, values, gates, retained, dmixed, table, mixed, branch
):
    own = queries.shape[1]
    heads = values.shape[0]
    rows, depth = size * own, branch.shape[-1]
    low, full = jnp.bfloat16, jnp.float32
    dma = pltpu.SemaphoreType.DMA
    anywhere = pl.BlockSpec(memory_space=pl.ANY)
    inputs = (queries, keys, values, gates, retained, dmixed, table, mixed, branch)
    slots = [
        jax.ShapeDtypeStruct((2,) + item.shape[2:], item.dtype) if 3 <= place < 7 else item
        for place, item in enumerate(inputs)
    ]
    total = jax.ShapeDtypeStruct((heads * VD, depth), low)
    shapes = (
        queries.shape,
        keys.shape,
        (size, own, heads * VD),
        (size, own, heads * VD),
    )
    return pl.pallas_call(
        functools.partial(retain_kernel, size, bits, heads),
        out_shape=tuple(jax.ShapeDtypeStruct(shape, low) for shape in shapes) + ([total],),
        in_specs=[anywhere] * len(inputs),
        out_specs=(anywhere,) * 4 + ([anywhere],),
        scratch_shapes=[pltpu.VMEM(item.shape, item.dtype) for item in slots]
        + [pltpu.VMEM(shape, low) for shape in shapes]
        + [
            pltpu.VMEM((heads * VD, rows), low),
            pltpu.VMEM((own, rows), full),
            pltpu.VMEM((own, rows), full),
            pltpu.VMEM((own, rows), low),
            pltpu.VMEM((own, rows), low),
            pltpu.VMEM((own, VD), low),
            pltpu.VMEM((size, own, KD), full),
            pltpu.VMEM((size, own, VD), full),
            dma((4,)),
            dma((5, heads, size)),
            dma((4, size)),
        ]
        + cube_scratch(bits, [(half[1], depth) for half in halves(total.shape[0])]),
        compiler_params=pltpu.CompilerParams(
            collective_id=4, has_side_effects=True, vmem_limit_bytes=VMEM_BYTES
        ),
        cost_estimate=pl.CostEstimate(flops=2**34, bytes_accessed=2**26, transcendentals=0),
    )(*inputs)


def cast_kernel(count, *refs):
    for src, dst in zip(refs[:count], refs[count:]):
        dst[...] = src[...].astype(dst.dtype)


def cast_all(items, kept):
    specs = []
    shapes = [jax.ShapeDtypeStruct(item.shape, jnp.float32) for item in items]
    shapes += [jax.ShapeDtypeStruct(item.shape, item.dtype) for item in kept]
    items = [*items, *kept]
    for item in items:
        blocks = max(count for count in BLOCKS if item.shape[0] % (count * LINE) == 0)
        specs.append(
            pl.BlockSpec(
                (item.shape[0] // blocks, item.shape[1]),
                lambda step, last=blocks - 1: (jnp.minimum(step, last), 0),
            )
        )
    return pl.pallas_call(
        functools.partial(cast_kernel, len(items)),
        out_shape=shapes,
        grid=(max(BLOCKS),),
        in_specs=specs,
        out_specs=specs,
        compiler_params=pltpu.CompilerParams(vmem_limit_bytes=VMEM_BYTES),
    )(*items)


def per_device(
    tokens,
    first_gain,
    first_bias,
    query_weight,
    key_weight,
    value_weight,
    gate_weight,
    out_weight,
    second_gain,
    second_bias,
    hidden_gate,
    hidden_up,
    hidden_down,
    segments,
    cotangent,
):
    size = lax.axis_size("tensor")
    group_rows = segments.size
    head_local = query_weight.shape[1] // KD
    head_index = (lax.axis_index("tensor") * head_local + jnp.arange(head_local)).astype(
        jnp.float32
    )
    rates = -jnp.log1p(-jnp.exp2(-5.0 - head_index))
    first_all, queries, keys, values, gates, retained, mixed, table, seed_first = first_part(
        size,
        CHUNKS,
        tokens,
        cotangent,
        first_gain[None],
        first_bias[None],
        segments,
        rates,
        query_weight,
        key_weight,
        value_weight.T,
        gate_weight.T,
    )
    bits = lax.axis_size("dp").bit_length() - 1
    own = tokens.shape[0]
    (
        second_all,
        seed_all,
        inner,
        gate_in_low,
        lin_in_low,
        partial,
        middle,
        grad_middle,
        branch,
        second_sums,
    ) = feed_forward(
        size,
        CHUNKS,
        mixed,
        out_weight,
        tokens,
        cotangent,
        seed_first,
        hidden_gate.T,
        hidden_up.T,
        hidden_down,
        second_gain[None],
        second_bias[None],
    )

    branch_all, grad_mixed, output, feed_grads = feed_back(
        size,
        bits,
        CHUNKS,
        partial,
        out_weight,
        branch,
        middle,
        seed_all,
        second_all,
        (inner, gate_in_low, lin_in_low),
    )
    grad_queries, grad_keys, grad_values, grad_gates, (grad_outw,) = retain_back(
        size,
        bits,
        queries,
        keys,
        values,
        gates,
        retained,
        grad_mixed,
        table,
        mixed,
        branch_all,
    )
    grad_tokens, sums, grads = last_sums(
        size,
        bits,
        CHUNKS,
        (query_weight, key_weight, value_weight.T, gate_weight.T),
        tokens,
        grad_middle,
        first_gain[None],
        second_sums,
        first_all,
        (grad_values, grad_gates, grad_queries, grad_keys),
    )
    grad_sgain, grad_sbias, grad_fgain, grad_fbias = sums[0], sums[1], sums[2], sums[3]
    (
        grad_outw,
        grad_valuew,
        grad_gatew,
        grad_queryw,
        grad_keyw,
        grad_hdown,
        grad_hgate,
        grad_hup,
        output,
        grad_tokens,
    ) = cast_all([grad_outw, *grads, *feed_grads], [output, grad_tokens])
    grad_valuew, grad_gatew, grad_hgate, grad_hup = (
        item.T for item in (grad_valuew, grad_gatew, grad_hgate, grad_hup)
    )
    return (
        output,
        grad_tokens,
        grad_fgain,
        grad_fbias,
        grad_queryw,
        grad_keyw,
        grad_valuew,
        grad_gatew,
        grad_outw,
        grad_sgain,
        grad_sbias,
        grad_hgate,
        grad_hup,
        grad_hdown,
    )


def solution(mesh):
    return jax.shard_map(
        per_device,
        mesh=mesh,
        in_specs=(
            P(("dp", "tensor"), None),
            P(),
            P(),
            P(None, "tensor"),
            P(None, "tensor"),
            P(None, "tensor"),
            P(None, "tensor"),
            P("tensor", None),
            P(),
            P(),
            P(None, "tensor"),
            P(None, "tensor"),
            P("tensor", None),
            P("dp", None),
            P(("dp", "tensor"), None),
        ),
        out_specs=(
            P(("dp", "tensor"), None),
            P(("dp", "tensor"), None),
            P(),
            P(),
            P(None, "tensor"),
            P(None, "tensor"),
            P(None, "tensor"),
            P(None, "tensor"),
            P("tensor", None),
            P(),
            P(),
            P(None, "tensor"),
            P(None, "tensor"),
            P("tensor", None),
        ),
        check_vma=False,
    )
```

```python
import functools
import itertools

import jax
import jax.numpy as jnp
from jax import lax
from jax.experimental import pallas as pl
from jax.experimental.pallas import tpu as pltpu
from jax.sharding import PartitionSpec as P

KD = 256
VD = 432


EPS = 1e-05
GROUP_EPS = 0.1
GELU_SCALE = 0.7978845608028654
CHUNKS = 4

MESH = pl.DeviceIdType.MESH
VMEM_BYTES = 60 * 2**20
TILE = 1024
LINE = 16
BAND = 64
ACT = 64
WHOLE = 256
BLOCKS = (1, 8, 9, 16, 18)


def for_columns(width, body):
    full = width // TILE

    def step(index, carry):
        body(pl.multiple_of(index * TILE, TILE), TILE)
        return carry

    if full:
        lax.fori_loop(0, full, step, 0)
    if width % TILE:
        body(full * TILE, width % TILE)


def for_rows(count, body, size=None):
    size = min(count, size or BAND)

    def step(index, carry):
        body(pl.ds(pl.multiple_of(index * size, LINE), size))
        return carry

    lax.fori_loop(0, count // size, step, 0)


def dot_nn(left, right):
    return lax.dot_general(left, right, (((1,), (0,)), ((), ())), preferred_element_type=jnp.float32)


def dot_nt(left, right):
    return lax.dot_general(left, right, (((1,), (1,)), ((), ())), preferred_element_type=jnp.float32)


def dot_tn(left, right):
    return lax.dot_general(left, right, (((0,), (0,)), ((), ())), preferred_element_type=jnp.float32)


def enter(peers, line):
    barrier = pltpu.get_barrier_semaphore()
    for peer in peers:
        pl.semaphore_signal(barrier, inc=1, device_id=peer, device_id_type=MESH)
    if line is not None:
        size, me = line

        @pl.when(me > 0)
        def _():
            pl.semaphore_signal(barrier, inc=1, device_id={"tensor": me - 1}, device_id_type=MESH)

        @pl.when(me < size - 1)
        def _():
            pl.semaphore_signal(barrier, inc=1, device_id={"tensor": me + 1}, device_id_type=MESH)

    count = len(peers)
    if line is not None:
        count = count + (me > 0).astype(jnp.int32) + (me < size - 1).astype(jnp.int32)
    pl.semaphore_wait(barrier, count)


class LineScatter:
    def __init__(self, size, me, rows, part, inbox, send, recv):
        self.size, self.me, self.rows = size, me, rows
        self.part, self.inbox, self.send, self.recv = part, inbox, send, recv

    def at(self, chunk):
        return pl.ds(chunk * self.rows, self.rows)

    def copy(self, target, slot, chunk, device):
        return pltpu.make_async_remote_copy(
            src_ref=self.part.at[target, self.at(chunk)],
            dst_ref=self.inbox.at[slot, self.at(chunk)],
            send_sem=self.send.at[target, chunk],
            recv_sem=self.recv.at[slot, chunk],
            device_id={"tensor": device},
            device_id_type=MESH,
        )

    def add(self, target, chunk):
        def body(rows):
            at = pl.ds(chunk * self.rows + rows.start, rows.size)
            total = self.part[target, at, :].astype(jnp.float32)
            total = total + self.inbox[target, at, :].astype(jnp.float32)
            self.part[target, at, :] = total.astype(jnp.bfloat16)

        for_rows(self.rows, body)

    def go_right(self, chunk, target):
        self.copy(target, target, chunk, self.me + 1).start()

    def go_left(self, chunk, target):
        last = self.me - 1 == target
        self.copy(target, jnp.where(last, self.size, target), chunk, self.me - 1).start()

    def begin(self, chunk):
        @pl.when(self.me == 0)
        def _():
            for target in range(self.size - 1, 0, -1):
                self.go_right(chunk, target)

        @pl.when(self.me == self.size - 1)
        def _():
            for target in range(self.size - 1):
                self.go_left(chunk, target)

    def right(self, chunk, target):
        @pl.when((self.me < target) & (self.me > 0))
        def _():
            self.copy(target, target, chunk, self.me).wait_recv()
            self.add(target, chunk)
            self.go_right(chunk, target)

    def left(self, chunk, target):
        @pl.when((self.me > target) & (self.me < self.size - 1))
        def _():
            self.copy(target, target, chunk, self.me).wait_recv()
            self.add(target, chunk)
            self.go_left(chunk, target)

    def calls(self, chunk):
        for step in range(self.size - 1):
            if step < self.size - 2:
                yield functools.partial(self.right, chunk, self.size - 1 - step)
                yield functools.partial(self.left, chunk, step)

    def arrive(self, chunk):
        size, me = self.size, self.me

        @pl.when(me > 0)
        def _():
            self.copy(me, me, chunk, me - 1).wait_recv()

        @pl.when(me < size - 1)
        def _():
            self.copy(me, size, chunk, me + 1).wait_recv()

    def total(self, rows):
        size, me = self.size, self.me
        own = self.part[me, rows, :].astype(jnp.float32)
        low = self.inbox[me, rows, :].astype(jnp.float32)
        high = self.inbox[size, rows, :].astype(jnp.float32)
        return own + jnp.where(me > 0, low, 0.0) + jnp.where(me < size - 1, high, 0.0)

    def drain(self, chunk):
        for target in range(self.size):

            @pl.when(self.me != target)
            def _():
                self.copy(target, target, chunk, self.me).wait_send()


class LineGather:
    def __init__(self, size, me, rows, held, send, recv):
        self.size, self.me, self.rows = size, me, rows
        self.held, self.send, self.recv = held, send, recv

    def copy(self, block, chunk, way, device):
        at = pl.ds(chunk * self.rows, self.rows)
        return pltpu.make_async_remote_copy(
            src_ref=self.held.at[block, at],
            dst_ref=self.held.at[block, at],
            send_sem=self.send.at[way, block, chunk],
            recv_sem=self.recv.at[block, chunk],
            device_id={"tensor": device},
            device_id_type=MESH,
        )

    def begin(self, chunk):
        self.right(chunk, 0)
        self.left(chunk, 0)

    def right(self, chunk, step):
        size, me = self.size, self.me

        @pl.when(me >= step)
        def _():
            if step:
                self.copy(me - step, chunk, 0, me).wait_recv()

            @pl.when(me < size - 1)
            def _():
                self.copy(me - step, chunk, 0, me + 1).start()

    def left(self, chunk, step):
        size, me = self.size, self.me

        @pl.when(me + step < size)
        def _():
            if step:
                self.copy(me + step, chunk, 1, me).wait_recv()

            @pl.when(me > 0)
            def _():
                self.copy(me + step, chunk, 1, me - 1).start()

    def calls(self, chunk):
        for step in range(1, self.size):
            yield functools.partial(self.right, chunk, step)
            yield functools.partial(self.left, chunk, step)

    def drain(self, chunk):
        size, me = self.size, self.me
        for step in range(size):

            @pl.when((me >= step) & (me < size - 1))
            def _():
                self.copy(me - step, chunk, 0, me + 1).wait_send()

            @pl.when((me + step < size) & (me > 0))
            def _():
                self.copy(me + step, chunk, 1, me - 1).wait_send()


class CubeSum:
    def __init__(self, bits, me, results, parts, firsts, nexts, store, send, recv, free):
        self.bits, self.me = bits, me
        self.results, self.parts = results, parts
        self.firsts, self.nexts = firsts, nexts
        self.store_sem, self.send, self.recv = store, send, recv
        self.free = free
        self.orders = (tuple(range(bits)), (0,) + tuple(range(bits - 1, 0, -1)))
        self.mine = [(me // 2**bit) % 2 for bit in range(bits)]

    def partner(self, bit):
        return self.me + (1 - 2 * self.mine[bit]) * 2**bit

    def band(self, which, color):
        count = self.parts[which].shape[-2]
        cut = cut_rows(count)
        return ((0, cut), (cut, count - cut), (0, count))[color]

    def lead(self, fixed):
        return tuple(fixed.get(bit, slice(None)) for bit in range(self.bits - 1, -1, -1))

    def moved(self, src, dst, which, color, step, bit):
        return pltpu.make_async_remote_copy(
            src_ref=src,
            dst_ref=dst,
            send_sem=self.send.at[which, color % 2, step],
            recv_sem=self.recv.at[which, color % 2, step],
            device_id={"dp": self.partner(bit)},
            device_id_type=MESH,
        )

    def halve(self, which, color, step):
        order = self.orders[color % 2]
        start, count = self.band(which, color)
        fixed = {bit: self.mine[bit] for bit in order[:step]}
        fixed[order[step]] = 1 - self.mine[order[step]]
        src = self.parts[which].at[self.lead(fixed) + (pl.ds(start, count), slice(None))]
        dst = self.firsts[which] if step == 0 else self.nexts[which][color][step - 1]
        return self.moved(src, dst, which, color, step, order[step])

    def double(self, which, color, step):
        order = self.orders[color % 2]
        start, count = self.band(which, color)
        fixed = {bit: self.mine[bit] for bit in order[: step + 1]}
        held = self.parts[which].at[self.lead(fixed) + (pl.ds(start, count), slice(None))]
        return self.moved(held, held, which, color, 2 * self.bits - 1 - step, order[step])

    def freed(self, which, color, step):
        return self.free.at[which, color % 2, step]

    def land(self, which, color, step):
        copy = self.halve(which, color, step)
        copy.wait_send()
        partner = {"dp": self.partner(self.orders[color % 2][step])}
        pl.semaphore_signal(
            self.freed(which, color, step), inc=1, device_id=partner, device_id_type=MESH
        )
        copy.wait_recv()
        self.add(which, color, step)

    def grow(self, which, color, step):
        pl.semaphore_wait(self.freed(which, color, step), 1)
        self.double(which, color, step).start()

    def add(self, which, color, step):
        order = self.orders[color % 2]
        part, (start, count) = self.parts[which], self.band(which, color)
        box = self.firsts[which] if step == 0 else self.nexts[which][color][step - 1]
        fixed = {bit: self.mine[bit] for bit in order[: step + 1]}
        free = [bit for bit in range(self.bits - 1, -1, -1) if bit not in fixed]
        for choice in itertools.product((0, 1), repeat=len(free)):
            lead = self.lead({**fixed, **dict(zip(free, choice))})

            def body(begin, size):
                there = lead + (pl.ds(start + begin, size), slice(None))
                total = part[there].astype(jnp.float32)
                total = total + box[choice + (pl.ds(begin, size), slice(None))].astype(jnp.float32)
                part[there] = total.astype(jnp.bfloat16)

            for_blocks(count, part.shape[-1], body)

    def slices(self, which, ref):
        rows, columns = self.parts[which].shape[-2:]
        for index in range(2**self.bits):
            lead = tuple((index >> bit) & 1 for bit in range(self.bits - 1, -1, -1))
            if ref.shape[0] == rows:
                whole = ref.at[:, pl.ds(index * columns, columns)]
            else:
                whole = ref.at[pl.ds(index * rows, rows), :]
            yield index, self.parts[which].at[lead], whole

    def make_wide(self, which, left, right):
        columns = self.parts[which].shape[-1]
        half = 2 ** (self.bits - 1)

        def some(start):
            for index in range(start, start + half):
                lead = tuple((index >> bit) & 1 for bit in range(self.bits - 1, -1, -1))
                value = dot_nn(left[...], right(pl.ds(index * columns, columns)))
                self.parts[which][lead] = value.astype(jnp.bfloat16)

        return [functools.partial(some, 0), functools.partial(some, half)]

    def open(self, which):
        self.halve(which, 2, 0).start()

    def split(self, which):
        self.land(which, 2, 0)
        for color in range(2):
            self.halve(which, color, 1).start()

    def down(self, which, color, step):
        self.land(which, color, step - 1)
        self.halve(which, color, step).start()

    def turn(self, which, color):
        self.land(which, color, self.bits - 1)
        self.grow(which, color, self.bits - 1)

    def up(self, which, color, step):
        self.double(which, color, step + 1).wait_recv()
        self.grow(which, color, step)

    def join(self, which):
        for color in range(2):
            self.double(which, color, 1).wait_recv()
        self.grow(which, 2, 0)

    def close(self, which):
        self.double(which, 2, 0).wait_recv()
        for index, part, whole in self.slices(which, self.results[which]):
            pltpu.make_async_copy(part, whole, self.store_sem.at[which, index]).start()

    def calls(self, which):
        yield functools.partial(self.open, which)
        yield functools.partial(self.split, which)
        for step in range(2, self.bits):
            for color in range(2):
                yield functools.partial(self.down, which, color, step)
        for color in range(2):
            yield functools.partial(self.turn, which, color)
        for step in range(self.bits - 2, 0, -1):
            for color in range(2):
                yield functools.partial(self.up, which, color, step)
        yield functools.partial(self.join, which)
        yield functools.partial(self.close, which)

    def drain(self):
        for which in range(len(self.parts)):
            self.double(which, 2, 0).wait_send()
            for color in range(2):
                for step in range(1, self.bits):
                    self.double(which, color, step).wait_send()
            for index, part, whole in self.slices(which, self.results[which]):
                pltpu.make_async_copy(part, whole, self.store_sem.at[which, index]).wait()


def cut_rows(count):
    return count // (2 * LINE) * LINE


def halves(rows):
    first = rows // 2 // LINE * LINE
    return ((0, first), (first, rows - first))


def for_blocks(count, columns, body):
    lines = count // LINE
    fits = [part for part in range(1, lines + 1) if lines % part == 0 and part * LINE * columns <= 2**14]
    size = fits[-1] * LINE

    def step(index, carry):
        body(pl.multiple_of(index * size, LINE), size)
        return carry

    lax.fori_loop(0, count // size, step, 0)


def cube_scratch(bits, shapes):
    low = jnp.bfloat16
    parts, firsts, nexts = [], [], []
    for rows, columns in shapes:
        if columns >= rows:
            columns = columns // 2**bits
        else:
            rows = rows // 2**bits
        cut = cut_rows(rows)
        parts.append(pltpu.VMEM((2,) * bits + (rows, columns), low))
        firsts.append(pltpu.VMEM((2,) * (bits - 1) + (rows, columns), low))
        nexts.append(
            [
                [
                    pltpu.VMEM((2,) * (bits - 1 - step) + (count, columns), low)
                    for step in range(1, bits)
                ]
                for count in (cut, rows - cut)
            ]
        )
    dma = pltpu.SemaphoreType.DMA
    return [
        parts,
        firsts,
        nexts,
        dma((len(shapes), 2**bits)),
        dma((len(shapes), 2, 2 * bits)),
        dma((len(shapes), 2, 2 * bits)),
        pltpu.SemaphoreType.REGULAR((len(shapes), 2, bits)),
    ]


ORDERS = {
    ("first", 4, 4, 2): (
        0, 1, 0, 2, 1, 3, 4, 0, 1, 2, 0, 2, 0, 0, 4, 4, 4, 3, 0, 3, 0, 4, 0, 4,
        4, 2, 1, 2, 3, 1, 3, 6, 2, 1, 4, 1, 2, 0, 2, 2, 0, 1, 2, 1, 0, 1, 3, 3,
        3, 3, 3, 1, 3, 2, 3, 1, 2, 5, 5, 5, 6, 6, 5, 5, 5, 5, 5, 5, 6, 6, 6, 6,
    ),
    ("feed", 4, 4): (
        4, 0, 5, 1, 6, 0, 4, 5, 0, 5, 0, 0, 4, 4, 5, 1, 0, 2, 3, 5, 6, 4, 0, 1,
        6, 0, 0, 2, 0, 4, 4, 5, 0, 1, 0, 2, 1, 5, 6, 2, 2, 0, 1, 2, 3, 1, 1, 0,
        0, 0, 1, 2, 1, 1, 3, 1, 3, 3, 2, 0, 1, 1, 3, 1, 1, 1, 2, 2, 2, 2, 0, 2,
        2, 3, 2, 3, 2, 3, 2, 1, 6, 3, 3, 1, 1, 0, 2, 3, 0, 6, 0, 6, 1, 3, 3, 3,
        3, 3, 3, 2, 2, 1, 3, 3, 0, 2, 3, 2, 3,
    ),
    ("back", 4, 4, 3): (
        0, 8, 8, 8, 8, 1, 4, 9, 9, 9, 9, 0, 8, 10, 10, 5, 10, 1, 0, 2, 0, 9, 10, 10,
        1, 4, 8, 1, 8, 9, 3, 9, 5, 10, 0, 10, 2, 8, 8, 1, 3, 5, 9, 5, 9, 4, 3, 2,
        6, 1, 10, 10, 0, 8, 2, 7, 8, 9, 9, 0, 3, 6, 4, 2, 5, 0, 10, 3, 10, 1, 2, 1,
        3, 3, 4, 7, 7, 8, 7, 2, 9, 4, 6, 6, 7, 5, 8, 6, 2, 10, 7, 3, 9, 10, 6,
    ),
    ("retain", 4, 3, 2): (
        0, 0, 0, 0, 1, 1, 1, 0, 2, 1, 2, 2, 0, 0, 2, 1, 1, 0, 0, 1, 1, 0, 0, 2,
        1, 1, 2, 2, 0, 2, 1, 0, 1,
    ),
    ("last", 4, 4, 3): (
        4, 4, 4, 4, 0, 6, 6, 4, 6, 6, 7, 5, 6, 2, 7, 5, 5, 5, 4, 4, 6, 0, 7, 7,
        5, 2, 0, 0, 4, 4, 3, 6, 2, 2, 6, 5, 5, 1, 4, 2, 4, 0, 3, 7, 7, 6, 6, 5,
        5, 1, 1, 7, 7, 1, 0, 3, 5, 1, 5, 3, 7, 6, 4, 3, 7, 1, 6, 2, 3, 8, 5, 8,
        4, 6, 8, 5, 6,
    ),
}


def run_streams(streams, order, after):
    streams = [list(stream) for stream in streams]
    done = [0] * len(streams)

    def ready(stream):
        place = done[stream]
        return place < len(streams[stream]) and all(
            done[other] >= count for other, count in after.get((stream, place), ())
        )

    def take(stream):
        streams[stream][done[stream]]()
        done[stream] += 1

    if order is not None:
        for stream in order:
            assert ready(stream)
            take(stream)
    while any(done[index] < len(stream) for index, stream in enumerate(streams)):
        for stream in range(len(streams)):
            if ready(stream):
                take(stream)


def feed_kernel(
    size,
    chunks,
    mixed_hbm,
    out_hbm,
    tokens_hbm,
    seed_hbm,
    seed_first_hbm,
    gate_hbm,
    up_hbm,
    down_hbm,
    gain_ref,
    bias_ref,
    second_hbm,
    seeds_hbm,
    inner_hbm,
    dgate_hbm,
    dlin_hbm,
    outp_hbm,
    middle_hbm,
    dmiddle_hbm,
    branch_hbm,
    sums_ref,
    middle_ref,
    dmiddle_ref,
    branch_ref,
    mixed,
    out_weight,
    tokens,
    hidden_gate,
    hidden_up,
    hidden_down,
    second,
    seeds,
    part,
    inbox,
    gate_in,
    lin_in,
    dinner,
    inner,
    dgate,
    dlin,
    wide,
    load_sem,
    store_sem,
    own_sem,
    rs_send,
    rs_recv,
    back_send,
    back_recv,
    ag_send,
    ag_recv,
    seed_send,
    seed_recv,
):
    me = lax.axis_index("tensor")
    own, depth = tokens.shape
    rows = own // chunks
    hidden = inner.shape[-1]
    loads = [
        pltpu.make_async_copy(src, dst, load_sem.at[index])
        for index, (src, dst) in enumerate(
            (
                (mixed_hbm, mixed),
                (out_hbm, out_weight),
                (seed_hbm.at[pl.ds(rows, own - rows)], seeds.at[me, pl.ds(rows, own - rows)]),
                (tokens_hbm, tokens),
                (gate_hbm, hidden_gate),
                (up_hbm, hidden_up),
                (down_hbm, hidden_down),
                (seed_first_hbm, seeds.at[:, pl.ds(0, rows)]),
            )
        )
    ]
    for load in loads:
        load.start()
    enter((), (size, me))
    scatter = LineScatter(size, me, rows, part, inbox, rs_send, rs_recv)
    scatter_back = LineScatter(size, me, rows, part, inbox, back_send, back_recv)
    gather = LineGather(size, me, rows, second, ag_send, ag_recv)
    gather_seed = LineGather(size, me, rows, seeds, seed_send, seed_recv)

    def at(chunk):
        return pl.ds(chunk * rows, rows)

    def flat(ref, chunk):
        value = ref[:, at(chunk), :]
        return value.reshape(size * rows, value.shape[-1])

    def store(kind, chunk):
        slot = chunk % 2
        src, dst = (
            (second.at[:, at(chunk)], second_hbm),
            (seeds.at[:, at(chunk)], seeds_hbm),
            (inner.at[slot], inner_hbm),
            (dgate.at[slot], dgate_hbm),
            (dlin.at[slot], dlin_hbm),
            (wide.at[slot], outp_hbm),
        )[kind]
        return pltpu.make_async_copy(src, dst.at[:, at(chunk)], store_sem.at[kind, chunk])

    waited = set()

    def need(*indices):
        for index in indices:
            if index not in waited:
                waited.add(index)
                loads[index].wait()

    def project(chunk):
        need(0, 1)

        def body(start, width):
            value = dot_nn(flat(mixed, chunk), out_weight[:, pl.ds(start, width)])
            part[:, at(chunk), pl.ds(start, width)] = value.astype(jnp.bfloat16).reshape(
                size, rows, width
            )

        for_columns(depth, body)
        scatter.begin(chunk)

    def normalize(chunk):
        need(3)
        scatter.arrive(chunk)

        def body(block):
            here = pl.ds(chunk * rows + block.start, block.size)
            middle = tokens[here, :].astype(jnp.float32) + scatter.total(here)
            middle_ref[here, :] = middle
            centered = middle - jnp.mean(middle, axis=-1, keepdims=True)
            scale = lax.rsqrt(jnp.mean(centered * centered, axis=-1, keepdims=True) + EPS)
            value = centered * scale * gain_ref[...] + bias_ref[...]
            second[me, here, :] = value.astype(jnp.bfloat16)

        for_rows(rows, body)
        gather.begin(chunk)

    def feed_in(chunk):
        need(4, 5)

        def body(start, width):
            columns = pl.ds(start, width)
            gate_in[:, columns] = dot_nt(flat(second, chunk), hidden_gate[columns, :])
            lin_in[:, columns] = dot_nt(flat(second, chunk), hidden_up[columns, :])

        for_columns(hidden, body)
        store(0, chunk).start()

    def feed_seed(chunk):
        need(6, 7)

        def body(start, width):
            columns = pl.ds(start, width)
            dinner[:, columns] = dot_nt(flat(seeds, chunk), hidden_down[columns, :])

        for_columns(hidden, body)
        store(1, chunk).start()

    def feed_act(chunk):
        slot = chunk % 2
        if chunk >= 2:
            for kind in range(2, 5):
                store(kind, chunk - 2).wait()

        def body(block):
            gate, lin, grad = gate_in[block, :], lin_in[block, :], dinner[block, :]
            cube = GELU_SCALE * (gate + 0.044715 * (gate * gate * gate))
            tanh = jnp.tanh(cube)
            half = 0.5 * (1.0 + tanh)
            active = gate * half
            slope = half + 0.5 * gate * (1.0 - tanh * tanh) * (
                GELU_SCALE * (1.0 + 3.0 * 0.044715 * (gate * gate))
            )
            owner = block.start // rows
            inside = pl.ds(block.start - owner * rows, block.size)
            inner[slot, owner, inside, :] = (active * lin).astype(jnp.bfloat16)
            dlin[slot, owner, inside, :] = (grad * active).astype(jnp.bfloat16)
            dgate[slot, owner, inside, :] = (grad * lin * slope).astype(jnp.bfloat16)

        for_rows(size * rows, body, min(ACT, rows))
        for kind in range(2, 5):
            store(kind, chunk).start()

    def feed_back(chunk):
        slot = chunk % 2
        scatter.drain(chunk)

        def body(start, width):
            columns = pl.ds(start, width)
            dgate_all = dgate[slot].reshape(size * rows, hidden)
            dlin_all = dlin[slot].reshape(size * rows, hidden)
            grad = dot_nn(dgate_all, hidden_gate[:, columns])
            grad = grad + dot_nn(dlin_all, hidden_up[:, columns])
            part[:, at(chunk), columns] = grad.astype(jnp.bfloat16).reshape(size, rows, width)

        for_columns(depth, body)
        scatter_back.begin(chunk)

    def feed_out(chunk):
        slot = chunk % 2
        if chunk >= 2:
            store(5, chunk - 2).wait()

        def body(start, width):
            columns = pl.ds(start, width)
            inner_all = inner[slot].reshape(size * rows, hidden)
            value = dot_nn(inner_all, hidden_down[:, columns])
            wide[slot, :, :, columns] = value.astype(jnp.bfloat16).reshape(size, rows, width)

        for_columns(depth, body)
        store(5, chunk).start()

    def normalize_back(chunk):
        scatter_back.arrive(chunk)

        def body(block):
            here = pl.ds(chunk * rows + block.start, block.size)
            middle = middle_ref[here, :]
            centered = middle - jnp.mean(middle, axis=-1, keepdims=True)
            scale = lax.rsqrt(jnp.mean(centered * centered, axis=-1, keepdims=True) + EPS)
            normed = centered * scale
            grad = scatter_back.total(here)
            shaped = grad * gain_ref[...]
            sums_ref[0:1, :] += jnp.sum(grad * normed, axis=0, keepdims=True)
            sums_ref[1:2, :] += jnp.sum(grad, axis=0, keepdims=True)
            dmiddle = seeds[me, here, :].astype(jnp.float32) + scale * (
                shaped
                - jnp.mean(shaped, axis=-1, keepdims=True)
                - normed * jnp.mean(shaped * normed, axis=-1, keepdims=True)
            )
            dmiddle_ref[here, :] = dmiddle
            branch_ref[here, :] = dmiddle.astype(jnp.bfloat16)

        for_rows(rows, body)
        for kind in range(3):
            store_own(kind, chunk).start()

    def store_own(kind, chunk):
        src, dst = (
            (middle_ref, middle_hbm),
            (dmiddle_ref, dmiddle_hbm),
            (branch_ref, branch_hbm),
        )[kind]
        return pltpu.make_async_copy(src.at[at(chunk)], dst.at[at(chunk)], own_sem.at[kind, chunk])

    def begin_seed(chunk):
        need(2)
        gather_seed.begin(chunk)

    streams, after = [], {}
    for chunk in range(chunks):
        steps = [project, *scatter.calls(chunk), normalize, *gather.calls(chunk)]
        first_feed = len(steps)
        steps += [feed_in, feed_seed, feed_act, feed_back, feed_out]
        steps += [*scatter_back.calls(chunk), normalize_back]
        streams.append(
            [step if isinstance(step, functools.partial) else functools.partial(step, chunk) for step in steps]
        )
        if chunk:
            after[chunk, first_feed] = ((chunk - 1, first_feed + 5),)
            after[chunk, first_feed + 1] = ((chunks + chunk - 1, 2 * size - 1),)
    for chunk in range(1, chunks):
        streams.append([functools.partial(begin_seed, chunk), *gather_seed.calls(chunk)])
    sums_ref[...] = jnp.zeros_like(sums_ref)
    run_streams(streams, ORDERS.get(("feed", size, chunks)), after)
    for chunk in range(chunks):
        scatter_back.drain(chunk)
        gather.drain(chunk)
        if chunk:
            gather_seed.drain(chunk)
        for kind in range(6 if chunk >= chunks - 2 else 2):
            store(kind, chunk).wait()
        for kind in range(3):
            store_own(kind, chunk).wait()


def feed_forward(size, chunks, mixed, out_weight, tokens, cotangent, seed_first, hidden_gate, hidden_up, hidden_down, gain, bias):
    own, depth = tokens.shape
    hidden = hidden_gate.shape[0]
    rows = own // chunks
    low, full = jnp.bfloat16, jnp.float32

    def blocks(width):
        return jax.ShapeDtypeStruct((size, own, width), low)

    dma = pltpu.SemaphoreType.DMA
    wide, thin = (size, own, depth), (2, size, rows, hidden)
    return pl.pallas_call(
        functools.partial(feed_kernel, size, chunks),
        out_shape=(
            blocks(depth),
            blocks(depth),
            blocks(hidden),
            blocks(hidden),
            blocks(hidden),
            blocks(depth),
            jax.ShapeDtypeStruct((own, depth), full),
            jax.ShapeDtypeStruct((own, depth), full),
            jax.ShapeDtypeStruct((own, depth), low),
            jax.ShapeDtypeStruct((8, depth), full),
        ),
        in_specs=[pl.BlockSpec(memory_space=pl.ANY)] * 8
        + [pl.BlockSpec(memory_space=pltpu.VMEM)] * 2,
        out_specs=(pl.BlockSpec(memory_space=pl.ANY),) * 9
        + (pl.BlockSpec(memory_space=pltpu.VMEM),),
        scratch_shapes=[
            pltpu.VMEM((own, depth), full),
            pltpu.VMEM((own, depth), full),
            pltpu.VMEM((own, depth), low),
            pltpu.VMEM((size, own, mixed.shape[-1]), low),
            pltpu.VMEM(out_weight.shape, low),
            pltpu.VMEM((own, depth), low),
            pltpu.VMEM((hidden, depth), low),
            pltpu.VMEM((hidden, depth), low),
            pltpu.VMEM((hidden, depth), low),
            pltpu.VMEM(wide, low),
            pltpu.VMEM(wide, low),
            pltpu.VMEM(wide, low),
            pltpu.VMEM((size + 1, own, depth), low),
            pltpu.VMEM((size * rows, hidden), full),
            pltpu.VMEM((size * rows, hidden), full),
            pltpu.VMEM((size * rows, hidden), full),
            pltpu.VMEM(thin, low),
            pltpu.VMEM(thin, low),
            pltpu.VMEM(thin, low),
            pltpu.VMEM((2, size, rows, depth), low),
            dma((8,)),
            dma((6, chunks)),
            dma((3, chunks)),
            dma((size, chunks)),
            dma((size + 1, chunks)),
            dma((size, chunks)),
            dma((size + 1, chunks)),
            dma((2, size, chunks)),
            dma((size, chunks)),
            dma((2, size, chunks)),
            dma((size, chunks)),
        ],
        compiler_params=pltpu.CompilerParams(
            collective_id=0, has_side_effects=True, vmem_limit_bytes=VMEM_BYTES
        ),
        cost_estimate=pl.CostEstimate(
            flops=14 * size * own * depth * hidden, bytes_accessed=2**26, transcendentals=0
        ),
    )(mixed, out_weight, tokens, cotangent, seed_first, hidden_gate, hidden_up, hidden_down, gain, bias)


def back_kernel(
    size,
    bits,
    chunks,
    outp_hbm,
    out_hbm,
    own_hbm,
    middle_ref,
    seeds_hbm,
    second_hbm,
    inner_hbm,
    dgate_hbm,
    dlin_hbm,
    branch_hbm,
    dmixed_hbm,
    output_ref,
    totals_hbm,
    part,
    out_weight,
    branch,
    inbox,
    dmixed,
    seeds,
    second,
    thin,
    turned,
    load_sem,
    grad_sem,
    store_sem,
    rs_send,
    rs_recv,
    ag_send,
    ag_recv,
    cube_parts,
    cube_firsts,
    cube_nexts,
    cube_store,
    cube_send,
    cube_recv,
    cube_free,
):
    me = lax.axis_index("tensor")
    own, depth = middle_ref.shape
    rows = own // chunks
    load_own = pltpu.make_async_copy(own_hbm, branch.at[me], load_sem.at[0])
    load_part = pltpu.make_async_copy(outp_hbm, part, load_sem.at[1])
    load_out = pltpu.make_async_copy(out_hbm, out_weight, load_sem.at[2])
    load_own.start()
    load_part.start()
    cube = CubeSum(
        bits,
        lax.axis_index("dp"),
        totals_hbm,
        cube_parts,
        cube_firsts,
        cube_nexts,
        cube_store,
        cube_send,
        cube_recv,
        cube_free,
    )
    grad_loads = [
        pltpu.make_async_copy(src, dst, grad_sem.at[index])
        for index, (src, dst) in enumerate(
            (
                (inner_hbm, thin.at[0]),
                (seeds_hbm, seeds),
                (dgate_hbm, thin.at[1]),
                (second_hbm, second),
                (dlin_hbm, thin.at[0]),
            )
        )
    ]
    for load in grad_loads[:4]:
        load.start()
    load_out.start()
    enter([{"dp": cube.partner(bit)} for bit in range(bits)], (size, me))
    scatter = LineScatter(size, me, rows, part, inbox, rs_send, rs_recv)
    gather = LineGather(size, me, rows, branch, ag_send, ag_recv)

    def at(chunk):
        return pl.ds(chunk * rows, rows)

    def store(kind, chunk):
        if kind == 0:
            src, dst = branch.at[:, at(chunk)], branch_hbm
        else:
            return pltpu.make_async_copy(
                dmixed.at[chunk % 2], dmixed_hbm.at[:, :, at(chunk)], store_sem.at[kind, chunk]
            )
        return pltpu.make_async_copy(src, dst.at[:, at(chunk)], store_sem.at[kind, chunk])

    def finish(chunk):
        scatter.arrive(chunk)

        def body(block):
            here = pl.ds(chunk * rows + block.start, block.size)
            output_ref[here, :] = (middle_ref[here, :] + scatter.total(here)).astype(jnp.bfloat16)

        for_rows(rows, body)

    def unproject(chunk):
        if chunk == 0:
            load_out.wait()
        if chunk >= 2:
            store(1, chunk - 2).wait()

        def body(start, width):
            columns = pl.ds(start, width)
            left = branch[:, at(chunk), :].reshape(size * rows, depth)
            for head in range(dmixed.shape[1]):
                value = dot_nt(left, out_weight[pl.ds(head * VD + start, width), :])
                dmixed[chunk % 2, head, :, :, columns] = value.reshape(size, rows, width)

        for_columns(VD, body)
        for kind in range(2):
            store(kind, chunk).start()

    def begin_branch(chunk):
        if chunk == 0:
            load_own.wait()
        gather.begin(chunk)

    def begin_out(chunk):
        if chunk == 0:
            load_part.wait()
        scatter.begin(chunk)

    def turn(which):
        needs = ((0, 1), (2, 3), (4,))[which]
        for index in needs:
            grad_loads[index].wait()
        for owner in range(size):
            turned[:, pl.ds(owner * own, own)] = thin[which % 2, owner].T
        if which == 0:
            grad_loads[4].start()

    def wide_columns(which):
        ref = (seeds, second, second)[which]
        return lambda columns: ref[:, :, columns].reshape(size * own, columns.size)

    streams, after = [], {}
    for chunk in range(chunks):
        steps = [functools.partial(begin_branch, chunk), *gather.calls(chunk)]
        if chunk:
            after[chunk, 0] = ((chunk - 1, 1),)
            after[chunk, len(steps)] = ((chunk - 1, len(steps) + 1),)
        streams.append(steps + [functools.partial(unproject, chunk)])
    for chunk in range(chunks):
        steps = [functools.partial(begin_out, chunk), *scatter.calls(chunk)]
        if chunk:
            after[chunks + chunk, 0] = ((chunks + chunk - 1, 1),)
        streams.append(steps + [functools.partial(finish, chunk)])
    for which in range(len(cube_parts)):
        if which:
            after[2 * chunks + which, 0] = ((2 * chunks + which - 1, 3),)
        streams.append(
            [
                functools.partial(turn, which),
                *cube.make_wide(which, turned, wide_columns(which)),
                *cube.calls(which),
            ]
        )
    run_streams(streams, ORDERS.get(("back", size, chunks, bits)), after)
    for chunk in range(chunks):
        scatter.drain(chunk)
        gather.drain(chunk)
        for kind in range(2 if chunk >= chunks - 2 else 1):
            store(kind, chunk).wait()
    cube.drain()


def feed_back(size, bits, chunks, partial, out_weight, branch, middle, seeds, second, thins):
    own, depth = middle.shape
    rows = own // chunks
    width = out_weight.shape[0]
    low, full = jnp.bfloat16, jnp.float32
    dma = pltpu.SemaphoreType.DMA
    vmem, anywhere = pl.BlockSpec(memory_space=pltpu.VMEM), pl.BlockSpec(memory_space=pl.ANY)
    grads = [jax.ShapeDtypeStruct((thin.shape[-1], depth), low) for thin in thins]
    many = [anywhere] * len(grads)
    return pl.pallas_call(
        functools.partial(back_kernel, size, bits, chunks),
        out_shape=(
            jax.ShapeDtypeStruct((size, own, depth), low),
            jax.ShapeDtypeStruct((width // VD, size, own, VD), full),
            jax.ShapeDtypeStruct((own, depth), low),
            grads,
        ),
        in_specs=[anywhere, anywhere, anywhere, vmem] + [anywhere] * 5,
        out_specs=(anywhere, anywhere, vmem, many),
        scratch_shapes=[
            pltpu.VMEM((size, own, depth), low),
            pltpu.VMEM(out_weight.shape, low),
            pltpu.VMEM((size, own, depth), low),
            pltpu.VMEM((size + 1, own, depth), low),
            pltpu.VMEM((2, width // VD, size, rows, VD), full),
            pltpu.VMEM((size, own, depth), low),
            pltpu.VMEM((size, own, depth), low),
            pltpu.VMEM((2,) + thins[0].shape, low),
            pltpu.VMEM((thins[0].shape[-1], size * own), low),
            dma((3,)),
            dma((5,)),
            dma((2, chunks)),
            dma((size, chunks)),
            dma((size + 1, chunks)),
            dma((2, size, chunks)),
            dma((size, chunks)),
        ]
        + cube_scratch(bits, [grad.shape for grad in grads]),
        compiler_params=pltpu.CompilerParams(
            collective_id=1, has_side_effects=True, vmem_limit_bytes=VMEM_BYTES
        ),
        cost_estimate=pl.CostEstimate(
            flops=2 * size * own * depth * width, bytes_accessed=2**26, transcendentals=0
        ),
    )(partial, out_weight, branch, middle, seeds, second, *thins)


def last_kernel(
    size,
    bits,
    chunks,
    query_hbm,
    key_hbm,
    value_hbm,
    gate_hbm,
    tokens_ref,
    dmiddle_ref,
    gain_ref,
    sums_ref,
    firsts_hbm,
    dvalues_hbm,
    dgates_hbm,
    dqueries_hbm,
    dkeys_hbm,
    dtokens_hbm,
    totals_ref,
    totals_hbm,
    dtokens_ref,
    own_sem,
    first_part,
    first_inbox,
    line_box,
    dp_box,
    firsts,
    dvalues,
    dgates,
    dqueries,
    dkeys,
    turned,
    slice_turned,
    query_weight,
    key_weight,
    value_weight,
    gate_weight,
    load_sem,
    line_send,
    line_recv,
    dp_send,
    dp_recv,
    rs_send,
    rs_recv,
    cube_parts,
    cube_firsts,
    cube_nexts,
    cube_store,
    cube_send,
    cube_recv,
    cube_free,
):
    me = lax.axis_index("tensor")
    mine = lax.axis_index("dp")
    own = tokens_ref.shape[0]
    rows = own // chunks
    cube = CubeSum(
        bits,
        mine,
        totals_hbm,
        cube_parts,
        cube_firsts,
        cube_nexts,
        cube_store,
        cube_send,
        cube_recv,
        cube_free,
    )
    loads = [
        pltpu.make_async_copy(src, dst, load_sem.at[index])
        for index, (src, dst) in enumerate(
            (
                (dvalues_hbm, dvalues),
                (firsts_hbm, firsts),
                (dgates_hbm, dgates),
                (dqueries_hbm, dqueries),
                (dkeys_hbm, dkeys),
                (query_hbm, query_weight),
                (key_hbm, key_weight),
                (value_hbm, value_weight),
                (gate_hbm, gate_weight),
            )
        )
    ]
    for load in loads:
        load.start()
    groups = 2**bits
    peers = [{"dp": (mine + step) % groups} for step in range(1, groups)]
    others = [{"tensor": (me + step) % size} for step in range(1, size)]
    enter(peers + others, None)
    first = LineScatter(size, me, rows, first_part, first_inbox, rs_send, rs_recv)

    def back(chunk):
        first.arrive(chunk)

        def body(block):
            here = pl.ds(chunk * rows + block.start, block.size)
            values = tokens_ref[here, :].astype(jnp.float32)
            centered = values - jnp.mean(values, axis=-1, keepdims=True)
            scale = lax.rsqrt(jnp.mean(centered * centered, axis=-1, keepdims=True) + EPS)
            normed = centered * scale
            grad = first.total(here)
            shaped = grad * gain_ref[...]
            line_box[me, 2:3, :] += jnp.sum(grad * normed, axis=0, keepdims=True)
            line_box[me, 3:4, :] += jnp.sum(grad, axis=0, keepdims=True)
            dtokens_ref[here, :] = dmiddle_ref[here, :] + scale * (
                shaped
                - jnp.mean(shaped, axis=-1, keepdims=True)
                - normed * jnp.mean(shaped * normed, axis=-1, keepdims=True)
            )

        for_rows(rows, body)
        store_own(chunk).start()

    def store_own(chunk):
        here = pl.ds(chunk * rows, rows)
        return pltpu.make_async_copy(dtokens_ref.at[here], dtokens_hbm.at[here], own_sem.at[chunk])

    def line_copy(step, slot):
        return pltpu.make_async_remote_copy(
            src_ref=line_box.at[me],
            dst_ref=line_box.at[slot],
            send_sem=line_send.at[step],
            recv_sem=line_recv.at[slot],
            device_id={"tensor": (me + step) % size},
            device_id_type=MESH,
        )

    def dp_copy(step, slot):
        return pltpu.make_async_remote_copy(
            src_ref=dp_box.at[mine],
            dst_ref=dp_box.at[slot],
            send_sem=dp_send.at[step],
            recv_sem=dp_recv.at[slot],
            device_id={"dp": (mine + step) % groups},
            device_id_type=MESH,
        )

    def sums_on_line():
        for step in range(1, size):
            line_copy(step, me).start()

    def sums_on_dp():
        for step in range(1, size):
            line_copy(step, (me + step) % size).wait_recv()
        dp_box[mine] = jnp.sum(line_box[...], axis=0)
        for step in range(1, groups):
            dp_copy(step, mine).start()

    def sums_done():
        for step in range(1, groups):
            dp_copy(step, (mine + step) % groups).wait_recv()
        totals_ref[...] = jnp.sum(dp_box[...], axis=0)

    line_box[me] = sums_ref[...]
    waited = set()

    def need(*indices):
        for index in indices:
            if index not in waited:
                waited.add(index)
                loads[index].wait()

    def combine(chunk):
        need(0, 2, 3, 4, 5, 6, 7, 8)
        at = pl.ds(chunk * rows, rows)

        def flat(ref):
            return ref[:, at, :].reshape(size * rows, ref.shape[-1])

        def body(start, width):
            columns = pl.ds(start, width)
            total = dot_nt(flat(dqueries), query_weight[columns, :])
            total = total + dot_nt(flat(dkeys), key_weight[columns, :])
            total = total + dot_nn(flat(dvalues), value_weight[:, columns])
            total = total + dot_nn(flat(dgates), gate_weight[:, columns])
            first_part[:, at, columns] = total.astype(jnp.bfloat16).reshape(size, rows, width)

        for_columns(first_part.shape[-1], body)
        first.begin(chunk)

    def turn(which):
        need(*((0, 1), (2,))[which])
        ref = (dvalues, dgates)[which]
        for owner in range(size):
            turned[:, pl.ds(owner * own, own)] = ref[owner].T

    def first_columns(columns):
        return firsts[:, :, columns].reshape(size * own, columns.size)

    def make_tall(start):
        need(1, 3, 4)
        lines = cube_parts[2].shape[-2]
        for index in range(start, start + groups // 4):
            lead = tuple((index >> bit) & 1 for bit in range(bits - 1, -1, -1))
            for owner in range(size):
                piece = firsts[owner, :, pl.ds(index * lines, lines)]
                slice_turned[:, pl.ds(owner * own, own)] = piece.T
            for which, ref in ((2, dqueries), (3, dkeys)):
                value = dot_nn(slice_turned[...], ref[...].reshape(size * own, ref.shape[-1]))
                cube_parts[which][lead] = value.astype(jnp.bfloat16)

    streams = []
    for chunk in range(chunks):
        streams.append(
            [
                functools.partial(combine, chunk),
                *first.calls(chunk),
                functools.partial(back, chunk),
            ]
        )
    after = {(chunks + 4, 0): [(chunk, 2 * size - 2) for chunk in range(chunks)]}
    for which in range(2):
        if which:
            after[chunks + which, 0] = ((chunks + which - 1, 3),)
        streams.append(
            [
                functools.partial(turn, which),
                *cube.make_wide(which, turned, first_columns),
                *cube.calls(which),
            ]
        )
    quarters = [functools.partial(make_tall, quarter * (groups // 4)) for quarter in range(4)]
    after[chunks + 2, 0] = ((chunks, 1),)
    after[chunks + 3, 0] = ((chunks + 2, 4),)
    streams.append([*quarters, *cube.calls(2)])
    streams.append(cube.calls(3))
    streams.append([sums_on_line, sums_on_dp, sums_done])
    run_streams(streams, ORDERS.get(("last", size, chunks, bits)), after)
    for chunk in range(chunks):
        first.drain(chunk)
        store_own(chunk).wait()
    for step in range(1, size):
        line_copy(step, me).wait_send()
    for step in range(1, groups):
        dp_copy(step, mine).wait_send()
    cube.drain()


def last_sums(size, bits, chunks, weights, tokens, dmiddle, gain, sums, firsts, parts):
    own, depth = tokens.shape
    low, full = jnp.bfloat16, jnp.float32
    dma = pltpu.SemaphoreType.DMA
    vmem, anywhere = pl.BlockSpec(memory_space=pltpu.VMEM), pl.BlockSpec(memory_space=pl.ANY)
    grads = [
        jax.ShapeDtypeStruct((part.shape[-1], depth) if place < 2 else (depth, part.shape[-1]), low)
        for place, part in enumerate(parts)
    ]
    many = [anywhere] * len(grads)
    group = size * own
    return pl.pallas_call(
        functools.partial(last_kernel, size, bits, chunks),
        out_shape=(
            jax.ShapeDtypeStruct((own, depth), full),
            jax.ShapeDtypeStruct((8, depth), full),
            grads,
        ),
        in_specs=[anywhere] * 4 + [vmem] * 4 + [anywhere] * 5,
        out_specs=(anywhere, vmem, many),
        scratch_shapes=[
            pltpu.VMEM((own, depth), full),
            dma((chunks,)),
            pltpu.VMEM((size, own, depth), low),
            pltpu.VMEM((size + 1, own, depth), low),
            pltpu.VMEM((size, 8, depth), full),
            pltpu.VMEM((2**bits, 8, depth), full),
            pltpu.VMEM(firsts.shape, low),
            *[pltpu.VMEM(part.shape, low) for part in parts],
            pltpu.VMEM((parts[0].shape[-1], group), low),
            pltpu.VMEM((depth // 2**bits, group), low),
            *[pltpu.VMEM(weight.shape, low) for weight in weights],
            dma((9,)),
            dma((size,)),
            dma((size,)),
            dma((2**bits,)),
            dma((2**bits,)),
            dma((size, chunks)),
            dma((size + 1, chunks)),
        ]
        + cube_scratch(bits, [grad.shape for grad in grads]),
        compiler_params=pltpu.CompilerParams(
            collective_id=2, has_side_effects=True, vmem_limit_bytes=VMEM_BYTES
        ),
        cost_estimate=pl.CostEstimate(flops=2**30, bytes_accessed=2**26, transcendentals=0),
    )(*weights, tokens, dmiddle, gain, sums, firsts, *parts)


def decay_rows(rate, column, row, first):
    shape = (column.shape[0], row.shape[1])
    here = first + lax.broadcasted_iota(jnp.int32, shape, 0)
    offset = here - lax.broadcasted_iota(jnp.int32, shape, 1)
    inside = (column == row) & (offset >= 0)
    distance = jnp.maximum(offset, 0).astype(jnp.float32)
    decay = jnp.where(inside, jnp.exp(-rate * distance), 0.0)
    return decay * lax.rsqrt(jnp.sum(decay, axis=-1, keepdims=True))


def group_parts(values):
    centered = values - jnp.mean(values, axis=-1, keepdims=True)
    scale = lax.rsqrt(jnp.mean(centered * centered, axis=-1, keepdims=True) + GROUP_EPS)
    return centered * scale, scale


def sigmoid(values):
    return 1.0 / (1.0 + jnp.exp(-values))


def first_kernel(
    size,
    chunks,
    heads,
    tokens_ref,
    seed_hbm,
    gain_ref,
    bias_ref,
    column_ref,
    row_ref,
    rates_ref,
    query_hbm,
    key_hbm,
    value_hbm,
    gate_hbm,
    first_hbm,
    queries_hbm,
    keys_hbm,
    values_hbm,
    gates_hbm,
    retained_hbm,
    mixed_hbm,
    table_hbm,
    seeds_hbm,
    query_weight,
    key_weight,
    value_weight,
    gate_weight,
    first,
    queries,
    keys,
    values,
    gates,
    retained,
    mixed,
    table,
    seeds,
    raw,
    retain,
    load_sem,
    store_sem,
    done_sem,
    ag_send,
    ag_recv,
    seed_send,
    seed_recv,
):
    me = lax.axis_index("tensor")
    own, depth = tokens_ref.shape
    rows = own // chunks
    pairs = (
        (query_hbm, query_weight),
        (key_hbm, key_weight),
        (value_hbm, value_weight),
        (gate_hbm, gate_weight),
        (seed_hbm.at[pl.ds(0, rows)], seeds.at[me]),
    )
    loads = [
        pltpu.make_async_copy(src, dst, load_sem.at[index])
        for index, (src, dst) in enumerate(pairs)
    ]
    for load in loads:
        load.start()
    enter((), (size, me))
    gather = LineGather(size, me, rows, first, ag_send, ag_recv)
    gather_seed = LineGather(size, me, rows, seeds, seed_send, seed_recv)
    waited = set()

    def need(index):
        if index not in waited:
            waited.add(index)
            loads[index].wait()

    def at(chunk):
        return pl.ds(chunk * rows, rows)

    def flat(chunk):
        return first[:, at(chunk), :].reshape(size * rows, depth)

    def store(kind, block):
        src, dst = (
            (queries, queries_hbm),
            (keys, keys_hbm),
            (first, first_hbm),
            (mixed, mixed_hbm),
        )[kind]
        return pltpu.make_async_copy(src.at[block], dst.at[block], store_sem.at[kind, block])

    def store_head(kind, head, block):
        src, dst = (
            (values, values_hbm),
            (gates, gates_hbm),
            (retained, retained_hbm),
            (table, table_hbm),
        )[kind]
        return pltpu.make_async_copy(
            src.at[head, block], dst.at[head, block], done_sem.at[kind, head, block]
        )

    def normalize(chunk):
        def body(block):
            here = pl.ds(chunk * rows + block.start, block.size)
            tokens = tokens_ref[here, :].astype(jnp.float32)
            centered = tokens - jnp.mean(tokens, axis=-1, keepdims=True)
            scale = lax.rsqrt(jnp.mean(centered * centered, axis=-1, keepdims=True) + EPS)
            value = centered * scale * gain_ref[...] + bias_ref[...]
            first[me, here, :] = value.astype(jnp.bfloat16)

        for_rows(rows, body)
        gather.begin(chunk)

    def project_pair(chunk):
        need(0)
        need(1)

        def body(start, width):
            columns = pl.ds(start, width)
            value = dot_nn(flat(chunk), query_weight[:, columns])
            queries[:, at(chunk), columns] = value.astype(jnp.bfloat16).reshape(size, rows, width)
            value = dot_nn(flat(chunk), key_weight[:, columns])
            keys[:, at(chunk), columns] = value.astype(jnp.bfloat16).reshape(size, rows, width)

        for_columns(heads * KD, body)

    def project_value(chunk, head):
        need(2)

        def body(start, width):
            weight = value_weight[pl.ds(head * VD + start, width), :]
            value = dot_nt(flat(chunk), weight).astype(jnp.bfloat16)
            values[head, :, at(chunk), pl.ds(start, width)] = value.reshape(size, rows, width)

        for_columns(VD, body)

    def project_gate(chunk, head):
        need(3)

        def body(start, width):
            weight = gate_weight[pl.ds(head * VD + start, width), :]
            value = dot_nt(flat(chunk), weight)
            gates[head, :, at(chunk), pl.ds(start, width)] = value.reshape(size, rows, width)

        for_columns(VD, body)

    def tabulate(head, block):
        seen = (block + 1) * own

        def body(part):
            there = pl.ds(block * own + part.start, part.size)
            table[head, block, part, :seen] = decay_rows(
                rates_ref[head], column_ref[there, :], row_ref[:, :seen], block * own + part.start
            )

        for_rows(own, body, WHOLE)
        store_head(3, head, block).start()

    def attend(head, block):
        seen = (block + 1) * own
        lanes = pl.ds(head * KD, KD)
        query = queries[block, :, lanes]
        raw[:, :seen] = dot_nt(query, keys[: block + 1, :, lanes].reshape(seen, KD))

        def body(part):
            weighted = raw[part, :seen] * (KD**-0.5) * table[head, block, part, :seen]
            total = jnp.sum(weighted, axis=-1, keepdims=True)
            retain[part, :seen] = (weighted * lax.rsqrt(total * total + 1.0)).astype(jnp.bfloat16)

        for_rows(own, body, WHOLE)
        value = values[head, : block + 1].reshape(seen, VD)
        retained[head, block] = dot_nn(retain[:, :seen], value)

        def body_mix(part):
            normed, _ = group_parts(retained[head, block, part, :])
            gate = gates[head, block, part, :]
            value = (gate * sigmoid(gate) * normed).astype(jnp.bfloat16)
            mixed[block, part, pl.ds(head * VD, VD)] = value

        for_rows(own, body_mix, WHOLE)
        store_head(2, head, block).start()
        if head == heads - 1:
            store(3, block).start()

    def flush():
        for block in range(size):
            for kind in range(3):
                store(kind, block).start()
            for head in range(heads):
                for kind in range(2):
                    store_head(kind, head, block).start()

    def begin_seed():
        need(4)
        gather_seed.begin(0)

    places = [(head, block) for head in range(heads) for block in range(size)]
    streams, after = [], {}
    for chunk in range(chunks):
        steps = [functools.partial(normalize, chunk), *gather.calls(chunk)]
        if chunk:
            after[chunk, 0] = ((chunk - 1, 1),)
        steps.append(functools.partial(project_pair, chunk))
        for head in range(heads):
            steps.append(functools.partial(project_value, chunk, head))
            steps.append(functools.partial(project_gate, chunk, head))
        streams.append(steps)
    streams.append([functools.partial(tabulate, *place) for place in places])
    streams.append([flush] + [functools.partial(attend, *place) for place in places])
    after[chunks + 1, 0] = [(chunk, len(streams[chunk])) for chunk in range(chunks)]
    for index in range(len(places)):
        after[chunks + 1, index + 1] = ((chunks, index + 1),)
    streams.append([begin_seed, *gather_seed.calls(0)])
    run_streams(streams, ORDERS.get(("first", size, chunks, heads)), after)
    store_seeds = pltpu.make_async_copy(seeds, seeds_hbm, load_sem.at[5])
    store_seeds.start()
    gather_seed.drain(0)
    store_seeds.wait()
    for chunk in range(chunks):
        gather.drain(chunk)
    for block in range(size):
        for kind in range(4):
            store(kind, block).wait()
        for head in range(heads):
            for kind in range(4):
                store_head(kind, head, block).wait()


def first_part(size, chunks, tokens, seed, gain, bias, segments, rates, query, key, value, gate):
    own, depth = tokens.shape
    heads = query.shape[1] // KD
    rows = size * own
    low, full = jnp.bfloat16, jnp.float32
    dma = pltpu.SemaphoreType.DMA
    vmem, anywhere = pl.BlockSpec(memory_space=pltpu.VMEM), pl.BlockSpec(memory_space=pl.ANY)
    shapes = (
        ((size, own, depth), low),
        ((size, own, heads * KD), low),
        ((size, own, heads * KD), low),
        ((heads, size, own, VD), low),
        ((heads, size, own, VD), full),
        ((heads, size, own, VD), full),
        ((size, own, heads * VD), low),
        ((heads, size, own, rows), full),
        ((size, own // chunks, depth), low),
    )
    return pl.pallas_call(
        functools.partial(first_kernel, size, chunks, heads),
        out_shape=tuple(jax.ShapeDtypeStruct(*item) for item in shapes),
        in_specs=[vmem, anywhere] + [vmem] * 4 + [pl.BlockSpec(memory_space=pltpu.SMEM)] + [anywhere] * 4,
        out_specs=(anywhere,) * 9,
        scratch_shapes=[pltpu.VMEM(item.shape, low) for item in (query, key, value, gate)]
        + [pltpu.VMEM(*item) for item in shapes]
        + [
            pltpu.VMEM((own, rows), full),
            pltpu.VMEM((own, rows), low),
            dma((6,)),
            dma((4, size)),
            dma((4, heads, size)),
            dma((2, size, chunks)),
            dma((size, chunks)),
            dma((2, size, 1)),
            dma((size, 1)),
        ],
        compiler_params=pltpu.CompilerParams(
            collective_id=3, has_side_effects=True, vmem_limit_bytes=VMEM_BYTES
        ),
        cost_estimate=pl.CostEstimate(flops=2**33, bytes_accessed=2**26, transcendentals=0),
    )(
        tokens,
        seed,
        gain,
        bias,
        segments.reshape(rows, 1),
        segments.reshape(1, rows),
        rates,
        query,
        key,
        value,
        gate,
    )


def retain_kernel(
    size,
    bits,
    heads,
    queries_hbm,
    keys_hbm,
    values_hbm,
    gates_hbm,
    retained_hbm,
    dmixed_hbm,
    table_hbm,
    mixed_hbm,
    branch_hbm,
    dqueries_hbm,
    dkeys_hbm,
    dvalues_hbm,
    dgates_hbm,
    totals_hbm,
    queries,
    keys,
    values,
    gates,
    retained,
    dmixed,
    table,
    mixed,
    branch,
    dqueries,
    dkeys,
    dvalues,
    dgates,
    turned,
    raw,
    grad,
    retain,
    dscores,
    dretained,
    dkey_sum,
    dvalue_sum,
    load_sem,
    block_sem,
    store_sem,
    cube_parts,
    cube_firsts,
    cube_nexts,
    cube_store,
    cube_send,
    cube_recv,
    cube_free,
):
    own = queries.shape[1]

    def load_whole(kind):
        src, dst = (
            (queries_hbm, queries),
            (keys_hbm, keys),
            (mixed_hbm, mixed),
            (branch_hbm, branch),
        )[kind]
        return pltpu.make_async_copy(src, dst, load_sem.at[kind])

    def load_block(kind, head, block):
        slot = (head * size + block) % 2
        src, dst = (
            (values_hbm, values.at[head, block]),
            (gates_hbm, gates.at[slot]),
            (retained_hbm, retained.at[slot]),
            (dmixed_hbm, dmixed.at[slot]),
            (table_hbm, table.at[slot]),
        )[kind]
        return pltpu.make_async_copy(src.at[head, block], dst, block_sem.at[kind, head, block])

    def load_blocks(place):
        if place < heads * size:
            for kind in range(5):
                load_block(kind, place // size, place % size).start()

    def store(kind, block):
        src, dst = (
            (dqueries, dqueries_hbm),
            (dkeys, dkeys_hbm),
            (dvalues, dvalues_hbm),
            (dgates, dgates_hbm),
        )[kind]
        return pltpu.make_async_copy(src.at[block], dst.at[block], store_sem.at[kind, block])

    for kind in range(2):
        load_whole(kind).start()
    load_blocks(0)
    for kind in range(2, 4):
        load_whole(kind).start()
    load_blocks(1)
    cube = CubeSum(
        bits,
        lax.axis_index("dp"),
        [ref.at[pl.ds(*half)] for ref in totals_hbm for half in halves(ref.shape[0])],
        cube_parts,
        cube_firsts,
        cube_nexts,
        cube_store,
        cube_send,
        cube_recv,
        cube_free,
    )
    enter([{"dp": cube.partner(bit)} for bit in range(bits)], None)

    def attend(head, block):
        seen = (block + 1) * own
        slot = (head * size + block) % 2
        if head == 0 and block == 0:
            for kind in range(2):
                load_whole(kind).wait()
        lanes = pl.ds(head * KD, KD)

        for kind in range(5):
            load_block(kind, head, block).wait()

        def body_mix(part):
            normed, scale = group_parts(retained[slot, part, :])
            gate = gates[slot, part, :]
            dmix = dmixed[slot, part, :]
            half = sigmoid(gate)
            dgate = dmix * normed * (half * (1.0 + gate * (1.0 - half)))
            dgates[block, part, pl.ds(head * VD, VD)] = dgate.astype(jnp.bfloat16)
            dnormed = dmix * (gate * half)
            value = scale * (
                dnormed
                - jnp.mean(dnormed, axis=-1, keepdims=True)
                - normed * jnp.mean(dnormed * normed, axis=-1, keepdims=True)
            )
            dretained[part, :] = value.astype(jnp.bfloat16)

        for_rows(own, body_mix, WHOLE)
        query = queries[block, :, lanes]
        key = keys[: block + 1, :, lanes].reshape(seen, KD)
        raw[:, :seen] = dot_nt(query, key)
        value = values[head, : block + 1].reshape(seen, VD)
        grad[:, :seen] = dot_nt(dretained[...], value)

        def body(part):
            decay = table[slot, part, :seen]
            weighted = raw[part, :seen] * (KD**-0.5) * decay
            dretain = grad[part, :seen]
            total = jnp.sum(weighted, axis=-1, keepdims=True)
            along = jnp.sum(dretain * weighted, axis=-1, keepdims=True)
            inverse = lax.rsqrt(total * total + 1.0)
            retain[part, :seen] = (weighted * inverse).astype(jnp.bfloat16)
            along = along * total * inverse * inverse
            dscores[part, :seen] = (decay * inverse * (dretain - along)).astype(jnp.bfloat16)

        for_rows(own, body, WHOLE)
        dquery = dot_nn(dscores[:, :seen], key) * (KD**-0.5)
        dqueries[block, :, lanes] = dquery.astype(jnp.bfloat16)
        for other in range(block + 1):
            there = pl.ds(other * own, own)
            dkey = dot_tn(dscores[:, there], query)
            dvalue = dot_tn(retain[:, there], dretained[...])
            if other == block:
                dkey_sum[other] = dkey
                dvalue_sum[other] = dvalue
            else:
                dkey_sum[other] += dkey
                dvalue_sum[other] += dvalue

        load_blocks(head * size + block + 2)
        if block == size - 1:
            for other in range(size):
                dkeys[other, :, lanes] = (dkey_sum[other] * (KD**-0.5)).astype(jnp.bfloat16)
                there = pl.ds(head * VD, VD)
                dvalues[other, :, there] = dvalue_sum[other].astype(jnp.bfloat16)
                if head == heads - 1:
                    for kind in range(4):
                        store(kind, other).start()

    def turn():
        for kind in range(2, 4):
            load_whole(kind).wait()
        for owner in range(size):
            turned[:, pl.ds(owner * own, own)] = mixed[owner].T

    def branch_columns(columns):
        return branch[:, :, columns].reshape(size * own, columns.size)

    steps = [
        functools.partial(attend, head, block) for head in range(heads) for block in range(size)
    ]
    streams = []
    for index, (start, count) in enumerate(halves(turned.shape[0])):
        part = turned.at[pl.ds(start, count)]
        streams.append([*cube.make_wide(index, part, branch_columns), *cube.calls(index)])
    streams[0].insert(0, turn)
    streams.append(steps)
    run_streams(streams, ORDERS.get(("retain", size, bits, heads)), {(1, 0): ((0, 1),)})
    for block in range(size):
        for kind in range(4):
            store(kind, block).wait()
    cube.drain()


def retain_back(
    size, bits, queries, keys, values, gates, retained, dmixed, table, mixed, branch
):
    own = queries.shape[1]
    heads = values.shape[0]
    rows, depth = size * own, branch.shape[-1]
    low, full = jnp.bfloat16, jnp.float32
    dma = pltpu.SemaphoreType.DMA
    anywhere = pl.BlockSpec(memory_space=pl.ANY)
    inputs = (queries, keys, values, gates, retained, dmixed, table, mixed, branch)
    slots = [
        jax.ShapeDtypeStruct((2,) + item.shape[2:], item.dtype) if 3 <= place < 7 else item
        for place, item in enumerate(inputs)
    ]
    total = jax.ShapeDtypeStruct((heads * VD, depth), low)
    shapes = (
        queries.shape,
        keys.shape,
        (size, own, heads * VD),
        (size, own, heads * VD),
    )
    return pl.pallas_call(
        functools.partial(retain_kernel, size, bits, heads),
        out_shape=tuple(jax.ShapeDtypeStruct(shape, low) for shape in shapes) + ([total],),
        in_specs=[anywhere] * len(inputs),
        out_specs=(anywhere,) * 4 + ([anywhere],),
        scratch_shapes=[pltpu.VMEM(item.shape, item.dtype) for item in slots]
        + [pltpu.VMEM(shape, low) for shape in shapes]
        + [
            pltpu.VMEM((heads * VD, rows), low),
            pltpu.VMEM((own, rows), full),
            pltpu.VMEM((own, rows), full),
            pltpu.VMEM((own, rows), low),
            pltpu.VMEM((own, rows), low),
            pltpu.VMEM((own, VD), low),
            pltpu.VMEM((size, own, KD), full),
            pltpu.VMEM((size, own, VD), full),
            dma((4,)),
            dma((5, heads, size)),
            dma((4, size)),
        ]
        + cube_scratch(bits, [(half[1], depth) for half in halves(total.shape[0])]),
        compiler_params=pltpu.CompilerParams(
            collective_id=4, has_side_effects=True, vmem_limit_bytes=VMEM_BYTES
        ),
        cost_estimate=pl.CostEstimate(flops=2**34, bytes_accessed=2**26, transcendentals=0),
    )(*inputs)


def cast_kernel(count, *refs):
    for src, dst in zip(refs[:count], refs[count:]):
        dst[...] = src[...].astype(dst.dtype)


def cast_all(items, kept):
    specs = []
    shapes = [jax.ShapeDtypeStruct(item.shape, jnp.float32) for item in items]
    shapes += [jax.ShapeDtypeStruct(item.shape, item.dtype) for item in kept]
    items = [*items, *kept]
    for item in items:
        blocks = max(count for count in BLOCKS if item.shape[0] % (count * LINE) == 0)
        specs.append(
            pl.BlockSpec(
                (item.shape[0] // blocks, item.shape[1]),
                lambda step, last=blocks - 1: (jnp.minimum(step, last), 0),
            )
        )
    return pl.pallas_call(
        functools.partial(cast_kernel, len(items)),
        out_shape=shapes,
        grid=(max(BLOCKS),),
        in_specs=specs,
        out_specs=specs,
        compiler_params=pltpu.CompilerParams(vmem_limit_bytes=VMEM_BYTES),
    )(*items)


def per_device(
    tokens,
    first_gain,
    first_bias,
    query_weight,
    key_weight,
    value_weight,
    gate_weight,
    out_weight,
    second_gain,
    second_bias,
    hidden_gate,
    hidden_up,
    hidden_down,
    segments,
    cotangent,
):
    size = lax.axis_size("tensor")
    group_rows = segments.size
    head_local = query_weight.shape[1] // KD
    head_index = (lax.axis_index("tensor") * head_local + jnp.arange(head_local)).astype(
        jnp.float32
    )
    rates = -jnp.log1p(-jnp.exp2(-5.0 - head_index))
    first_all, queries, keys, values, gates, retained, mixed, table, seed_first = first_part(
        size,
        CHUNKS,
        tokens,
        cotangent,
        first_gain[None],
        first_bias[None],
        segments,
        rates,
        query_weight,
        key_weight,
        value_weight.T,
        gate_weight.T,
    )
    bits = lax.axis_size("dp").bit_length() - 1
    own = tokens.shape[0]
    (
        second_all,
        seed_all,
        inner,
        gate_in_low,
        lin_in_low,
        partial,
        middle,
        grad_middle,
        branch,
        second_sums,
    ) = feed_forward(
        size,
        CHUNKS,
        mixed,
        out_weight,
        tokens,
        cotangent,
        seed_first,
        hidden_gate.T,
        hidden_up.T,
        hidden_down,
        second_gain[None],
        second_bias[None],
    )

    branch_all, grad_mixed, output, feed_grads = feed_back(
        size,
        bits,
        CHUNKS,
        partial,
        out_weight,
        branch,
        middle,
        seed_all,
        second_all,
        (inner, gate_in_low, lin_in_low),
    )
    grad_queries, grad_keys, grad_values, grad_gates, (grad_outw,) = retain_back(
        size,
        bits,
        queries,
        keys,
        values,
        gates,
        retained,
        grad_mixed,
        table,
        mixed,
        branch_all,
    )
    grad_tokens, sums, grads = last_sums(
        size,
        bits,
        CHUNKS,
        (query_weight, key_weight, value_weight.T, gate_weight.T),
        tokens,
        grad_middle,
        first_gain[None],
        second_sums,
        first_all,
        (grad_values, grad_gates, grad_queries, grad_keys),
    )
    grad_sgain, grad_sbias, grad_fgain, grad_fbias = sums[0], sums[1], sums[2], sums[3]
    (
        grad_outw,
        grad_valuew,
        grad_gatew,
        grad_queryw,
        grad_keyw,
        grad_hdown,
        grad_hgate,
        grad_hup,
        output,
        grad_tokens,
    ) = cast_all([grad_outw, *grads, *feed_grads], [output, grad_tokens])
    grad_valuew, grad_gatew, grad_hgate, grad_hup = (
        item.T for item in (grad_valuew, grad_gatew, grad_hgate, grad_hup)
    )
    return (
        output,
        grad_tokens,
        grad_fgain,
        grad_fbias,
        grad_queryw,
        grad_keyw,
        grad_valuew,
        grad_gatew,
        grad_outw,
        grad_sgain,
        grad_sbias,
        grad_hgate,
        grad_hup,
        grad_hdown,
    )


def solution(mesh):
    return jax.shard_map(
        per_device,
        mesh=mesh,
        in_specs=(
            P(("dp", "tensor"), None),
            P(),
            P(),
            P(None, "tensor"),
            P(None, "tensor"),
            P(None, "tensor"),
            P(None, "tensor"),
            P("tensor", None),
            P(),
            P(),
            P(None, "tensor"),
            P(None, "tensor"),
            P("tensor", None),
            P("dp", None),
            P(("dp", "tensor"), None),
        ),
        out_specs=(
            P(("dp", "tensor"), None),
            P(("dp", "tensor"), None),
            P(),
            P(),
            P(None, "tensor"),
            P(None, "tensor"),
            P(None, "tensor"),
            P(None, "tensor"),
            P("tensor", None),
            P(),
            P(),
            P(None, "tensor"),
            P(None, "tensor"),
            P("tensor", None),
        ),
        check_vma=False,
    )
```
